512 devices in a mesh: stream: 32 (over y_hi, z), azim: 16 (over x, y_lo, core).
Axes of the slice: x: 4, y: 4 (y_hi: 2, y_lo: 2; y = y_hi * 2 + y_lo), z: 16, core: 2. Of those that a mesh axis runs over, the one named last changes fastest.
Arguments:
- element_load: float32 [512, 32, 2048], P(None, 'stream', 'azim'), may hold values from -180 to 180
- metric: float32 [3, 512, 32, 2048], P(None, None, 'stream', 'azim'), may hold values from 0.4 to 2.5
- element_order: int32 [32, 2048], P('stream', 'azim'), may hold values from 0 to 127, as said below
Outputs:
- correction: float32 [512, 32, 2048], P(None, 'stream', 'azim')
The draws below stay inside these ranges and needn't reach their ends.
Inputs may be any that keep to these rules, and one draw needn't show every extreme that they name: `element_order`: within each device's block of 128 columns, each row lists every index 0 to 127 once.
All inputs are finite; a program needn't handle non-finite values.
Results may differ from the reference program's by a relative error of at most 0.0003.
Values sent between devices are 32-bit elements; how exact they have to be, the bound alone decides.
No kernel may reach another device: no remote copies, remote signals or barrier semaphores. Data moves between devices by JAX's collectives and lax.ppermute only.
A program may use at most 128 MiB of HBM per device.

```python
import math
import jax
import jax.numpy as jnp
import numpy as np
from jax import lax

FINE_POINTS = 8
NODES = 512
EA = 8
ER = 16
ITERS = 6
NSE = 32
NAER = 2048


def draw_element_load(key, part):
    key = jax.random.fold_in(key, 11)
    noise_key, scale_key = jax.random.split(key)
    stream_place = jnp.arange(NSE, dtype=jnp.float32)[None, :, None] / max(NSE - 1, 1)
    rising = jnp.exp(stream_place * jnp.log(3.0))
    spread = jnp.exp(jax.random.uniform(scale_key, (1, NSE, NAER), minval=0.0, maxval=jnp.log(10.0)))
    base_values = jnp.clip(jax.random.normal(noise_key, (NODES, NSE, NAER)), -6.0, 6.0)
    return (base_values * spread * rising).astype(jnp.float32)


def draw_element_order(key, part):
    key = jax.random.fold_in(key, 23)
    per_device = EA * ER
    blocks = NSE * (NAER // per_device)
    block_keys = jax.random.split(key, blocks)
    slot_table = jax.vmap(lambda one_key: jax.random.permutation(one_key, per_device))(block_keys)
    return slot_table.reshape(NSE, NAER).astype(jnp.int32)


def shard_levels(rng, extent, pieces, low, high):
    gain, own = 1.0, jax.random.fold_in(rng, 6)
    for position, shards_of in pieces:
        heights = jnp.exp(jax.random.uniform(jax.random.fold_in(own, position), (shards_of,), jnp.float32, low / len(pieces), high / len(pieces)))
        gain = gain * jnp.repeat(heights, extent[position] // shards_of).reshape([-1 if axis == position else 1 for axis in range(len(extent))])
    return gain


def setup_inputs(seed: int = 0) -> dict:
    key_list = jax.random.split(jax.random.key(seed), 4)
    return {
        "element_load": draw_element_load(jax.random.fold_in(key_list[3], 71), 0),
        "metric": jnp.clip(jnp.exp(math.log(2.5) - 1.8325814 * jax.random.uniform(key_list[1], (3, NODES, NSE, NAER), jnp.float32) ** shard_levels(key_list[1], (3, NODES, NSE, NAER), ((2, 32), (3, 16)), -0.2, 0.2)), 0.4, 2.5),
        "element_order": draw_element_order(jax.random.fold_in(key_list[3], 71), 0),
    }


LOW_EIG = 0.3
HIGH_EIG = 3.0
CENTER = 0.5 * (HIGH_EIG + LOW_EIG)
HALF_WIDTH = 0.5 * (HIGH_EIG - LOW_EIG)
FIRST_RHO = HALF_WIDTH / CENTER
SECOND_RHO = 1.0 / (2.0 * CENTER / HALF_WIDTH - FIRST_RHO)
EINSUM_FORMS = ("ia,abcsx->ibcsx", "ib,abcsx->aicsx", "ic,abcsx->abisx")


def legendre_pair(degree, places):
    previous = places * 0.0 + 1.0
    current = places.copy()
    for order_index in range(2, degree + 1):
        following = ((2 * order_index - 1) * places * current - (order_index - 1) * previous) / order_index
        previous = current
        current = following
    return current, previous


def gll_table(points):
    degree = points - 1
    places = np.cos(np.pi * np.arange(points) / degree)
    for newton_step in range(60):
        top_value, below_value = legendre_pair(degree, places)
        places = places - (places * top_value - below_value) / (points * top_value)
    gll_nodes = np.sort(places)
    gll_nodes[0] = -1.0
    gll_nodes[-1] = 1.0
    at_nodes = legendre_pair(degree, gll_nodes)[0]
    gll_weights = 2.0 / (degree * (degree + 1) * at_nodes ** 2)
    derivative = np.zeros((points, points))
    for row_index in range(points):
        for col_index in range(points):
            if row_index != col_index:
                derivative[row_index, col_index] = at_nodes[row_index] / (at_nodes[col_index] * (gll_nodes[row_index] - gll_nodes[col_index]))
    derivative[0, 0] = -degree * (degree + 1) / 4.0
    derivative[-1, -1] = degree * (degree + 1) / 4.0
    return gll_nodes, gll_weights, derivative


def lagrange_table(source_nodes, target_nodes):
    weights_out = np.ones((len(target_nodes), len(source_nodes)))
    for col_index in range(len(source_nodes)):
        for other_index in range(len(source_nodes)):
            if other_index != col_index:
                weights_out[:, col_index] *= (target_nodes - source_nodes[other_index]) / (source_nodes[col_index] - source_nodes[other_index])
    return weights_out


def level_tables(points):
    gll_nodes, gll_weights, derivative = gll_table(points)
    weight_cube = gll_weights[:, None, None] * gll_weights[None, :, None] * gll_weights[None, None, :]
    positions = np.arange(points)
    edge_factor = np.where((positions == 0) | (positions == points - 1), 0.5, 1.0)
    share_cube = edge_factor[:, None, None] * edge_factor[None, :, None] * edge_factor[None, None, :]
    return (jnp.asarray(derivative, dtype=jnp.float32), jnp.asarray(weight_cube[:, :, :, None, None], dtype=jnp.float32), jnp.asarray(share_cube[:, :, :, None, None], dtype=jnp.float32))


def prolong_table(coarse_points, fine_points):
    return jnp.asarray(lagrange_table(gll_table(coarse_points)[0], gll_table(fine_points)[0]), dtype=jnp.float32)


def apply_axis(matrix, values, axis_number):
    return jnp.einsum(EINSUM_FORMS[axis_number], matrix, values, precision=lax.Precision.HIGHEST)


def apply_cube(matrix, values):
    for axis_number in range(3):
        values = apply_axis(matrix, values, axis_number)
    return values


def element_operator(values, level_metric, derivative):
    result = apply_axis(derivative.T, level_metric[0] * apply_axis(derivative, values, 0), 0)
    for axis_number in (1, 2):
        gradient = apply_axis(derivative, values, axis_number)
        result = result + apply_axis(derivative.T, level_metric[axis_number] * gradient, axis_number)
    return result


def element_diagonal(level_metric, derivative):
    squared = (derivative * derivative).T
    result = apply_axis(squared, level_metric[0], 0)
    for axis_number in (1, 2):
        result = result + apply_axis(squared, level_metric[axis_number], axis_number)
    return result


def interior_mask(points, columns):
    radial_node = jnp.arange(points, dtype=jnp.int32)[None, None, :, None, None]
    radial_element = (jnp.arange(columns, dtype=jnp.int32) % ER)[None, None, None, None, :]
    on_wall = ((radial_node == 0) & (radial_element == 0)) | ((radial_node == points - 1) & (radial_element == ER - 1))
    return jnp.where(on_wall, 0.0, 1.0).astype(jnp.float32)


def coarse_metric(log_metric, sample, weight_cube):
    return jnp.stack([jnp.exp(apply_cube(sample, log_metric[direction])) for direction in range(3)]) * weight_cube


def assemble(values):
    points = values.shape[0]
    streams = values.shape[3]
    shaped = values.reshape(points, points, points, streams, -1, ER)
    lower_face = shaped[:, :, 0]
    upper_face = shaped[:, :, -1]
    shared = upper_face[..., :-1] + lower_face[..., 1:]
    zero_face = jnp.zeros_like(lower_face[..., :1])
    shaped = shaped.at[:, :, 0].set(jnp.concatenate([zero_face, shared], axis=-1))
    shaped = shaped.at[:, :, -1].set(jnp.concatenate([shared, zero_face], axis=-1))
    lower_face = shaped[0]
    upper_face = shaped[-1]
    shared = lower_face + jnp.roll(upper_face, 1, axis=2)
    shaped = shaped.at[0].set(shared).at[-1].set(jnp.roll(shared, -1, axis=2))
    lower_face = shaped[:, 0]
    upper_face = shaped[:, -1]
    shared = lower_face + jnp.roll(upper_face, 1, axis=3)
    shaped = shaped.at[:, 0].set(shared).at[:, -1].set(jnp.roll(shared, -1, axis=3))
    return shaped.reshape(values.shape)


def inverse_diagonal(level_metric, derivative, points, columns):
    diagonal = assemble(element_diagonal(level_metric, derivative))
    mask = interior_mask(points, columns)
    return mask / (diagonal + 1.0 - mask)


def pre_smooth(residual, operate, inverse):
    update = inverse * residual / CENTER
    solution = update
    residual = residual - operate(update)
    update = SECOND_RHO * FIRST_RHO * update + (2.0 * SECOND_RHO / HALF_WIDTH) * inverse * residual
    solution = solution + update
    residual = residual - operate(update)
    return solution, residual


def post_smooth(solution, added, residual, operate, inverse):
    solution = solution + added
    residual = residual - operate(added)
    update = inverse * residual / CENTER
    solution = solution + update
    residual = residual - operate(update)
    update = SECOND_RHO * FIRST_RHO * update + (2.0 * SECOND_RHO / HALF_WIDTH) * inverse * residual
    return solution + update


def coarse_solve(residual, operate, inverse, share_cube):
    solution = jnp.zeros_like(residual)
    precond = inverse * residual
    direction = precond
    gamma_now = jnp.sum(share_cube * residual * precond)
    for step_index in range(ITERS):
        applied = operate(direction)
        step_size = gamma_now / jnp.sum(share_cube * direction * applied)
        solution = solution + step_size * direction
        residual = residual - step_size * applied
        if step_index + 1 < ITERS:
            precond = inverse * residual
            gamma_next = jnp.sum(share_cube * residual * precond)
            direction = precond + (gamma_next / gamma_now) * direction
            gamma_now = gamma_next
    return solution


def reference(element_load, metric, element_order):
    streams = element_load.shape[1]
    columns = element_load.shape[2]
    fine_points = FINE_POINTS
    mid_points = FINE_POINTS // 2
    low_points = 2
    block_size = EA * ER
    offset = (jnp.arange(columns, dtype=jnp.int32) // block_size) * block_size
    global_slot = (element_order + offset[None, :]).astype(jnp.int32)
    ordered = jax.vmap(lambda row_values, row_slots: jnp.take(row_values, row_slots, axis=2), in_axes=(2, 0), out_axes=2)(metric, global_slot)
    fine_g = ordered.reshape(3, fine_points, fine_points, fine_points, streams, columns)
    fine_deriv, fine_weights, fine_share = level_tables(fine_points)
    mid_deriv, mid_weights, mid_share = level_tables(mid_points)
    low_deriv, low_weights, low_share = level_tables(low_points)
    mid_up = prolong_table(mid_points, fine_points)
    low_up = prolong_table(low_points, mid_points)
    log_metric = jnp.log(fine_g)
    fine_metric = fine_g * fine_weights
    mid_metric = coarse_metric(log_metric, prolong_table(fine_points, mid_points), mid_weights)
    low_metric = coarse_metric(log_metric, prolong_table(fine_points, low_points), low_weights)

    def fine_operate(values):
        return assemble(element_operator(values, fine_metric, fine_deriv))

    def mid_operate(values):
        return assemble(element_operator(values, mid_metric, mid_deriv))

    def low_operate(values):
        return assemble(element_operator(values, low_metric, low_deriv))

    fine_inverse = inverse_diagonal(fine_metric, fine_deriv, fine_points, columns)
    mid_inverse = inverse_diagonal(mid_metric, mid_deriv, mid_points, columns)
    low_inverse = inverse_diagonal(low_metric, low_deriv, low_points, columns)
    fine_residual = assemble(element_load.reshape(fine_points, fine_points, fine_points, streams, columns))
    fine_solution, fine_after = pre_smooth(fine_residual, fine_operate, fine_inverse)
    mid_residual = assemble(apply_cube(mid_up.T, fine_share * fine_after))
    mid_solution, mid_after = pre_smooth(mid_residual, mid_operate, mid_inverse)
    low_residual = assemble(apply_cube(low_up.T, mid_share * mid_after))
    low_solution = coarse_solve(low_residual, low_operate, low_inverse, low_share)
    mid_final = post_smooth(mid_solution, apply_cube(low_up, low_solution), mid_after, mid_operate, mid_inverse)
    fine_final = post_smooth(fine_solution, apply_cube(mid_up, mid_final), fine_after, fine_operate, fine_inverse)
    return fine_final.reshape(NODES, streams, columns)
```

```python
import jax
import jax.numpy as jnp
import numpy as np
from jax import lax
from jax.experimental import pallas as pl
from jax.experimental.pallas import tpu as pltpu
from jax.sharding import PartitionSpec as P

ITERS = 6
LOW_EIG = 0.3
HIGH_EIG = 3.0
CENTER = 0.5 * (HIGH_EIG + LOW_EIG)
HALF_WIDTH = 0.5 * (HIGH_EIG - LOW_EIG)
FIRST_RHO = HALF_WIDTH / CENTER
SECOND_RHO = 1.0 / (2.0 * CENTER / HALF_WIDTH - FIRST_RHO)
KEEP = SECOND_RHO * FIRST_RHO
GAIN = 2.0 * SECOND_RHO / HALF_WIDTH
LANES = 128
HALF = 64
F32 = jnp.float32


def legendre_pair(degree, places):
    previous = places * 0.0 + 1.0
    current = places.copy()
    for k in range(2, degree + 1):
        following = ((2 * k - 1) * places * current - (k - 1) * previous) / k
        previous = current
        current = following
    return (current, previous)


def gll_table(points):
    degree = points - 1
    places = np.cos(np.pi * np.arange(points) / degree)
    for _ in range(60):
        top, below = legendre_pair(degree, places)
        places = places - (places * top - below) / (points * top)
    nodes = np.sort(places)
    nodes[0] = -1.0
    nodes[-1] = 1.0
    at_nodes = legendre_pair(degree, nodes)[0]
    weights = 2.0 / (degree * (degree + 1) * at_nodes**2)
    deriv = np.zeros((points, points))
    for i in range(points):
        for j in range(points):
            if i != j:
                deriv[i, j] = at_nodes[i] / (at_nodes[j] * (nodes[i] - nodes[j]))
    deriv[0, 0] = -degree * (degree + 1) / 4.0
    deriv[-1, -1] = degree * (degree + 1) / 4.0
    return (nodes, weights, deriv)


def lagrange_table(source, target):
    out = np.ones((len(target), len(source)))
    for j in range(len(source)):
        for k in range(len(source)):
            if k != j:
                out[:, j] *= (target - source[k]) / (source[j] - source[k])
    return out


N8, W8, D8 = gll_table(8)
N4, W4, D4 = gll_table(4)
N2, W2, D2 = gll_table(2)


def kron3(a, b, c):
    return np.kron(np.kron(a, b), c)


def cube(w):
    return (w[:, None, None] * w[None, :, None] * w[None, None, :]).reshape(-1)


def share(n):
    edge = np.ones(n)
    edge[0] = edge[-1] = 0.5
    return cube(edge)


def grads(d):
    i = np.eye(d.shape[0])
    return [kron3(d, i, i), kron3(i, d, i), kron3(i, i, d)]


def f32(x):
    return np.asarray(x, np.float32)


def lanes_of(column):
    return np.repeat(f32(column)[:, None], LANES, axis=1)


UP8 = lagrange_table(N4, N8)
UP4 = lagrange_table(N2, N4)
TO4 = lagrange_table(N8, N4)
TO2 = lagrange_table(N8, N2)

C_BD = f32(np.kron(np.eye(32), D8))
C_BDT = f32(np.kron(np.eye(32), D8.T))
C_BSQ = f32(np.kron(np.eye(32), (D8 * D8).T))
C_SAMPLE = f32(np.concatenate([kron3(TO4, TO4, TO4), kron3(TO2, TO2, TO2)]))
C_UP8 = f32(kron3(UP8, UP8, UP8))
C_DOWN8 = f32(kron3(UP8, UP8, UP8).T)
C_UP4 = f32(kron3(UP4, UP4, UP4))
C_DOWN4 = f32(kron3(UP4, UP4, UP4).T)
C_G4 = f32(np.concatenate(grads(D4)))
C_G4T = f32(np.concatenate(grads(D4)).T)
C_SQ4 = f32((np.concatenate(grads(D4)) ** 2).T)
C_W8 = lanes_of(W8)
C_W4 = lanes_of(cube(W4))
C_M4 = lanes_of(share(4))


def dot(a, b):
    return jnp.dot(a, b, preferred_element_type=F32, precision=lax.Precision.HIGHEST)


def iota(rows, axis):
    return lax.broadcasted_iota(jnp.int32, (rows, LANES), axis)


def wide(ref, start, size):
    return jnp.concatenate([ref[0, start : start + size], ref[1, start : start + size]], axis=1)


def put(ref, start, size, value):
    ref[0, start : start + size] = value[:, :LANES]
    ref[1, start : start + size] = value[:, LANES:]


def total(terms):
    out = terms[0]
    for t in terms[1:]:
        out = out + t
    return out


def contract(v, matrix, sign):
    n = len(v)
    h = n // 2
    even = [v[k] + v[n - 1 - k] for k in range(h)]
    odd = [v[k] - v[n - 1 - k] for k in range(h)]
    out = [None] * n
    for i in range(h):
        p = total([even[k] * float(0.5 * (matrix[i, k] + matrix[i, n - 1 - k])) for k in range(h)])
        q = total([odd[k] * float(0.5 * (matrix[i, k] - matrix[i, n - 1 - k])) for k in range(h)])
        out[i] = p + q
        out[n - 1 - i] = q - p if sign < 0 else p - q
    return out


def fine_rows(s, a):
    return s * 64 + a * 8


def fine_apply(u, g, acc, bd, bdt):
    for c in range(2):
        flux = dot(bd[...], wide(u, 256 * c, 256)) * wide(g, 1024 + 256 * c, 256)
        put(acc, 256 * c, 256, dot(bdt[...], flux))
    for h in range(2):
        for axis in range(2):
            for fixed in range(8):
                at = [fine_rows(k, fixed) if axis == 0 else fine_rows(fixed, k) for k in range(8)]
                grad = contract([u[h, r : r + 8] for r in at], D8, -1)
                flux = [grad[k] * g[h, 512 * axis + r : 512 * axis + r + 8] for k, r in enumerate(at)]
                back = contract(flux, D8.T, -1)
                for k, r in enumerate(at):
                    acc[h, r : r + 8] += back[k]


def left(x0, x1):
    near = iota(x0.shape[0], 1) < LANES - 16
    y0, y1 = pltpu.roll(x0, LANES - 16, 1), pltpu.roll(x1, LANES - 16, 1)
    return jnp.where(near, y0, y1), jnp.where(near, y1, y0)


def right(x0, x1):
    near = iota(x0.shape[0], 1) >= 16
    y0, y1 = pltpu.roll(x0, 16, 1), pltpu.roll(x1, 16, 1)
    return jnp.where(near, y0, y1), jnp.where(near, y1, y0)


def join_radial(x, points):
    rows = x.shape[1] // points
    place = iota(rows, 1) % 16
    first, last = pl.ds(0, rows, stride=points), pl.ds(points - 1, rows, stride=points)
    for h in range(2):
        view = x.at[h]
        low, high = view[first, :], view[last, :]
        view[first, :] = jnp.where(place == 0, 0.0, low + pltpu.roll(high, 1, 1))
        view[last, :] = jnp.where(place == 15, 0.0, high + pltpu.roll(low, LANES - 1, 1))


def join_fine(x):
    join_radial(x, 8)
    for s in range(8):
        lo, hi = fine_rows(s, 0), fine_rows(s, 7)
        low = [x[h, lo : lo + 8] for h in range(2)]
        high = [x[h, hi : hi + 8] for h in range(2)]
        to_low, to_high = right(*high), left(*low)
        for h in range(2):
            x[h, lo : lo + 8] = low[h] + to_low[h]
            x[h, hi : hi + 8] = high[h] + to_high[h]


def join_mid(x):
    join_radial(x, 4)
    first = iota(8, 0) < 4
    for s in range(4):
        lo, hi = s * 16, s * 16 + 8
        low = [x[h, lo : lo + 8] for h in range(2)]
        high = [x[h, hi : hi + 8] for h in range(2)]
        to_low = right(*[pltpu.roll(t, 4, 0) for t in high])
        to_high = left(*[pltpu.roll(t, 4, 0) for t in low])
        for h in range(2):
            x[h, lo : lo + 8] = low[h] + jnp.where(first, to_low[h], 0.0)
            x[h, hi : hi + 8] = high[h] + jnp.where(first, 0.0, to_high[h])


def plus_faces(h, r, value, below, above, plane, last, offset=0):
    if r < plane:
        return value + below[h, offset + r : offset + r + 8]
    if r >= last:
        return value + above[h, offset + r - last : offset + r - last + 8]
    return value


def fine_full(x, below, above, h, r, offset=0):
    return plus_faces(h, r, x[h, r : r + 8], below, above, 64, 448, offset)


def mid_full(x, below, above, h, r, offset=0):
    return plus_faces(h, r, x[h, r : r + 8], below, above, 16, 48, offset)


def send_faces(x, top, bottom, plane, offset=0):
    rows = x.shape[1]
    for h in range(2):
        bottom[h, offset : offset + plane] = x[h, 0:plane]
        top[h, offset : offset + plane] = x[h, rows - plane : rows]


def wall_mask(points):
    place, node = iota(8, 1) % 16, iota(8, 0) % points
    return ((node == 0) & (place == 0)) | ((node == points - 1) & (place == 15))


def own_part(half0, half1):
    near = iota(half0.shape[0], 1) < HALF
    return pltpu.roll(jnp.where(near, half1, half0), HALF, 1)


def tiles(rows):
    return [(h, r) for h in range(2) for r in range(0, rows, 8)]


def mid_apply(u, g4, acc, gm, gmt):
    flux = dot(gm[...], wide(u, 0, 64)) * wide(g4, 0, 192)
    put(acc, 0, 64, dot(gmt[...], flux))


def order_kernel(metric, load, order, rolled, up, down):
    near = iota(8, 1) < HALF
    slots = jnp.broadcast_to(pltpu.roll(order[...], HALF, 1), (8, LANES))

    def body(i, carry):
        r = pl.multiple_of(i * 8, 8)
        a = jnp.take_along_axis(metric[pl.ds(r, 8), :], slots, axis=1)
        rolled[pl.ds(r, 8), :] = a
        return carry

    lax.fori_loop(0, 192, body, 0, unroll=8)
    for r in range(0, 512, 8):
        rolled[1536 + r : 1536 + r + 8] = pltpu.roll(load[r : r + 8], HALF, 1)
    for r in range(0, 1024, 8):
        a, b = rolled[r : r + 8], rolled[1024 + r : 1024 + r + 8]
        up[r : r + 8] = jnp.where(near, a, pltpu.roll(b, HALF, 1))
        down[r : r + 8] = jnp.where(near, pltpu.roll(a, HALF, 1), b)


def setup_kernel(
    rolled, before, after, w8, w4, sample, bsq, sq4,
    g8, g4, load, diag8, diag4, edges, top, bottom, logs,
):
    near = iota(8, 1) < HALF
    wr = w8[...]

    def place(row, half0, half1):
        r = row % 512
        if row >= 1536:
            load[0, r : r + 8] = half0
            load[1, r : r + 8] = half1
            return
        scale = wr * float(W8[r // 64] * W8[(r // 8) % 8])
        g8[0, row : row + 8] = half0 * scale
        g8[1, row : row + 8] = half1 * scale
        logs[row : row + 8, :LANES] = jnp.log(half0)
        logs[row : row + 8, LANES:] = jnp.log(half1)

    for r in range(0, 1024, 8):
        a, b = rolled[r : r + 8], rolled[1024 + r : 1024 + r + 8]
        p, n = before[r : r + 8], after[r : r + 8]
        place(r, jnp.where(near, p, a), jnp.where(near, a, pltpu.roll(n, HALF, 1)))
        place(1024 + r, jnp.where(near, pltpu.roll(p, HALF, 1), b), jnp.where(near, b, n))
    low = []
    for d in range(3):
        coarse = jnp.exp(dot(sample[...], logs[512 * d : 512 * d + 512]))
        w = jnp.concatenate([w4[...], w4[...]], axis=1)
        put(g4, 64 * d, 64, coarse[:64] * w)
        low.append([coarse[64:72, :LANES], coarse[64:72, LANES:]])
    for c in range(2):
        put(diag8, 256 * c, 256, dot(bsq[...], wide(g8, 1024 + 256 * c, 256)))
    square = (D8 * D8).T
    for h in range(2):
        for axis in range(2):
            for fixed in range(8):
                at = [fine_rows(k, fixed) if axis == 0 else fine_rows(fixed, k) for k in range(8)]
                back = contract([g8[h, 512 * axis + r : 512 * axis + r + 8] for r in at], square, 1)
                for k, r in enumerate(at):
                    diag8[h, r : r + 8] += back[k]
    put(diag4, 0, 64, dot(sq4[...], wide(g4, 0, 192)))
    for x in (load, diag8):
        join_fine(x)
    join_mid(diag4)
    send_faces(load, top, bottom, 64)
    send_faces(diag8, top, bottom, 64, 64)
    send_faces(diag4, top, bottom, 16, 128)

    def corner(d, i, j, k):
        row = 4 * i + 2 * j + k
        return [t[row : row + 1] for t in low[d]]

    def add(x, y):
        return [x[0] + y[0], x[1] + y[1]]

    def quarter(x):
        return [0.25 * x[0], 0.25 * x[1]]

    def outward(x):
        return [pltpu.roll(x[0], 1, 1), pltpu.roll(x[1], 1, 1)]

    es = [[quarter(add(corner(0, 0, j, k), corner(0, 1, j, k))) for k in range(2)] for j in range(2)]
    ea = [[quarter(add(corner(1, i, 0, k), corner(1, i, 1, k))) for k in range(2)] for i in range(2)]
    er = [[quarter(add(corner(2, i, j, 0), corner(2, i, j, 1))) for j in range(2)] for i in range(2)]
    col = [add(es[0][k], list(right(*es[1][k]))) for k in range(2)]
    edge_s = add(col[0], outward(col[1]))
    edge_a = [add(ea[i][0], outward(ea[i][1])) for i in range(2)]
    edge_r = [add(er[i][0], list(right(*er[i][1]))) for i in range(2)]
    off_wall = iota(1, 1) % 16 != 0
    rows = [jnp.where(off_wall, own_part(*x), 0.0) for x in (edge_s, edge_a[0], edge_a[1])]
    rows += [own_part(*x) for x in edge_r]
    edges[...] = jnp.concatenate(rows + [jnp.zeros((3, LANES), F32)], axis=0)


def first_kernel(
    load, diag8, diag4, below, above, g8, bd, bdt, res, inv8, inv4, acc, top, bottom, u
):
    wall8, wall4 = wall_mask(8), wall_mask(4)
    for h, r in tiles(512):
        diag = fine_full(diag8, below, above, h, r, 64)
        inv = jnp.where(wall8, 0.0, 1.0 / jnp.where(wall8, 1.0, diag))
        full = fine_full(load, below, above, h, r)
        res[h, r : r + 8] = full
        inv8[h, r : r + 8] = inv
        u[h, r : r + 8] = inv * full * (1.0 / CENTER)
    for h, r in tiles(64):
        diag = mid_full(diag4, below, above, h, r, 128)
        inv4[h, r : r + 8] = jnp.where(wall4, 0.0, 1.0 / jnp.where(wall4, 1.0, diag))
    fine_apply(u, g8, acc, bd, bdt)
    join_fine(acc)
    send_faces(acc, top, bottom, 64)


def second_kernel(
    res, inv8, acc, below, above, g8, bd, bdt, down8, sol, rest, acc2, t4, top, bottom, u, part
):
    edge = jnp.where((iota(8, 0) == 0) | (iota(8, 0) == 7), 0.5, 1.0)
    for h, r in tiles(512):
        inv, before = inv8[h, r : r + 8], res[h, r : r + 8]
        now = before - fine_full(acc, below, above, h, r)
        old = inv * before * (1.0 / CENTER)
        new = KEEP * old + GAIN * inv * now
        rest[h, r : r + 8] = now
        sol[h, r : r + 8] = old + new
        u[h, r : r + 8] = new
    fine_apply(u, g8, acc2, bd, bdt)
    for h, r in tiles(512):
        s, a = r // 64, (r // 8) % 8
        scale = (0.5 if s in (0, 7) else 1.0) * (0.5 if a in (0, 7) else 1.0)
        part[r : r + 8, h * LANES : h * LANES + LANES] = (
            rest[h, r : r + 8] * (edge * scale) - acc2[h, r : r + 8]
        )
    put(t4, 0, 64, dot(down8[...], part[...]))
    join_mid(t4)
    join_fine(acc2)
    send_faces(acc2, top, bottom, 64)
    send_faces(t4, top, bottom, 16, 64)


def third_kernel(t4, inv4, below, above, g4, gm, gmt, res, acc, top, bottom, u):
    for h, r in tiles(64):
        full = mid_full(t4, below, above, h, r, 64)
        res[h, r : r + 8] = full
        u[h, r : r + 8] = inv4[h, r : r + 8] * full * (1.0 / CENTER)
    mid_apply(u, g4, acc, gm, gmt)
    join_mid(acc)
    send_faces(acc, top, bottom, 16)


def fourth_kernel(
    res, acc, inv4, below, above, g4, gm, gmt, m4, down4, corners, up, down, keep, part
):
    for h, r in tiles(64):
        inv, before = inv4[h, r : r + 8], res[h, r : r + 8]
        now = before - mid_full(acc, below, above, h, r)
        old = inv * before * (1.0 / CENTER)
        new = KEEP * old + GAIN * inv * now
        keep[h, r : r + 8] = now
        keep[h, 64 + r : 72 + r] = new
        keep[h, 128 + r : 136 + r] = old + new
    up[...] = keep[1]
    down[...] = keep[0]
    flux = dot(gm[...], wide(keep, 64, 64)) * wide(g4, 0, 192)
    put(part, 0, 64, dot(gmt[...], flux))
    for h, r in tiles(64):
        part[h, r : r + 8] = m4[r : r + 8] * keep[h, r : r + 8] - part[h, r : r + 8]
    low = dot(down4[...], wide(part, 0, 64))
    near = iota(8, 1) < HALF
    half0 = jnp.where(near, 0.0, low[:, :LANES])
    half1 = jnp.where(near, low[:, LANES:], 0.0)

    def corner(i, j, k):
        row = 4 * i + 2 * j + k
        return [half0[row : row + 1], half1[row : row + 1]]

    mine, extra = [], []
    for i in range(2):
        columns = []
        for k in range(2):
            shifted = right(*corner(i, 1, k))
            straight = corner(i, 0, k)
            columns.append([straight[0] + shifted[0], straight[1] + shifted[1]])
        both = [columns[0][h] + pltpu.roll(columns[1][h], 1, 1) for h in range(2)]
        both = [jnp.where(iota(1, 1) % 16 == 0, 0.0, t) for t in both]
        mine.append(own_part(*both))
        extra.append(jnp.where(iota(1, 1) < 16, pltpu.roll(both[1], HALF, 1), 0.0))
    corners[...] = jnp.concatenate(mine + extra, axis=0)


def side_kernel(keep, before, after, g4, gm, gmt, wider, acc, top, bottom, u):
    near = iota(8, 1) < HALF
    for r in range(0, 192, 8):
        half0 = jnp.where(near, before[r : r + 8], keep[0, r : r + 8])
        half1 = jnp.where(near, keep[1, r : r + 8], after[r : r + 8])
        for h, half in enumerate((half0, half1)):
            wider[h, r : r + 8] = half
            if 64 <= r < 128:
                u[h, r - 64 : r - 56] = half
    mid_apply(u, g4, acc, gm, gmt)
    join_mid(acc)
    send_faces(acc, top, bottom, 16)


def rest_kernel(wider, acc, below, above, rest8, acc8, below8, above8, s4, s8):
    for h, r in tiles(64):
        s4[h, r : r + 8] = wider[h, r : r + 8] - mid_full(acc, below, above, h, r)
    for h, r in tiles(512):
        s8[h, r : r + 8] = rest8[h, r : r + 8] - fine_full(acc8, below8, above8, h, r)


def coarse_kernel(
    place, corners, edges, g4, gm, gmt, up4, e4, acc, top, bottom, vals, x2, es, ea, er, dg, ri
):
    ns = x2.shape[0]
    na = x2.shape[1] // LANES
    width = na * LANES

    def field(ref, rows, k):
        return [ref[pl.ds(d * rows + k, ns, stride=na * rows), :] for d in range(na)]

    def later(x, axis=0):
        return pltpu.roll(x, 1, axis)

    def roll_l(x, k):
        return pltpu.roll(x, k % width, 1)

    wall = lax.broadcasted_iota(jnp.int32, (ns, width), 1) % 16 == 0
    lo, hi = field(corners, 4, 0), field(corners, 4, 1)
    lo_x, hi_x = field(corners, 4, 2), field(corners, 4, 3)
    low = jnp.concatenate([lo[d] + lo_x[d - 1] for d in range(na)], axis=1)
    high = jnp.concatenate([hi[d] + hi_x[d - 1] for d in range(na)], axis=1)
    r = low + later(high)
    es[...] = jnp.concatenate(field(edges, 8, 0), axis=1)
    ea[...] = jnp.concatenate(field(edges, 8, 1), axis=1) + later(
        jnp.concatenate(field(edges, 8, 2), axis=1)
    )
    er[...] = jnp.concatenate(field(edges, 8, 3), axis=1) + later(
        jnp.concatenate(field(edges, 8, 4), axis=1)
    )
    sum_all = es[...] + later(es[...]) + ea[...] + roll_l(ea[...], 16) + er[...] + roll_l(er[...], 1)
    dg[...] = jnp.where(wall, 0.0, sum_all)
    ri[...] = jnp.where(wall, 0.0, 1.0 / jnp.where(wall, 1.0, sum_all))

    def apply(p):
        q = dg[...] * p
        q = q - es[...] * pltpu.roll(p, ns - 1, 0) - later(es[...] * p)
        q = q - ea[...] * roll_l(p, -16) - roll_l(ea[...] * p, 16)
        q = q - er[...] * roll_l(p, -1) - roll_l(er[...] * p, 1)
        return jnp.where(wall, 0.0, q)

    def inner(a, b):
        return jnp.sum(jnp.sum(a * b, axis=0, keepdims=True), axis=1, keepdims=True)

    z = ri[...] * r
    p = z
    gz = inner(r, z)
    x = jnp.zeros_like(r)
    for it in range(ITERS):
        q = apply(p)
        alpha = gz / inner(p, q)
        x = x + alpha * p
        if it + 1 < ITERS:
            r = r - alpha * q
            z = ri[...] * r
            new = inner(r, z)
            p = z + (new / gz) * p
            gz = new
    x2[...] = x

    s, a = place[0], place[1]
    s_next = lax.rem(s + 1, ns)
    blocks = [lax.rem(a + na - 1, na), a, lax.rem(a + 1, na)]
    for i, row in enumerate((s, s_next)):
        line = x2[pl.ds(row, 1), :]
        for j in range(2):
            for k in range(2):
                n = 4 * i + 2 * j + k
                vals[n : n + 1, :] = roll_l(line, -(16 * j + k)) if j + k else line
    near = iota(8, 1) < HALF
    b = [
        pltpu.roll(vals[:, pl.ds(pl.multiple_of(t * LANES, LANES), LANES)], HALF, 1) for t in blocks
    ]
    ext = jnp.concatenate([jnp.where(near, b[0], b[1]), jnp.where(near, b[1], b[2])], axis=1)
    put(e4, 0, 64, dot(up4[...], ext))
    mid_apply(e4, g4, acc, gm, gmt)
    join_mid(acc)
    send_faces(acc, top, bottom, 16)


def fifth_kernel(
    s4, wider, e4, acc, below, above, inv4, g4, gm, gmt, res, u, sol, acc2, top, bottom
):
    for h, r in tiles(64):
        now = s4[h, r : r + 8] - mid_full(acc, below, above, h, r)
        new = inv4[h, r : r + 8] * now * (1.0 / CENTER)
        res[h, r : r + 8] = now
        u[h, r : r + 8] = new
        sol[h, r : r + 8] = wider[h, 128 + r : 136 + r] + e4[h, r : r + 8] + new
    mid_apply(u, g4, acc2, gm, gmt)
    join_mid(acc2)
    send_faces(acc2, top, bottom, 16)


def sixth_kernel(
    res, u, sol, acc, below, above, inv4, up8, g8, bd, bdt, e8, acc2, top, bottom, y4
):
    for h, r in tiles(64):
        now = res[h, r : r + 8] - mid_full(acc, below, above, h, r)
        new = KEEP * u[h, r : r + 8] + GAIN * inv4[h, r : r + 8] * now
        y4[h, r : r + 8] = sol[h, r : r + 8] + new
    put(e8, 0, 512, dot(up8[...], wide(y4, 0, 64)))
    fine_apply(e8, g8, acc2, bd, bdt)
    join_fine(acc2)
    send_faces(acc2, top, bottom, 64)


def seventh_kernel(
    s8, sol, e8, acc, below, above, inv8, g8, bd, bdt, res, out, u, acc2, top, bottom
):
    for h, r in tiles(512):
        now = s8[h, r : r + 8] - fine_full(acc, below, above, h, r)
        new = inv8[h, r : r + 8] * now * (1.0 / CENTER)
        res[h, r : r + 8] = now
        u[h, r : r + 8] = new
        out[h, r : r + 8] = sol[h, r : r + 8] + e8[h, r : r + 8] + new
    fine_apply(u, g8, acc2, bd, bdt)
    join_fine(acc2)
    send_faces(acc2, top, bottom, 64)


def last_kernel(res, sol, u, acc, below, above, inv8, out):
    for r in range(0, 512, 8):
        halves = []
        for h in range(2):
            now = res[h, r : r + 8] - fine_full(acc, below, above, h, r)
            new = KEEP * u[h, r : r + 8] + GAIN * inv8[h, r : r + 8] * now
            halves.append(sol[h, r : r + 8] + new)
        out[r : r + 8] = own_part(*halves)


def call(kernel, args, outs, scratch=(), scalars=0):
    vmem = pl.BlockSpec(memory_space=pltpu.VMEM)
    smem = pl.BlockSpec(memory_space=pltpu.SMEM)
    return pl.pallas_call(
        kernel,
        out_shape=[jax.ShapeDtypeStruct(s, F32) for s in outs],
        in_specs=[smem] * scalars + [vmem] * (len(args) - scalars),
        out_specs=[vmem] * len(outs),
        scratch_shapes=[pltpu.VMEM(s, F32) for s in scratch],
        compiler_params=pltpu.CompilerParams(vmem_limit_bytes=32 * 1024 * 1024),
        name=kernel.__name__,
    )(*args)


def exchange(forward, backward, axis):
    size = lax.axis_size(axis)
    up = [(i, (i + 1) % size) for i in range(size)]
    down = [(j, i) for i, j in up]
    return lax.ppermute(forward, axis, up), lax.ppermute(backward, axis, down)


def gather(x):
    x = lax.all_gather(x, "azim", axis=0, tiled=True)
    return lax.all_gather(x, "stream", axis=0, tiled=True)


def on_device(element_load, metric, element_order):
    ns, na = lax.axis_size("stream"), lax.axis_size("azim")
    fine, mid = (2, 512, LANES), (2, 64, LANES)
    face8, face4 = (2, 64, LANES), (2, 16, LANES)
    place = jnp.stack([lax.axis_index("stream"), lax.axis_index("azim")]).astype(jnp.int32)
    rolled, up, down = call(
        order_kernel,
        (metric.reshape(1536, LANES), element_load.reshape(512, LANES), element_order),
        [(2048, LANES), (1024, LANES), (1024, LANES)],
    )
    before, after = exchange(up, down, "azim")
    g8, g4, load, diag8, diag4, edges, top, bottom = call(
        setup_kernel,
        (rolled, before, after, C_W8, C_W4, C_SAMPLE, C_BSQ, C_SQ4),
        [(2, 1536, LANES), (2, 192, LANES), fine, fine, mid, (8, LANES)] + [(2, 144, LANES)] * 2,
        [(1536, 2 * LANES)],
    )
    below, above = exchange(top, bottom, "stream")
    all_edges = gather(edges)
    res8, inv8, inv4, acc, top, bottom = call(
        first_kernel,
        (load, diag8, diag4, below, above, g8, C_BD, C_BDT),
        [fine, fine, mid, fine, face8, face8],
        [fine],
    )
    below, above = exchange(top, bottom, "stream")
    sol8, rest8, acc8, t4, top, bottom = call(
        second_kernel,
        (res8, inv8, acc, below, above, g8, C_BD, C_BDT, C_DOWN8),
        [fine, fine, fine, mid] + [(2, 80, LANES)] * 2,
        [fine, (512, 2 * LANES)],
    )
    below8, above8 = exchange(top, bottom, "stream")
    res4, acc, top, bottom = call(
        third_kernel, (t4, inv4, below8, above8, g4, C_G4, C_G4T), [mid, mid, face4, face4], [mid]
    )
    below, above = exchange(top, bottom, "stream")
    corners, up, down, keep = call(
        fourth_kernel,
        (res4, acc, inv4, below, above, g4, C_G4, C_G4T, C_M4, C_DOWN4),
        [(4, LANES), (192, LANES), (192, LANES), (2, 192, LANES)],
        [mid],
    )
    all_corners = gather(corners)
    before, after = exchange(up, down, "azim")
    wider, acc, top, bottom = call(
        side_kernel,
        (keep, before, after, g4, C_G4, C_G4T),
        [(2, 192, LANES), mid, face4, face4],
        [mid],
    )
    below, above = exchange(top, bottom, "stream")
    s4, s8 = call(rest_kernel, (wider, acc, below, above, rest8, acc8, below8, above8), [mid, fine])
    whole = (ns, na * LANES)
    e4, acc, top, bottom = call(
        coarse_kernel,
        (place, all_corners, all_edges, g4, C_G4, C_G4T, C_UP4),
        [mid, mid, face4, face4],
        [(8, na * LANES)] + [whole] * 6,
        scalars=1,
    )
    below, above = exchange(top, bottom, "stream")
    res4, u4, sol4, acc, top, bottom = call(
        fifth_kernel,
        (s4, wider, e4, acc, below, above, inv4, g4, C_G4, C_G4T),
        [mid, mid, mid, mid, face4, face4],
    )
    below, above = exchange(top, bottom, "stream")
    e8, acc, top, bottom = call(
        sixth_kernel,
        (res4, u4, sol4, acc, below, above, inv4, C_UP8, g8, C_BD, C_BDT),
        [fine, fine, face8, face8],
        [mid],
    )
    below, above = exchange(top, bottom, "stream")
    res8, sol8, u8, acc, top, bottom = call(
        seventh_kernel,
        (s8, sol8, e8, acc, below, above, inv8, g8, C_BD, C_BDT),
        [fine, fine, fine, fine, face8, face8],
    )
    below, above = exchange(top, bottom, "stream")
    (out,) = call(last_kernel, (res8, sol8, u8, acc, below, above, inv8), [(512, LANES)])
    return out.reshape(element_load.shape)


def solution(mesh):
    placed = (P(None, "stream", "azim"), P(None, None, "stream", "azim"), P("stream", "azim"))
    return jax.shard_map(
        on_device, mesh=mesh, in_specs=placed, out_specs=P(None, "stream", "azim"), check_vma=False
    )
```

```python
import jax
import jax.numpy as jnp
import numpy as np
from jax import lax
from jax.experimental import pallas as pl
from jax.experimental.pallas import tpu as pltpu
from jax.sharding import PartitionSpec as P

ITERS = 6
LOW_EIG = 0.3
HIGH_EIG = 3.0
CENTER = 0.5 * (HIGH_EIG + LOW_EIG)
HALF_WIDTH = 0.5 * (HIGH_EIG - LOW_EIG)
FIRST_RHO = HALF_WIDTH / CENTER
SECOND_RHO = 1.0 / (2.0 * CENTER / HALF_WIDTH - FIRST_RHO)
KEEP = SECOND_RHO * FIRST_RHO
GAIN = 2.0 * SECOND_RHO / HALF_WIDTH
LANES = 128
HALF = 64
F32 = jnp.float32


def legendre_pair(degree, places):
    previous = places * 0.0 + 1.0
    current = places.copy()
    for k in range(2, degree + 1):
        following = ((2 * k - 1) * places * current - (k - 1) * previous) / k
        previous = current
        current = following
    return (current, previous)


def gll_table(points):
    degree = points - 1
    places = np.cos(np.pi * np.arange(points) / degree)
    for _ in range(60):
        top, below = legendre_pair(degree, places)
        places = places - (places * top - below) / (points * top)
    nodes = np.sort(places)
    nodes[0] = -1.0
    nodes[-1] = 1.0
    at_nodes = legendre_pair(degree, nodes)[0]
    weights = 2.0 / (degree * (degree + 1) * at_nodes**2)
    deriv = np.zeros((points, points))
    for i in range(points):
        for j in range(points):
            if i != j:
                deriv[i, j] = at_nodes[i] / (at_nodes[j] * (nodes[i] - nodes[j]))
    deriv[0, 0] = -degree * (degree + 1) / 4.0
    deriv[-1, -1] = degree * (degree + 1) / 4.0
    return (nodes, weights, deriv)


def lagrange_table(source, target):
    out = np.ones((len(target), len(source)))
    for j in range(len(source)):
        for k in range(len(source)):
            if k != j:
                out[:, j] *= (target - source[k]) / (source[j] - source[k])
    return out


N8, W8, D8 = gll_table(8)
N4, W4, D4 = gll_table(4)
N2, W2, D2 = gll_table(2)


def kron3(a, b, c):
    return np.kron(np.kron(a, b), c)


def cube(w):
    return (w[:, None, None] * w[None, :, None] * w[None, None, :]).reshape(-1)


def share(n):
    edge = np.ones(n)
    edge[0] = edge[-1] = 0.5
    return cube(edge)


def grads(d):
    i = np.eye(d.shape[0])
    return [kron3(d, i, i), kron3(i, d, i), kron3(i, i, d)]


def f32(x):
    return np.asarray(x, np.float32)


def lanes_of(column):
    return np.repeat(f32(column)[:, None], LANES, axis=1)


UP8 = lagrange_table(N4, N8)
UP4 = lagrange_table(N2, N4)
TO4 = lagrange_table(N8, N4)
TO2 = lagrange_table(N8, N2)

C_BD = f32(np.kron(np.eye(32), D8))
C_BDT = f32(np.kron(np.eye(32), D8.T))
C_BSQ = f32(np.kron(np.eye(32), (D8 * D8).T))
C_SAMPLE = f32(np.concatenate([kron3(TO4, TO4, TO4), kron3(TO2, TO2, TO2)]))
C_UP8 = f32(kron3(UP8, UP8, UP8))
C_DOWN8 = f32(kron3(UP8, UP8, UP8).T)
C_UP4 = f32(kron3(UP4, UP4, UP4))
C_DOWN4 = f32(kron3(UP4, UP4, UP4).T)
C_G4 = f32(np.concatenate(grads(D4)))
C_G4T = f32(np.concatenate(grads(D4)).T)
C_SQ4 = f32((np.concatenate(grads(D4)) ** 2).T)
C_W8 = lanes_of(W8)
C_W4 = lanes_of(cube(W4))
C_M4 = lanes_of(share(4))


def dot(a, b):
    return jnp.dot(a, b, preferred_element_type=F32, precision=lax.Precision.HIGHEST)


def iota(rows, axis):
    return lax.broadcasted_iota(jnp.int32, (rows, LANES), axis)


def wide(ref, start, size):
    return jnp.concatenate([ref[0, start : start + size], ref[1, start : start + size]], axis=1)


def put(ref, start, size, value):
    ref[0, start : start + size] = value[:, :LANES]
    ref[1, start : start + size] = value[:, LANES:]


def total(terms):
    out = terms[0]
    for t in terms[1:]:
        out = out + t
    return out


def contract(v, matrix, sign):
    n = len(v)
    h = n // 2
    even = [v[k] + v[n - 1 - k] for k in range(h)]
    odd = [v[k] - v[n - 1 - k] for k in range(h)]
    out = [None] * n
    for i in range(h):
        p = total([even[k] * float(0.5 * (matrix[i, k] + matrix[i, n - 1 - k])) for k in range(h)])
        q = total([odd[k] * float(0.5 * (matrix[i, k] - matrix[i, n - 1 - k])) for k in range(h)])
        out[i] = p + q
        out[n - 1 - i] = q - p if sign < 0 else p - q
    return out


def fine_rows(s, a):
    return s * 64 + a * 8


def fine_apply(u, g, acc, bd, bdt):
    for c in range(2):
        flux = dot(bd[...], wide(u, 256 * c, 256)) * wide(g, 1024 + 256 * c, 256)
        put(acc, 256 * c, 256, dot(bdt[...], flux))
    for h in range(2):
        for axis in range(2):
            for fixed in range(8):
                at = [fine_rows(k, fixed) if axis == 0 else fine_rows(fixed, k) for k in range(8)]
                grad = contract([u[h, r : r + 8] for r in at], D8, -1)
                flux = [grad[k] * g[h, 512 * axis + r : 512 * axis + r + 8] for k, r in enumerate(at)]
                back = contract(flux, D8.T, -1)
                for k, r in enumerate(at):
                    acc[h, r : r + 8] += back[k]


def left(x0, x1):
    near = iota(x0.shape[0], 1) < LANES - 16
    y0, y1 = pltpu.roll(x0, LANES - 16, 1), pltpu.roll(x1, LANES - 16, 1)
    return jnp.where(near, y0, y1), jnp.where(near, y1, y0)


def right(x0, x1):
    near = iota(x0.shape[0], 1) >= 16
    y0, y1 = pltpu.roll(x0, 16, 1), pltpu.roll(x1, 16, 1)
    return jnp.where(near, y0, y1), jnp.where(near, y1, y0)


def join_radial(x, points):
    rows = x.shape[1] // points
    place = iota(rows, 1) % 16
    first, last = pl.ds(0, rows, stride=points), pl.ds(points - 1, rows, stride=points)
    for h in range(2):
        view = x.at[h]
        low, high = view[first, :], view[last, :]
        view[first, :] = jnp.where(place == 0, 0.0, low + pltpu.roll(high, 1, 1))
        view[last, :] = jnp.where(place == 15, 0.0, high + pltpu.roll(low, LANES - 1, 1))


def join_fine(x):
    join_radial(x, 8)
    for s in range(8):
        lo, hi = fine_rows(s, 0), fine_rows(s, 7)
        low = [x[h, lo : lo + 8] for h in range(2)]
        high = [x[h, hi : hi + 8] for h in range(2)]
        to_low, to_high = right(*high), left(*low)
        for h in range(2):
            x[h, lo : lo + 8] = low[h] + to_low[h]
            x[h, hi : hi + 8] = high[h] + to_high[h]


def join_mid(x):
    join_radial(x, 4)
    first = iota(8, 0) < 4
    for s in range(4):
        lo, hi = s * 16, s * 16 + 8
        low = [x[h, lo : lo + 8] for h in range(2)]
        high = [x[h, hi : hi + 8] for h in range(2)]
        to_low = right(*[pltpu.roll(t, 4, 0) for t in high])
        to_high = left(*[pltpu.roll(t, 4, 0) for t in low])
        for h in range(2):
            x[h, lo : lo + 8] = low[h] + jnp.where(first, to_low[h], 0.0)
            x[h, hi : hi + 8] = high[h] + jnp.where(first, 0.0, to_high[h])


def is_even(place, k):
    return lax.rem(place[k], 2) == 0


def full_of(x, faces, h, r, offset=0):
    even, near, far = faces
    rows = x.shape[1]
    plane = {512: 64, 64: 16}[rows]
    value = x[h, r : r + 8]
    if r < plane:
        at = offset + r
        return value + jnp.where(even, far[h, at : at + 8], near[h, at : at + 8])
    if r >= rows - plane:
        at = offset + r - (rows - plane)
        return value + jnp.where(even, near[h, at : at + 8], far[h, at : at + 8])
    return value


def send_faces(x, even, near, far, plane, offset=0):
    rows = x.shape[1]
    last = rows - plane
    one = pl.multiple_of(jnp.where(even, last, 0), 8)
    two = pl.multiple_of(jnp.where(even, 0, last), 8)
    for h in range(2):
        near[h, offset : offset + plane] = x[h, pl.ds(one, plane), :]
        far[h, offset : offset + plane] = x[h, pl.ds(two, plane), :]


def wall_mask(points):
    place, node = iota(8, 1) % 16, iota(8, 0) % points
    return ((node == 0) & (place == 0)) | ((node == points - 1) & (place == 15))


def own_part(half0, half1):
    near = iota(half0.shape[0], 1) < HALF
    return pltpu.roll(jnp.where(near, half1, half0), HALF, 1)


def tiles(rows):
    return [(h, r) for h in range(2) for r in range(0, rows, 8)]


def mid_apply(u, g4, acc, gm, gmt):
    flux = dot(gm[...], wide(u, 0, 64)) * wide(g4, 0, 192)
    put(acc, 0, 64, dot(gmt[...], flux))


def order_kernel(place, metric, load, order, rolled, one, two):
    even = is_even(place, 1)
    near = iota(8, 1) < HALF
    slots = jnp.broadcast_to(pltpu.roll(order[...], HALF, 1), (8, LANES))

    def body(i, carry):
        r = pl.multiple_of(i * 8, 8)
        a = jnp.take_along_axis(metric[pl.ds(r, 8), :], slots, axis=1)
        rolled[pl.ds(r, 8), :] = a
        return carry

    lax.fori_loop(0, 192, body, 0, unroll=8)
    for r in range(0, 512, 8):
        rolled[1536 + r : 1536 + r + 8] = pltpu.roll(load[r : r + 8], HALF, 1)
    for r in range(0, 1024, 8):
        a, b = rolled[r : r + 8], rolled[1024 + r : 1024 + r + 8]
        up = jnp.where(near, a, pltpu.roll(b, HALF, 1))
        down = jnp.where(near, pltpu.roll(a, HALF, 1), b)
        one[r : r + 8] = jnp.where(even, up, down)
        two[r : r + 8] = jnp.where(even, down, up)


def setup_kernel(
    pos, rolled, one, two, w8, w4, sample, bsq, sq4,
    g8, g4, load, diag8, diag4, edges, face_a, face_b, logs,
):
    near = iota(8, 1) < HALF
    wr = w8[...]
    even, even_a = is_even(pos, 0), is_even(pos, 1)

    def place(row, half0, half1):
        r = row % 512
        if row >= 1536:
            load[0, r : r + 8] = half0
            load[1, r : r + 8] = half1
            return
        scale = wr * float(W8[r // 64] * W8[(r // 8) % 8])
        g8[0, row : row + 8] = half0 * scale
        g8[1, row : row + 8] = half1 * scale
        logs[row : row + 8, :LANES] = jnp.log(half0)
        logs[row : row + 8, LANES:] = jnp.log(half1)

    for r in range(0, 1024, 8):
        a, b = rolled[r : r + 8], rolled[1024 + r : 1024 + r + 8]
        x, y = one[r : r + 8], two[r : r + 8]
        p, n = jnp.where(even_a, y, x), jnp.where(even_a, x, y)
        place(r, jnp.where(near, p, a), jnp.where(near, a, pltpu.roll(n, HALF, 1)))
        place(1024 + r, jnp.where(near, pltpu.roll(p, HALF, 1), b), jnp.where(near, b, n))
    low = []
    for d in range(3):
        coarse = jnp.exp(dot(sample[...], logs[512 * d : 512 * d + 512]))
        w = jnp.concatenate([w4[...], w4[...]], axis=1)
        put(g4, 64 * d, 64, coarse[:64] * w)
        low.append([coarse[64:72, :LANES], coarse[64:72, LANES:]])
    for c in range(2):
        put(diag8, 256 * c, 256, dot(bsq[...], wide(g8, 1024 + 256 * c, 256)))
    square = (D8 * D8).T
    for h in range(2):
        for axis in range(2):
            for fixed in range(8):
                at = [fine_rows(k, fixed) if axis == 0 else fine_rows(fixed, k) for k in range(8)]
                back = contract([g8[h, 512 * axis + r : 512 * axis + r + 8] for r in at], square, 1)
                for k, r in enumerate(at):
                    diag8[h, r : r + 8] += back[k]
    put(diag4, 0, 64, dot(sq4[...], wide(g4, 0, 192)))
    for x in (load, diag8):
        join_fine(x)
    join_mid(diag4)
    send_faces(load, even, face_a, face_b, 64)
    send_faces(diag8, even, face_a, face_b, 64, 64)
    send_faces(diag4, even, face_a, face_b, 16, 128)

    def corner(d, i, j, k):
        row = 4 * i + 2 * j + k
        return [t[row : row + 1] for t in low[d]]

    def add(x, y):
        return [x[0] + y[0], x[1] + y[1]]

    def quarter(x):
        return [0.25 * x[0], 0.25 * x[1]]

    def outward(x):
        return [pltpu.roll(x[0], 1, 1), pltpu.roll(x[1], 1, 1)]

    es = [[quarter(add(corner(0, 0, j, k), corner(0, 1, j, k))) for k in range(2)] for j in range(2)]
    ea = [[quarter(add(corner(1, i, 0, k), corner(1, i, 1, k))) for k in range(2)] for i in range(2)]
    er = [[quarter(add(corner(2, i, j, 0), corner(2, i, j, 1))) for j in range(2)] for i in range(2)]
    col = [add(es[0][k], list(right(*es[1][k]))) for k in range(2)]
    edge_s = add(col[0], outward(col[1]))
    edge_a = [add(ea[i][0], outward(ea[i][1])) for i in range(2)]
    edge_r = [add(er[i][0], list(right(*er[i][1]))) for i in range(2)]
    off_wall = iota(1, 1) % 16 != 0
    rows = [jnp.where(off_wall, own_part(*x), 0.0) for x in (edge_s, edge_a[0], edge_a[1])]
    rows += [own_part(*x) for x in edge_r]
    none = jnp.zeros((5, LANES), F32)
    edges[...] = jnp.concatenate([rows[0], rows[1], rows[3], none], axis=0)
    upper = jnp.concatenate([rows[0], rows[2], rows[4], none], axis=0)
    for face in (face_a, face_b):
        face[0, 144:152] = upper
        face[1, 144:152] = upper


def first_kernel(
    pos, load, diag8, diag4, edges, a, b, g8, bd, bdt,
    res, inv8, inv4, edge, acc, face_a, face_b, u,
):
    even = is_even(pos, 0)
    got = (even, a, b)
    wall8, wall4 = wall_mask(8), wall_mask(4)
    for h, r in tiles(512):
        diag = full_of(diag8, got, h, r, 64)
        inv = jnp.where(wall8, 0.0, 1.0 / jnp.where(wall8, 1.0, diag))
        full = full_of(load, got, h, r)
        res[h, r : r + 8] = full
        inv8[h, r : r + 8] = inv
        u[h, r : r + 8] = inv * full * (1.0 / CENTER)
    for h, r in tiles(64):
        diag = full_of(diag4, got, h, r, 128)
        inv4[h, r : r + 8] = jnp.where(wall4, 0.0, 1.0 / jnp.where(wall4, 1.0, diag))
    lower = jnp.where(even, b[0, 144:152], a[0, 144:152])
    edge[...] = edges[...] + jnp.where(iota(8, 0) == 0, 0.0, lower)
    fine_apply(u, g8, acc, bd, bdt)
    join_fine(acc)
    send_faces(acc, even, face_a, face_b, 64)


def second_kernel(
    pos, res, inv8, acc, a, b, g8, bd, bdt, down8, sol, rest, u, t4, face_a, face_b, back, part
):
    even = is_even(pos, 0)
    got = (even, a, b)
    edge = jnp.where((iota(8, 0) == 0) | (iota(8, 0) == 7), 0.5, 1.0)
    for h, r in tiles(512):
        inv, before = inv8[h, r : r + 8], res[h, r : r + 8]
        now = before - full_of(acc, got, h, r)
        old = inv * before * (1.0 / CENTER)
        new = KEEP * old + GAIN * inv * now
        rest[h, r : r + 8] = now
        sol[h, r : r + 8] = old + new
        u[h, r : r + 8] = new
    fine_apply(u, g8, back, bd, bdt)
    for h, r in tiles(512):
        s, c = r // 64, (r // 8) % 8
        scale = (0.5 if s in (0, 7) else 1.0) * (0.5 if c in (0, 7) else 1.0)
        part[r : r + 8, h * LANES : h * LANES + LANES] = (
            rest[h, r : r + 8] * (edge * scale) - back[h, r : r + 8]
        )
    put(t4, 0, 64, dot(down8[...], part[...]))
    join_mid(t4)
    send_faces(t4, even, face_a, face_b, 16)


def third_kernel(pos, t4, inv4, a, b, g4, gm, gmt, res, acc, face_a, face_b, u):
    even = is_even(pos, 0)
    for h, r in tiles(64):
        full = full_of(t4, (even, a, b), h, r)
        res[h, r : r + 8] = full
        u[h, r : r + 8] = inv4[h, r : r + 8] * full * (1.0 / CENTER)
    mid_apply(u, g4, acc, gm, gmt)
    join_mid(acc)
    send_faces(acc, even, face_a, face_b, 16)


def fourth_kernel(
    pos, res, acc, inv4, edge, a, b, g4, gm, gmt, m4, down4, corners, one, two, keep, part
):
    got = (is_even(pos, 0), a, b)
    even_a = is_even(pos, 1)
    for h, r in tiles(64):
        inv, before = inv4[h, r : r + 8], res[h, r : r + 8]
        now = before - full_of(acc, got, h, r)
        old = inv * before * (1.0 / CENTER)
        new = KEEP * old + GAIN * inv * now
        keep[h, r : r + 8] = now
        keep[h, 64 + r : 72 + r] = new
        keep[h, 128 + r : 136 + r] = old + new
    one[...] = jnp.where(even_a, keep[1], keep[0])
    two[...] = jnp.where(even_a, keep[0], keep[1])
    flux = dot(gm[...], wide(keep, 64, 64)) * wide(g4, 0, 192)
    put(part, 0, 64, dot(gmt[...], flux))
    for h, r in tiles(64):
        part[h, r : r + 8] = m4[r : r + 8] * keep[h, r : r + 8] - part[h, r : r + 8]
    low = dot(down4[...], wide(part, 0, 64))
    near = iota(8, 1) < HALF
    half0 = jnp.where(near, 0.0, low[:, :LANES])
    half1 = jnp.where(near, low[:, LANES:], 0.0)

    def corner(i, j, k):
        row = 4 * i + 2 * j + k
        return [half0[row : row + 1], half1[row : row + 1]]

    lane = iota(1, 1)
    mine, extra = [], []
    for i in range(2):
        columns = []
        for k in range(2):
            shifted = right(*corner(i, 1, k))
            straight = corner(i, 0, k)
            columns.append([straight[0] + shifted[0], straight[1] + shifted[1]])
        both = [columns[0][h] + pltpu.roll(columns[1][h], 1, 1) for h in range(2)]
        both = [jnp.where(lane % 16 == 0, 0.0, t) for t in both]
        mine.append(own_part(*both))
        extra.append(both[1])
    sides = jnp.where(lane < 16, pltpu.roll(extra[0], HALF, 1), 0.0) + jnp.where(
        (lane >= 16) & (lane < 32), pltpu.roll(extra[1], HALF + 16, 1), 0.0
    )
    none = jnp.zeros((2, LANES), F32)
    corners[...] = jnp.concatenate(mine + [sides, edge[0:3], none], axis=0)


def column_kernel(rows, out):
    ns = rows.shape[0] // 8

    def field(k):
        return rows[pl.ds(k, ns, stride=8), :]

    def later(x):
        return pltpu.roll(x, 1, 0)

    sides = field(2)
    over = jnp.where(iota(ns, 1) < 16, sides + later(pltpu.roll(sides, LANES - 16, 1)), 0.0)
    out[0:ns] = field(0) + later(field(1))
    out[ns : 2 * ns] = over
    for k in range(3):
        out[(2 + k) * ns : (3 + k) * ns] = field(3 + k)


def coarse_kernel(
    pos, columns, keep, one, two, g4, gm, gmt, up4,
    res, sol, acc, face_a, face_b, vals, x2, es, ea, er, dg, ri, e4, up,
):
    ns = x2.shape[0]
    na = x2.shape[1] // LANES
    width = na * LANES

    def field(k):
        return [columns[d * 5 * ns + k * ns : d * 5 * ns + (k + 1) * ns] for d in range(na)]

    def later(x):
        return pltpu.roll(x, 1, 0)

    def roll_l(x, k):
        return pltpu.roll(x, k % width, 1)

    wall = lax.broadcasted_iota(jnp.int32, (ns, width), 1) % 16 == 0
    mine, sides = field(0), field(1)
    r = jnp.concatenate([mine[d] + sides[d - 1] for d in range(na)], axis=1)
    es[...] = jnp.concatenate(field(2), axis=1)
    ea[...] = jnp.concatenate(field(3), axis=1)
    er[...] = jnp.concatenate(field(4), axis=1)
    sum_all = es[...] + later(es[...]) + ea[...] + roll_l(ea[...], 16) + er[...] + roll_l(er[...], 1)
    dg[...] = jnp.where(wall, 0.0, sum_all)
    ri[...] = jnp.where(wall, 0.0, 1.0 / jnp.where(wall, 1.0, sum_all))

    def apply(p):
        q = dg[...] * p
        q = q - es[...] * pltpu.roll(p, ns - 1, 0) - later(es[...] * p)
        q = q - ea[...] * roll_l(p, -16) - roll_l(ea[...] * p, 16)
        q = q - er[...] * roll_l(p, -1) - roll_l(er[...] * p, 1)
        return jnp.where(wall, 0.0, q)

    def inner(x, y):
        return jnp.sum(jnp.sum(x * y, axis=0, keepdims=True), axis=1, keepdims=True)

    z = ri[...] * r
    p = z
    gz = inner(r, z)
    x = jnp.zeros_like(r)
    for it in range(ITERS):
        q = apply(p)
        alpha = gz / inner(p, q)
        x = x + alpha * p
        if it + 1 < ITERS:
            r = r - alpha * q
            z = ri[...] * r
            new = inner(r, z)
            p = z + (new / gz) * p
            gz = new
    x2[...] = x

    s, a = pos[0], pos[1]
    s_next = lax.rem(s + 1, ns)
    blocks = [lax.rem(a + na - 1, na), a, lax.rem(a + 1, na)]
    for i, row in enumerate((s, s_next)):
        line = x2[pl.ds(row, 1), :]
        for j in range(2):
            for k in range(2):
                n = 4 * i + 2 * j + k
                vals[n : n + 1, :] = roll_l(line, -(16 * j + k)) if j + k else line
    near = iota(8, 1) < HALF
    b = [
        pltpu.roll(vals[:, pl.ds(pl.multiple_of(t * LANES, LANES), LANES)], HALF, 1) for t in blocks
    ]
    ext = jnp.concatenate([jnp.where(near, b[0], b[1]), jnp.where(near, b[1], b[2])], axis=1)
    put(e4, 0, 64, dot(up4[...], ext))
    even_a = is_even(pos, 1)
    for r in range(0, 192, 8):
        x, y = one[r : r + 8], two[r : r + 8]
        before, after = jnp.where(even_a, y, x), jnp.where(even_a, x, y)
        half0 = jnp.where(near, before, keep[0, r : r + 8])
        half1 = jnp.where(near, keep[1, r : r + 8], after)
        for h, half in enumerate((half0, half1)):
            if r < 64:
                res[h, r : r + 8] = half
            elif r >= 128:
                sol[h, r - 128 : r - 120] = half + e4[h, r - 128 : r - 120]
            else:
                up[h, r - 64 : r - 56] = half + e4[h, r - 64 : r - 56]
    mid_apply(up, g4, acc, gm, gmt)
    join_mid(acc)
    send_faces(acc, is_even(pos, 0), face_a, face_b, 16)


def fifth_kernel(
    pos, before, sol, acc, a, b, inv4, g4, gm, gmt, res, u, out, acc2, face_a, face_b
):
    even = is_even(pos, 0)
    for h, r in tiles(64):
        now = before[h, r : r + 8] - full_of(acc, (even, a, b), h, r)
        new = inv4[h, r : r + 8] * now * (1.0 / CENTER)
        res[h, r : r + 8] = now
        u[h, r : r + 8] = new
        out[h, r : r + 8] = sol[h, r : r + 8] + new
    mid_apply(u, g4, acc2, gm, gmt)
    join_mid(acc2)
    send_faces(acc2, even, face_a, face_b, 16)


def sixth_kernel(
    pos, res, u, sol, acc, a, b, inv4, up8, sol8, u8, g8, bd, bdt,
    out, acc2, face_a, face_b, y4, v8,
):
    even = is_even(pos, 0)
    for h, r in tiles(64):
        now = res[h, r : r + 8] - full_of(acc, (even, a, b), h, r)
        new = KEEP * u[h, r : r + 8] + GAIN * inv4[h, r : r + 8] * now
        y4[h, r : r + 8] = sol[h, r : r + 8] + new
    put(v8, 0, 512, dot(up8[...], wide(y4, 0, 64)))
    for h, r in tiles(512):
        e8 = v8[h, r : r + 8]
        out[h, r : r + 8] = sol8[h, r : r + 8] + e8
        v8[h, r : r + 8] = u8[h, r : r + 8] + e8
    fine_apply(v8, g8, acc2, bd, bdt)
    join_fine(acc2)
    send_faces(acc2, even, face_a, face_b, 64)


def seventh_kernel(
    pos, rest, sol, acc, a, b, inv8, g8, bd, bdt, res, out, u, acc2, face_a, face_b
):
    even = is_even(pos, 0)
    for h, r in tiles(512):
        now = rest[h, r : r + 8] - full_of(acc, (even, a, b), h, r)
        new = inv8[h, r : r + 8] * now * (1.0 / CENTER)
        res[h, r : r + 8] = now
        u[h, r : r + 8] = new
        out[h, r : r + 8] = sol[h, r : r + 8] + new
    fine_apply(u, g8, acc2, bd, bdt)
    join_fine(acc2)
    send_faces(acc2, even, face_a, face_b, 64)


def last_kernel(pos, res, sol, u, acc, a, b, inv8, out):
    got = (is_even(pos, 0), a, b)
    for r in range(0, 512, 8):
        halves = []
        for h in range(2):
            now = res[h, r : r + 8] - full_of(acc, got, h, r)
            new = KEEP * u[h, r : r + 8] + GAIN * inv8[h, r : r + 8] * now
            halves.append(sol[h, r : r + 8] + new)
        out[r : r + 8] = own_part(*halves)


def call(kernel, args, outs, scratch=(), scalars=1):
    vmem = pl.BlockSpec(memory_space=pltpu.VMEM)
    smem = pl.BlockSpec(memory_space=pltpu.SMEM)
    return pl.pallas_call(
        kernel,
        out_shape=[jax.ShapeDtypeStruct(s, F32) for s in outs],
        in_specs=[smem] * scalars + [vmem] * (len(args) - scalars),
        out_specs=[vmem] * len(outs),
        scratch_shapes=[pltpu.VMEM(s, F32) for s in scratch],
        compiler_params=pltpu.CompilerParams(vmem_limit_bytes=32 * 1024 * 1024),
        name=kernel.__name__,
    )(*args)


def exchange(near, far, axis):
    size = lax.axis_size(axis)
    pairs_far = [(i, (i + 1 if i % 2 else i - 1) % size) for i in range(size)]
    pairs_near = [(i, i ^ 1) for i in range(size)]
    far = lax.ppermute(far, axis, pairs_far)
    near = lax.ppermute(near, axis, pairs_near)
    return near, far


def spread(x, axis):
    size = lax.axis_size(axis)
    copies = jnp.broadcast_to(x[None], (size,) + x.shape)
    return lax.all_to_all(copies, axis, 0, 0).reshape(-1, LANES)


def on_device(element_load, metric, element_order):
    ns, na = lax.axis_size("stream"), lax.axis_size("azim")
    fine, mid = (2, 512, LANES), (2, 64, LANES)
    face8, face4 = [(2, 64, LANES)] * 2, [(2, 16, LANES)] * 2
    pos = jnp.stack([lax.axis_index("stream"), lax.axis_index("azim")]).astype(jnp.int32)
    rolled, a, b = call(
        order_kernel,
        (pos, metric.reshape(1536, LANES), element_load.reshape(512, LANES), element_order),
        [(2048, LANES), (1024, LANES), (1024, LANES)],
    )
    a, b = exchange(a, b, "azim")
    g8, g4, load, diag8, diag4, edges, a, b = call(
        setup_kernel,
        (pos, rolled, a, b, C_W8, C_W4, C_SAMPLE, C_BSQ, C_SQ4),
        [(2, 1536, LANES), (2, 192, LANES), fine, fine, mid, (8, LANES)] + [(2, 152, LANES)] * 2,
        [(1536, 2 * LANES)],
    )
    a, b = exchange(a, b, "stream")
    res8, inv8, inv4, edges, acc, a, b = call(
        first_kernel,
        (pos, load, diag8, diag4, edges, a, b, g8, C_BD, C_BDT),
        [fine, fine, mid, (8, LANES), fine] + face8,
        [fine],
    )
    a, b = exchange(a, b, "stream")
    sol8, rest8, u8, t4, a, b = call(
        second_kernel,
        (pos, res8, inv8, acc, a, b, g8, C_BD, C_BDT, C_DOWN8),
        [fine, fine, fine, mid] + face4,
        [fine, (512, 2 * LANES)],
    )
    a, b = exchange(a, b, "stream")
    res4, acc, a, b = call(
        third_kernel, (pos, t4, inv4, a, b, g4, C_G4, C_G4T), [mid, mid] + face4, [mid]
    )
    a, b = exchange(a, b, "stream")
    corners, a, b, keep = call(
        fourth_kernel,
        (pos, res4, acc, inv4, edges, a, b, g4, C_G4, C_G4T, C_M4, C_DOWN4),
        [(8, LANES), (192, LANES), (192, LANES), (2, 192, LANES)],
        [mid],
    )
    a, b = exchange(a, b, "azim")
    (columns,) = call(column_kernel, (spread(corners, "stream"),), [(5 * ns, LANES)], scalars=0)
    columns = spread(columns, "azim")
    whole = (ns, na * LANES)
    res4, sol4, acc, a, b = call(
        coarse_kernel,
        (pos, columns, keep, a, b, g4, C_G4, C_G4T, C_UP4),
        [mid, mid, mid] + face4,
        [(8, na * LANES)] + [whole] * 6 + [mid, mid],
    )
    a, b = exchange(a, b, "stream")
    res4, u4, sol4, acc, a, b = call(
        fifth_kernel,
        (pos, res4, sol4, acc, a, b, inv4, g4, C_G4, C_G4T),
        [mid, mid, mid, mid] + face4,
    )
    a, b = exchange(a, b, "stream")
    sol8, acc, a, b = call(
        sixth_kernel,
        (pos, res4, u4, sol4, acc, a, b, inv4, C_UP8, sol8, u8, g8, C_BD, C_BDT),
        [fine, fine] + face8,
        [mid, fine],
    )
    a, b = exchange(a, b, "stream")
    res8, sol8, u8, acc, a, b = call(
        seventh_kernel,
        (pos, rest8, sol8, acc, a, b, inv8, g8, C_BD, C_BDT),
        [fine, fine, fine, fine] + face8,
    )
    a, b = exchange(a, b, "stream")
    (out,) = call(last_kernel, (pos, res8, sol8, u8, acc, a, b, inv8), [(512, LANES)])
    return out.reshape(element_load.shape)


def solution(mesh):
    placed = (P(None, "stream", "azim"), P(None, None, "stream", "azim"), P("stream", "azim"))
    return jax.shard_map(
        on_device, mesh=mesh, in_specs=placed, out_specs=P(None, "stream", "azim"), check_vma=False
    )
```

```python
import jax
import jax.numpy as jnp
import numpy as np
from jax import lax
from jax.experimental import pallas as pl
from jax.experimental.pallas import tpu as pltpu
from jax.sharding import PartitionSpec as P

ITERS = 6
LOW_EIG = 0.3
HIGH_EIG = 3.0
CENTER = 0.5 * (HIGH_EIG + LOW_EIG)
HALF_WIDTH = 0.5 * (HIGH_EIG - LOW_EIG)
FIRST_RHO = HALF_WIDTH / CENTER
SECOND_RHO = 1.0 / (2.0 * CENTER / HALF_WIDTH - FIRST_RHO)
KEEP = SECOND_RHO * FIRST_RHO
GAIN = 2.0 * SECOND_RHO / HALF_WIDTH
LANES = 128
HALF = 64
F32 = jnp.float32


def legendre_pair(degree, places):
    previous = places * 0.0 + 1.0
    current = places.copy()
    for k in range(2, degree + 1):
        following = ((2 * k - 1) * places * current - (k - 1) * previous) / k
        previous = current
        current = following
    return (current, previous)


def gll_table(points):
    degree = points - 1
    places = np.cos(np.pi * np.arange(points) / degree)
    for _ in range(60):
        top, below = legendre_pair(degree, places)
        places = places - (places * top - below) / (points * top)
    nodes = np.sort(places)
    nodes[0] = -1.0
    nodes[-1] = 1.0
    at_nodes = legendre_pair(degree, nodes)[0]
    weights = 2.0 / (degree * (degree + 1) * at_nodes**2)
    deriv = np.zeros((points, points))
    for i in range(points):
        for j in range(points):
            if i != j:
                deriv[i, j] = at_nodes[i] / (at_nodes[j] * (nodes[i] - nodes[j]))
    deriv[0, 0] = -degree * (degree + 1) / 4.0
    deriv[-1, -1] = degree * (degree + 1) / 4.0
    return (nodes, weights, deriv)


def lagrange_table(source, target):
    out = np.ones((len(target), len(source)))
    for j in range(len(source)):
        for k in range(len(source)):
            if k != j:
                out[:, j] *= (target - source[k]) / (source[j] - source[k])
    return out


N8, W8, D8 = gll_table(8)
N4, W4, D4 = gll_table(4)
N2, W2, D2 = gll_table(2)


def kron3(a, b, c):
    return np.kron(np.kron(a, b), c)


def cube(w):
    return (w[:, None, None] * w[None, :, None] * w[None, None, :]).reshape(-1)


def share(n):
    edge = np.ones(n)
    edge[0] = edge[-1] = 0.5
    return cube(edge)


def grads(d):
    i = np.eye(d.shape[0])
    return [kron3(d, i, i), kron3(i, d, i), kron3(i, i, d)]


def f32(x):
    return np.asarray(x, np.float32)


def lanes_of(column):
    return np.repeat(f32(column)[:, None], LANES, axis=1)


UP8 = lagrange_table(N4, N8)
UP4 = lagrange_table(N2, N4)
TO4 = lagrange_table(N8, N4)
TO2 = lagrange_table(N8, N2)

C_BD = f32(np.kron(np.eye(16), D8))
C_BDT = f32(np.kron(np.eye(16), D8.T))
C_BSQ = f32(np.kron(np.eye(16), (D8 * D8).T))
C_SAMPLE = f32(np.concatenate([kron3(TO4, TO4, TO4), kron3(TO2, TO2, TO2)]))
C_UP8 = f32(kron3(UP8, UP8, UP8))
C_DOWN8 = f32(kron3(UP8, UP8, UP8).T)
C_UP4 = f32(kron3(UP4, UP4, UP4))
C_DOWN4 = f32(kron3(UP4, UP4, UP4).T)
C_G4 = f32(np.concatenate(grads(D4)))
C_G4T = f32(np.concatenate(grads(D4)).T)
C_SQ4 = f32((np.concatenate(grads(D4)) ** 2).T)
C_W8 = lanes_of(W8)
C_W4 = lanes_of(cube(W4) / np.exp(kron3(TO4, TO4, TO4) @ np.log(cube(W8))))
C_W2 = lanes_of(cube(W2) / np.exp(kron3(TO2, TO2, TO2) @ np.log(cube(W8))))
C_M4 = lanes_of(share(4))
CONSTANTS = {
    "bd": C_BD, "bdt": C_BDT, "bsq": C_BSQ, "sample": C_SAMPLE, "w8": C_W8, "w4": C_W4, "w2": C_W2,
    "sq4": C_SQ4, "gm": C_G4, "gmt": C_G4T, "m4": C_M4, "down8": C_DOWN8, "down4": C_DOWN4,
    "up4": C_UP4, "up8": C_UP8,
}


def dot(a, b):
    return jnp.dot(a, b, preferred_element_type=F32, precision=lax.Precision.HIGHEST)


def iota(rows, axis):
    return lax.broadcasted_iota(jnp.int32, (rows, LANES), axis)


def wide(ref, start, size):
    return jnp.concatenate([ref[0, start : start + size], ref[1, start : start + size]], axis=1)


def put(ref, start, size, value):
    ref[0, start : start + size] = value[:, :LANES]
    ref[1, start : start + size] = value[:, LANES:]


def total(terms):
    out = terms[0]
    for t in terms[1:]:
        out = out + t
    return out


def contract(v, matrix, sign):
    n = len(v)
    h = n // 2
    even = [v[k] + v[n - 1 - k] for k in range(h)]
    odd = [v[k] - v[n - 1 - k] for k in range(h)]
    out = [None] * n
    for i in range(h):
        p = total([even[k] * float(0.5 * (matrix[i, k] + matrix[i, n - 1 - k])) for k in range(h)])
        q = total([odd[k] * float(0.5 * (matrix[i, k] - matrix[i, n - 1 - k])) for k in range(h)])
        out[i] = p + q
        out[n - 1 - i] = q - p if sign < 0 else p - q
    return out


def fine_rows(s, a):
    return s * 64 + a * 8


PLANES = [(0, 7), (1, 2), (3, 4), (5, 6)]


def pair(ref, p, base=0):
    return jnp.concatenate([wide(ref, base + 64 * s, 64) for s in p], axis=0)


def put_pair(ref, p, value):
    for k, s in enumerate(p):
        put(ref, 64 * s, 64, value[64 * k : 64 * k + 64])


def fine_stream(u, g, acc):
    for h in range(2):
        for a in range(8):
            at = [fine_rows(s, a) for s in range(8)]
            grad = contract([u[h, r : r + 8] for r in at], D8, -1)
            back = contract([grad[s] * g[h, r : r + 8] for s, r in enumerate(at)], D8.T, -1)
            for s, r in enumerate(at):
                acc[h, r : r + 8] = back[s]


def fine_cross(u, g, acc, bd, bdt, pairs):
    for p in pairs:
        flux = dot(bd[...], pair(u, p)) * pair(g, p, 1024)
        put_pair(acc, p, pair(acc, p) + dot(bdt[...], flux))
        for s in p:
            for h in range(2):
                at = [fine_rows(s, a) for a in range(8)]
                grad = contract([u[h, r : r + 8] for r in at], D8, -1)
                flux = [grad[a] * g[h, 512 + r : 520 + r] for a, r in enumerate(at)]
                back = contract(flux, D8.T, -1)
                for a, r in enumerate(at):
                    acc[h, r : r + 8] += back[a]


def fine_apply(u, g, acc, bd, bdt):
    fine_stream(u, g, acc)
    fine_cross(u, g, acc, bd, bdt, PLANES)


def fine_front(u, g, acc, bd, bdt):
    fine_stream(u, g, acc)
    fine_cross(u, g, acc, bd, bdt, PLANES[:1])
    join_fine(acc, (0, 7))


def left(x0, x1):
    near = iota(x0.shape[0], 1) < LANES - 16
    y0, y1 = pltpu.roll(x0, LANES - 16, 1), pltpu.roll(x1, LANES - 16, 1)
    return jnp.where(near, y0, y1), jnp.where(near, y1, y0)


def right(x0, x1):
    near = iota(x0.shape[0], 1) >= 16
    y0, y1 = pltpu.roll(x0, 16, 1), pltpu.roll(x1, 16, 1)
    return jnp.where(near, y0, y1), jnp.where(near, y1, y0)


def join_radial(x, points, start, rows):
    place = iota(rows, 1) % 16
    first = pl.ds(start, rows, stride=points)
    last = pl.ds(start + points - 1, rows, stride=points)
    for h in range(2):
        view = x.at[h]
        low, high = view[first, :], view[last, :]
        view[first, :] = jnp.where(place == 0, 0.0, low + pltpu.roll(high, 1, 1))
        view[last, :] = jnp.where(place == 15, 0.0, high + pltpu.roll(low, LANES - 1, 1))


def join_fine(x, planes=range(8)):
    for s in planes:
        join_radial(x, 8, 64 * s, 8)
        lo, hi = fine_rows(s, 0), fine_rows(s, 7)
        low = [x[h, lo : lo + 8] for h in range(2)]
        high = [x[h, hi : hi + 8] for h in range(2)]
        to_low, to_high = right(*high), left(*low)
        for h in range(2):
            x[h, lo : lo + 8] = low[h] + to_low[h]
            x[h, hi : hi + 8] = high[h] + to_high[h]


def join_mid(x):
    join_radial(x, 4, 0, 16)
    first = iota(8, 0) < 4
    for s in range(4):
        lo, hi = s * 16, s * 16 + 8
        low = [x[h, lo : lo + 8] for h in range(2)]
        high = [x[h, hi : hi + 8] for h in range(2)]
        to_low = right(*[pltpu.roll(t, 4, 0) for t in high])
        to_high = left(*[pltpu.roll(t, 4, 0) for t in low])
        for h in range(2):
            x[h, lo : lo + 8] = low[h] + jnp.where(first, to_low[h], 0.0)
            x[h, hi : hi + 8] = high[h] + jnp.where(first, 0.0, to_high[h])


def is_even(place, k):
    return lax.rem(place[k], 2) == 0


def full_of(x, faces, h, r, offset=0):
    even, far, near = faces
    rows = x.shape[1]
    plane = {512: 64, 64: 16}[rows]
    value = x[h, r : r + 8]
    if r < plane:
        at = offset + r
        return value + jnp.where(even, far[h, at : at + 8], near[h, at : at + 8])
    if r >= rows - plane:
        at = offset + r - (rows - plane)
        return value + jnp.where(even, near[h, at : at + 8], far[h, at : at + 8])
    return value


def send_faces(x, even, far, near, plane, offset=0):
    rows = x.shape[1]
    last = rows - plane
    one = pl.multiple_of(jnp.where(even, last, 0), 8)
    two = pl.multiple_of(jnp.where(even, 0, last), 8)
    for h in range(2):
        near[h, offset : offset + plane] = x[h, pl.ds(one, plane), :]
        far[h, offset : offset + plane] = x[h, pl.ds(two, plane), :]


def wall_mask(points):
    place, node = iota(8, 1) % 16, iota(8, 0) % points
    return ((node == 0) & (place == 0)) | ((node == points - 1) & (place == 15))


def own_part(half0, half1):
    near = iota(half0.shape[0], 1) < HALF
    return pltpu.roll(jnp.where(near, half1, half0), HALF, 1)


def tiles(rows):
    return [(h, r) for h in range(2) for r in range(0, rows, 8)]


def mid_apply(u, g4, acc, gm, gmt):
    flux = dot(gm[...], wide(u, 0, 64)) * wide(g4, 0, 192)
    put(acc, 0, 64, dot(gmt[...], flux))


def order_kernel(place, metric_in, load_in, order_in, *refs):
    n = len(CONSTANTS)
    held, (rolled, one, two) = refs[:n], refs[n : n + 3]
    consts = refs[n + 3 : 2 * n + 3]
    metric, load, order, sems = refs[2 * n + 3 :]
    copies = [pltpu.make_async_copy(order_in, order, sems.at[0])]
    copies.append(pltpu.make_async_copy(load_in, load, sems.at[1]))
    for k in range(3):
        part = pl.ds(512 * k, 512)
        copies.append(pltpu.make_async_copy(metric_in.at[part], metric.at[part], sems.at[2 + k]))
    for k in range(n):
        copies.append(pltpu.make_async_copy(held[k], consts[k], sems.at[5 + k]))
    for copy in copies:
        copy.start()
    even = is_even(place, 1)
    near = iota(8, 1) < HALF
    copies[0].wait()
    slots = jnp.broadcast_to(pltpu.roll(order[...], HALF, 1), (8, LANES))

    def body(i, carry):
        r = pl.multiple_of(i * 8, 8)
        a = jnp.take_along_axis(metric[pl.ds(r, 8), :], slots, axis=1)
        rolled[pl.ds(r, 8), :] = a
        return carry

    for k in range(3):
        copies[2 + k].wait()
        lax.fori_loop(64 * k, 64 * k + 64, body, 0, unroll=8)
    copies[1].wait()
    for r in range(0, 512, 8):
        rolled[1536 + r : 1536 + r + 8] = pltpu.roll(load[r : r + 8], HALF, 1)
    for r in range(0, 1024, 8):
        a, b = rolled[r : r + 8], rolled[1024 + r : 1024 + r + 8]
        up = jnp.where(near, a, pltpu.roll(b, HALF, 1))
        down = jnp.where(near, pltpu.roll(a, HALF, 1), b)
        one[r : r + 8] = jnp.where(even, down, up)
        two[r : r + 8] = jnp.where(even, up, down)
    for copy in copies[5:]:
        copy.wait()


def setup_kernel(pos, rolled, one, two, w8, bsq, g8, load, diag8, face_a, face_b):
    near = iota(8, 1) < HALF
    wr = w8[...]
    even, even_a = is_even(pos, 0), is_even(pos, 1)

    def place(row, half0, half1):
        r = row % 512
        if row >= 1536:
            load[0, r : r + 8] = half0
            load[1, r : r + 8] = half1
            return
        scale = wr * float(W8[r // 64] * W8[(r // 8) % 8])
        g8[0, row : row + 8] = half0 * scale
        g8[1, row : row + 8] = half1 * scale

    for r in range(0, 1024, 8):
        a, b = rolled[r : r + 8], rolled[1024 + r : 1024 + r + 8]
        x, y = one[r : r + 8], two[r : r + 8]
        p, n = jnp.where(even_a, x, y), jnp.where(even_a, y, x)
        place(r, jnp.where(near, p, a), jnp.where(near, a, pltpu.roll(n, HALF, 1)))
        place(1024 + r, jnp.where(near, pltpu.roll(p, HALF, 1), b), jnp.where(near, b, n))
    for p in PLANES:
        put_pair(diag8, p, dot(bsq[...], pair(g8, p, 1024)))
    square = (D8 * D8).T
    for h in range(2):
        for axis in range(2):
            for fixed in range(8):
                at = [fine_rows(k, fixed) if axis == 0 else fine_rows(fixed, k) for k in range(8)]
                back = contract([g8[h, 512 * axis + r : 512 * axis + r + 8] for r in at], square, 1)
                for k, r in enumerate(at):
                    diag8[h, r : r + 8] += back[k]
    for x in (load, diag8):
        join_fine(x)
    send_faces(load, even, face_a, face_b, 64)
    send_faces(diag8, even, face_a, face_b, 64, 64)


def coarsen_kernel(g8, w4, w2, sample, sq4, g4, diag4, edges, upper):
    low = []
    for d in range(3):
        coarse = jnp.exp(dot(sample[...], jnp.log(wide(g8, 512 * d, 512))))
        put(g4, 64 * d, 64, coarse[:64] * jnp.concatenate([w4[...], w4[...]], axis=1))
        low.append([coarse[64:72, :LANES] * w2[...], coarse[64:72, LANES:] * w2[...]])
    put(diag4, 0, 64, dot(sq4[...], wide(g4, 0, 192)))
    join_mid(diag4)

    def corner(d, i, j, k):
        row = 4 * i + 2 * j + k
        return [t[row : row + 1] for t in low[d]]

    def add(x, y):
        return [x[0] + y[0], x[1] + y[1]]

    def quarter(x):
        return [0.25 * x[0], 0.25 * x[1]]

    def outward(x):
        return [pltpu.roll(x[0], 1, 1), pltpu.roll(x[1], 1, 1)]

    es = [[quarter(add(corner(0, 0, j, k), corner(0, 1, j, k))) for k in range(2)] for j in range(2)]
    ea = [[quarter(add(corner(1, i, 0, k), corner(1, i, 1, k))) for k in range(2)] for i in range(2)]
    er = [[quarter(add(corner(2, i, j, 0), corner(2, i, j, 1))) for j in range(2)] for i in range(2)]
    col = [add(es[0][k], list(right(*es[1][k]))) for k in range(2)]
    edge_s = add(col[0], outward(col[1]))
    edge_a = [add(ea[i][0], outward(ea[i][1])) for i in range(2)]
    edge_r = [add(er[i][0], list(right(*er[i][1]))) for i in range(2)]
    off_wall = iota(1, 1) % 16 != 0
    rows = [jnp.where(off_wall, own_part(*x), 0.0) for x in (edge_s, edge_a[0], edge_a[1])]
    rows += [own_part(*x) for x in edge_r]
    none = jnp.zeros((5, LANES), F32)
    edges[...] = jnp.concatenate([rows[0], rows[1], rows[3], none], axis=0)
    upper[...] = jnp.concatenate([rows[0], rows[2], rows[4], none], axis=0)


def first_kernel(
    pos, load, diag8, a, b, g8, diag4, upper, bd, bdt, res, inv8, u, acc, face_a, face_b
):
    even = is_even(pos, 0)
    got = (even, a, b)
    wall8 = wall_mask(8)
    for h, r in tiles(512):
        diag = full_of(diag8, got, h, r, 64)
        inv = jnp.where(wall8, 0.0, 1.0 / jnp.where(wall8, 1.0, diag))
        full = full_of(load, got, h, r)
        res[h, r : r + 8] = full
        inv8[h, r : r + 8] = inv
        u[h, r : r + 8] = inv * full * (1.0 / CENTER)
    fine_front(u, g8, acc, bd, bdt)
    send_faces(acc, even, face_a, face_b, 64)
    send_faces(diag4, even, face_a, face_b, 16, 64)
    for face in (face_a, face_b):
        for h in range(2):
            face[h, 80:88] = upper[...]


def inner_kernel(u, g8, bd, bdt, start, acc):
    for h, r in tiles(384):
        acc[h, 64 + r : 72 + r] = start[h, 64 + r : 72 + r]
    fine_cross(u, g8, acc, bd, bdt, PLANES[1:])
    join_fine(acc, range(1, 7))


def second_kernel(
    pos, res, inv8, acc, a, b, diag4, edges, g8, bd, bdt, down8,
    sol, rest, u, t4, inv4, edge_out, face_a, face_b, back, part,
):
    even = is_even(pos, 0)
    got = (even, a, b)
    edge = jnp.where((iota(8, 0) == 0) | (iota(8, 0) == 7), 0.5, 1.0)
    for h, r in tiles(512):
        inv, before = inv8[h, r : r + 8], res[h, r : r + 8]
        now = before - full_of(acc, got, h, r)
        old = inv * before * (1.0 / CENTER)
        new = KEEP * old + GAIN * inv * now
        rest[h, r : r + 8] = now
        sol[h, r : r + 8] = old + new
        u[h, r : r + 8] = new
    fine_apply(u, g8, back, bd, bdt)
    for h, r in tiles(512):
        s, c = r // 64, (r // 8) % 8
        scale = (0.5 if s in (0, 7) else 1.0) * (0.5 if c in (0, 7) else 1.0)
        part[r : r + 8, h * LANES : h * LANES + LANES] = (
            rest[h, r : r + 8] * (edge * scale) - back[h, r : r + 8]
        )
    put(t4, 0, 64, dot(down8[...], part[...]))
    join_mid(t4)
    send_faces(t4, even, face_a, face_b, 16)
    wall4 = wall_mask(4)
    for h, r in tiles(64):
        diag = full_of(diag4, got, h, r, 64)
        inv4[h, r : r + 8] = jnp.where(wall4, 0.0, 1.0 / jnp.where(wall4, 1.0, diag))
    lower = jnp.where(even, a[0, 80:88], b[0, 80:88])
    edge_out[...] = edges[...] + jnp.where(iota(8, 0) == 0, 0.0, lower)


def third_kernel(pos, t4, inv4, a, b, g4, gm, gmt, res, acc, face_a, face_b, u):
    even = is_even(pos, 0)
    for h, r in tiles(64):
        full = full_of(t4, (even, a, b), h, r)
        res[h, r : r + 8] = full
        u[h, r : r + 8] = inv4[h, r : r + 8] * full * (1.0 / CENTER)
    mid_apply(u, g4, acc, gm, gmt)
    join_mid(acc)
    send_faces(acc, even, face_a, face_b, 16)


def fourth_kernel(
    pos, res, acc, inv4, edge, a, b, g4, gm, gmt, m4, down4, corners, one, two, keep, part
):
    got = (is_even(pos, 0), a, b)
    even_a = is_even(pos, 1)
    for h, r in tiles(64):
        inv, before = inv4[h, r : r + 8], res[h, r : r + 8]
        now = before - full_of(acc, got, h, r)
        old = inv * before * (1.0 / CENTER)
        new = KEEP * old + GAIN * inv * now
        keep[h, r : r + 8] = now
        keep[h, 64 + r : 72 + r] = new
        keep[h, 128 + r : 136 + r] = old + new
    one[...] = jnp.where(even_a, keep[0], keep[1])
    two[...] = jnp.where(even_a, keep[1], keep[0])
    flux = dot(gm[...], wide(keep, 64, 64)) * wide(g4, 0, 192)
    put(part, 0, 64, dot(gmt[...], flux))
    for h, r in tiles(64):
        part[h, r : r + 8] = m4[r : r + 8] * keep[h, r : r + 8] - part[h, r : r + 8]
    low = dot(down4[...], wide(part, 0, 64))
    near = iota(8, 1) < HALF
    half0 = jnp.where(near, 0.0, low[:, :LANES])
    half1 = jnp.where(near, low[:, LANES:], 0.0)

    def corner(i, j, k):
        row = 4 * i + 2 * j + k
        return [half0[row : row + 1], half1[row : row + 1]]

    lane = iota(1, 1)
    mine, extra = [], []
    for i in range(2):
        columns = []
        for k in range(2):
            shifted = right(*corner(i, 1, k))
            straight = corner(i, 0, k)
            columns.append([straight[0] + shifted[0], straight[1] + shifted[1]])
        both = [columns[0][h] + pltpu.roll(columns[1][h], 1, 1) for h in range(2)]
        both = [jnp.where(lane % 16 == 0, 0.0, t) for t in both]
        mine.append(own_part(*both))
        extra.append(both[1])
    sides = jnp.where(lane < 16, pltpu.roll(extra[0], HALF, 1), 0.0) + jnp.where(
        (lane >= 16) & (lane < 32), pltpu.roll(extra[1], HALF + 16, 1), 0.0
    )
    none = jnp.zeros((2, LANES), F32)
    corners[...] = jnp.concatenate(mine + [sides, edge[0:3], none], axis=0)


def groups(ns):
    return max(1, ns // 8)


def column_kernel(rows, one, two, out):
    ns = rows.shape[0] // 8
    n = ns // groups(ns)

    def field(k):
        return rows[pl.ds(k, ns, stride=8), :]

    def later(x):
        return pltpu.roll(x, 1, 0)

    sides = field(2)
    over = jnp.where(iota(ns, 1) < 16, sides + later(pltpu.roll(sides, LANES - 16, 1)), 0.0)
    out[0:ns] = field(0) + later(field(1))
    for k in range(3):
        out[(1 + k) * ns : (2 + k) * ns] = field(3 + k)
    parts = [over[k * n : k * n + n] for k in range(groups(ns))]
    out[4 * ns : 4 * ns + n] = total(
        [pltpu.roll(p, 16 * k, 1) if k else p for k, p in enumerate(parts)]
    )


def coarse_kernel(
    pos, columns, keep, one, two, g4, gm, gmt, up4,
    res, sol, acc, face_a, face_b, vals, x2, es, ea, er, dg, ri, e4, up,
):
    ns = x2.shape[0]
    na = x2.shape[1] // LANES
    width = na * LANES

    n = ns // groups(ns)
    size = 4 * ns + n

    def field(k):
        return [columns[d * size + k * ns : d * size + (k + 1) * ns] for d in range(na)]

    def side(d):
        packed = columns[d * size + 4 * ns : (d + 1) * size]
        parts = [pltpu.roll(packed, LANES - 16 * k, 1) if k else packed for k in range(groups(ns))]
        return jnp.where(iota(ns, 1) < 16, jnp.concatenate(parts, axis=0), 0.0)

    def later(x):
        return pltpu.roll(x, 1, 0)

    def roll_l(x, k):
        return pltpu.roll(x, k % width, 1)

    wall = lax.broadcasted_iota(jnp.int32, (ns, width), 1) % 16 == 0
    mine = field(0)
    r = jnp.concatenate([mine[d] + side((d - 1) % na) for d in range(na)], axis=1)
    es[...] = jnp.concatenate(field(1), axis=1)
    ea[...] = jnp.concatenate(field(2), axis=1)
    er[...] = jnp.concatenate(field(3), axis=1)
    sum_all = es[...] + later(es[...]) + ea[...] + roll_l(ea[...], 16) + er[...] + roll_l(er[...], 1)
    dg[...] = jnp.where(wall, 0.0, sum_all)
    ri[...] = jnp.where(wall, 0.0, 1.0 / jnp.where(wall, 1.0, sum_all))

    def apply(p):
        q = dg[...] * p
        q = q - es[...] * pltpu.roll(p, ns - 1, 0) - later(es[...] * p)
        q = q - ea[...] * roll_l(p, -16) - roll_l(ea[...] * p, 16)
        q = q - er[...] * roll_l(p, -1) - roll_l(er[...] * p, 1)
        return jnp.where(wall, 0.0, q)

    def inner(x, y):
        return jnp.sum(jnp.sum(x * y, axis=0, keepdims=True), axis=1, keepdims=True)

    z = ri[...] * r
    p = z
    gz = inner(r, z)
    x = jnp.zeros_like(r)
    for it in range(ITERS):
        q = apply(p)
        alpha = gz / inner(p, q)
        x = x + alpha * p
        if it + 1 < ITERS:
            r = r - alpha * q
            z = ri[...] * r
            new = inner(r, z)
            p = z + (new / gz) * p
            gz = new
    x2[...] = x

    s, a = pos[0], pos[1]
    s_next = lax.rem(s + 1, ns)
    blocks = [lax.rem(a + na - 1, na), a, lax.rem(a + 1, na)]
    for i, row in enumerate((s, s_next)):
        line = x2[pl.ds(row, 1), :]
        for j in range(2):
            for k in range(2):
                n = 4 * i + 2 * j + k
                vals[n : n + 1, :] = roll_l(line, -(16 * j + k)) if j + k else line
    near = iota(8, 1) < HALF
    b = [
        pltpu.roll(vals[:, pl.ds(pl.multiple_of(t * LANES, LANES), LANES)], HALF, 1) for t in blocks
    ]
    ext = jnp.concatenate([jnp.where(near, b[0], b[1]), jnp.where(near, b[1], b[2])], axis=1)
    put(e4, 0, 64, dot(up4[...], ext))
    even_a = is_even(pos, 1)
    for r in range(0, 192, 8):
        x, y = one[r : r + 8], two[r : r + 8]
        before, after = jnp.where(even_a, x, y), jnp.where(even_a, y, x)
        half0 = jnp.where(near, before, keep[0, r : r + 8])
        half1 = jnp.where(near, keep[1, r : r + 8], after)
        for h, half in enumerate((half0, half1)):
            if r < 64:
                res[h, r : r + 8] = half
            elif r >= 128:
                sol[h, r - 128 : r - 120] = half + e4[h, r - 128 : r - 120]
            else:
                up[h, r - 64 : r - 56] = half + e4[h, r - 64 : r - 56]
    mid_apply(up, g4, acc, gm, gmt)
    join_mid(acc)
    send_faces(acc, is_even(pos, 0), face_a, face_b, 16)


def fifth_kernel(
    pos, before, sol, acc, a, b, inv4, g4, gm, gmt, res, u, out, acc2, face_a, face_b
):
    even = is_even(pos, 0)
    for h, r in tiles(64):
        now = before[h, r : r + 8] - full_of(acc, (even, a, b), h, r)
        new = inv4[h, r : r + 8] * now * (1.0 / CENTER)
        res[h, r : r + 8] = now
        u[h, r : r + 8] = new
        out[h, r : r + 8] = sol[h, r : r + 8] + new
    mid_apply(u, g4, acc2, gm, gmt)
    join_mid(acc2)
    send_faces(acc2, even, face_a, face_b, 16)


def sixth_kernel(
    pos, res, u, sol, acc, a, b, inv4, up8, sol8, u8, g8, bd, bdt,
    out, v8, acc2, face_a, face_b, y4,
):
    even = is_even(pos, 0)
    for h, r in tiles(64):
        now = res[h, r : r + 8] - full_of(acc, (even, a, b), h, r)
        new = KEEP * u[h, r : r + 8] + GAIN * inv4[h, r : r + 8] * now
        y4[h, r : r + 8] = sol[h, r : r + 8] + new
    put(v8, 0, 512, dot(up8[...], wide(y4, 0, 64)))
    for h, r in tiles(512):
        e8 = v8[h, r : r + 8]
        out[h, r : r + 8] = sol8[h, r : r + 8] + e8
        v8[h, r : r + 8] = u8[h, r : r + 8] + e8
    fine_front(v8, g8, acc2, bd, bdt)
    send_faces(acc2, even, face_a, face_b, 64)


def seventh_kernel(
    pos, rest, sol, acc, a, b, inv8, g8, bd, bdt, res, out, u, acc2, face_a, face_b
):
    even = is_even(pos, 0)
    for h, r in tiles(512):
        now = rest[h, r : r + 8] - full_of(acc, (even, a, b), h, r)
        new = inv8[h, r : r + 8] * now * (1.0 / CENTER)
        res[h, r : r + 8] = now
        u[h, r : r + 8] = new
        out[h, r : r + 8] = sol[h, r : r + 8] + new
    fine_front(u, g8, acc2, bd, bdt)
    send_faces(acc2, even, face_a, face_b, 64)


def last_kernel(pos, res, sol, u, acc, a, b, inv8, out):
    got = (is_even(pos, 0), a, b)
    for r in range(0, 512, 8):
        halves = []
        for h in range(2):
            now = res[h, r : r + 8] - full_of(acc, got, h, r)
            new = KEEP * u[h, r : r + 8] + GAIN * inv8[h, r : r + 8] * now
            halves.append(sol[h, r : r + 8] + new)
        out[r : r + 8] = own_part(*halves)


def call(kernel, args, outs, scratch=(), scalars=1, held=0, **options):
    vmem = pl.BlockSpec(memory_space=pltpu.VMEM)
    smem = pl.BlockSpec(memory_space=pltpu.SMEM)
    hbm = pl.BlockSpec(memory_space=pltpu.HBM)
    return pl.pallas_call(
        kernel,
        out_shape=[jax.ShapeDtypeStruct(s, F32) for s in outs],
        in_specs=[smem] * scalars + [hbm] * held + [vmem] * (len(args) - scalars - held),
        out_specs=[vmem] * len(outs),
        scratch_shapes=[pltpu.VMEM(s, F32) if isinstance(s, tuple) else s for s in scratch],
        compiler_params=pltpu.CompilerParams(vmem_limit_bytes=32 * 1024 * 1024),
        name=kernel.__name__,
        **options,
    )(*args)


def exchange(far, near, axis):
    size = lax.axis_size(axis)
    pairs_far = [(i, (i + 1 if i % 2 else i - 1) % size) for i in range(size)]
    pairs_near = [(i, i ^ 1) for i in range(size)]
    return lax.ppermute(far, axis, pairs_far), lax.ppermute(near, axis, pairs_near)


def spread(x, axis):
    size = lax.axis_size(axis)
    copies = jnp.broadcast_to(x[None], (size,) + x.shape)
    return lax.all_to_all(copies, axis, 0, 0).reshape(-1, LANES)


def on_device(element_load, metric, element_order):
    ns, na = lax.axis_size("stream"), lax.axis_size("azim")
    fine, mid = (2, 512, LANES), (2, 64, LANES)
    face8, face4 = [(2, 64, LANES)] * 2, [(2, 16, LANES)] * 2
    pos = jnp.stack([lax.axis_index("stream"), lax.axis_index("azim")]).astype(jnp.int32)
    held = list(CONSTANTS.values())
    rolled, a, b, *held = call(
        order_kernel,
        (pos, metric.reshape(1536, LANES), element_load.reshape(512, LANES), element_order, *held),
        [(2048, LANES), (1024, LANES), (1024, LANES)] + [c.shape for c in held],
        [
            (1536, LANES),
            (512, LANES),
            pltpu.VMEM((1, LANES), jnp.int32),
            pltpu.SemaphoreType.DMA((5 + len(held),)),
        ],
        held=3 + len(held),
    )
    c = dict(zip(CONSTANTS, held))
    bd, bdt, gm, gmt = c["bd"], c["bdt"], c["gm"], c["gmt"]

    def inner(u, acc):
        (acc,) = call(inner_kernel, (u, g8, bd, bdt, acc), [fine], (), 0, input_output_aliases={4: 0})
        return acc

    a, b = exchange(a, b, "azim")
    g8, load, diag8, a, b = call(
        setup_kernel,
        (pos, rolled, a, b, c["w8"], c["bsq"]),
        [(2, 1536, LANES), fine, fine] + [(2, 128, LANES)] * 2,
    )
    a, b = exchange(a, b, "stream")
    g4, diag4, edges, upper = call(
        coarsen_kernel,
        (g8, c["w4"], c["w2"], c["sample"], c["sq4"]),
        [(2, 192, LANES), mid, (8, LANES), (8, LANES)],
        scalars=0,
    )
    res8, inv8, u8, acc, a, b = call(
        first_kernel,
        (pos, load, diag8, a, b, g8, diag4, upper, bd, bdt),
        [fine, fine, fine, fine] + [(2, 88, LANES)] * 2,
    )
    a, b = exchange(a, b, "stream")
    acc = inner(u8, acc)
    sol8, rest8, u8, t4, inv4, edges, a, b = call(
        second_kernel,
        (pos, res8, inv8, acc, a, b, diag4, edges, g8, bd, bdt, c["down8"]),
        [fine, fine, fine, mid, mid, (8, LANES)] + face4,
        [fine, (512, 2 * LANES)],
    )
    a, b = exchange(a, b, "stream")
    res4, acc, a, b = call(
        third_kernel, (pos, t4, inv4, a, b, g4, gm, gmt), [mid, mid] + face4, [mid]
    )
    a, b = exchange(a, b, "stream")
    corners, a, b, keep = call(
        fourth_kernel,
        (pos, res4, acc, inv4, edges, a, b, g4, gm, gmt, c["m4"], c["down4"]),
        [(8, LANES), (192, LANES), (192, LANES), (2, 192, LANES)],
        [mid],
    )
    a, b = exchange(a, b, "azim")
    size = 4 * ns + ns // groups(ns)
    (columns,) = call(column_kernel, (spread(corners, "stream"), a, b), [(size, LANES)], (), 0)
    columns = spread(columns, "azim")
    whole = (ns, na * LANES)
    res4, sol4, acc, a, b = call(
        coarse_kernel,
        (pos, columns, keep, a, b, g4, gm, gmt, c["up4"]),
        [mid, mid, mid] + face4,
        [(8, na * LANES)] + [whole] * 6 + [mid, mid],
    )
    a, b = exchange(a, b, "stream")
    res4, u4, sol4, acc, a, b = call(
        fifth_kernel,
        (pos, res4, sol4, acc, a, b, inv4, g4, gm, gmt),
        [mid, mid, mid, mid] + face4,
    )
    a, b = exchange(a, b, "stream")
    sol8, v8, acc, a, b = call(
        sixth_kernel,
        (pos, res4, u4, sol4, acc, a, b, inv4, c["up8"], sol8, u8, g8, bd, bdt),
        [fine, fine, fine] + face8,
        [mid],
    )
    a, b = exchange(a, b, "stream")
    acc = inner(v8, acc)
    res8, sol8, u8, acc, a, b = call(
        seventh_kernel,
        (pos, rest8, sol8, acc, a, b, inv8, g8, bd, bdt),
        [fine, fine, fine, fine] + face8,
    )
    a, b = exchange(a, b, "stream")
    acc = inner(u8, acc)
    (out,) = call(last_kernel, (pos, res8, sol8, u8, acc, a, b, inv8), [(512, LANES)])
    return out.reshape(element_load.shape)


def solution(mesh):
    placed = (P(None, "stream", "azim"), P(None, None, "stream", "azim"), P("stream", "azim"))
    return jax.shard_map(
        on_device, mesh=mesh, in_specs=placed, out_specs=P(None, "stream", "azim"), check_vma=False
    )
```

```python
import jax
import jax.numpy as jnp
import numpy as np
from jax import lax
from jax.experimental import pallas as pl
from jax.experimental.pallas import tpu as pltpu
from jax.sharding import PartitionSpec as P

ITERS = 6
LOW_EIG = 0.3
HIGH_EIG = 3.0
CENTER = 0.5 * (HIGH_EIG + LOW_EIG)
HALF_WIDTH = 0.5 * (HIGH_EIG - LOW_EIG)
FIRST_RHO = HALF_WIDTH / CENTER
SECOND_RHO = 1.0 / (2.0 * CENTER / HALF_WIDTH - FIRST_RHO)
KEEP = SECOND_RHO * FIRST_RHO
GAIN = 2.0 * SECOND_RHO / HALF_WIDTH
LANES = 128
HALF = 64
F32 = jnp.float32


def legendre_pair(degree, places):
    previous = places * 0.0 + 1.0
    current = places.copy()
    for k in range(2, degree + 1):
        following = ((2 * k - 1) * places * current - (k - 1) * previous) / k
        previous = current
        current = following
    return (current, previous)


def gll_table(points):
    degree = points - 1
    places = np.cos(np.pi * np.arange(points) / degree)
    for _ in range(60):
        top, below = legendre_pair(degree, places)
        places = places - (places * top - below) / (points * top)
    nodes = np.sort(places)
    nodes[0] = -1.0
    nodes[-1] = 1.0
    at_nodes = legendre_pair(degree, nodes)[0]
    weights = 2.0 / (degree * (degree + 1) * at_nodes**2)
    deriv = np.zeros((points, points))
    for i in range(points):
        for j in range(points):
            if i != j:
                deriv[i, j] = at_nodes[i] / (at_nodes[j] * (nodes[i] - nodes[j]))
    deriv[0, 0] = -degree * (degree + 1) / 4.0
    deriv[-1, -1] = degree * (degree + 1) / 4.0
    return (nodes, weights, deriv)


def lagrange_table(source, target):
    out = np.ones((len(target), len(source)))
    for j in range(len(source)):
        for k in range(len(source)):
            if k != j:
                out[:, j] *= (target - source[k]) / (source[j] - source[k])
    return out


N8, W8, D8 = gll_table(8)
N4, W4, D4 = gll_table(4)
N2, W2, D2 = gll_table(2)


def kron3(a, b, c):
    return np.kron(np.kron(a, b), c)


def cube(w):
    return (w[:, None, None] * w[None, :, None] * w[None, None, :]).reshape(-1)


def share(n):
    edge = np.ones(n)
    edge[0] = edge[-1] = 0.5
    return cube(edge)


def grads(d):
    i = np.eye(d.shape[0])
    return [kron3(d, i, i), kron3(i, d, i), kron3(i, i, d)]


def f32(x):
    return np.asarray(x, np.float32)


def lanes_of(column):
    return np.repeat(f32(column)[:, None], LANES, axis=1)


UP8 = lagrange_table(N4, N8)
UP4 = lagrange_table(N2, N4)
TO4 = lagrange_table(N8, N4)
TO2 = lagrange_table(N8, N2)

C_BD = f32(np.kron(np.eye(16), D8))
C_BDT = f32(np.kron(np.eye(16), D8.T))
C_BSQ = f32(np.kron(np.eye(16), (D8 * D8).T))
C_SAMPLE = f32(np.concatenate([kron3(TO4, TO4, TO4), kron3(TO2, TO2, TO2)]))
C_UP8 = f32(kron3(UP8, UP8, UP8))
C_DOWN8 = f32(kron3(UP8, UP8, UP8).T)
C_UP4 = f32(kron3(UP4, UP4, UP4))
C_DOWN4 = f32(kron3(UP4, UP4, UP4).T)
C_UP4X3 = np.zeros((192, 16), np.float32)
for layer in range(3):
    C_UP4X3[64 * layer : 64 * layer + 64, 4 * layer : 4 * layer + 8] = C_UP4
C_G4 = f32(np.concatenate(grads(D4)))
C_G4T = f32(np.concatenate(grads(D4)).T)
C_SQ4 = f32((np.concatenate(grads(D4)) ** 2).T)
C_W8 = lanes_of(W8)
C_W4 = lanes_of(cube(W4) / np.exp(kron3(TO4, TO4, TO4) @ np.log(cube(W8))))
C_W2 = lanes_of(cube(W2) / np.exp(kron3(TO2, TO2, TO2) @ np.log(cube(W8))))
C_M4 = lanes_of(share(4))
CONSTANTS = {
    "bd": C_BD, "bdt": C_BDT, "bsq": C_BSQ, "sample": C_SAMPLE, "w8": C_W8, "w4": C_W4, "w2": C_W2,
    "sq4": C_SQ4, "gm": C_G4, "gmt": C_G4T, "m4": C_M4, "down8": C_DOWN8, "down4": C_DOWN4,
    "up4": C_UP4X3, "up8": C_UP8,
}


def pack_constants():
    rows, places, start = [], {}, 0
    for name, value in CONSTANTS.items():
        blocks = -(-value.shape[1] // LANES)
        padded = np.zeros((value.shape[0], blocks * LANES), np.float32)
        padded[:, : value.shape[1]] = value
        rows += [padded[:, k * LANES : (k + 1) * LANES] for k in range(blocks)]
        places[name] = (start, value.shape, blocks)
        start += value.shape[0] * blocks
    return np.concatenate(rows), places


PACK, PLACES = pack_constants()


class Constant:
    def __init__(self, ref, name):
        self.ref, self.name = ref, name

    def __getitem__(self, index):
        start, (rows, columns), blocks = PLACES[self.name]
        parts = []
        for k in range(blocks):
            width = min(LANES, columns - k * LANES)
            parts.append(self.ref[start + k * rows : start + (k + 1) * rows, :width])
        value = parts[0] if blocks == 1 else jnp.concatenate(parts, axis=1)
        return value if index is Ellipsis else value[index]


def dot(a, b):
    return jnp.dot(a, b, preferred_element_type=F32, precision=lax.Precision.HIGHEST)


def iota(rows, axis):
    return lax.broadcasted_iota(jnp.int32, (rows, LANES), axis)


def wide(ref, start, size):
    return jnp.concatenate([ref[0, start : start + size], ref[1, start : start + size]], axis=1)


def put(ref, start, size, value):
    ref[0, start : start + size] = value[:, :LANES]
    ref[1, start : start + size] = value[:, LANES:]


def total(terms):
    out = terms[0]
    for t in terms[1:]:
        out = out + t
    return out


def contract(v, matrix, sign):
    n = len(v)
    h = n // 2
    even = [v[k] + v[n - 1 - k] for k in range(h)]
    odd = [v[k] - v[n - 1 - k] for k in range(h)]
    out = [None] * n
    for i in range(h):
        p = total([even[k] * float(0.5 * (matrix[i, k] + matrix[i, n - 1 - k])) for k in range(h)])
        q = total([odd[k] * float(0.5 * (matrix[i, k] - matrix[i, n - 1 - k])) for k in range(h)])
        out[i] = p + q
        out[n - 1 - i] = q - p if sign < 0 else p - q
    return out


def fine_rows(s, a):
    return s * 64 + a * 8


PLANES = [(0, 7), (1, 2), (3, 4), (5, 6)]


def pair(ref, p, base=0):
    return jnp.concatenate([wide(ref, base + 64 * s, 64) for s in p], axis=0)


def put_pair(ref, p, value):
    for k, s in enumerate(p):
        put(ref, 64 * s, 64, value[64 * k : 64 * k + 64])


def fine_stream(u, g, acc):
    for h in range(2):
        for a in range(8):
            at = [fine_rows(s, a) for s in range(8)]
            grad = contract([u[h, r : r + 8] for r in at], D8, -1)
            back = contract([grad[s] * g[h, r : r + 8] for s, r in enumerate(at)], D8.T, -1)
            for s, r in enumerate(at):
                acc[h, r : r + 8] = back[s]


def fine_cross(u, g, acc, bd, bdt, pairs):
    for p in pairs:
        flux = dot(bd[...], pair(u, p)) * pair(g, p, 1024)
        put_pair(acc, p, pair(acc, p) + dot(bdt[...], flux))
        for s in p:
            for h in range(2):
                at = [fine_rows(s, a) for a in range(8)]
                grad = contract([u[h, r : r + 8] for r in at], D8, -1)
                flux = [grad[a] * g[h, 512 + r : 520 + r] for a, r in enumerate(at)]
                back = contract(flux, D8.T, -1)
                for a, r in enumerate(at):
                    acc[h, r : r + 8] += back[a]


def fine_apply(u, g, acc, bd, bdt):
    fine_stream(u, g, acc)
    fine_cross(u, g, acc, bd, bdt, PLANES)


def fine_front(u, g, acc, bd, bdt):
    fine_stream(u, g, acc)
    fine_cross(u, g, acc, bd, bdt, PLANES[:1])
    join_fine(acc, (0, 7))


def left(x0, x1):
    near = iota(x0.shape[0], 1) < LANES - 16
    y0, y1 = pltpu.roll(x0, LANES - 16, 1), pltpu.roll(x1, LANES - 16, 1)
    return jnp.where(near, y0, y1), jnp.where(near, y1, y0)


def right(x0, x1):
    near = iota(x0.shape[0], 1) >= 16
    y0, y1 = pltpu.roll(x0, 16, 1), pltpu.roll(x1, 16, 1)
    return jnp.where(near, y0, y1), jnp.where(near, y1, y0)


def join_radial(x, points, start, rows):
    place = iota(rows, 1) % 16
    first = pl.ds(start, rows, stride=points)
    last = pl.ds(start + points - 1, rows, stride=points)
    for h in range(2):
        view = x.at[h]
        low, high = view[first, :], view[last, :]
        view[first, :] = jnp.where(place == 0, 0.0, low + pltpu.roll(high, 1, 1))
        view[last, :] = jnp.where(place == 15, 0.0, high + pltpu.roll(low, LANES - 1, 1))


def join_fine(x, planes=range(8)):
    for s in planes:
        join_radial(x, 8, 64 * s, 8)
        lo, hi = fine_rows(s, 0), fine_rows(s, 7)
        low = [x[h, lo : lo + 8] for h in range(2)]
        high = [x[h, hi : hi + 8] for h in range(2)]
        to_low, to_high = right(*high), left(*low)
        for h in range(2):
            x[h, lo : lo + 8] = low[h] + to_low[h]
            x[h, hi : hi + 8] = high[h] + to_high[h]


def join_mid(x):
    join_radial(x, 4, 0, 16)
    first = iota(8, 0) < 4
    for s in range(4):
        lo, hi = s * 16, s * 16 + 8
        low = [x[h, lo : lo + 8] for h in range(2)]
        high = [x[h, hi : hi + 8] for h in range(2)]
        to_low = right(*[pltpu.roll(t, 4, 0) for t in high])
        to_high = left(*[pltpu.roll(t, 4, 0) for t in low])
        for h in range(2):
            x[h, lo : lo + 8] = low[h] + jnp.where(first, to_low[h], 0.0)
            x[h, hi : hi + 8] = high[h] + jnp.where(first, 0.0, to_high[h])


def is_even(place, k):
    return lax.rem(place[k], 2) == 0


def full_of(x, faces, h, r, offset=0):
    even, far, near = faces
    rows = x.shape[1]
    plane = {512: 64, 64: 16}[rows]
    value = x[h, r : r + 8]
    if r < plane:
        at = offset + r
        return value + jnp.where(even, far[h, at : at + 8], near[h, at : at + 8])
    if r >= rows - plane:
        at = offset + r - (rows - plane)
        return value + jnp.where(even, near[h, at : at + 8], far[h, at : at + 8])
    return value


def send_faces(x, even, far, near, plane, offset=0):
    rows = x.shape[1]
    last = rows - plane
    one = pl.multiple_of(jnp.where(even, last, 0), 8)
    two = pl.multiple_of(jnp.where(even, 0, last), 8)
    for h in range(2):
        near[h, offset : offset + plane] = x[h, pl.ds(one, plane), :]
        far[h, offset : offset + plane] = x[h, pl.ds(two, plane), :]


def wall_mask(points):
    place, node = iota(8, 1) % 16, iota(8, 0) % points
    return ((node == 0) & (place == 0)) | ((node == points - 1) & (place == 15))


def own_part(half0, half1):
    near = iota(half0.shape[0], 1) < HALF
    return pltpu.roll(jnp.where(near, half1, half0), HALF, 1)


def tiles(rows):
    return [(h, r) for h in range(2) for r in range(0, rows, 8)]


def mid_apply(u, g4, acc, gm, gmt):
    flux = dot(gm[...], wide(u, 0, 64)) * wide(g4, 0, 192)
    put(acc, 0, 64, dot(gmt[...], flux))


def order_kernel(place, metric, load, order, rolled, one, two):
    even = is_even(place, 1)
    near = iota(8, 1) < HALF
    slots = jnp.broadcast_to(pltpu.roll(order[...], HALF, 1), (8, LANES))

    def body(i, carry):
        r = pl.multiple_of(i * 8, 8)
        a = jnp.take_along_axis(metric[pl.ds(r, 8), :], slots, axis=1)
        rolled[pl.ds(r, 8), :] = a
        return carry

    lax.fori_loop(0, 192, body, 0, unroll=48)
    for r in range(0, 512, 8):
        rolled[1536 + r : 1536 + r + 8] = pltpu.roll(load[r : r + 8], HALF, 1)
    for r in range(0, 1024, 8):
        a, b = rolled[r : r + 8], rolled[1024 + r : 1024 + r + 8]
        up = jnp.where(near, a, pltpu.roll(b, HALF, 1))
        down = jnp.where(near, pltpu.roll(a, HALF, 1), b)
        one[r : r + 8] = jnp.where(even, down, up)
        two[r : r + 8] = jnp.where(even, up, down)


def setup_kernel(pos, rolled, one, two, w8, bsq, g8, load, diag8, face_a, face_b):
    near = iota(8, 1) < HALF
    wr = w8[...]
    even, even_a = is_even(pos, 0), is_even(pos, 1)

    def place(row, half0, half1):
        r = row % 512
        if row >= 1536:
            load[0, r : r + 8] = half0
            load[1, r : r + 8] = half1
            return
        scale = wr * float(W8[r // 64] * W8[(r // 8) % 8])
        g8[0, row : row + 8] = half0 * scale
        g8[1, row : row + 8] = half1 * scale

    for r in range(0, 1024, 8):
        a, b = rolled[r : r + 8], rolled[1024 + r : 1024 + r + 8]
        x, y = one[r : r + 8], two[r : r + 8]
        p, n = jnp.where(even_a, x, y), jnp.where(even_a, y, x)
        place(r, jnp.where(near, p, a), jnp.where(near, a, pltpu.roll(n, HALF, 1)))
        place(1024 + r, jnp.where(near, pltpu.roll(p, HALF, 1), b), jnp.where(near, b, n))
    for p in PLANES:
        put_pair(diag8, p, dot(bsq[...], pair(g8, p, 1024)))
    square = (D8 * D8).T
    for h in range(2):
        for axis in range(2):
            for fixed in range(8):
                at = [fine_rows(k, fixed) if axis == 0 else fine_rows(fixed, k) for k in range(8)]
                back = contract([g8[h, 512 * axis + r : 512 * axis + r + 8] for r in at], square, 1)
                for k, r in enumerate(at):
                    diag8[h, r : r + 8] += back[k]
    for x in (load, diag8):
        join_fine(x)
    send_faces(load, even, face_a, face_b, 64)
    send_faces(diag8, even, face_a, face_b, 64, 64)


def coarsen_kernel(g8, w4, w2, sample, sq4, g4, diag4, edges, upper):
    low = []
    for d in range(3):
        coarse = jnp.exp(dot(sample[...], jnp.log(wide(g8, 512 * d, 512))))
        put(g4, 64 * d, 64, coarse[:64] * jnp.concatenate([w4[...], w4[...]], axis=1))
        low.append([coarse[64:72, :LANES] * w2[...], coarse[64:72, LANES:] * w2[...]])
    put(diag4, 0, 64, dot(sq4[...], wide(g4, 0, 192)))
    join_mid(diag4)

    def corner(d, i, j, k):
        row = 4 * i + 2 * j + k
        return [t[row : row + 1] for t in low[d]]

    def add(x, y):
        return [x[0] + y[0], x[1] + y[1]]

    def quarter(x):
        return [0.25 * x[0], 0.25 * x[1]]

    def outward(x):
        return [pltpu.roll(x[0], 1, 1), pltpu.roll(x[1], 1, 1)]

    es = [[quarter(add(corner(0, 0, j, k), corner(0, 1, j, k))) for k in range(2)] for j in range(2)]
    ea = [[quarter(add(corner(1, i, 0, k), corner(1, i, 1, k))) for k in range(2)] for i in range(2)]
    er = [[quarter(add(corner(2, i, j, 0), corner(2, i, j, 1))) for j in range(2)] for i in range(2)]
    col = [add(es[0][k], list(right(*es[1][k]))) for k in range(2)]
    edge_s = add(col[0], outward(col[1]))
    edge_a = [add(ea[i][0], outward(ea[i][1])) for i in range(2)]
    edge_r = [add(er[i][0], list(right(*er[i][1]))) for i in range(2)]
    off_wall = iota(1, 1) % 16 != 0
    rows = [jnp.where(off_wall, own_part(*x), 0.0) for x in (edge_s, edge_a[0], edge_a[1])]
    rows += [own_part(*x) for x in edge_r]
    none = jnp.zeros((5, LANES), F32)
    edges[...] = jnp.concatenate([rows[0], rows[1], rows[3], none], axis=0)
    upper[...] = jnp.concatenate([rows[0], rows[2], rows[4], none], axis=0)


def first_kernel(
    pos, load, diag8, a, b, g8, diag4, upper, bd, bdt, res, inv8, u, acc, face_a, face_b
):
    even = is_even(pos, 0)
    got = (even, a, b)
    wall8 = wall_mask(8)
    for h, r in tiles(512):
        diag = full_of(diag8, got, h, r, 64)
        inv = jnp.where(wall8, 0.0, 1.0 / jnp.where(wall8, 1.0, diag))
        full = full_of(load, got, h, r)
        res[h, r : r + 8] = full
        inv8[h, r : r + 8] = inv
        u[h, r : r + 8] = inv * full * (1.0 / CENTER)
    fine_front(u, g8, acc, bd, bdt)
    send_faces(acc, even, face_a, face_b, 64)
    send_faces(diag4, even, face_a, face_b, 16, 64)
    for face in (face_a, face_b):
        for h in range(2):
            face[h, 80:88] = upper[...]


def inner_kernel(u, g8, start, bd, bdt, acc):
    for h, r in tiles(512):
        acc[h, r : r + 8] = start[h, r : r + 8]
    fine_cross(u, g8, acc, bd, bdt, PLANES[1:])
    join_fine(acc, range(1, 7))


def second_kernel(
    pos, res, inv8, acc, a, b, diag4, edges, g8, bd, bdt, down8,
    sol, rest, u, t4, inv4, edge_out, face_a, face_b, back, part,
):
    even = is_even(pos, 0)
    got = (even, a, b)
    edge = jnp.where((iota(8, 0) == 0) | (iota(8, 0) == 7), 0.5, 1.0)
    for h, r in tiles(512):
        inv, before = inv8[h, r : r + 8], res[h, r : r + 8]
        now = before - full_of(acc, got, h, r)
        old = inv * before * (1.0 / CENTER)
        new = KEEP * old + GAIN * inv * now
        rest[h, r : r + 8] = now
        sol[h, r : r + 8] = old + new
        u[h, r : r + 8] = new
    fine_apply(u, g8, back, bd, bdt)
    for h, r in tiles(512):
        s, c = r // 64, (r // 8) % 8
        scale = (0.5 if s in (0, 7) else 1.0) * (0.5 if c in (0, 7) else 1.0)
        part[r : r + 8, h * LANES : h * LANES + LANES] = (
            rest[h, r : r + 8] * (edge * scale) - back[h, r : r + 8]
        )
    put(t4, 0, 64, dot(down8[...], part[...]))
    join_mid(t4)
    send_faces(t4, even, face_a, face_b, 16)
    wall4 = wall_mask(4)
    for h, r in tiles(64):
        diag = full_of(diag4, got, h, r, 64)
        inv4[h, r : r + 8] = jnp.where(wall4, 0.0, 1.0 / jnp.where(wall4, 1.0, diag))
    lower = jnp.where(even, a[0, 80:88], b[0, 80:88])
    edge_out[...] = edges[...] + jnp.where(iota(8, 0) == 0, 0.0, lower)


def third_kernel(pos, t4, inv4, a, b, g4, gm, gmt, res, acc, face_a, face_b, u):
    even = is_even(pos, 0)
    for h, r in tiles(64):
        full = full_of(t4, (even, a, b), h, r)
        res[h, r : r + 8] = full
        u[h, r : r + 8] = inv4[h, r : r + 8] * full * (1.0 / CENTER)
    mid_apply(u, g4, acc, gm, gmt)
    join_mid(acc)
    send_faces(acc, even, face_a, face_b, 16)


def fourth_kernel(
    pos, res, acc, inv4, edge, a, b, g4, gm, gmt, m4, down4, corners, one, two, keep, part
):
    got = (is_even(pos, 0), a, b)
    even_a = is_even(pos, 1)
    for h, r in tiles(64):
        inv, before = inv4[h, r : r + 8], res[h, r : r + 8]
        now = before - full_of(acc, got, h, r)
        old = inv * before * (1.0 / CENTER)
        new = KEEP * old + GAIN * inv * now
        keep[h, r : r + 8] = now
        keep[h, 64 + r : 72 + r] = new
        keep[h, 128 + r : 136 + r] = old + new
    one[...] = jnp.where(even_a, keep[0], keep[1])
    two[...] = jnp.where(even_a, keep[1], keep[0])
    flux = dot(gm[...], wide(keep, 64, 64)) * wide(g4, 0, 192)
    put(part, 0, 64, dot(gmt[...], flux))
    for h, r in tiles(64):
        part[h, r : r + 8] = m4[r : r + 8] * keep[h, r : r + 8] - part[h, r : r + 8]
    low = dot(down4[...], wide(part, 0, 64))
    near = iota(8, 1) < HALF
    half0 = jnp.where(near, 0.0, low[:, :LANES])
    half1 = jnp.where(near, low[:, LANES:], 0.0)

    def corner(i, j, k):
        row = 4 * i + 2 * j + k
        return [half0[row : row + 1], half1[row : row + 1]]

    lane = iota(1, 1)
    mine, extra = [], []
    for i in range(2):
        columns = []
        for k in range(2):
            shifted = right(*corner(i, 1, k))
            straight = corner(i, 0, k)
            columns.append([straight[0] + shifted[0], straight[1] + shifted[1]])
        both = [columns[0][h] + pltpu.roll(columns[1][h], 1, 1) for h in range(2)]
        both = [jnp.where(lane % 16 == 0, 0.0, t) for t in both]
        mine.append(own_part(*both))
        extra.append(both[1])
    sides = jnp.where(lane < 16, pltpu.roll(extra[0], HALF, 1), 0.0) + jnp.where(
        (lane >= 16) & (lane < 32), pltpu.roll(extra[1], HALF + 16, 1), 0.0
    )
    none = jnp.zeros((2, LANES), F32)
    corners[...] = jnp.concatenate(mine + [sides, edge[0:3], none], axis=0)


def groups(ns):
    return max(1, ns // 8)


def side_kernel(pos, keep, one, two, g4, wider, message):
    near = iota(8, 1) < HALF
    even_a = is_even(pos, 1)
    for r in range(0, 192, 8):
        x, y = one[r : r + 8], two[r : r + 8]
        before, after = jnp.where(even_a, x, y), jnp.where(even_a, y, x)
        halves = (jnp.where(near, before, keep[0, r : r + 8]), jnp.where(near, keep[1, r : r + 8], after))
        for h in range(2):
            wider[h, r : r + 8] = halves[h]
            message[h, r : r + 8] = g4[h, r : r + 8]
            if 64 <= r < 128:
                message[h, 128 + r : 136 + r] = halves[h]


def column_kernel(rows, one, two, out):
    ns = rows.shape[0] // 8
    n = ns // groups(ns)

    def field(k):
        return rows[pl.ds(k, ns, stride=8), :]

    def later(x):
        return pltpu.roll(x, 1, 0)

    sides = field(2)
    over = jnp.where(iota(ns, 1) < 16, sides + later(pltpu.roll(sides, LANES - 16, 1)), 0.0)
    out[0:ns] = field(0) + later(field(1))
    for k in range(3):
        out[(1 + k) * ns : (2 + k) * ns] = field(3 + k)
    parts = [over[k * n : k * n + n] for k in range(groups(ns))]
    out[4 * ns : 4 * ns + n] = total(
        [pltpu.roll(p, 16 * k, 1) if k else p for k, p in enumerate(parts)]
    )


def coarse_kernel(
    pos, columns, others, wider, far, near_side, g4, inv4, gm, gmt, up4,
    res, u, sol, acc, face_a, face_b, vals, x2, es, ea, er, dg, ri,
):
    ns = x2.shape[0]
    na = x2.shape[1] // LANES
    width = na * LANES

    n = ns // groups(ns)
    size = 4 * ns + n
    even_a = is_even(pos, 1)

    def rows_of(d, start, count):
        at = d // 2 * size + start
        x, y = columns[at : at + count], others[at : at + count]
        return jnp.where(even_a, x, y) if d % 2 == 0 else jnp.where(even_a, y, x)

    def field(k):
        return [rows_of(d, k * ns, ns) for d in range(na)]

    def side(d):
        packed = rows_of(d, 4 * ns, n)
        parts = [pltpu.roll(packed, LANES - 16 * k, 1) if k else packed for k in range(groups(ns))]
        return jnp.where(iota(ns, 1) < 16, jnp.concatenate(parts, axis=0), 0.0)

    def later(x):
        return pltpu.roll(x, 1, 0)

    def roll_l(x, k):
        return pltpu.roll(x, k % width, 1)

    wall = lax.broadcasted_iota(jnp.int32, (ns, width), 1) % 16 == 0
    mine = field(0)
    r = jnp.concatenate([mine[d] + side((d - 1) % na) for d in range(na)], axis=1)
    es[...] = jnp.concatenate(field(1), axis=1)
    ea[...] = jnp.concatenate(field(2), axis=1)
    er[...] = jnp.concatenate(field(3), axis=1)
    sum_all = es[...] + later(es[...]) + ea[...] + roll_l(ea[...], 16) + er[...] + roll_l(er[...], 1)
    dg[...] = jnp.where(wall, 0.0, sum_all)
    ri[...] = jnp.where(wall, 0.0, 1.0 / jnp.where(wall, 1.0, sum_all))

    def apply(p):
        q = dg[...] * p
        q = q - es[...] * pltpu.roll(p, ns - 1, 0) - later(es[...] * p)
        q = q - ea[...] * roll_l(p, -16) - roll_l(ea[...] * p, 16)
        q = q - er[...] * roll_l(p, -1) - roll_l(er[...] * p, 1)
        return jnp.where(wall, 0.0, q)

    def inner(x, y):
        return jnp.sum(jnp.sum(x * y, axis=0, keepdims=True), axis=1, keepdims=True)

    z = ri[...] * r
    p = z
    gz = inner(r, z)
    x = jnp.zeros_like(r)
    for it in range(ITERS):
        q = apply(p)
        alpha = gz / inner(p, q)
        x = x + alpha * p
        if it + 1 < ITERS:
            r = r - alpha * q
            z = ri[...] * r
            new = inner(r, z)
            p = z + (new / gz) * p
            gz = new
    x2[...] = x

    s, a = pos[0], pos[1]
    blocks = [lax.rem(a + na - 1, na), a, lax.rem(a + 1, na)]
    for t in range(4):
        line = x2[pl.ds(lax.rem(s + ns - 1 + t, ns), 1), :]
        for j in range(2):
            for k in range(2):
                n = 4 * t + 2 * j + k
                vals[n : n + 1, :] = roll_l(line, -(16 * j + k)) if j + k else line
    near = iota(16, 1) < HALF
    b = [
        pltpu.roll(vals[:, pl.ds(pl.multiple_of(t * LANES, LANES), LANES)], HALF, 1) for t in blocks
    ]
    ext = jnp.concatenate([jnp.where(near, b[0], b[1]), jnp.where(near, b[1], b[2])], axis=1)
    rise = dot(up4[...], ext)
    even = is_even(pos, 0)
    below = [jnp.where(even, wide(far, r, 64), wide(near_side, r, 64)) for r in range(0, 256, 64)]
    above = [jnp.where(even, wide(near_side, r, 64), wide(far, r, 64)) for r in range(0, 256, 64)]
    mine = [wide(g4, r, 64) for r in range(0, 192, 64)] + [wide(wider, 64, 64)]
    layers = [below, mine, above]
    v = jnp.concatenate([rise[64 * q : 64 * q + 64] + layers[q][3] for q in range(3)], axis=1)
    weight = jnp.concatenate([jnp.concatenate(x[:3], axis=0) for x in layers], axis=1)
    back = dot(gmt[...], dot(gm[...], v) * weight)
    low, mid, high = [back[:, 256 * q : 256 * q + 256] for q in range(3)]
    put(acc, 0, 16, mid[:16] + low[48:])
    put(acc, 16, 32, mid[16:48])
    put(acc, 48, 16, mid[48:] + high[:16])
    join_mid(acc)
    put(sol, 0, 64, wide(wider, 128, 64) + rise[64:128])
    for h, r in tiles(64):
        now = wider[h, r : r + 8] - acc[h, r : r + 8]
        new = inv4[h, r : r + 8] * now * (1.0 / CENTER)
        res[h, r : r + 8] = now
        u[h, r : r + 8] = new
        sol[h, r : r + 8] += new
    mid_apply(u, g4, acc, gm, gmt)
    join_mid(acc)
    send_faces(acc, even, face_a, face_b, 16)


def sixth_kernel(
    pos, res, u, sol, acc, a, b, inv4, up8, sol8, u8, g8, bd, bdt,
    out, v8, acc2, face_a, face_b, y4,
):
    even = is_even(pos, 0)
    for h, r in tiles(64):
        now = res[h, r : r + 8] - full_of(acc, (even, a, b), h, r)
        new = KEEP * u[h, r : r + 8] + GAIN * inv4[h, r : r + 8] * now
        y4[h, r : r + 8] = sol[h, r : r + 8] + new
    put(v8, 0, 512, dot(up8[...], wide(y4, 0, 64)))
    for h, r in tiles(512):
        e8 = v8[h, r : r + 8]
        out[h, r : r + 8] = sol8[h, r : r + 8] + e8
        v8[h, r : r + 8] = u8[h, r : r + 8] + e8
    fine_front(v8, g8, acc2, bd, bdt)
    send_faces(acc2, even, face_a, face_b, 64)


def seventh_kernel(
    pos, rest, sol, acc, a, b, inv8, g8, bd, bdt, res, out, u, acc2, face_a, face_b
):
    even = is_even(pos, 0)
    for h, r in tiles(512):
        now = rest[h, r : r + 8] - full_of(acc, (even, a, b), h, r)
        new = inv8[h, r : r + 8] * now * (1.0 / CENTER)
        res[h, r : r + 8] = now
        u[h, r : r + 8] = new
        out[h, r : r + 8] = sol[h, r : r + 8] + new
    fine_front(u, g8, acc2, bd, bdt)
    send_faces(acc2, even, face_a, face_b, 64)


def last_kernel(pos, res, sol, u, acc, a, b, inv8, out):
    got = (is_even(pos, 0), a, b)
    for r in range(0, 512, 8):
        halves = []
        for h in range(2):
            now = res[h, r : r + 8] - full_of(acc, got, h, r)
            new = KEEP * u[h, r : r + 8] + GAIN * inv8[h, r : r + 8] * now
            halves.append(sol[h, r : r + 8] + new)
        out[r : r + 8] = own_part(*halves)


def call(kernel, args, outs, scratch=(), scalars=1, **options):
    vmem = pl.BlockSpec(memory_space=pltpu.VMEM)
    smem = pl.BlockSpec(memory_space=pltpu.SMEM)
    arrays = [x for x in args if not isinstance(x, str)]
    named = len(arrays) < len(args)

    def body(*refs):
        rest = iter(refs)
        given = [next(rest) for _ in arrays[: len(arrays) - named]]
        held = next(rest) if named else None
        given = iter(given)
        full = [Constant(held, x) if isinstance(x, str) else next(given) for x in args]
        kernel(*full, *rest)

    if named:
        arrays.append(PACK)
    return pl.pallas_call(
        body,
        out_shape=[jax.ShapeDtypeStruct(s, F32) for s in outs],
        in_specs=[smem] * scalars + [vmem] * (len(arrays) - scalars),
        out_specs=[vmem] * len(outs),
        scratch_shapes=[pltpu.VMEM(s, F32) for s in scratch],
        compiler_params=pltpu.CompilerParams(vmem_limit_bytes=32 * 1024 * 1024),
        name=kernel.__name__,
        **options,
    )(*arrays)


def exchange(far, near, axis):
    size = lax.axis_size(axis)
    pairs_far = [(i, (i + 1 if i % 2 else i - 1) % size) for i in range(size)]
    pairs_near = [(i, i ^ 1) for i in range(size)]
    return lax.ppermute(far, axis, pairs_far), lax.ppermute(near, axis, pairs_near)


def spread(x, axis, groups=None):
    size = len(groups[0]) if groups else lax.axis_size(axis)
    copies = jnp.broadcast_to(x[None], (size,) + x.shape)
    return lax.all_to_all(copies, axis, 0, 0, axis_index_groups=groups).reshape(-1, LANES)


def on_device(element_load, metric, element_order):
    ns, na = lax.axis_size("stream"), lax.axis_size("azim")
    fine, mid = (2, 512, LANES), (2, 64, LANES)
    face8, face4 = [(2, 64, LANES)] * 2, [(2, 16, LANES)] * 2
    pos = jnp.stack([lax.axis_index("stream"), lax.axis_index("azim")]).astype(jnp.int32)
    rolled, a, b = call(
        order_kernel,
        (pos, metric.reshape(1536, LANES), element_load.reshape(512, LANES), element_order),
        [(2048, LANES), (1024, LANES), (1024, LANES)],
    )

    def inner(u, acc):
        (acc,) = call(inner_kernel, (u, g8, acc, "bd", "bdt"), [fine], (), 0)
        return acc

    a, b = exchange(a, b, "azim")
    g8, load, diag8, a, b = call(
        setup_kernel,
        (pos, rolled, a, b, "w8", "bsq"),
        [(2, 1536, LANES), fine, fine] + [(2, 128, LANES)] * 2,
    )
    a, b = exchange(a, b, "stream")
    g4, diag4, edges, upper = call(
        coarsen_kernel,
        (g8, "w4", "w2", "sample", "sq4"),
        [(2, 192, LANES), mid, (8, LANES), (8, LANES)],
        scalars=0,
    )
    res8, inv8, u8, acc, a, b = call(
        first_kernel,
        (pos, load, diag8, a, b, g8, diag4, upper, "bd", "bdt"),
        [fine, fine, fine, fine] + [(2, 88, LANES)] * 2,
    )
    a, b = exchange(a, b, "stream")
    acc = inner(u8, acc)
    sol8, rest8, u8, t4, inv4, edges, a, b = call(
        second_kernel,
        (pos, res8, inv8, acc, a, b, diag4, edges, g8, "bd", "bdt", "down8"),
        [fine, fine, fine, mid, mid, (8, LANES)] + face4,
        [fine, (512, 2 * LANES)],
    )
    a, b = exchange(a, b, "stream")
    res4, acc, a, b = call(
        third_kernel, (pos, t4, inv4, a, b, g4, "gm", "gmt"), [mid, mid] + face4, [mid]
    )
    a, b = exchange(a, b, "stream")
    corners, a, b, keep = call(
        fourth_kernel,
        (pos, res4, acc, inv4, edges, a, b, g4, "gm", "gmt", "m4", "down4"),
        [(8, LANES), (192, LANES), (192, LANES), (2, 192, LANES)],
        [mid],
    )
    a, b = exchange(a, b, "azim")
    size = 4 * ns + ns // groups(ns)
    (columns,) = call(column_kernel, (spread(corners, "stream"), a, b), [(size, LANES)], (), 0)
    cores = [list(range(core, na, 2)) for core in range(2)]
    columns = spread(columns, "azim", cores)
    others = lax.ppermute(columns, "azim", [(i, i ^ 1) for i in range(na)])
    wider, message = call(
        side_kernel, (pos, keep, a, b, g4), [(2, 192, LANES), (2, 256, LANES)]
    )
    sides = exchange(message, message, "stream")
    whole = (ns, na * LANES)
    res4, u4, sol4, acc, a, b = call(
        coarse_kernel,
        (pos, columns, others, wider, *sides, g4, inv4, "gm", "gmt", "up4"),
        [mid, mid, mid, mid] + face4,
        [(16, na * LANES)] + [whole] * 6,
    )
    a, b = exchange(a, b, "stream")
    sol8, v8, acc, a, b = call(
        sixth_kernel,
        (pos, res4, u4, sol4, acc, a, b, inv4, "up8", sol8, u8, g8, "bd", "bdt"),
        [fine, fine, fine] + face8,
        [mid],
    )
    a, b = exchange(a, b, "stream")
    acc = inner(v8, acc)
    res8, sol8, u8, acc, a, b = call(
        seventh_kernel,
        (pos, rest8, sol8, acc, a, b, inv8, g8, "bd", "bdt"),
        [fine, fine, fine, fine] + face8,
    )
    a, b = exchange(a, b, "stream")
    acc = inner(u8, acc)
    (out,) = call(last_kernel, (pos, res8, sol8, u8, acc, a, b, inv8), [(512, LANES)])
    return out.reshape(element_load.shape)


def solution(mesh):
    placed = (P(None, "stream", "azim"), P(None, None, "stream", "azim"), P("stream", "azim"))
    return jax.shard_map(
        on_device, mesh=mesh, in_specs=placed, out_specs=P(None, "stream", "azim"), check_vma=False
    )
```

```python
import jax
import jax.numpy as jnp
import numpy as np
from jax import lax
from jax.experimental import pallas as pl
from jax.experimental.pallas import tpu as pltpu
from jax.sharding import PartitionSpec as P

ITERS = 6
LOW_EIG = 0.3
HIGH_EIG = 3.0
CENTER = 0.5 * (HIGH_EIG + LOW_EIG)
HALF_WIDTH = 0.5 * (HIGH_EIG - LOW_EIG)
FIRST_RHO = HALF_WIDTH / CENTER
SECOND_RHO = 1.0 / (2.0 * CENTER / HALF_WIDTH - FIRST_RHO)
KEEP = SECOND_RHO * FIRST_RHO
GAIN = 2.0 * SECOND_RHO / HALF_WIDTH
LANES = 128
HALF = 64
F32 = jnp.float32


def legendre_pair(degree, places):
    previous = places * 0.0 + 1.0
    current = places.copy()
    for k in range(2, degree + 1):
        following = ((2 * k - 1) * places * current - (k - 1) * previous) / k
        previous = current
        current = following
    return (current, previous)


def gll_table(points):
    degree = points - 1
    places = np.cos(np.pi * np.arange(points) / degree)
    for _ in range(60):
        top, below = legendre_pair(degree, places)
        places = places - (places * top - below) / (points * top)
    nodes = np.sort(places)
    nodes[0] = -1.0
    nodes[-1] = 1.0
    at_nodes = legendre_pair(degree, nodes)[0]
    weights = 2.0 / (degree * (degree + 1) * at_nodes**2)
    deriv = np.zeros((points, points))
    for i in range(points):
        for j in range(points):
            if i != j:
                deriv[i, j] = at_nodes[i] / (at_nodes[j] * (nodes[i] - nodes[j]))
    deriv[0, 0] = -degree * (degree + 1) / 4.0
    deriv[-1, -1] = degree * (degree + 1) / 4.0
    return (nodes, weights, deriv)


def lagrange_table(source, target):
    out = np.ones((len(target), len(source)))
    for j in range(len(source)):
        for k in range(len(source)):
            if k != j:
                out[:, j] *= (target - source[k]) / (source[j] - source[k])
    return out


N8, W8, D8 = gll_table(8)
N4, W4, D4 = gll_table(4)
N2, W2, D2 = gll_table(2)


def kron3(a, b, c):
    return np.kron(np.kron(a, b), c)


def cube(w):
    return (w[:, None, None] * w[None, :, None] * w[None, None, :]).reshape(-1)


def share(n):
    edge = np.ones(n)
    edge[0] = edge[-1] = 0.5
    return cube(edge)


def grads(d):
    i = np.eye(d.shape[0])
    return [kron3(d, i, i), kron3(i, d, i), kron3(i, i, d)]


def f32(x):
    return np.asarray(x, np.float32)


def lanes_of(column):
    return np.repeat(f32(column)[:, None], LANES, axis=1)


UP8 = lagrange_table(N4, N8)
UP4 = lagrange_table(N2, N4)
TO4 = lagrange_table(N8, N4)
TO2 = lagrange_table(N8, N2)

C_BD = f32(np.kron(np.eye(16), D8))
C_BDT = f32(np.kron(np.eye(16), D8.T))
C_BSQ = f32(np.kron(np.eye(16), (D8 * D8).T))
C_SAMPLE = f32(np.concatenate([kron3(TO4, TO4, TO4), kron3(TO2, TO2, TO2)]))
C_UP8 = f32(kron3(UP8, UP8, UP8))
C_DOWN8 = f32(kron3(UP8, UP8, UP8).T)
C_UP4 = f32(kron3(UP4, UP4, UP4))
C_DOWN4 = f32(kron3(UP4, UP4, UP4).T)
C_UP4X3 = np.zeros((192, 16), np.float32)
for layer in range(3):
    C_UP4X3[64 * layer : 64 * layer + 64, 4 * layer : 4 * layer + 8] = C_UP4
C_G4 = f32(np.concatenate(grads(D4)))
C_G4T = f32(np.concatenate(grads(D4)).T)
C_SQ4 = f32((np.concatenate(grads(D4)) ** 2).T)
C_W8 = lanes_of(W8)
C_W4 = lanes_of(cube(W4) / np.exp(kron3(TO4, TO4, TO4) @ np.log(cube(W8))))
C_W2 = lanes_of(cube(W2) / np.exp(kron3(TO2, TO2, TO2) @ np.log(cube(W8))))
C_M4 = lanes_of(share(4))
CONSTANTS = {
    "bd": C_BD, "bdt": C_BDT, "bsq": C_BSQ, "sample": C_SAMPLE, "w8": C_W8, "w4": C_W4, "w2": C_W2,
    "sq4": C_SQ4, "gm": C_G4, "gmt": C_G4T, "m4": C_M4, "down8": C_DOWN8, "down4": C_DOWN4,
    "up4": C_UP4X3, "up8": C_UP8,
}


def pack_constants():
    rows, places, start = [], {}, 0
    for name, value in CONSTANTS.items():
        blocks = -(-value.shape[1] // LANES)
        padded = np.zeros((value.shape[0], blocks * LANES), np.float32)
        padded[:, : value.shape[1]] = value
        rows += [padded[:, k * LANES : (k + 1) * LANES] for k in range(blocks)]
        places[name] = (start, value.shape, blocks)
        start += value.shape[0] * blocks
    return np.concatenate(rows), places


PACK, PLACES = pack_constants()


class Constant:
    def __init__(self, ref, name):
        self.ref, self.name = ref, name

    def __getitem__(self, index):
        start, (rows, columns), blocks = PLACES[self.name]
        parts = []
        for k in range(blocks):
            width = min(LANES, columns - k * LANES)
            parts.append(self.ref[start + k * rows : start + (k + 1) * rows, :width])
        value = parts[0] if blocks == 1 else jnp.concatenate(parts, axis=1)
        return value if index is Ellipsis else value[index]


def dot(a, b):
    return jnp.dot(a, b, preferred_element_type=F32, precision=lax.Precision.HIGHEST)


def iota(rows, axis):
    return lax.broadcasted_iota(jnp.int32, (rows, LANES), axis)


def wide(ref, start, size):
    return jnp.concatenate([ref[0, start : start + size], ref[1, start : start + size]], axis=1)


def put(ref, start, size, value):
    ref[0, start : start + size] = value[:, :LANES]
    ref[1, start : start + size] = value[:, LANES:]


def total(terms):
    out = terms[0]
    for t in terms[1:]:
        out = out + t
    return out


def contract(v, matrix, sign):
    n = len(v)
    h = n // 2
    even = [v[k] + v[n - 1 - k] for k in range(h)]
    odd = [v[k] - v[n - 1 - k] for k in range(h)]
    out = [None] * n
    for i in range(h):
        p = total([even[k] * float(0.5 * (matrix[i, k] + matrix[i, n - 1 - k])) for k in range(h)])
        q = total([odd[k] * float(0.5 * (matrix[i, k] - matrix[i, n - 1 - k])) for k in range(h)])
        out[i] = p + q
        out[n - 1 - i] = q - p if sign < 0 else p - q
    return out


def fine_rows(s, a):
    return s * 64 + a * 8


PLANES = [(0, 7), (1, 2), (3, 4), (5, 6)]


def pair(ref, p, base=0):
    return jnp.concatenate([wide(ref, base + 64 * s, 64) for s in p], axis=0)


def put_pair(ref, p, value):
    for k, s in enumerate(p):
        put(ref, 64 * s, 64, value[64 * k : 64 * k + 64])


def fine_stream(u, g, acc):
    for h in range(2):
        for a in range(8):
            at = [fine_rows(s, a) for s in range(8)]
            grad = contract([u[h, r : r + 8] for r in at], D8, -1)
            back = contract([grad[s] * g[h, r : r + 8] for s, r in enumerate(at)], D8.T, -1)
            for s, r in enumerate(at):
                acc[h, r : r + 8] = back[s]


def fine_cross(u, g, acc, bd, bdt, pairs):
    for p in pairs:
        flux = dot(bd[...], pair(u, p)) * pair(g, p, 1024)
        put_pair(acc, p, pair(acc, p) + dot(bdt[...], flux))
        for s in p:
            for h in range(2):
                at = [fine_rows(s, a) for a in range(8)]
                grad = contract([u[h, r : r + 8] for r in at], D8, -1)
                flux = [grad[a] * g[h, 512 + r : 520 + r] for a, r in enumerate(at)]
                back = contract(flux, D8.T, -1)
                for a, r in enumerate(at):
                    acc[h, r : r + 8] += back[a]


def fine_apply(u, g, acc, bd, bdt):
    fine_stream(u, g, acc)
    fine_cross(u, g, acc, bd, bdt, PLANES)


def fine_front(u, g, acc, bd, bdt):
    fine_stream(u, g, acc)
    fine_cross(u, g, acc, bd, bdt, PLANES[:1])
    join_fine(acc, (0, 7))


def left(x0, x1):
    near = iota(x0.shape[0], 1) < LANES - 16
    y0, y1 = pltpu.roll(x0, LANES - 16, 1), pltpu.roll(x1, LANES - 16, 1)
    return jnp.where(near, y0, y1), jnp.where(near, y1, y0)


def right(x0, x1):
    near = iota(x0.shape[0], 1) >= 16
    y0, y1 = pltpu.roll(x0, 16, 1), pltpu.roll(x1, 16, 1)
    return jnp.where(near, y0, y1), jnp.where(near, y1, y0)


def join_radial(x, points, start, rows):
    place = iota(rows, 1) % 16
    first = pl.ds(start, rows, stride=points)
    last = pl.ds(start + points - 1, rows, stride=points)
    for h in range(2):
        view = x.at[h]
        low, high = view[first, :], view[last, :]
        view[first, :] = jnp.where(place == 0, 0.0, low + pltpu.roll(high, 1, 1))
        view[last, :] = jnp.where(place == 15, 0.0, high + pltpu.roll(low, LANES - 1, 1))


def join_fine(x, planes=range(8)):
    for s in planes:
        join_radial(x, 8, 64 * s, 8)
        lo, hi = fine_rows(s, 0), fine_rows(s, 7)
        low = [x[h, lo : lo + 8] for h in range(2)]
        high = [x[h, hi : hi + 8] for h in range(2)]
        to_low, to_high = right(*high), left(*low)
        for h in range(2):
            x[h, lo : lo + 8] = low[h] + to_low[h]
            x[h, hi : hi + 8] = high[h] + to_high[h]


def join_mid(x):
    join_radial(x, 4, 0, 16)
    first = iota(8, 0) < 4
    for s in range(4):
        lo, hi = s * 16, s * 16 + 8
        low = [x[h, lo : lo + 8] for h in range(2)]
        high = [x[h, hi : hi + 8] for h in range(2)]
        to_low = right(*[pltpu.roll(t, 4, 0) for t in high])
        to_high = left(*[pltpu.roll(t, 4, 0) for t in low])
        for h in range(2):
            x[h, lo : lo + 8] = low[h] + jnp.where(first, to_low[h], 0.0)
            x[h, hi : hi + 8] = high[h] + jnp.where(first, 0.0, to_high[h])


def is_even(place, k):
    return lax.rem(place[k], 2) == 0


def full_of(x, faces, h, r, offset=0):
    even, far, near = faces
    rows = x.shape[1]
    plane = {512: 64, 64: 16}[rows]
    value = x[h, r : r + 8]
    if r < plane:
        at = offset + r
        return value + jnp.where(even, far[h, at : at + 8], near[h, at : at + 8])
    if r >= rows - plane:
        at = offset + r - (rows - plane)
        return value + jnp.where(even, near[h, at : at + 8], far[h, at : at + 8])
    return value


def send_faces(x, even, far, near, plane, offset=0):
    rows = x.shape[1]
    last = rows - plane
    one = pl.multiple_of(jnp.where(even, last, 0), 8)
    two = pl.multiple_of(jnp.where(even, 0, last), 8)
    for h in range(2):
        near[h, offset : offset + plane] = x[h, pl.ds(one, plane), :]
        far[h, offset : offset + plane] = x[h, pl.ds(two, plane), :]


def wall_mask(points):
    place, node = iota(8, 1) % 16, iota(8, 0) % points
    return ((node == 0) & (place == 0)) | ((node == points - 1) & (place == 15))


def own_part(half0, half1):
    near = iota(half0.shape[0], 1) < HALF
    return pltpu.roll(jnp.where(near, half1, half0), HALF, 1)


def tiles(rows):
    return [(h, r) for h in range(2) for r in range(0, rows, 8)]


def mid_apply(u, g4, acc, gm, gmt):
    flux = dot(gm[...], wide(u, 0, 64)) * wide(g4, 0, 192)
    put(acc, 0, 64, dot(gmt[...], flux))


def fine_diagonal(g, diag, bsq):
    square = (D8 * D8).T
    for c in range(4):
        rows = slice(128 * c, 128 * c + 128)
        diag[rows] = dot(bsq[...], g[1024 + 128 * c : 1152 + 128 * c])
    for axis in range(2):
        for fixed in range(8):
            at = [fine_rows(k, fixed) if axis == 0 else fine_rows(fixed, k) for k in range(8)]
            back = contract([g[512 * axis + r : 512 * axis + r + 8] for r in at], square, 1)
            for k, r in enumerate(at):
                diag[r : r + 8] += back[k]


def halves_up_down(a, b):
    near = iota(8, 1) < HALF
    up = jnp.where(near, a, pltpu.roll(b, HALF, 1))
    return up, jnp.where(near, pltpu.roll(a, HALF, 1), b)


def before_after(even, x, y):
    p, n = jnp.where(even, x, y), jnp.where(even, y, x)
    near = iota(8, 1) < HALF
    first = (jnp.where(near, p, 0.0), jnp.where(near, 0.0, pltpu.roll(n, HALF, 1)))
    second = (jnp.where(near, pltpu.roll(p, HALF, 1), 0.0), jnp.where(near, 0.0, n))
    return first, second


def order_kernel(pos, metric, load, order, w8, bsq, g, rolled, diag, far, near):
    even = is_even(pos, 1)
    slots = jnp.broadcast_to(pltpu.roll(order[...], HALF, 1), (8, LANES))
    wr = w8[...]
    for r in range(0, 1536, 8):
        scale = wr * float(W8[(r % 512) // 64] * W8[(r // 8) % 8])
        g[r : r + 8] = jnp.take_along_axis(metric[r : r + 8], slots, axis=1) * scale
    for r in range(0, 512, 8):
        rolled[r : r + 8] = pltpu.roll(load[r : r + 8], HALF, 1)
    fine_diagonal(g, diag, bsq)
    for r in range(0, 128, 8):
        at = r if r < 64 else 384 + r
        up, down = halves_up_down(rolled[at : at + 8], diag[at : at + 8])
        far[r : r + 8] = jnp.where(even, down, up)
        near[r : r + 8] = jnp.where(even, up, down)


def bulk_kernel(pos, g, rolled, first, second, far, near):
    even = is_even(pos, 1)
    for r in range(0, 1024, 8):
        other = g[1024 + r : 1032 + r] if r < 512 else rolled[r - 512 : r - 504]
        up, down = halves_up_down(g[r : r + 8], other)
        far[r : r + 8] = jnp.where(even, down, up)
        near[r : r + 8] = jnp.where(even, up, down)


def face_kernel(pos, rolled, diag, x, y, face_a, face_b, planes):
    even, even_a = is_even(pos, 0), is_even(pos, 1)
    near = iota(8, 1) < HALF
    for r in range(0, 128, 8):
        at = r if r < 64 else 384 + r
        ghosts = before_after(even_a, x[r : r + 8], y[r : r + 8])
        for k, (mine, ghost) in enumerate(zip((rolled, diag), ghosts)):
            own = mine[at : at + 8]
            planes[0, 128 * k + r : 128 * k + r + 8] = jnp.where(near, ghost[0], own)
            planes[1, 128 * k + r : 128 * k + r + 8] = jnp.where(near, own, ghost[1])
    join_fine(planes, range(4))
    one = pl.multiple_of(jnp.where(even, 0, 64), 8)
    two = pl.multiple_of(jnp.where(even, 64, 0), 8)
    for h in range(2):
        for k in range(2):
            face_a[h, 64 * k : 64 * k + 64] = planes[h, pl.ds(128 * k + one, 64), :]
            face_b[h, 64 * k : 64 * k + 64] = planes[h, pl.ds(128 * k + two, 64), :]


def setup_kernel(pos, g, rolled, diag, x, y, bsq, g8, load, diag8, ghost, ghost_diag):
    near = iota(8, 1) < HALF
    even_a = is_even(pos, 1)

    def place(out, row, own, sides):
        out[0, row : row + 8] = jnp.where(near, sides[0], own)
        out[1, row : row + 8] = jnp.where(near, own, sides[1])

    for r in range(0, 1024, 8):
        first, second = before_after(even_a, x[r : r + 8], y[r : r + 8])
        place(g8, r, g[r : r + 8], first)
        ghost[r : r + 8] = first[0] + first[1]
        if r < 512:
            place(g8, 1024 + r, g[1024 + r : 1032 + r], second)
            ghost[1024 + r : 1032 + r] = second[0] + second[1]
        else:
            place(load, r - 512, rolled[r - 512 : r - 504], second)
    fine_diagonal(ghost, ghost_diag, bsq)
    for r in range(0, 512, 8):
        side = ghost_diag[r : r + 8]
        place(diag8, r, diag[r : r + 8], (side, side))
    for x in (load, diag8):
        join_fine(x)


def coarsen_kernel(g8, w4, w2, sample, sq4, g4, diag4, edges, upper):
    low = []
    for d in range(3):
        coarse = jnp.exp(dot(sample[...], jnp.log(wide(g8, 512 * d, 512))))
        put(g4, 64 * d, 64, coarse[:64] * jnp.concatenate([w4[...], w4[...]], axis=1))
        low.append([coarse[64:72, :LANES] * w2[...], coarse[64:72, LANES:] * w2[...]])
    put(diag4, 0, 64, dot(sq4[...], wide(g4, 0, 192)))
    join_mid(diag4)

    def corner(d, i, j, k):
        row = 4 * i + 2 * j + k
        return [t[row : row + 1] for t in low[d]]

    def add(x, y):
        return [x[0] + y[0], x[1] + y[1]]

    def quarter(x):
        return [0.25 * x[0], 0.25 * x[1]]

    def outward(x):
        return [pltpu.roll(x[0], 1, 1), pltpu.roll(x[1], 1, 1)]

    es = [[quarter(add(corner(0, 0, j, k), corner(0, 1, j, k))) for k in range(2)] for j in range(2)]
    ea = [[quarter(add(corner(1, i, 0, k), corner(1, i, 1, k))) for k in range(2)] for i in range(2)]
    er = [[quarter(add(corner(2, i, j, 0), corner(2, i, j, 1))) for j in range(2)] for i in range(2)]
    col = [add(es[0][k], list(right(*es[1][k]))) for k in range(2)]
    edge_s = add(col[0], outward(col[1]))
    edge_a = [add(ea[i][0], outward(ea[i][1])) for i in range(2)]
    edge_r = [add(er[i][0], list(right(*er[i][1]))) for i in range(2)]
    off_wall = iota(1, 1) % 16 != 0
    rows = [jnp.where(off_wall, own_part(*x), 0.0) for x in (edge_s, edge_a[0], edge_a[1])]
    rows += [own_part(*x) for x in edge_r]
    none = jnp.zeros((5, LANES), F32)
    edges[...] = jnp.concatenate([rows[0], rows[1], rows[3], none], axis=0)
    upper[...] = jnp.concatenate([rows[0], rows[2], rows[4], none], axis=0)


def first_kernel(
    pos, load, diag8, a, b, g8, bd, bdt, res, inv8, u, acc, face_a, face_b
):
    even = is_even(pos, 0)
    got = (even, a, b)
    wall8 = wall_mask(8)
    for h, r in tiles(512):
        diag = full_of(diag8, got, h, r, 64)
        inv = jnp.where(wall8, 0.0, 1.0 / jnp.where(wall8, 1.0, diag))
        full = full_of(load, got, h, r)
        res[h, r : r + 8] = full
        inv8[h, r : r + 8] = inv
        u[h, r : r + 8] = inv * full * (1.0 / CENTER)
    fine_front(u, g8, acc, bd, bdt)
    send_faces(acc, even, face_a, face_b, 64)


def inner_kernel(u, g8, start, bd, bdt, acc):
    for h, r in tiles(512):
        acc[h, r : r + 8] = start[h, r : r + 8]
    fine_cross(u, g8, acc, bd, bdt, PLANES[1:])
    join_fine(acc, range(1, 7))


def second_kernel(
    pos, res, inv8, acc, a, b, diag4, upper, g8, bd, bdt, down8,
    kept, t4, face_a, face_b, u, back, part,
):
    even = is_even(pos, 0)
    got = (even, a, b)
    edge = jnp.where((iota(8, 0) == 0) | (iota(8, 0) == 7), 0.5, 1.0)
    for h, r in tiles(512):
        inv, before = inv8[h, r : r + 8], res[h, r : r + 8]
        now = before - full_of(acc, got, h, r)
        old = inv * before * (1.0 / CENTER)
        new = KEEP * old + GAIN * inv * now
        kept[h, r : r + 8] = old + new
        kept[h, 512 + r : 520 + r] = now
        kept[h, 1024 + r : 1032 + r] = new
        u[h, r : r + 8] = new
    fine_apply(u, g8, back, bd, bdt)
    for h, r in tiles(512):
        s, c = r // 64, (r // 8) % 8
        scale = (0.5 if s in (0, 7) else 1.0) * (0.5 if c in (0, 7) else 1.0)
        part[r : r + 8, h * LANES : h * LANES + LANES] = (
            kept[h, 512 + r : 520 + r] * (edge * scale) - back[h, r : r + 8]
        )
    put(t4, 0, 64, dot(down8[...], part[...]))
    join_mid(t4)
    send_faces(t4, even, face_a, face_b, 16)
    send_faces(diag4, even, face_a, face_b, 16, 16)
    for face in (face_a, face_b):
        for h in range(2):
            face[h, 32:40] = upper[...]


def third_kernel(
    pos, t4, diag4, edges, a, b, g4, gm, gmt, res, inv4, edge, acc, face_a, face_b, u
):
    even = is_even(pos, 0)
    got = (even, a, b)
    wall = wall_mask(4)
    for h, r in tiles(64):
        full = full_of(t4, got, h, r)
        diag = full_of(diag4, got, h, r, 16)
        inv = jnp.where(wall, 0.0, 1.0 / jnp.where(wall, 1.0, diag))
        res[h, r : r + 8] = full
        inv4[h, r : r + 8] = inv
        u[h, r : r + 8] = inv * full * (1.0 / CENTER)
    lower = jnp.where(even, a[0, 32:40], b[0, 32:40])
    edge[...] = edges[...] + jnp.where(iota(8, 0) == 0, 0.0, lower)
    mid_apply(u, g4, acc, gm, gmt)
    join_mid(acc)
    send_faces(acc, even, face_a, face_b, 16)


def fourth_kernel(
    pos, res, acc, inv4, edge, a, b, g4, gm, gmt, m4, down4, corners, keep, part
):
    got = (is_even(pos, 0), a, b)
    for h, r in tiles(64):
        inv, before = inv4[h, r : r + 8], res[h, r : r + 8]
        now = before - full_of(acc, got, h, r)
        old = inv * before * (1.0 / CENTER)
        new = KEEP * old + GAIN * inv * now
        keep[h, r : r + 8] = now
        keep[h, 64 + r : 72 + r] = new
        keep[h, 128 + r : 136 + r] = old + new
    flux = dot(gm[...], wide(keep, 64, 64)) * wide(g4, 0, 192)
    put(part, 0, 64, dot(gmt[...], flux))
    for h, r in tiles(64):
        part[h, r : r + 8] = m4[r : r + 8] * keep[h, r : r + 8] - part[h, r : r + 8]
    low = dot(down4[...], wide(part, 0, 64))
    near = iota(8, 1) < HALF
    half0 = jnp.where(near, 0.0, low[:, :LANES])
    half1 = jnp.where(near, low[:, LANES:], 0.0)

    def corner(i, j, k):
        row = 4 * i + 2 * j + k
        return [half0[row : row + 1], half1[row : row + 1]]

    lane = iota(1, 1)
    mine, extra = [], []
    for i in range(2):
        columns = []
        for k in range(2):
            shifted = right(*corner(i, 1, k))
            straight = corner(i, 0, k)
            columns.append([straight[0] + shifted[0], straight[1] + shifted[1]])
        both = [columns[0][h] + pltpu.roll(columns[1][h], 1, 1) for h in range(2)]
        both = [jnp.where(lane % 16 == 0, 0.0, t) for t in both]
        mine.append(own_part(*both))
        extra.append(both[1])
    sides = jnp.where(lane < 16, pltpu.roll(extra[0], HALF, 1), 0.0) + jnp.where(
        (lane >= 16) & (lane < 32), pltpu.roll(extra[1], HALF + 16, 1), 0.0
    )
    none = jnp.zeros((2, LANES), F32)
    corners[...] = jnp.concatenate(mine + [sides, edge[0:3], none], axis=0)


def groups(ns):
    return max(1, ns // 8)


def side_kernel(pos, keep, one, two, g4, wider, message):
    near = iota(8, 1) < HALF
    even_a = is_even(pos, 1)
    for r in range(0, 192, 8):
        before = jnp.where(even_a, one[1, r : r + 8], two[1, r : r + 8])
        after = jnp.where(even_a, two[0, r : r + 8], one[0, r : r + 8])
        halves = (jnp.where(near, before, keep[0, r : r + 8]), jnp.where(near, keep[1, r : r + 8], after))
        for h in range(2):
            wider[h, r : r + 8] = halves[h]
            message[h, r : r + 8] = g4[h, r : r + 8]
            if 64 <= r < 128:
                message[h, 128 + r : 136 + r] = halves[h]


def column_kernel(rows, one, two, out):
    ns = rows.shape[0] // 8
    n = ns // groups(ns)

    def field(k):
        return rows[pl.ds(k, ns, stride=8), :]

    def later(x):
        return pltpu.roll(x, 1, 0)

    sides = field(2)
    over = jnp.where(iota(ns, 1) < 16, sides + later(pltpu.roll(sides, LANES - 16, 1)), 0.0)
    out[0:ns] = field(0) + later(field(1))
    for k in range(3):
        out[(1 + k) * ns : (2 + k) * ns] = field(3 + k)
    parts = [over[k * n : k * n + n] for k in range(groups(ns))]
    out[4 * ns : 4 * ns + n] = total(
        [pltpu.roll(p, 16 * k, 1) if k else p for k, p in enumerate(parts)]
    )


def coarse_kernel(
    pos, columns, others, wider, far, near_side, g4, inv4, gm, gmt, up4,
    res, u, sol, acc, face_a, face_b, vals, x2, es, ea, er, es0, ea0, er0, dg, ri,
):
    ns = x2.shape[0]
    na = x2.shape[1] // LANES
    width = na * LANES

    n = ns // groups(ns)
    size = 4 * ns + n
    even_a = is_even(pos, 1)

    def rows_of(d, start, count):
        at = d // 2 * size + start
        x, y = columns[at : at + count], others[at : at + count]
        return jnp.where(even_a, x, y) if d % 2 == 0 else jnp.where(even_a, y, x)

    def field(k):
        return [rows_of(d, k * ns, ns) for d in range(na)]

    def side(d):
        packed = rows_of(d, 4 * ns, n)
        parts = [pltpu.roll(packed, LANES - 16 * k, 1) if k else packed for k in range(groups(ns))]
        return jnp.where(iota(ns, 1) < 16, jnp.concatenate(parts, axis=0), 0.0)

    def roll_l(x, k):
        return pltpu.roll(x, k % width, 1)

    lane = iota(ns, 1)
    wall, top = lane % 16 == 0, lane % 16 == 15
    at = [slice(d * LANES, d * LANES + LANES) for d in range(na)]

    def towards_next(y, d):
        return jnp.where(lane < LANES - 16, y[d], y[(d + 1) % na])

    def towards_last(y, d):
        return jnp.where(lane < 16, y[d - 1], y[d])

    ea_all, er_all = field(2), field(3)
    ea_roll = [pltpu.roll(t, 16, 1) for t in ea_all]
    for d, es_d in enumerate(field(1)):
        es0_d, ea0_d = pltpu.roll(es_d, 1, 0), towards_last(ea_roll, d)
        er0_d = pltpu.roll(er_all[d], 1, 1)
        both = es_d + es0_d + ea_all[d] + ea0_d + er_all[d] + er0_d
        es[:, at[d]], ea[:, at[d]] = es_d, ea_all[d]
        es0[:, at[d]], ea0[:, at[d]] = es0_d, ea0_d
        er[:, at[d]] = jnp.where(wall | top, 0.0, er_all[d])
        er0[:, at[d]] = jnp.where(wall | (lane % 16 == 1), 0.0, er0_d)
        dg[:, at[d]] = jnp.where(wall, 0.0, both)
        ri[:, at[d]] = jnp.where(wall, 0.0, 1.0 / jnp.where(wall, 1.0, both))

    def inner(terms):
        return jnp.sum(jnp.sum(total(terms), axis=0, keepdims=True), axis=1, keepdims=True)

    first = field(0)
    r = [first[d] + side((d - 1) % na) for d in range(na)]
    p = [ri[:, at[d]] * r[d] for d in range(na)]
    gz = inner([r[d] * p[d] for d in range(na)])
    x = [jnp.zeros_like(t) for t in r]
    for it in range(ITERS):
        ahead = [pltpu.roll(t, LANES - 16, 1) for t in p]
        behind = [pltpu.roll(t, 16, 1) for t in p]
        q, terms = [], []
        for d in range(na):
            t, k = p[d], at[d]
            out = dg[:, k] * t
            out = out - es[:, k] * pltpu.roll(t, ns - 1, 0) - es0[:, k] * pltpu.roll(t, 1, 0)
            out = out - ea[:, k] * towards_next(ahead, d) - ea0[:, k] * towards_last(behind, d)
            out = out - er[:, k] * pltpu.roll(t, LANES - 1, 1) - er0[:, k] * pltpu.roll(t, 1, 1)
            q.append(out)
            terms.append(t * out)
        alpha = gz / inner(terms)
        x = [x[d] + alpha * p[d] for d in range(na)]
        if it + 1 < ITERS:
            r = [r[d] - alpha * q[d] for d in range(na)]
            z = [ri[:, at[d]] * r[d] for d in range(na)]
            new = inner([r[d] * z[d] for d in range(na)])
            beta = new / gz
            p = [z[d] + beta * p[d] for d in range(na)]
            gz = new
    for d in range(na):
        x2[:, at[d]] = x[d]

    s, a = pos[0], pos[1]
    blocks = [lax.rem(a + na - 1, na), a, lax.rem(a + 1, na)]
    for t in range(4):
        line = x2[pl.ds(lax.rem(s + ns - 1 + t, ns), 1), :]
        for j in range(2):
            for k in range(2):
                n = 4 * t + 2 * j + k
                vals[n : n + 1, :] = roll_l(line, -(16 * j + k)) if j + k else line
    near = iota(16, 1) < HALF
    b = [
        pltpu.roll(vals[:, pl.ds(pl.multiple_of(t * LANES, LANES), LANES)], HALF, 1) for t in blocks
    ]
    ext = jnp.concatenate([jnp.where(near, b[0], b[1]), jnp.where(near, b[1], b[2])], axis=1)
    rise = dot(up4[...], ext)
    even = is_even(pos, 0)
    below = [jnp.where(even, wide(far, r, 64), wide(near_side, r, 64)) for r in range(0, 256, 64)]
    above = [jnp.where(even, wide(near_side, r, 64), wide(far, r, 64)) for r in range(0, 256, 64)]
    mine = [wide(g4, r, 64) for r in range(0, 192, 64)] + [wide(wider, 64, 64)]
    layers = [below, mine, above]
    v = jnp.concatenate([rise[64 * q : 64 * q + 64] + layers[q][3] for q in range(3)], axis=1)
    weight = jnp.concatenate([jnp.concatenate(x[:3], axis=0) for x in layers], axis=1)
    back = dot(gmt[...], dot(gm[...], v) * weight)
    low, mid, high = [back[:, 256 * q : 256 * q + 256] for q in range(3)]
    put(acc, 0, 16, mid[:16] + low[48:])
    put(acc, 16, 32, mid[16:48])
    put(acc, 48, 16, mid[48:] + high[:16])
    join_mid(acc)
    put(sol, 0, 64, wide(wider, 128, 64) + rise[64:128])
    for h, r in tiles(64):
        now = wider[h, r : r + 8] - acc[h, r : r + 8]
        new = inv4[h, r : r + 8] * now * (1.0 / CENTER)
        res[h, r : r + 8] = now
        u[h, r : r + 8] = new
        sol[h, r : r + 8] += new
    mid_apply(u, g4, acc, gm, gmt)
    join_mid(acc)
    send_faces(acc, even, face_a, face_b, 16)


def sixth_kernel(
    pos, res, u, sol, acc, a, b, inv4, up8, kept, g8, bd, bdt,
    out, v8, acc2, face_a, face_b, y4,
):
    even = is_even(pos, 0)
    for h, r in tiles(64):
        now = res[h, r : r + 8] - full_of(acc, (even, a, b), h, r)
        new = KEEP * u[h, r : r + 8] + GAIN * inv4[h, r : r + 8] * now
        y4[h, r : r + 8] = sol[h, r : r + 8] + new
    put(v8, 0, 512, dot(up8[...], wide(y4, 0, 64)))
    for h, r in tiles(512):
        e8 = v8[h, r : r + 8]
        out[h, r : r + 8] = kept[h, r : r + 8] + e8
        v8[h, r : r + 8] = kept[h, 1024 + r : 1032 + r] + e8
    fine_front(v8, g8, acc2, bd, bdt)
    send_faces(acc2, even, face_a, face_b, 64)


def seventh_kernel(
    pos, kept, sol, acc, a, b, inv8, g8, bd, bdt, res, out, u, acc2, face_a, face_b
):
    even = is_even(pos, 0)
    for h, r in tiles(512):
        now = kept[h, 512 + r : 520 + r] - full_of(acc, (even, a, b), h, r)
        new = inv8[h, r : r + 8] * now * (1.0 / CENTER)
        res[h, r : r + 8] = now
        u[h, r : r + 8] = new
        out[h, r : r + 8] = sol[h, r : r + 8] + new
    fine_front(u, g8, acc2, bd, bdt)
    send_faces(acc2, even, face_a, face_b, 64)


def last_kernel(pos, res, sol, u, acc, a, b, inv8, out):
    got = (is_even(pos, 0), a, b)
    for r in range(0, 512, 8):
        halves = []
        for h in range(2):
            now = res[h, r : r + 8] - full_of(acc, got, h, r)
            new = KEEP * u[h, r : r + 8] + GAIN * inv8[h, r : r + 8] * now
            halves.append(sol[h, r : r + 8] + new)
        out[r : r + 8] = own_part(*halves)


def call(kernel, args, outs, scratch=(), scalars=1, unread=0, **options):
    vmem = pl.BlockSpec(memory_space=pltpu.VMEM)
    smem = pl.BlockSpec(memory_space=pltpu.SMEM)
    arrays = [x for x in args if not isinstance(x, str)]
    named = len(arrays) < len(args)

    def body(*refs):
        rest = iter(refs)
        given = [next(rest) for _ in arrays[: len(arrays) - named]]
        held = next(rest) if named else None
        given = iter(given)
        full = [Constant(held, x) if isinstance(x, str) else next(given) for x in args]
        kernel(*full, *rest)

    if named:
        arrays.append(PACK)
    return pl.pallas_call(
        body,
        out_shape=[jax.ShapeDtypeStruct(s, F32) for s in outs],
        in_specs=[smem] * scalars
        + [vmem] * (len(arrays) - scalars - unread)
        + [pl.BlockSpec(memory_space=pl.ANY)] * unread,
        out_specs=[vmem] * len(outs),
        scratch_shapes=[pltpu.VMEM(s, F32) for s in scratch],
        compiler_params=pltpu.CompilerParams(vmem_limit_bytes=32 * 1024 * 1024),
        name=kernel.__name__,
        **options,
    )(*arrays)


def exchange(far, near, axis):
    size = lax.axis_size(axis)
    pairs_far = [(i, (i + 1 if i % 2 else i - 1) % size) for i in range(size)]
    pairs_near = [(i, i ^ 1) for i in range(size)]
    return lax.ppermute(far, axis, pairs_far), lax.ppermute(near, axis, pairs_near)


def spread(x, axis, groups=None):
    size = len(groups[0]) if groups else lax.axis_size(axis)
    copies = jnp.broadcast_to(x[None], (size,) + x.shape)
    return lax.all_to_all(copies, axis, 0, 0, axis_index_groups=groups).reshape(-1, LANES)


def on_device(element_load, metric, element_order):
    ns, na = lax.axis_size("stream"), lax.axis_size("azim")
    fine, mid = (2, 512, LANES), (2, 64, LANES)
    face8, face4 = [(2, 64, LANES)] * 2, [(2, 16, LANES)] * 2
    pos = jnp.stack([lax.axis_index("stream"), lax.axis_index("azim")]).astype(jnp.int32)
    g, rolled, diag, a, b = call(
        order_kernel,
        (
            pos,
            metric.reshape(1536, LANES),
            element_load.reshape(512, LANES),
            element_order,
            "w8",
            "bsq",
        ),
        [(1536, LANES), (512, LANES), (512, LANES), (128, LANES), (128, LANES)],
    )
    a, b = exchange(a, b, "azim")
    bulk = call(bulk_kernel, (pos, g, rolled, a, b), [(1024, LANES)] * 2, unread=2)
    bulk = exchange(*bulk, "azim")
    a, b = call(face_kernel, (pos, rolled, diag, a, b), [(2, 128, LANES)] * 2, [(2, 256, LANES)])
    a, b = exchange(a, b, "stream")

    def inner(u, acc):
        (acc,) = call(inner_kernel, (u, g8, acc, "bd", "bdt"), [fine], (), 0)
        return acc

    g8, load, diag8 = call(
        setup_kernel,
        (pos, g, rolled, diag, *bulk, "bsq"),
        [(2, 1536, LANES), fine, fine],
        [(1536, LANES), (512, LANES)],
    )
    res8, inv8, u8, acc, a, b = call(
        first_kernel,
        (pos, load, diag8, a, b, g8, "bd", "bdt"),
        [fine, fine, fine, fine] + face8,
    )
    a, b = exchange(a, b, "stream")
    acc = inner(u8, acc)
    g4, diag4, edges, upper = call(
        coarsen_kernel,
        (g8, "w4", "w2", "sample", "sq4"),
        [(2, 192, LANES), mid, (8, LANES), (8, LANES)],
        scalars=0,
    )
    kept, t4, a, b = call(
        second_kernel,
        (pos, res8, inv8, acc, a, b, diag4, upper, g8, "bd", "bdt", "down8"),
        [(2, 1536, LANES), mid] + [(2, 40, LANES)] * 2,
        [fine, fine, (512, 2 * LANES)],
    )
    a, b = exchange(a, b, "stream")
    res4, inv4, edges, acc, a, b = call(
        third_kernel,
        (pos, t4, diag4, edges, a, b, g4, "gm", "gmt"),
        [mid, mid, (8, LANES), mid] + face4,
        [mid],
    )
    a, b = exchange(a, b, "stream")
    corners, keep = call(
        fourth_kernel,
        (pos, res4, acc, inv4, edges, a, b, g4, "gm", "gmt", "m4", "down4"),
        [(8, LANES), (2, 192, LANES)],
        [mid],
    )
    columns = spread(corners, "stream")
    a, b = exchange(keep, keep, "azim")
    wider, message = call(
        side_kernel, (pos, keep, a, b, g4), [(2, 192, LANES), (2, 256, LANES)]
    )
    sides = exchange(message, message, "stream")
    size = 4 * ns + ns // groups(ns)
    (columns,) = call(
        column_kernel, (columns, *sides), [(size, LANES)], (), 0, unread=2
    )
    cores = [list(range(core, na, 2)) for core in range(2)]
    columns = spread(columns, "azim", cores)
    others = lax.ppermute(columns, "azim", [(i, i ^ 1) for i in range(na)])
    whole = (ns, na * LANES)
    res4, u4, sol4, acc, a, b = call(
        coarse_kernel,
        (pos, columns, others, wider, *sides, g4, inv4, "gm", "gmt", "up4"),
        [mid, mid, mid, mid] + face4,
        [(16, na * LANES)] + [whole] * 9,
    )
    a, b = exchange(a, b, "stream")
    sol8, v8, acc, a, b = call(
        sixth_kernel,
        (pos, res4, u4, sol4, acc, a, b, inv4, "up8", kept, g8, "bd", "bdt"),
        [fine, fine, fine] + face8,
        [mid],
    )
    a, b = exchange(a, b, "stream")
    acc = inner(v8, acc)
    res8, sol8, u8, acc, a, b = call(
        seventh_kernel,
        (pos, kept, sol8, acc, a, b, inv8, g8, "bd", "bdt"),
        [fine, fine, fine, fine] + face8,
    )
    a, b = exchange(a, b, "stream")
    acc = inner(u8, acc)
    (out,) = call(last_kernel, (pos, res8, sol8, u8, acc, a, b, inv8), [(512, LANES)])
    return out.reshape(element_load.shape)


def solution(mesh):
    placed = (P(None, "stream", "azim"), P(None, None, "stream", "azim"), P("stream", "azim"))
    return jax.shard_map(
        on_device, mesh=mesh, in_specs=placed, out_specs=P(None, "stream", "azim"), check_vma=False
    )
```

```python
import jax
import jax.numpy as jnp
import numpy as np
from jax import lax
from jax.experimental import pallas as pl
from jax.experimental.pallas import tpu as pltpu
from jax.sharding import PartitionSpec as P

ITERS = 6
LOW_EIG = 0.3
HIGH_EIG = 3.0
CENTER = 0.5 * (HIGH_EIG + LOW_EIG)
HALF_WIDTH = 0.5 * (HIGH_EIG - LOW_EIG)
FIRST_RHO = HALF_WIDTH / CENTER
SECOND_RHO = 1.0 / (2.0 * CENTER / HALF_WIDTH - FIRST_RHO)
KEEP = SECOND_RHO * FIRST_RHO
GAIN = 2.0 * SECOND_RHO / HALF_WIDTH
LANES = 128
HALF = 64
F32 = jnp.float32


def legendre_pair(degree, places):
    previous = places * 0.0 + 1.0
    current = places.copy()
    for k in range(2, degree + 1):
        following = ((2 * k - 1) * places * current - (k - 1) * previous) / k
        previous = current
        current = following
    return (current, previous)


def gll_table(points):
    degree = points - 1
    places = np.cos(np.pi * np.arange(points) / degree)
    for _ in range(60):
        top, below = legendre_pair(degree, places)
        places = places - (places * top - below) / (points * top)
    nodes = np.sort(places)
    nodes[0] = -1.0
    nodes[-1] = 1.0
    at_nodes = legendre_pair(degree, nodes)[0]
    weights = 2.0 / (degree * (degree + 1) * at_nodes**2)
    deriv = np.zeros((points, points))
    for i in range(points):
        for j in range(points):
            if i != j:
                deriv[i, j] = at_nodes[i] / (at_nodes[j] * (nodes[i] - nodes[j]))
    deriv[0, 0] = -degree * (degree + 1) / 4.0
    deriv[-1, -1] = degree * (degree + 1) / 4.0
    return (nodes, weights, deriv)


def lagrange_table(source, target):
    out = np.ones((len(target), len(source)))
    for j in range(len(source)):
        for k in range(len(source)):
            if k != j:
                out[:, j] *= (target - source[k]) / (source[j] - source[k])
    return out


N8, W8, D8 = gll_table(8)
N4, W4, D4 = gll_table(4)
N2, W2, D2 = gll_table(2)


def kron3(a, b, c):
    return np.kron(np.kron(a, b), c)


def cube(w):
    return (w[:, None, None] * w[None, :, None] * w[None, None, :]).reshape(-1)


def share(n):
    edge = np.ones(n)
    edge[0] = edge[-1] = 0.5
    return cube(edge)


def grads(d):
    i = np.eye(d.shape[0])
    return [kron3(d, i, i), kron3(i, d, i), kron3(i, i, d)]


def f32(x):
    return np.asarray(x, np.float32)


def lanes_of(column):
    return np.repeat(f32(column)[:, None], LANES, axis=1)


UP8 = lagrange_table(N4, N8)
UP4 = lagrange_table(N2, N4)
TO4 = lagrange_table(N8, N4)
TO2 = lagrange_table(N8, N2)

C_BD = f32(np.kron(np.eye(16), D8))
C_BDT = f32(np.kron(np.eye(16), D8.T))
C_BSQ = f32(np.kron(np.eye(16), (D8 * D8).T))
C_SAMPLE = f32(np.concatenate([kron3(TO4, TO4, TO4), kron3(TO2, TO2, TO2)]))
C_UP8 = f32(kron3(UP8, UP8, UP8))
C_DOWN8 = f32(kron3(UP8, UP8, UP8).T)
C_UP4 = f32(kron3(UP4, UP4, UP4))
C_DOWN4 = f32(kron3(UP4, UP4, UP4).T)
C_UP4X3 = np.zeros((192, 16), np.float32)
for layer in range(3):
    C_UP4X3[64 * layer : 64 * layer + 64, 4 * layer : 4 * layer + 8] = C_UP4
C_G4 = f32(np.concatenate(grads(D4)))
C_G4T = f32(np.concatenate(grads(D4)).T)
C_SQ4 = f32((np.concatenate(grads(D4)) ** 2).T)
C_W4 = lanes_of(cube(W4) / np.exp(kron3(TO4, TO4, TO4) @ np.log(cube(W8))))
C_W2 = lanes_of(cube(W2) / np.exp(kron3(TO2, TO2, TO2) @ np.log(cube(W8))))
C_M4 = lanes_of(share(4))
FIRST = np.r_[0:64, 64:80, 128:144]
LAST = np.r_[0:64, 112:128, 176:192]
CONSTANTS = {
    "bd": C_BD, "bdt": C_BDT, "bsq": C_BSQ, "sample": C_SAMPLE, "w4": C_W4, "w2": C_W2,
    "sq4": C_SQ4, "gm": C_G4, "gmt": C_G4T, "m4": C_M4, "down8": C_DOWN8, "down4": C_DOWN4,
    "up4": C_UP4X3, "up8": C_UP8, "gm_first": C_G4[FIRST], "gmt_first": C_G4T[:16, FIRST],
    "gm_last": C_G4[LAST], "gmt_last": C_G4T[48:, LAST],
}


def pack_constants():
    rows, places, start = [], {}, 0
    for name, value in CONSTANTS.items():
        blocks = -(-value.shape[1] // LANES)
        padded = np.zeros((value.shape[0], blocks * LANES), np.float32)
        padded[:, : value.shape[1]] = value
        rows += [padded[:, k * LANES : (k + 1) * LANES] for k in range(blocks)]
        places[name] = (start, value.shape, blocks)
        start += value.shape[0] * blocks
    return np.concatenate(rows), places


PACK, PLACES = pack_constants()


class Constant:
    def __init__(self, ref, name):
        self.ref, self.name = ref, name

    def __getitem__(self, index):
        start, (rows, columns), blocks = PLACES[self.name]
        parts = []
        for k in range(blocks):
            width = min(LANES, columns - k * LANES)
            parts.append(self.ref[start + k * rows : start + (k + 1) * rows, :width])
        value = parts[0] if blocks == 1 else jnp.concatenate(parts, axis=1)
        return value if index is Ellipsis else value[index]


def dot(a, b):
    return jnp.dot(a, b, preferred_element_type=F32, precision=lax.Precision.HIGHEST)


def iota(rows, axis):
    return lax.broadcasted_iota(jnp.int32, (rows, LANES), axis)


def wide(ref, start, size):
    return jnp.concatenate([ref[0, start : start + size], ref[1, start : start + size]], axis=1)


def put(ref, start, size, value):
    ref[0, start : start + size] = value[:, :LANES]
    ref[1, start : start + size] = value[:, LANES:]


def total(terms):
    out = terms[0]
    for t in terms[1:]:
        out = out + t
    return out


def contract(v, matrix, sign):
    n = len(v)
    h = n // 2
    even = [v[k] + v[n - 1 - k] for k in range(h)]
    odd = [v[k] - v[n - 1 - k] for k in range(h)]
    out = [None] * n
    for i in range(h):
        p = total([even[k] * float(0.5 * (matrix[i, k] + matrix[i, n - 1 - k])) for k in range(h)])
        q = total([odd[k] * float(0.5 * (matrix[i, k] - matrix[i, n - 1 - k])) for k in range(h)])
        out[i] = p + q
        out[n - 1 - i] = q - p if sign < 0 else p - q
    return out


def fine_rows(s, a):
    return s * 64 + a * 8


PLANES = [(0, 7), (1, 2), (3, 4), (5, 6)]


def pair(ref, p, base=0):
    return jnp.concatenate([wide(ref, base + 64 * s, 64) for s in p], axis=0)


def put_pair(ref, p, value):
    for k, s in enumerate(p):
        put(ref, 64 * s, 64, value[64 * k : 64 * k + 64])


def fine_stream(u, g, acc):
    for h in range(2):
        for a in range(8):
            at = [fine_rows(s, a) for s in range(8)]
            grad = contract([u[h, r : r + 8] for r in at], D8, -1)
            back = contract([grad[s] * g[h, r : r + 8] for s, r in enumerate(at)], D8.T, -1)
            for s, r in enumerate(at):
                acc[h, r : r + 8] = back[s]


def fine_cross(u, g, acc, bd, bdt, pairs):
    for p in pairs:
        flux = dot(bd[...], pair(u, p)) * pair(g, p, 1024)
        put_pair(acc, p, pair(acc, p) + dot(bdt[...], flux))
        for s in p:
            for h in range(2):
                at = [fine_rows(s, a) for a in range(8)]
                grad = contract([u[h, r : r + 8] for r in at], D8, -1)
                flux = [grad[a] * g[h, 512 + r : 520 + r] for a, r in enumerate(at)]
                back = contract(flux, D8.T, -1)
                for a, r in enumerate(at):
                    acc[h, r : r + 8] += back[a]


def fine_apply(u, g, acc, bd, bdt):
    fine_stream(u, g, acc)
    fine_cross(u, g, acc, bd, bdt, PLANES)


def fine_front(u, g, acc, bd, bdt):
    fine_stream(u, g, acc)
    fine_cross(u, g, acc, bd, bdt, PLANES[:1])
    join_fine(acc, (0, 7))


def left(x0, x1):
    near = iota(x0.shape[0], 1) < LANES - 16
    y0, y1 = pltpu.roll(x0, LANES - 16, 1), pltpu.roll(x1, LANES - 16, 1)
    return jnp.where(near, y0, y1), jnp.where(near, y1, y0)


def right(x0, x1):
    near = iota(x0.shape[0], 1) >= 16
    y0, y1 = pltpu.roll(x0, 16, 1), pltpu.roll(x1, 16, 1)
    return jnp.where(near, y0, y1), jnp.where(near, y1, y0)


def join_radial(x, points, start, rows):
    place = iota(rows, 1) % 16
    first = pl.ds(start, rows, stride=points)
    last = pl.ds(start + points - 1, rows, stride=points)
    for h in range(2):
        view = x.at[h]
        low, high = view[first, :], view[last, :]
        view[first, :] = jnp.where(place == 0, 0.0, low + pltpu.roll(high, 1, 1))
        view[last, :] = jnp.where(place == 15, 0.0, high + pltpu.roll(low, LANES - 1, 1))


def join_fine(x, planes=range(8)):
    for s in planes:
        join_radial(x, 8, 64 * s, 8)
        lo, hi = fine_rows(s, 0), fine_rows(s, 7)
        low = [x[h, lo : lo + 8] for h in range(2)]
        high = [x[h, hi : hi + 8] for h in range(2)]
        to_low, to_high = right(*high), left(*low)
        for h in range(2):
            x[h, lo : lo + 8] = low[h] + to_low[h]
            x[h, hi : hi + 8] = high[h] + to_high[h]


def join_mid(x):
    join_radial(x, 4, 0, 16)
    first = iota(8, 0) < 4
    for s in range(4):
        lo, hi = s * 16, s * 16 + 8
        low = [x[h, lo : lo + 8] for h in range(2)]
        high = [x[h, hi : hi + 8] for h in range(2)]
        to_low = right(*[pltpu.roll(t, 4, 0) for t in high])
        to_high = left(*[pltpu.roll(t, 4, 0) for t in low])
        for h in range(2):
            x[h, lo : lo + 8] = low[h] + jnp.where(first, to_low[h], 0.0)
            x[h, hi : hi + 8] = high[h] + jnp.where(first, 0.0, to_high[h])


def is_even(place, k):
    return lax.rem(place[k], 2) == 0


def full_of(x, faces, h, r, offset=0):
    even, far, near = faces
    rows = x.shape[1]
    plane = {512: 64, 64: 16}[rows]
    value = x[h, r : r + 8]
    if r < plane:
        at = offset + r
        return value + jnp.where(even, far[h, at : at + 8], near[h, at : at + 8])
    if r >= rows - plane:
        at = offset + r - (rows - plane)
        return value + jnp.where(even, near[h, at : at + 8], far[h, at : at + 8])
    return value


def send_faces(x, even, far, near, plane, offset=0):
    rows = x.shape[1]
    last = rows - plane
    one = pl.multiple_of(jnp.where(even, last, 0), 8)
    two = pl.multiple_of(jnp.where(even, 0, last), 8)
    for h in range(2):
        near[h, offset : offset + plane] = x[h, pl.ds(one, plane), :]
        far[h, offset : offset + plane] = x[h, pl.ds(two, plane), :]


def wall_mask(points):
    place, node = iota(8, 1) % 16, iota(8, 0) % points
    return ((node == 0) & (place == 0)) | ((node == points - 1) & (place == 15))


def own_part(half0, half1):
    near = iota(half0.shape[0], 1) < HALF
    return pltpu.roll(jnp.where(near, half1, half0), HALF, 1)


def tiles(rows):
    return [(h, r) for h in range(2) for r in range(0, rows, 8)]


def mid_apply(u, g4, acc, gm, gmt):
    flux = dot(gm[...], wide(u, 0, 64)) * wide(g4, 0, 192)
    put(acc, 0, 64, dot(gmt[...], flux))


def fine_diagonal(g, diag, bsq):
    square = (D8 * D8).T
    for c in range(4):
        rows = slice(128 * c, 128 * c + 128)
        diag[rows] = dot(bsq[...], g[1024 + 128 * c : 1152 + 128 * c])
    for axis in range(2):
        for fixed in range(8):
            at = [fine_rows(k, fixed) if axis == 0 else fine_rows(fixed, k) for k in range(8)]
            back = contract([g[512 * axis + r : 512 * axis + r + 8] for r in at], square, 1)
            for k, r in enumerate(at):
                diag[r : r + 8] += back[k]


def halves_up_down(a, b):
    near = iota(8, 1) < HALF
    up = jnp.where(near, a, pltpu.roll(b, HALF, 1))
    return up, jnp.where(near, pltpu.roll(a, HALF, 1), b)


def before_after(even, x, y):
    p, n = jnp.where(even, x, y), jnp.where(even, y, x)
    near = iota(8, 1) < HALF
    first = (jnp.where(near, p, 0.0), jnp.where(near, 0.0, pltpu.roll(n, HALF, 1)))
    second = (jnp.where(near, pltpu.roll(p, HALF, 1), 0.0), jnp.where(near, 0.0, n))
    return first, second


def order_kernel(pos, metric, load, order, g, rolled, far, near):
    even = is_even(pos, 1)
    slots = jnp.broadcast_to(pltpu.roll(order[...], HALF, 1), (8, LANES))
    wr = total([jnp.where(iota(8, 0) == k, float(W8[k]), 0.0) for k in range(8)])
    for r in range(0, 1536, 8):
        scale = wr * float(W8[(r % 512) // 64] * W8[(r // 8) % 8])
        g[r : r + 8] = jnp.take_along_axis(metric[r : r + 8], slots, axis=1) * scale
    for r in range(0, 512, 8):
        rolled[r : r + 8] = pltpu.roll(load[r : r + 8], HALF, 1)
    for r in range(0, 1024, 8):
        other = g[1024 + r : 1032 + r] if r < 512 else rolled[r - 512 : r - 504]
        up, down = halves_up_down(g[r : r + 8], other)
        far[r : r + 8] = jnp.where(even, down, up)
        near[r : r + 8] = jnp.where(even, up, down)


def own_kernel(g, bsq, diag):
    fine_diagonal(g, diag, bsq)


def setup_kernel(
    pos, g, rolled, diag, x, y, bsq, g8, load, diag8, face_a, face_b, ghost, ghost_diag
):
    near = iota(8, 1) < HALF
    even_a = is_even(pos, 1)

    def place(out, row, own, sides):
        out[0, row : row + 8] = jnp.where(near, sides[0], own)
        out[1, row : row + 8] = jnp.where(near, own, sides[1])

    for r in range(0, 1024, 8):
        first, second = before_after(even_a, x[r : r + 8], y[r : r + 8])
        place(g8, r, g[r : r + 8], first)
        ghost[r : r + 8] = first[0] + first[1]
        if r < 512:
            place(g8, 1024 + r, g[1024 + r : 1032 + r], second)
            ghost[1024 + r : 1032 + r] = second[0] + second[1]
        else:
            place(load, r - 512, rolled[r - 512 : r - 504], second)
    fine_diagonal(ghost, ghost_diag, bsq)
    for r in range(0, 512, 8):
        side = ghost_diag[r : r + 8]
        place(diag8, r, diag[r : r + 8], (side, side))
    for x in (load, diag8):
        join_fine(x)
    even = is_even(pos, 0)
    send_faces(load, even, face_a, face_b, 64)
    send_faces(diag8, even, face_a, face_b, 64, 64)


def coarsen_kernel(g8, w4, w2, sample, sq4, g4, diag4, edges, upper):
    low = []
    for d in range(3):
        coarse = jnp.exp(dot(sample[...], jnp.log(wide(g8, 512 * d, 512))))
        put(g4, 64 * d, 64, coarse[:64] * jnp.concatenate([w4[...], w4[...]], axis=1))
        low.append([coarse[64:72, :LANES] * w2[...], coarse[64:72, LANES:] * w2[...]])
    put(diag4, 0, 64, dot(sq4[...], wide(g4, 0, 192)))
    join_mid(diag4)

    def corner(d, i, j, k):
        row = 4 * i + 2 * j + k
        return [t[row : row + 1] for t in low[d]]

    def add(x, y):
        return [x[0] + y[0], x[1] + y[1]]

    def quarter(x):
        return [0.25 * x[0], 0.25 * x[1]]

    def outward(x):
        return [pltpu.roll(x[0], 1, 1), pltpu.roll(x[1], 1, 1)]

    es = [[quarter(add(corner(0, 0, j, k), corner(0, 1, j, k))) for k in range(2)] for j in range(2)]
    ea = [[quarter(add(corner(1, i, 0, k), corner(1, i, 1, k))) for k in range(2)] for i in range(2)]
    er = [[quarter(add(corner(2, i, j, 0), corner(2, i, j, 1))) for j in range(2)] for i in range(2)]
    col = [add(es[0][k], list(right(*es[1][k]))) for k in range(2)]
    edge_s = add(col[0], outward(col[1]))
    edge_a = [add(ea[i][0], outward(ea[i][1])) for i in range(2)]
    edge_r = [add(er[i][0], list(right(*er[i][1]))) for i in range(2)]
    off_wall = iota(1, 1) % 16 != 0
    rows = [jnp.where(off_wall, own_part(*x), 0.0) for x in (edge_s, edge_a[0], edge_a[1])]
    rows += [own_part(*x) for x in edge_r]
    none = jnp.zeros((5, LANES), F32)
    edges[...] = jnp.concatenate([rows[0], rows[1], rows[3], none], axis=0)
    upper[...] = jnp.concatenate([rows[0], rows[2], rows[4], none], axis=0)


def first_kernel(
    pos, load, diag8, a, b, g8, bd, bdt, res, inv8, u, acc, face_a, face_b
):
    even = is_even(pos, 0)
    got = (even, a, b)
    wall8 = wall_mask(8)
    for h, r in tiles(512):
        diag = full_of(diag8, got, h, r, 64)
        inv = jnp.where(wall8, 0.0, 1.0 / jnp.where(wall8, 1.0, diag))
        full = full_of(load, got, h, r)
        res[h, r : r + 8] = full
        inv8[h, r : r + 8] = inv
        u[h, r : r + 8] = inv * full * (1.0 / CENTER)
    fine_front(u, g8, acc, bd, bdt)
    send_faces(acc, even, face_a, face_b, 64)


def inner_kernel(u, g8, start, bd, bdt, acc):
    for h, r in tiles(512):
        acc[h, r : r + 8] = start[h, r : r + 8]
    fine_cross(u, g8, acc, bd, bdt, PLANES[1:])
    join_fine(acc, range(1, 7))


def second_kernel(
    pos, res, inv8, acc, a, b, diag4, upper, g8, bd, bdt, down8,
    kept, t4, face_a, face_b, u, back, part,
):
    even = is_even(pos, 0)
    got = (even, a, b)
    edge = jnp.where((iota(8, 0) == 0) | (iota(8, 0) == 7), 0.5, 1.0)
    for h, r in tiles(512):
        inv, before = inv8[h, r : r + 8], res[h, r : r + 8]
        now = before - full_of(acc, got, h, r)
        old = inv * before * (1.0 / CENTER)
        new = KEEP * old + GAIN * inv * now
        kept[h, r : r + 8] = old + new
        kept[h, 512 + r : 520 + r] = now
        kept[h, 1024 + r : 1032 + r] = new
        u[h, r : r + 8] = new
    fine_apply(u, g8, back, bd, bdt)
    for h, r in tiles(512):
        s, c = r // 64, (r // 8) % 8
        scale = (0.5 if s in (0, 7) else 1.0) * (0.5 if c in (0, 7) else 1.0)
        part[r : r + 8, h * LANES : h * LANES + LANES] = (
            kept[h, 512 + r : 520 + r] * (edge * scale) - back[h, r : r + 8]
        )
    put(t4, 0, 64, dot(down8[...], part[...]))
    join_mid(t4)
    send_faces(t4, even, face_a, face_b, 16)
    send_faces(diag4, even, face_a, face_b, 16, 16)
    for face in (face_a, face_b):
        for h in range(2):
            face[h, 32:40] = upper[...]


def third_kernel(
    pos, t4, diag4, edges, a, b, g4, gm, gmt, res, inv4, edge, acc, face_a, face_b, u
):
    even = is_even(pos, 0)
    got = (even, a, b)
    wall = wall_mask(4)
    for h, r in tiles(64):
        full = full_of(t4, got, h, r)
        diag = full_of(diag4, got, h, r, 16)
        inv = jnp.where(wall, 0.0, 1.0 / jnp.where(wall, 1.0, diag))
        res[h, r : r + 8] = full
        inv4[h, r : r + 8] = inv
        u[h, r : r + 8] = inv * full * (1.0 / CENTER)
    lower = jnp.where(even, a[0, 32:40], b[0, 32:40])
    edge[...] = edges[...] + jnp.where(iota(8, 0) == 0, 0.0, lower)
    mid_apply(u, g4, acc, gm, gmt)
    join_mid(acc)
    send_faces(acc, even, face_a, face_b, 16)


def fourth_kernel(
    pos, res, acc, inv4, edge, a, b, g4, gm, gmt, m4, down4, corners, one, two, keep, part
):
    got = (is_even(pos, 0), a, b)
    for h, r in tiles(64):
        inv, before = inv4[h, r : r + 8], res[h, r : r + 8]
        now = before - full_of(acc, got, h, r)
        old = inv * before * (1.0 / CENTER)
        new = KEEP * old + GAIN * inv * now
        keep[h, r : r + 8] = now
        keep[h, 64 + r : 72 + r] = new
        keep[h, 128 + r : 136 + r] = old + new
    even_a = is_even(pos, 1)
    one[...] = jnp.where(even_a, keep[0], keep[1])
    two[...] = jnp.where(even_a, keep[1], keep[0])
    flux = dot(gm[...], wide(keep, 64, 64)) * wide(g4, 0, 192)
    put(part, 0, 64, dot(gmt[...], flux))
    for h, r in tiles(64):
        part[h, r : r + 8] = m4[r : r + 8] * keep[h, r : r + 8] - part[h, r : r + 8]
    low = dot(down4[...], wide(part, 0, 64))
    near = iota(8, 1) < HALF
    half0 = jnp.where(near, 0.0, low[:, :LANES])
    half1 = jnp.where(near, low[:, LANES:], 0.0)

    def corner(i, j, k):
        row = 4 * i + 2 * j + k
        return [half0[row : row + 1], half1[row : row + 1]]

    lane = iota(1, 1)
    mine, extra = [], []
    for i in range(2):
        columns = []
        for k in range(2):
            shifted = right(*corner(i, 1, k))
            straight = corner(i, 0, k)
            columns.append([straight[0] + shifted[0], straight[1] + shifted[1]])
        both = [columns[0][h] + pltpu.roll(columns[1][h], 1, 1) for h in range(2)]
        both = [jnp.where(lane % 16 == 0, 0.0, t) for t in both]
        mine.append(own_part(*both))
        extra.append(both[1])
    sides = jnp.where(lane < 16, pltpu.roll(extra[0], HALF, 1), 0.0) + jnp.where(
        (lane >= 16) & (lane < 32), pltpu.roll(extra[1], HALF + 16, 1), 0.0
    )
    none = jnp.zeros((2, LANES), F32)
    corners[...] = jnp.concatenate(mine + [sides, edge[0:3], none], axis=0)


def groups(ns):
    return max(1, ns // 8)


def side_kernel(pos, keep, one, two, g4, gm, gmt, wider, far, near_side, back):
    near = iota(8, 1) < HALF
    even, even_a = is_even(pos, 0), is_even(pos, 1)
    for r in range(0, 192, 8):
        x, y = one[r : r + 8], two[r : r + 8]
        before, after = jnp.where(even_a, x, y), jnp.where(even_a, y, x)
        halves = (jnp.where(near, before, keep[0, r : r + 8]), jnp.where(near, keep[1, r : r + 8], after))
        for h in range(2):
            wider[h, r : r + 8] = halves[h]
    flux = dot(gm[...], wide(wider, 64, 64)) * wide(g4, 0, 192)
    put(back, 0, 64, dot(gmt[...], flux))
    one = pl.multiple_of(jnp.where(even, 48, 0), 8)
    two = pl.multiple_of(jnp.where(even, 0, 48), 8)
    for out, plane in ((near_side, one), (far, two)):
        for h in range(2):
            out[h, 0:64] = g4[h, 0:64]
            out[h, 64:80] = g4[h, pl.ds(64 + plane, 16), :]
            out[h, 80:96] = g4[h, pl.ds(128 + plane, 16), :]
            out[h, 96:112] = back[h, pl.ds(plane, 16), :]


def column_kernel(rows, one, two, out):
    ns = rows.shape[0] // 8
    n = ns // groups(ns)

    def field(k):
        return rows[pl.ds(k, ns, stride=8), :]

    def later(x):
        return pltpu.roll(x, 1, 0)

    sides = field(2)
    over = jnp.where(iota(ns, 1) < 16, sides + later(pltpu.roll(sides, LANES - 16, 1)), 0.0)
    out[0:ns] = field(0) + later(field(1))
    for k in range(3):
        out[(1 + k) * ns : (2 + k) * ns] = field(3 + k)
    parts = [over[k * n : k * n + n] for k in range(groups(ns))]
    out[4 * ns : 4 * ns + n] = total(
        [pltpu.roll(p, 16 * k, 1) if k else p for k, p in enumerate(parts)]
    )


def coarse_kernel(
    pos, columns, others, wider, far, near_side, g4, inv4, gm, gmt, up4, gm_first, gmt_first,
    gm_last, gmt_last,
    res, u, sol, acc, face_a, face_b, vals, x2, es, ea, er, es0, ea0, er0, dg, ri,
):
    ns = x2.shape[0]
    na = x2.shape[1] // LANES
    width = na * LANES

    n = ns // groups(ns)
    size = 4 * ns + n
    even_a = is_even(pos, 1)

    def rows_of(d, start, count):
        at = d // 2 * size + start
        x, y = columns[at : at + count], others[at : at + count]
        return jnp.where(even_a, x, y) if d % 2 == 0 else jnp.where(even_a, y, x)

    def field(k):
        return [rows_of(d, k * ns, ns) for d in range(na)]

    def side(d):
        packed = rows_of(d, 4 * ns, n)
        parts = [pltpu.roll(packed, LANES - 16 * k, 1) if k else packed for k in range(groups(ns))]
        return jnp.where(iota(ns, 1) < 16, jnp.concatenate(parts, axis=0), 0.0)

    def roll_l(x, k):
        return pltpu.roll(x, k % width, 1)

    lane = iota(ns, 1)
    wall, top = lane % 16 == 0, lane % 16 == 15
    at = [slice(d * LANES, d * LANES + LANES) for d in range(na)]

    def towards_next(y, d):
        return jnp.where(lane < LANES - 16, y[d], y[(d + 1) % na])

    def towards_last(y, d):
        return jnp.where(lane < 16, y[d - 1], y[d])

    ea_all, er_all = field(2), field(3)
    ea_roll = [pltpu.roll(t, 16, 1) for t in ea_all]
    for d, es_d in enumerate(field(1)):
        es0_d, ea0_d = pltpu.roll(es_d, 1, 0), towards_last(ea_roll, d)
        er0_d = pltpu.roll(er_all[d], 1, 1)
        both = es_d + es0_d + ea_all[d] + ea0_d + er_all[d] + er0_d
        es[:, at[d]], ea[:, at[d]] = es_d, ea_all[d]
        es0[:, at[d]], ea0[:, at[d]] = es0_d, ea0_d
        er[:, at[d]] = jnp.where(wall | top, 0.0, er_all[d])
        er0[:, at[d]] = jnp.where(wall | (lane % 16 == 1), 0.0, er0_d)
        dg[:, at[d]] = jnp.where(wall, 0.0, both)
        ri[:, at[d]] = jnp.where(wall, 0.0, 1.0 / jnp.where(wall, 1.0, both))

    def inner(terms):
        return jnp.sum(jnp.sum(total(terms), axis=0, keepdims=True), axis=1, keepdims=True)

    first = field(0)
    r = [first[d] + side((d - 1) % na) for d in range(na)]
    p = [ri[:, at[d]] * r[d] for d in range(na)]
    gz = inner([r[d] * p[d] for d in range(na)])
    x = [jnp.zeros_like(t) for t in r]
    for it in range(ITERS):
        ahead = [pltpu.roll(t, LANES - 16, 1) for t in p]
        behind = [pltpu.roll(t, 16, 1) for t in p]
        q, terms = [], []
        for d in range(na):
            t, k = p[d], at[d]
            out = dg[:, k] * t
            out = out - es[:, k] * pltpu.roll(t, ns - 1, 0) - es0[:, k] * pltpu.roll(t, 1, 0)
            out = out - ea[:, k] * towards_next(ahead, d) - ea0[:, k] * towards_last(behind, d)
            out = out - er[:, k] * pltpu.roll(t, LANES - 1, 1) - er0[:, k] * pltpu.roll(t, 1, 1)
            q.append(out)
            terms.append(t * out)
        alpha = gz / inner(terms)
        x = [x[d] + alpha * p[d] for d in range(na)]
        if it + 1 < ITERS:
            r = [r[d] - alpha * q[d] for d in range(na)]
            z = [ri[:, at[d]] * r[d] for d in range(na)]
            new = inner([r[d] * z[d] for d in range(na)])
            beta = new / gz
            p = [z[d] + beta * p[d] for d in range(na)]
            gz = new
    for d in range(na):
        x2[:, at[d]] = x[d]

    s, a = pos[0], pos[1]
    blocks = [lax.rem(a + na - 1, na), a, lax.rem(a + 1, na)]
    for t in range(4):
        line = x2[pl.ds(lax.rem(s + ns - 1 + t, ns), 1), :]
        for j in range(2):
            for k in range(2):
                n = 4 * t + 2 * j + k
                vals[n : n + 1, :] = roll_l(line, -(16 * j + k)) if j + k else line
    near = iota(16, 1) < HALF
    b = [
        pltpu.roll(vals[:, pl.ds(pl.multiple_of(t * LANES, LANES), LANES)], HALF, 1) for t in blocks
    ]
    ext = jnp.concatenate([jnp.where(near, b[0], b[1]), jnp.where(near, b[1], b[2])], axis=1)
    rise = dot(up4[...], ext)
    even = is_even(pos, 0)
    x, y = wide(far, 0, 112), wide(near_side, 0, 112)
    below, above = jnp.where(even, x, y), jnp.where(even, y, x)
    low = dot(gmt_last[...], dot(gm_last[...], rise[:64]) * below[:96]) + below[96:]
    high = dot(gmt_first[...], dot(gm_first[...], rise[128:]) * above[:96]) + above[96:]
    flux = dot(gm[...], rise[64:128] + wide(wider, 64, 64)) * wide(g4, 0, 192)
    back = dot(gmt[...], flux)
    put(acc, 0, 16, back[:16] + low)
    put(acc, 16, 32, back[16:48])
    put(acc, 48, 16, back[48:] + high)
    join_mid(acc)
    put(sol, 0, 64, wide(wider, 128, 64) + rise[64:128])
    for h, r in tiles(64):
        now = wider[h, r : r + 8] - acc[h, r : r + 8]
        new = inv4[h, r : r + 8] * now * (1.0 / CENTER)
        res[h, r : r + 8] = now
        u[h, r : r + 8] = new
        sol[h, r : r + 8] += new
    mid_apply(u, g4, acc, gm, gmt)
    join_mid(acc)
    send_faces(acc, even, face_a, face_b, 16)


def sixth_kernel(
    pos, res, u, sol, acc, a, b, inv4, up8, kept, g8, bd, bdt,
    out, v8, acc2, face_a, face_b, y4,
):
    even = is_even(pos, 0)
    for h, r in tiles(64):
        now = res[h, r : r + 8] - full_of(acc, (even, a, b), h, r)
        new = KEEP * u[h, r : r + 8] + GAIN * inv4[h, r : r + 8] * now
        y4[h, r : r + 8] = sol[h, r : r + 8] + new
    put(v8, 0, 512, dot(up8[...], wide(y4, 0, 64)))
    for h, r in tiles(512):
        e8 = v8[h, r : r + 8]
        out[h, r : r + 8] = kept[h, r : r + 8] + e8
        v8[h, r : r + 8] = kept[h, 1024 + r : 1032 + r] + e8
    fine_front(v8, g8, acc2, bd, bdt)
    send_faces(acc2, even, face_a, face_b, 64)


def seventh_kernel(
    pos, kept, sol, acc, a, b, inv8, g8, bd, bdt, res, out, u, acc2, face_a, face_b
):
    even = is_even(pos, 0)
    for h, r in tiles(512):
        now = kept[h, 512 + r : 520 + r] - full_of(acc, (even, a, b), h, r)
        new = inv8[h, r : r + 8] * now * (1.0 / CENTER)
        res[h, r : r + 8] = now
        u[h, r : r + 8] = new
        out[h, r : r + 8] = sol[h, r : r + 8] + new
    fine_front(u, g8, acc2, bd, bdt)
    send_faces(acc2, even, face_a, face_b, 64)


def last_kernel(pos, res, sol, u, acc, a, b, inv8, out):
    got = (is_even(pos, 0), a, b)
    for r in range(0, 512, 8):
        halves = []
        for h in range(2):
            now = res[h, r : r + 8] - full_of(acc, got, h, r)
            new = KEEP * u[h, r : r + 8] + GAIN * inv8[h, r : r + 8] * now
            halves.append(sol[h, r : r + 8] + new)
        out[r : r + 8] = own_part(*halves)


def call(kernel, args, outs, scratch=(), scalars=1, unread=0, **options):
    vmem = pl.BlockSpec(memory_space=pltpu.VMEM)
    smem = pl.BlockSpec(memory_space=pltpu.SMEM)
    arrays = [x for x in args if not isinstance(x, str)]
    named = len(arrays) < len(args)

    def body(*refs):
        rest = iter(refs)
        given = [next(rest) for _ in arrays[: len(arrays) - named]]
        held = next(rest) if named else None
        given = iter(given)
        full = [Constant(held, x) if isinstance(x, str) else next(given) for x in args]
        kernel(*full, *rest)

    if named:
        arrays.append(PACK)
    return pl.pallas_call(
        body,
        out_shape=[jax.ShapeDtypeStruct(s, F32) for s in outs],
        in_specs=[smem] * scalars
        + [vmem] * (len(arrays) - scalars - unread)
        + [pl.BlockSpec(memory_space=pl.ANY)] * unread,
        out_specs=[vmem] * len(outs),
        scratch_shapes=[pltpu.VMEM(s, F32) for s in scratch],
        compiler_params=pltpu.CompilerParams(vmem_limit_bytes=32 * 1024 * 1024),
        name=kernel.__name__,
        **options,
    )(*arrays)


def exchange(far, near, axis):
    size = lax.axis_size(axis)
    pairs_far = [(i, (i + 1 if i % 2 else i - 1) % size) for i in range(size)]
    pairs_near = [(i, i ^ 1) for i in range(size)]
    return lax.ppermute(far, axis, pairs_far), lax.ppermute(near, axis, pairs_near)


def spread(x, axis, groups=None):
    size = len(groups[0]) if groups else lax.axis_size(axis)
    copies = jnp.broadcast_to(x[None], (size,) + x.shape)
    return lax.all_to_all(copies, axis, 0, 0, axis_index_groups=groups).reshape(-1, LANES)


def on_device(element_load, metric, element_order):
    ns, na = lax.axis_size("stream"), lax.axis_size("azim")
    fine, mid = (2, 512, LANES), (2, 64, LANES)
    face8, face4 = [(2, 64, LANES)] * 2, [(2, 16, LANES)] * 2
    pos = jnp.stack([lax.axis_index("stream"), lax.axis_index("azim")]).astype(jnp.int32)
    g, rolled, a, b = call(
        order_kernel,
        (pos, metric.reshape(1536, LANES), element_load.reshape(512, LANES), element_order),
        [(1536, LANES), (512, LANES), (1024, LANES), (1024, LANES)],
    )
    a, b = exchange(a, b, "azim")
    (diag,) = call(own_kernel, (g, "bsq"), [(512, LANES)], scalars=0)

    def inner(u, acc):
        (acc,) = call(inner_kernel, (u, g8, acc, "bd", "bdt"), [fine], (), 0)
        return acc

    g8, load, diag8, a, b = call(
        setup_kernel,
        (pos, g, rolled, diag, a, b, "bsq"),
        [(2, 1536, LANES), fine, fine] + [(2, 128, LANES)] * 2,
        [(1536, LANES), (512, LANES)],
    )
    a, b = exchange(a, b, "stream")
    res8, inv8, u8, acc, a, b = call(
        first_kernel,
        (pos, load, diag8, a, b, g8, "bd", "bdt"),
        [fine, fine, fine, fine] + face8,
    )
    a, b = exchange(a, b, "stream")
    acc = inner(u8, acc)
    g4, diag4, edges, upper = call(
        coarsen_kernel,
        (g8, "w4", "w2", "sample", "sq4"),
        [(2, 192, LANES), mid, (8, LANES), (8, LANES)],
        scalars=0,
    )
    kept, t4, a, b = call(
        second_kernel,
        (pos, res8, inv8, acc, a, b, diag4, upper, g8, "bd", "bdt", "down8"),
        [(2, 1536, LANES), mid] + [(2, 40, LANES)] * 2,
        [fine, fine, (512, 2 * LANES)],
    )
    a, b = exchange(a, b, "stream")
    res4, inv4, edges, acc, a, b = call(
        third_kernel,
        (pos, t4, diag4, edges, a, b, g4, "gm", "gmt"),
        [mid, mid, (8, LANES), mid] + face4,
        [mid],
    )
    a, b = exchange(a, b, "stream")
    corners, a, b, keep = call(
        fourth_kernel,
        (pos, res4, acc, inv4, edges, a, b, g4, "gm", "gmt", "m4", "down4"),
        [(8, LANES), (192, LANES), (192, LANES), (2, 192, LANES)],
        [mid],
    )
    columns = spread(corners, "stream")
    a, b = exchange(a, b, "azim")
    wider, a, b = call(
        side_kernel,
        (pos, keep, a, b, g4, "gm", "gmt"),
        [(2, 192, LANES)] + [(2, 112, LANES)] * 2,
        [mid],
    )
    sides = exchange(a, b, "stream")
    size = 4 * ns + ns // groups(ns)
    (columns,) = call(
        column_kernel, (columns, *sides), [(size, LANES)], (), 0, unread=2
    )
    cores = [list(range(core, na, 2)) for core in range(2)]
    columns = spread(columns, "azim", cores)
    others = lax.ppermute(columns, "azim", [(i, i ^ 1) for i in range(na)])
    whole = (ns, na * LANES)
    res4, u4, sol4, acc, a, b = call(
        coarse_kernel,
        (
            pos,
            columns,
            others,
            wider,
            *sides,
            g4,
            inv4,
            "gm",
            "gmt",
            "up4",
            "gm_first",
            "gmt_first",
            "gm_last",
            "gmt_last",
        ),
        [mid, mid, mid, mid] + face4,
        [(16, na * LANES)] + [whole] * 9,
    )
    a, b = exchange(a, b, "stream")
    sol8, v8, acc, a, b = call(
        sixth_kernel,
        (pos, res4, u4, sol4, acc, a, b, inv4, "up8", kept, g8, "bd", "bdt"),
        [fine, fine, fine] + face8,
        [mid],
    )
    a, b = exchange(a, b, "stream")
    acc = inner(v8, acc)
    res8, sol8, u8, acc, a, b = call(
        seventh_kernel,
        (pos, kept, sol8, acc, a, b, inv8, g8, "bd", "bdt"),
        [fine, fine, fine, fine] + face8,
    )
    a, b = exchange(a, b, "stream")
    acc = inner(u8, acc)
    (out,) = call(last_kernel, (pos, res8, sol8, u8, acc, a, b, inv8), [(512, LANES)])
    return out.reshape(element_load.shape)


def solution(mesh):
    placed = (P(None, "stream", "azim"), P(None, None, "stream", "azim"), P("stream", "azim"))
    return jax.shard_map(
        on_device, mesh=mesh, in_specs=placed, out_specs=P(None, "stream", "azim"), check_vma=False
    )
```

```python
import jax
import jax.numpy as jnp
import numpy as np
from jax import lax
from jax.experimental import pallas as pl
from jax.experimental.pallas import tpu as pltpu
from jax.sharding import PartitionSpec as P

ITERS = 6
LOW_EIG = 0.3
HIGH_EIG = 3.0
CENTER = 0.5 * (HIGH_EIG + LOW_EIG)
HALF_WIDTH = 0.5 * (HIGH_EIG - LOW_EIG)
FIRST_RHO = HALF_WIDTH / CENTER
SECOND_RHO = 1.0 / (2.0 * CENTER / HALF_WIDTH - FIRST_RHO)
KEEP = SECOND_RHO * FIRST_RHO
GAIN = 2.0 * SECOND_RHO / HALF_WIDTH
LANES = 128
HALF = 64
F32 = jnp.float32


def legendre_pair(degree, places):
    previous = places * 0.0 + 1.0
    current = places.copy()
    for k in range(2, degree + 1):
        following = ((2 * k - 1) * places * current - (k - 1) * previous) / k
        previous = current
        current = following
    return (current, previous)


def gll_table(points):
    degree = points - 1
    places = np.cos(np.pi * np.arange(points) / degree)
    for _ in range(60):
        top, below = legendre_pair(degree, places)
        places = places - (places * top - below) / (points * top)
    nodes = np.sort(places)
    nodes[0] = -1.0
    nodes[-1] = 1.0
    at_nodes = legendre_pair(degree, nodes)[0]
    weights = 2.0 / (degree * (degree + 1) * at_nodes**2)
    deriv = np.zeros((points, points))
    for i in range(points):
        for j in range(points):
            if i != j:
                deriv[i, j] = at_nodes[i] / (at_nodes[j] * (nodes[i] - nodes[j]))
    deriv[0, 0] = -degree * (degree + 1) / 4.0
    deriv[-1, -1] = degree * (degree + 1) / 4.0
    return (nodes, weights, deriv)


def lagrange_table(source, target):
    out = np.ones((len(target), len(source)))
    for j in range(len(source)):
        for k in range(len(source)):
            if k != j:
                out[:, j] *= (target - source[k]) / (source[j] - source[k])
    return out


N8, W8, D8 = gll_table(8)
N4, W4, D4 = gll_table(4)
N2, W2, D2 = gll_table(2)


def kron3(a, b, c):
    return np.kron(np.kron(a, b), c)


def cube(w):
    return (w[:, None, None] * w[None, :, None] * w[None, None, :]).reshape(-1)


def share(n):
    edge = np.ones(n)
    edge[0] = edge[-1] = 0.5
    return cube(edge)


def grads(d):
    i = np.eye(d.shape[0])
    return [kron3(d, i, i), kron3(i, d, i), kron3(i, i, d)]


def f32(x):
    return np.asarray(x, np.float32)


def lanes_of(column):
    return np.repeat(f32(column)[:, None], LANES, axis=1)


UP8 = lagrange_table(N4, N8)
UP4 = lagrange_table(N2, N4)
TO4 = lagrange_table(N8, N4)
TO2 = lagrange_table(N8, N2)

C_BD = f32(np.kron(np.eye(16), D8))
C_BDT = f32(np.kron(np.eye(16), D8.T))
C_BSQ = f32(np.kron(np.eye(16), (D8 * D8).T))
C_SAMPLE = f32(np.concatenate([kron3(TO4, TO4, TO4), kron3(TO2, TO2, TO2)]))
C_UP8 = f32(kron3(UP8, UP8, UP8))
C_DOWN8 = f32(kron3(UP8, UP8, UP8).T)
C_UP4 = f32(kron3(UP4, UP4, UP4))
C_DOWN4 = f32(kron3(UP4, UP4, UP4).T)
C_UP4X3 = np.zeros((192, 16), np.float32)
for layer in range(3):
    C_UP4X3[64 * layer : 64 * layer + 64, 4 * layer : 4 * layer + 8] = C_UP4
C_G4 = f32(np.concatenate(grads(D4)))
C_G4T = f32(np.concatenate(grads(D4)).T)
C_SQ4 = f32((np.concatenate(grads(D4)) ** 2).T)
C_W4 = lanes_of(cube(W4) / np.exp(kron3(TO4, TO4, TO4) @ np.log(cube(W8))))
C_W2 = lanes_of(cube(W2) / np.exp(kron3(TO2, TO2, TO2) @ np.log(cube(W8))))
C_M4 = lanes_of(share(4))
FIRST = np.r_[0:64, 64:80, 128:144]
LAST = np.r_[0:64, 112:128, 176:192]
CONSTANTS = {
    "bd": C_BD, "bdt": C_BDT, "bsq": C_BSQ, "sample": C_SAMPLE, "w4": C_W4, "w2": C_W2,
    "sq4": C_SQ4, "gm": C_G4, "gmt": C_G4T, "m4": C_M4, "down8": C_DOWN8, "down4": C_DOWN4,
    "up4": C_UP4X3, "up8": C_UP8, "gm_first": C_G4[FIRST], "gmt_first": C_G4T[:16, FIRST],
    "gm_last": C_G4[LAST], "gmt_last": C_G4T[48:, LAST],
}


def pack_constants():
    rows, places, start = [], {}, 0
    for name, value in CONSTANTS.items():
        blocks = -(-value.shape[1] // LANES)
        padded = np.zeros((value.shape[0], blocks * LANES), np.float32)
        padded[:, : value.shape[1]] = value
        rows += [padded[:, k * LANES : (k + 1) * LANES] for k in range(blocks)]
        places[name] = (start, value.shape, blocks)
        start += value.shape[0] * blocks
    return np.concatenate(rows), places


PACK, PLACES = pack_constants()


class Constant:
    def __init__(self, ref, name):
        self.ref, self.name = ref, name

    def __getitem__(self, index):
        start, (rows, columns), blocks = PLACES[self.name]
        parts = []
        for k in range(blocks):
            width = min(LANES, columns - k * LANES)
            parts.append(self.ref[start + k * rows : start + (k + 1) * rows, :width])
        value = parts[0] if blocks == 1 else jnp.concatenate(parts, axis=1)
        return value if index is Ellipsis else value[index]


def dot(a, b):
    return jnp.dot(a, b, preferred_element_type=F32, precision=lax.Precision.HIGHEST)


def iota(rows, axis):
    return lax.broadcasted_iota(jnp.int32, (rows, LANES), axis)


def wide(ref, start, size):
    return jnp.concatenate([ref[0, start : start + size], ref[1, start : start + size]], axis=1)


def put(ref, start, size, value):
    ref[0, start : start + size] = value[:, :LANES]
    ref[1, start : start + size] = value[:, LANES:]


def total(terms):
    out = terms[0]
    for t in terms[1:]:
        out = out + t
    return out


def contract(v, matrix, sign):
    n = len(v)
    h = n // 2
    even = [v[k] + v[n - 1 - k] for k in range(h)]
    odd = [v[k] - v[n - 1 - k] for k in range(h)]
    out = [None] * n
    for i in range(h):
        p = total([even[k] * float(0.5 * (matrix[i, k] + matrix[i, n - 1 - k])) for k in range(h)])
        q = total([odd[k] * float(0.5 * (matrix[i, k] - matrix[i, n - 1 - k])) for k in range(h)])
        out[i] = p + q
        out[n - 1 - i] = q - p if sign < 0 else p - q
    return out


def fine_rows(s, a):
    return s * 64 + a * 8


PLANES = [(0, 7), (1, 2), (3, 4), (5, 6)]


def pair(ref, p, base=0):
    return jnp.concatenate([wide(ref, base + 64 * s, 64) for s in p], axis=0)


def put_pair(ref, p, value):
    for k, s in enumerate(p):
        put(ref, 64 * s, 64, value[64 * k : 64 * k + 64])


def fine_stream(u, g, acc):
    for h in range(2):
        for a in range(8):
            at = [fine_rows(s, a) for s in range(8)]
            grad = contract([u[h, r : r + 8] for r in at], D8, -1)
            back = contract([grad[s] * g[h, r : r + 8] for s, r in enumerate(at)], D8.T, -1)
            for s, r in enumerate(at):
                acc[h, r : r + 8] = back[s]


def fine_cross(u, g, acc, bd, bdt, pairs):
    for p in pairs:
        flux = dot(bd[...], pair(u, p)) * pair(g, p, 1024)
        put_pair(acc, p, pair(acc, p) + dot(bdt[...], flux))
        for s in p:
            for h in range(2):
                at = [fine_rows(s, a) for a in range(8)]
                grad = contract([u[h, r : r + 8] for r in at], D8, -1)
                flux = [grad[a] * g[h, 512 + r : 520 + r] for a, r in enumerate(at)]
                back = contract(flux, D8.T, -1)
                for a, r in enumerate(at):
                    acc[h, r : r + 8] += back[a]


def fine_apply(u, g, acc, bd, bdt):
    fine_stream(u, g, acc)
    fine_cross(u, g, acc, bd, bdt, PLANES)


def fine_front(u, g, acc, bd, bdt):
    fine_stream(u, g, acc)
    fine_cross(u, g, acc, bd, bdt, PLANES[:1])
    join_fine(acc, (0, 7))


def left(x0, x1):
    near = iota(x0.shape[0], 1) < LANES - 16
    y0, y1 = pltpu.roll(x0, LANES - 16, 1), pltpu.roll(x1, LANES - 16, 1)
    return jnp.where(near, y0, y1), jnp.where(near, y1, y0)


def right(x0, x1):
    near = iota(x0.shape[0], 1) >= 16
    y0, y1 = pltpu.roll(x0, 16, 1), pltpu.roll(x1, 16, 1)
    return jnp.where(near, y0, y1), jnp.where(near, y1, y0)


def join_radial(x, points, start, rows):
    place = iota(rows, 1) % 16
    first = pl.ds(start, rows, stride=points)
    last = pl.ds(start + points - 1, rows, stride=points)
    for h in range(2):
        view = x.at[h]
        low, high = view[first, :], view[last, :]
        view[first, :] = jnp.where(place == 0, 0.0, low + pltpu.roll(high, 1, 1))
        view[last, :] = jnp.where(place == 15, 0.0, high + pltpu.roll(low, LANES - 1, 1))


def join_fine(x, planes=range(8)):
    for s in planes:
        join_radial(x, 8, 64 * s, 8)
        lo, hi = fine_rows(s, 0), fine_rows(s, 7)
        low = [x[h, lo : lo + 8] for h in range(2)]
        high = [x[h, hi : hi + 8] for h in range(2)]
        to_low, to_high = right(*high), left(*low)
        for h in range(2):
            x[h, lo : lo + 8] = low[h] + to_low[h]
            x[h, hi : hi + 8] = high[h] + to_high[h]


def join_mid(x):
    join_radial(x, 4, 0, 16)
    first = iota(8, 0) < 4
    for s in range(4):
        lo, hi = s * 16, s * 16 + 8
        low = [x[h, lo : lo + 8] for h in range(2)]
        high = [x[h, hi : hi + 8] for h in range(2)]
        to_low = right(*[pltpu.roll(t, 4, 0) for t in high])
        to_high = left(*[pltpu.roll(t, 4, 0) for t in low])
        for h in range(2):
            x[h, lo : lo + 8] = low[h] + jnp.where(first, to_low[h], 0.0)
            x[h, hi : hi + 8] = high[h] + jnp.where(first, 0.0, to_high[h])


def is_even(place, k):
    return lax.rem(place[k], 2) == 0


def full_of(x, faces, h, r, offset=0):
    even, far, near = faces
    rows = x.shape[1]
    plane = {512: 64, 64: 16}[rows]
    value = x[h, r : r + 8]
    if r < plane:
        at = offset + r
        return value + jnp.where(even, far[h, at : at + 8], near[h, at : at + 8])
    if r >= rows - plane:
        at = offset + r - (rows - plane)
        return value + jnp.where(even, near[h, at : at + 8], far[h, at : at + 8])
    return value


def send_faces(x, even, far, near, plane, offset=0):
    rows = x.shape[1]
    last = rows - plane
    one = pl.multiple_of(jnp.where(even, last, 0), 8)
    two = pl.multiple_of(jnp.where(even, 0, last), 8)
    for h in range(2):
        near[h, offset : offset + plane] = x[h, pl.ds(one, plane), :]
        far[h, offset : offset + plane] = x[h, pl.ds(two, plane), :]


def wall_mask(points):
    place, node = iota(8, 1) % 16, iota(8, 0) % points
    return ((node == 0) & (place == 0)) | ((node == points - 1) & (place == 15))


def own_part(half0, half1):
    near = iota(half0.shape[0], 1) < HALF
    return pltpu.roll(jnp.where(near, half1, half0), HALF, 1)


def tiles(rows):
    return [(h, r) for h in range(2) for r in range(0, rows, 8)]


def mid_apply(u, g4, acc, gm, gmt):
    flux = dot(gm[...], wide(u, 0, 64)) * wide(g4, 0, 192)
    put(acc, 0, 64, dot(gmt[...], flux))


def fine_diagonal(g, diag, bsq):
    square = (D8 * D8).T
    for c in range(4):
        rows = slice(128 * c, 128 * c + 128)
        diag[rows] = dot(bsq[...], g[1024 + 128 * c : 1152 + 128 * c])
    for axis in range(2):
        for fixed in range(8):
            at = [fine_rows(k, fixed) if axis == 0 else fine_rows(fixed, k) for k in range(8)]
            back = contract([g[512 * axis + r : 512 * axis + r + 8] for r in at], square, 1)
            for k, r in enumerate(at):
                diag[r : r + 8] += back[k]


def halves_up_down(a, b):
    near = iota(8, 1) < HALF
    up = jnp.where(near, a, pltpu.roll(b, HALF, 1))
    return up, jnp.where(near, pltpu.roll(a, HALF, 1), b)


def before_after(even, x, y):
    p, n = jnp.where(even, x, y), jnp.where(even, y, x)
    near = iota(8, 1) < HALF
    first = (jnp.where(near, p, 0.0), jnp.where(near, 0.0, pltpu.roll(n, HALF, 1)))
    second = (jnp.where(near, pltpu.roll(p, HALF, 1), 0.0), jnp.where(near, 0.0, n))
    return first, second


def order_kernel(pos, metric, load, order, g, rolled, far, near):
    even = is_even(pos, 1)
    slots = jnp.broadcast_to(pltpu.roll(order[...], HALF, 1), (8, LANES))
    wr = total([jnp.where(iota(8, 0) == k, float(W8[k]), 0.0) for k in range(8)])
    for r in range(0, 1536, 8):
        scale = wr * float(W8[(r % 512) // 64] * W8[(r // 8) % 8])
        g[r : r + 8] = jnp.take_along_axis(metric[r : r + 8], slots, axis=1) * scale
    for r in range(0, 512, 8):
        rolled[r : r + 8] = pltpu.roll(load[r : r + 8], HALF, 1)
    for r in range(0, 1024, 8):
        other = g[1024 + r : 1032 + r] if r < 512 else rolled[r - 512 : r - 504]
        up, down = halves_up_down(g[r : r + 8], other)
        far[r : r + 8] = jnp.where(even, down, up)
        near[r : r + 8] = jnp.where(even, up, down)


def own_kernel(g, bsq, diag):
    fine_diagonal(g, diag, bsq)


def setup_kernel(
    pos, g, rolled, diag, x, y, bsq, g8, load, diag8, face_a, face_b, ghost, ghost_diag
):
    near = iota(8, 1) < HALF
    even_a = is_even(pos, 1)

    def place(out, row, own, sides):
        out[0, row : row + 8] = jnp.where(near, sides[0], own)
        out[1, row : row + 8] = jnp.where(near, own, sides[1])

    for r in range(0, 1024, 8):
        first, second = before_after(even_a, x[r : r + 8], y[r : r + 8])
        place(g8, r, g[r : r + 8], first)
        ghost[r : r + 8] = first[0] + first[1]
        if r < 512:
            place(g8, 1024 + r, g[1024 + r : 1032 + r], second)
            ghost[1024 + r : 1032 + r] = second[0] + second[1]
        else:
            place(load, r - 512, rolled[r - 512 : r - 504], second)
    fine_diagonal(ghost, ghost_diag, bsq)
    for r in range(0, 512, 8):
        side = ghost_diag[r : r + 8]
        place(diag8, r, diag[r : r + 8], (side, side))
    for x in (load, diag8):
        join_fine(x)
    even = is_even(pos, 0)
    send_faces(load, even, face_a, face_b, 64)
    send_faces(diag8, even, face_a, face_b, 64, 64)


def coarsen_kernel(g8, w4, w2, sample, sq4, g4, diag4, edges, upper):
    low = []
    for d in range(3):
        coarse = jnp.exp(dot(sample[...], jnp.log(wide(g8, 512 * d, 512))))
        put(g4, 64 * d, 64, coarse[:64] * jnp.concatenate([w4[...], w4[...]], axis=1))
        low.append([coarse[64:72, :LANES] * w2[...], coarse[64:72, LANES:] * w2[...]])
    put(diag4, 0, 64, dot(sq4[...], wide(g4, 0, 192)))
    join_mid(diag4)

    def corner(d, i, j, k):
        row = 4 * i + 2 * j + k
        return [t[row : row + 1] for t in low[d]]

    def add(x, y):
        return [x[0] + y[0], x[1] + y[1]]

    def quarter(x):
        return [0.25 * x[0], 0.25 * x[1]]

    def outward(x):
        return [pltpu.roll(x[0], 1, 1), pltpu.roll(x[1], 1, 1)]

    es = [[quarter(add(corner(0, 0, j, k), corner(0, 1, j, k))) for k in range(2)] for j in range(2)]
    ea = [[quarter(add(corner(1, i, 0, k), corner(1, i, 1, k))) for k in range(2)] for i in range(2)]
    er = [[quarter(add(corner(2, i, j, 0), corner(2, i, j, 1))) for j in range(2)] for i in range(2)]
    col = [add(es[0][k], list(right(*es[1][k]))) for k in range(2)]
    edge_s = add(col[0], outward(col[1]))
    edge_a = [add(ea[i][0], outward(ea[i][1])) for i in range(2)]
    edge_r = [add(er[i][0], list(right(*er[i][1]))) for i in range(2)]
    off_wall = iota(1, 1) % 16 != 0
    rows = [jnp.where(off_wall, own_part(*x), 0.0) for x in (edge_s, edge_a[0], edge_a[1])]
    rows += [own_part(*x) for x in edge_r]
    none = jnp.zeros((5, LANES), F32)
    edges[...] = jnp.concatenate([rows[0], rows[1], rows[3], none], axis=0)
    upper[...] = jnp.concatenate([rows[0], rows[2], rows[4], none], axis=0)


def first_kernel(
    pos, load, diag8, a, b, g8, bd, bdt, res, inv8, u, acc, face_a, face_b
):
    even = is_even(pos, 0)
    got = (even, a, b)
    wall8 = wall_mask(8)
    for h, r in tiles(512):
        diag = full_of(diag8, got, h, r, 64)
        inv = jnp.where(wall8, 0.0, 1.0 / jnp.where(wall8, 1.0, diag))
        full = full_of(load, got, h, r)
        res[h, r : r + 8] = full
        inv8[h, r : r + 8] = inv
        u[h, r : r + 8] = inv * full * (1.0 / CENTER)
    fine_front(u, g8, acc, bd, bdt)
    send_faces(acc, even, face_a, face_b, 64)


def inner_kernel(u, g8, start, bd, bdt, acc):
    for h, r in tiles(512):
        acc[h, r : r + 8] = start[h, r : r + 8]
    fine_cross(u, g8, acc, bd, bdt, PLANES[1:])
    join_fine(acc, range(1, 7))


def second_kernel(
    pos, res, inv8, acc, a, b, diag4, upper, g8, bd, bdt, down8,
    kept, t4, face_a, face_b, u, back, part,
):
    even = is_even(pos, 0)
    got = (even, a, b)
    edge = jnp.where((iota(8, 0) == 0) | (iota(8, 0) == 7), 0.5, 1.0)
    for h, r in tiles(512):
        inv, before = inv8[h, r : r + 8], res[h, r : r + 8]
        now = before - full_of(acc, got, h, r)
        old = inv * before * (1.0 / CENTER)
        new = KEEP * old + GAIN * inv * now
        kept[h, r : r + 8] = old + new
        kept[h, 512 + r : 520 + r] = now
        kept[h, 1024 + r : 1032 + r] = new
        u[h, r : r + 8] = new
    fine_apply(u, g8, back, bd, bdt)
    for h, r in tiles(512):
        s, c = r // 64, (r // 8) % 8
        scale = (0.5 if s in (0, 7) else 1.0) * (0.5 if c in (0, 7) else 1.0)
        part[r : r + 8, h * LANES : h * LANES + LANES] = (
            kept[h, 512 + r : 520 + r] * (edge * scale) - back[h, r : r + 8]
        )
    put(t4, 0, 64, dot(down8[...], part[...]))
    join_mid(t4)
    send_faces(t4, even, face_a, face_b, 16)
    send_faces(diag4, even, face_a, face_b, 16, 16)
    for face in (face_a, face_b):
        for h in range(2):
            face[h, 32:40] = upper[...]


def third_kernel(
    pos, t4, diag4, edges, a, b, g4, gm, gmt, res, inv4, edge, acc, face_a, face_b, u
):
    even = is_even(pos, 0)
    got = (even, a, b)
    wall = wall_mask(4)
    for h, r in tiles(64):
        full = full_of(t4, got, h, r)
        diag = full_of(diag4, got, h, r, 16)
        inv = jnp.where(wall, 0.0, 1.0 / jnp.where(wall, 1.0, diag))
        res[h, r : r + 8] = full
        inv4[h, r : r + 8] = inv
        u[h, r : r + 8] = inv * full * (1.0 / CENTER)
    lower = jnp.where(even, a[0, 32:40], b[0, 32:40])
    edge[...] = edges[...] + jnp.where(iota(8, 0) == 0, 0.0, lower)
    mid_apply(u, g4, acc, gm, gmt)
    join_mid(acc)
    send_faces(acc, even, face_a, face_b, 16)


def fourth_kernel(
    pos, res, acc, inv4, edge, a, b, g4, gm, gmt, m4, down4, corners, one, two, keep, part
):
    got = (is_even(pos, 0), a, b)
    for h, r in tiles(64):
        inv, before = inv4[h, r : r + 8], res[h, r : r + 8]
        now = before - full_of(acc, got, h, r)
        old = inv * before * (1.0 / CENTER)
        new = KEEP * old + GAIN * inv * now
        keep[h, r : r + 8] = now
        keep[h, 64 + r : 72 + r] = new
        keep[h, 128 + r : 136 + r] = old + new
    even_a = is_even(pos, 1)
    one[...] = jnp.where(even_a, keep[0], keep[1])
    two[...] = jnp.where(even_a, keep[1], keep[0])
    flux = dot(gm[...], wide(keep, 64, 64)) * wide(g4, 0, 192)
    put(part, 0, 64, dot(gmt[...], flux))
    for h, r in tiles(64):
        part[h, r : r + 8] = m4[r : r + 8] * keep[h, r : r + 8] - part[h, r : r + 8]
    low = dot(down4[...], wide(part, 0, 64))
    near = iota(8, 1) < HALF
    half0 = jnp.where(near, 0.0, low[:, :LANES])
    half1 = jnp.where(near, low[:, LANES:], 0.0)

    def corner(i, j, k):
        row = 4 * i + 2 * j + k
        return [half0[row : row + 1], half1[row : row + 1]]

    lane = iota(1, 1)
    mine, extra = [], []
    for i in range(2):
        columns = []
        for k in range(2):
            shifted = right(*corner(i, 1, k))
            straight = corner(i, 0, k)
            columns.append([straight[0] + shifted[0], straight[1] + shifted[1]])
        both = [columns[0][h] + pltpu.roll(columns[1][h], 1, 1) for h in range(2)]
        both = [jnp.where(lane % 16 == 0, 0.0, t) for t in both]
        mine.append(own_part(*both))
        extra.append(both[1])
    sides = jnp.where(lane < 16, pltpu.roll(extra[0], HALF, 1), 0.0) + jnp.where(
        (lane >= 16) & (lane < 32), pltpu.roll(extra[1], HALF + 16, 1), 0.0
    )
    none = jnp.zeros((2, LANES), F32)
    corners[...] = jnp.concatenate(mine + [sides, edge[0:3], none], axis=0)


def groups(ns):
    return max(1, ns // 8)


def side_kernel(pos, to_far, to_near, one, two, g4, gm, gmt, wider, far, near_side, back):
    near = iota(8, 1) < HALF
    even, even_a = is_even(pos, 0), is_even(pos, 1)
    for r in range(0, 192, 8):
        x, y = one[r : r + 8], two[r : r + 8]
        before, after = jnp.where(even_a, x, y), jnp.where(even_a, y, x)
        x, y = to_far[r : r + 8], to_near[r : r + 8]
        lower, upper = jnp.where(even_a, x, y), jnp.where(even_a, y, x)
        halves = (jnp.where(near, before, lower), jnp.where(near, upper, after))
        for h in range(2):
            wider[h, r : r + 8] = halves[h]
    flux = dot(gm[...], wide(wider, 64, 64)) * wide(g4, 0, 192)
    put(back, 0, 64, dot(gmt[...], flux))
    one = pl.multiple_of(jnp.where(even, 48, 0), 8)
    two = pl.multiple_of(jnp.where(even, 0, 48), 8)
    for out, plane in ((near_side, one), (far, two)):
        for h in range(2):
            out[h, 0:64] = g4[h, 0:64]
            out[h, 64:80] = g4[h, pl.ds(64 + plane, 16), :]
            out[h, 80:96] = g4[h, pl.ds(128 + plane, 16), :]
            out[h, 96:112] = back[h, pl.ds(plane, 16), :]


def column_kernel(rows, first, out):
    ns = rows.shape[0] // 8
    n = ns // groups(ns)

    def field(k):
        return rows[pl.ds(k, ns, stride=8), :]

    def later(x):
        return pltpu.roll(x, 1, 0)

    sides = field(2)
    over = jnp.where(iota(ns, 1) < 16, sides + later(pltpu.roll(sides, LANES - 16, 1)), 0.0)
    out[0:ns] = field(0) + later(field(1))
    for k in range(3):
        out[(1 + k) * ns : (2 + k) * ns] = field(3 + k)
    parts = [over[k * n : k * n + n] for k in range(groups(ns))]
    out[4 * ns : 4 * ns + n] = total(
        [pltpu.roll(p, 16 * k, 1) if k else p for k, p in enumerate(parts)]
    )


def pass_kernel(rows, first, second, out):
    out[...] = rows[...]


def coarse_kernel(
    pos, columns, others, wider, far, near_side, g4, inv4, gm, gmt, up4, gm_first, gmt_first,
    gm_last, gmt_last,
    res, u, sol, acc, face_a, face_b, vals, x2, es, ea, er, es0, ea0, er0, dg, ri,
):
    ns = x2.shape[0]
    na = x2.shape[1] // LANES
    width = na * LANES

    n = ns // groups(ns)
    size = 4 * ns + n
    even_a = is_even(pos, 1)

    def rows_of(d, start, count):
        at = d // 2 * size + start
        x, y = columns[at : at + count], others[at : at + count]
        return jnp.where(even_a, x, y) if d % 2 == 0 else jnp.where(even_a, y, x)

    def field(k):
        return [rows_of(d, k * ns, ns) for d in range(na)]

    def side(d):
        packed = rows_of(d, 4 * ns, n)
        parts = [pltpu.roll(packed, LANES - 16 * k, 1) if k else packed for k in range(groups(ns))]
        return jnp.where(iota(ns, 1) < 16, jnp.concatenate(parts, axis=0), 0.0)

    def roll_l(x, k):
        return pltpu.roll(x, k % width, 1)

    lane = iota(ns, 1)
    wall, top = lane % 16 == 0, lane % 16 == 15
    at = [slice(d * LANES, d * LANES + LANES) for d in range(na)]

    def towards_next(y, d):
        return jnp.where(lane < LANES - 16, y[d], y[(d + 1) % na])

    def towards_last(y, d):
        return jnp.where(lane < 16, y[d - 1], y[d])

    ea_all, er_all = field(2), field(3)
    ea_roll = [pltpu.roll(t, 16, 1) for t in ea_all]
    for d, es_d in enumerate(field(1)):
        es0_d, ea0_d = pltpu.roll(es_d, 1, 0), towards_last(ea_roll, d)
        er0_d = pltpu.roll(er_all[d], 1, 1)
        both = es_d + es0_d + ea_all[d] + ea0_d + er_all[d] + er0_d
        es[:, at[d]], ea[:, at[d]] = es_d, ea_all[d]
        es0[:, at[d]], ea0[:, at[d]] = es0_d, ea0_d
        er[:, at[d]] = jnp.where(wall | top, 0.0, er_all[d])
        er0[:, at[d]] = jnp.where(wall | (lane % 16 == 1), 0.0, er0_d)
        dg[:, at[d]] = jnp.where(wall, 0.0, both)
        ri[:, at[d]] = jnp.where(wall, 0.0, 1.0 / jnp.where(wall, 1.0, both))

    def inner(terms):
        return jnp.sum(jnp.sum(total(terms), axis=0, keepdims=True), axis=1, keepdims=True)

    first = field(0)
    r = [first[d] + side((d - 1) % na) for d in range(na)]
    p = [ri[:, at[d]] * r[d] for d in range(na)]
    gz = inner([r[d] * p[d] for d in range(na)])
    x = [jnp.zeros_like(t) for t in r]
    for it in range(ITERS):
        ahead = [pltpu.roll(t, LANES - 16, 1) for t in p]
        behind = [pltpu.roll(t, 16, 1) for t in p]
        q, terms = [], []
        for d in range(na):
            t, k = p[d], at[d]
            out = dg[:, k] * t
            out = out - es[:, k] * pltpu.roll(t, ns - 1, 0) - es0[:, k] * pltpu.roll(t, 1, 0)
            out = out - ea[:, k] * towards_next(ahead, d) - ea0[:, k] * towards_last(behind, d)
            out = out - er[:, k] * pltpu.roll(t, LANES - 1, 1) - er0[:, k] * pltpu.roll(t, 1, 1)
            q.append(out)
            terms.append(t * out)
        alpha = gz / inner(terms)
        x = [x[d] + alpha * p[d] for d in range(na)]
        if it + 1 < ITERS:
            r = [r[d] - alpha * q[d] for d in range(na)]
            z = [ri[:, at[d]] * r[d] for d in range(na)]
            new = inner([r[d] * z[d] for d in range(na)])
            beta = new / gz
            p = [z[d] + beta * p[d] for d in range(na)]
            gz = new
    for d in range(na):
        x2[:, at[d]] = x[d]

    s, a = pos[0], pos[1]
    blocks = [lax.rem(a + na - 1, na), a, lax.rem(a + 1, na)]
    for t in range(4):
        line = x2[pl.ds(lax.rem(s + ns - 1 + t, ns), 1), :]
        for j in range(2):
            for k in range(2):
                n = 4 * t + 2 * j + k
                vals[n : n + 1, :] = roll_l(line, -(16 * j + k)) if j + k else line
    near = iota(16, 1) < HALF
    b = [
        pltpu.roll(vals[:, pl.ds(pl.multiple_of(t * LANES, LANES), LANES)], HALF, 1) for t in blocks
    ]
    ext = jnp.concatenate([jnp.where(near, b[0], b[1]), jnp.where(near, b[1], b[2])], axis=1)
    rise = dot(up4[...], ext)
    even = is_even(pos, 0)
    x, y = wide(far, 0, 112), wide(near_side, 0, 112)
    below, above = jnp.where(even, x, y), jnp.where(even, y, x)
    low = dot(gmt_last[...], dot(gm_last[...], rise[:64]) * below[:96]) + below[96:]
    high = dot(gmt_first[...], dot(gm_first[...], rise[128:]) * above[:96]) + above[96:]
    flux = dot(gm[...], rise[64:128] + wide(wider, 64, 64)) * wide(g4, 0, 192)
    back = dot(gmt[...], flux)
    put(acc, 0, 16, back[:16] + low)
    put(acc, 16, 32, back[16:48])
    put(acc, 48, 16, back[48:] + high)
    join_mid(acc)
    put(sol, 0, 64, wide(wider, 128, 64) + rise[64:128])
    for h, r in tiles(64):
        now = wider[h, r : r + 8] - acc[h, r : r + 8]
        new = inv4[h, r : r + 8] * now * (1.0 / CENTER)
        res[h, r : r + 8] = now
        u[h, r : r + 8] = new
        sol[h, r : r + 8] += new
    mid_apply(u, g4, acc, gm, gmt)
    join_mid(acc)
    send_faces(acc, even, face_a, face_b, 16)


def sixth_kernel(
    pos, res, u, sol, acc, a, b, inv4, up8, kept, g8, bd, bdt,
    out, v8, acc2, face_a, face_b, y4,
):
    even = is_even(pos, 0)
    for h, r in tiles(64):
        now = res[h, r : r + 8] - full_of(acc, (even, a, b), h, r)
        new = KEEP * u[h, r : r + 8] + GAIN * inv4[h, r : r + 8] * now
        y4[h, r : r + 8] = sol[h, r : r + 8] + new
    put(v8, 0, 512, dot(up8[...], wide(y4, 0, 64)))
    for h, r in tiles(512):
        e8 = v8[h, r : r + 8]
        out[h, r : r + 8] = kept[h, r : r + 8] + e8
        v8[h, r : r + 8] = kept[h, 1024 + r : 1032 + r] + e8
    fine_front(v8, g8, acc2, bd, bdt)
    send_faces(acc2, even, face_a, face_b, 64)


def seventh_kernel(
    pos, kept, sol, acc, a, b, inv8, g8, bd, bdt, res, out, u, acc2, face_a, face_b
):
    even = is_even(pos, 0)
    for h, r in tiles(512):
        now = kept[h, 512 + r : 520 + r] - full_of(acc, (even, a, b), h, r)
        new = inv8[h, r : r + 8] * now * (1.0 / CENTER)
        res[h, r : r + 8] = now
        u[h, r : r + 8] = new
        out[h, r : r + 8] = sol[h, r : r + 8] + new
    fine_front(u, g8, acc2, bd, bdt)
    send_faces(acc2, even, face_a, face_b, 64)


def inner_last_kernel(u, g8, acc, res, sol, inv8, bd, bdt, out, full):
    for h, r in tiles(384):
        full[h, 64 + r : 72 + r] = acc[h, 64 + r : 72 + r]
    fine_cross(u, g8, full, bd, bdt, PLANES[1:])
    join_fine(full, range(1, 7))
    for r in range(64, 448, 8):
        halves = []
        for h in range(2):
            now = res[h, r : r + 8] - full[h, r : r + 8]
            new = KEEP * u[h, r : r + 8] + GAIN * inv8[h, r : r + 8] * now
            halves.append(sol[h, r : r + 8] + new)
        out[r - 64 : r - 56] = own_part(*halves)


def last_kernel(pos, res, sol, u, acc, a, b, inv8, inner, out):
    got = (is_even(pos, 0), a, b)
    out[64:448] = inner[...]
    for r in [*range(0, 64, 8), *range(448, 512, 8)]:
        halves = []
        for h in range(2):
            now = res[h, r : r + 8] - full_of(acc, got, h, r)
            new = KEEP * u[h, r : r + 8] + GAIN * inv8[h, r : r + 8] * now
            halves.append(sol[h, r : r + 8] + new)
        out[r : r + 8] = own_part(*halves)


def call(kernel, args, outs, scratch=(), scalars=1, unread=0, **options):
    vmem = pl.BlockSpec(memory_space=pltpu.VMEM)
    smem = pl.BlockSpec(memory_space=pltpu.SMEM)
    arrays = [x for x in args if not isinstance(x, str)]
    named = len(arrays) < len(args)

    def body(*refs):
        rest = iter(refs)
        given = [next(rest) for _ in arrays[: len(arrays) - named]]
        held = next(rest) if named else None
        given = iter(given)
        full = [Constant(held, x) if isinstance(x, str) else next(given) for x in args]
        kernel(*full, *rest)

    if named:
        arrays.append(PACK)
    return pl.pallas_call(
        body,
        out_shape=[jax.ShapeDtypeStruct(s, F32) for s in outs],
        in_specs=[smem] * scalars
        + [vmem] * (len(arrays) - scalars - unread)
        + [pl.BlockSpec(memory_space=pl.ANY)] * unread,
        out_specs=[vmem] * len(outs),
        scratch_shapes=[pltpu.VMEM(s, F32) for s in scratch],
        compiler_params=pltpu.CompilerParams(vmem_limit_bytes=32 * 1024 * 1024),
        name=kernel.__name__,
        **options,
    )(*arrays)


def exchange(far, near, axis):
    size = lax.axis_size(axis)
    pairs_far = [(i, (i + 1 if i % 2 else i - 1) % size) for i in range(size)]
    pairs_near = [(i, i ^ 1) for i in range(size)]
    return lax.ppermute(far, axis, pairs_far), lax.ppermute(near, axis, pairs_near)


def spread(x, axis, groups=None):
    size = len(groups[0]) if groups else lax.axis_size(axis)
    copies = jnp.broadcast_to(x[None], (size,) + x.shape)
    return lax.all_to_all(copies, axis, 0, 0, axis_index_groups=groups).reshape(-1, LANES)


def on_device(element_load, metric, element_order):
    ns, na = lax.axis_size("stream"), lax.axis_size("azim")
    fine, mid = (2, 512, LANES), (2, 64, LANES)
    face8, face4 = [(2, 64, LANES)] * 2, [(2, 16, LANES)] * 2
    pos = jnp.stack([lax.axis_index("stream"), lax.axis_index("azim")]).astype(jnp.int32)
    g, rolled, a, b = call(
        order_kernel,
        (pos, metric.reshape(1536, LANES), element_load.reshape(512, LANES), element_order),
        [(1536, LANES), (512, LANES), (1024, LANES), (1024, LANES)],
    )
    a, b = exchange(a, b, "azim")
    (diag,) = call(own_kernel, (g, "bsq"), [(512, LANES)], scalars=0)

    def inner(u, acc):
        (acc,) = call(inner_kernel, (u, g8, acc, "bd", "bdt"), [fine], (), 0)
        return acc

    g8, load, diag8, a, b = call(
        setup_kernel,
        (pos, g, rolled, diag, a, b, "bsq"),
        [(2, 1536, LANES), fine, fine] + [(2, 128, LANES)] * 2,
        [(1536, LANES), (512, LANES)],
    )
    a, b = exchange(a, b, "stream")
    res8, inv8, u8, acc, a, b = call(
        first_kernel,
        (pos, load, diag8, a, b, g8, "bd", "bdt"),
        [fine, fine, fine, fine] + face8,
    )
    a, b = exchange(a, b, "stream")
    acc = inner(u8, acc)
    g4, diag4, edges, upper = call(
        coarsen_kernel,
        (g8, "w4", "w2", "sample", "sq4"),
        [(2, 192, LANES), mid, (8, LANES), (8, LANES)],
        scalars=0,
    )
    kept, t4, a, b = call(
        second_kernel,
        (pos, res8, inv8, acc, a, b, diag4, upper, g8, "bd", "bdt", "down8"),
        [(2, 1536, LANES), mid] + [(2, 40, LANES)] * 2,
        [fine, fine, (512, 2 * LANES)],
    )
    a, b = exchange(a, b, "stream")
    res4, inv4, edges, acc, a, b = call(
        third_kernel,
        (pos, t4, diag4, edges, a, b, g4, "gm", "gmt"),
        [mid, mid, (8, LANES), mid] + face4,
        [mid],
    )
    a, b = exchange(a, b, "stream")
    corners, *kept4 = call(
        fourth_kernel,
        (pos, res4, acc, inv4, edges, a, b, g4, "gm", "gmt", "m4", "down4"),
        [(8, LANES), (192, LANES), (192, LANES)],
        [(2, 192, LANES), mid],
    )
    columns = spread(corners, "stream")
    a, b = exchange(*kept4, "azim")
    wider, a, b = call(
        side_kernel,
        (pos, *kept4, a, b, g4, "gm", "gmt"),
        [(2, 192, LANES)] + [(2, 112, LANES)] * 2,
        [mid],
    )
    sides = exchange(a, b, "stream")
    size = 4 * ns + ns // groups(ns)
    (columns,) = call(
        column_kernel, (columns, wider), [(size, LANES)], (), 0, unread=1
    )
    cores = [list(range(core, na, 2)) for core in range(2)]
    columns = spread(columns, "azim", cores)
    (columns,) = call(pass_kernel, (columns, *sides), [columns.shape], (), 0, unread=2)
    others = lax.ppermute(columns, "azim", [(i, i ^ 1) for i in range(na)])
    whole = (ns, na * LANES)
    res4, u4, sol4, acc, a, b = call(
        coarse_kernel,
        (
            pos,
            columns,
            others,
            wider,
            *sides,
            g4,
            inv4,
            "gm",
            "gmt",
            "up4",
            "gm_first",
            "gmt_first",
            "gm_last",
            "gmt_last",
        ),
        [mid, mid, mid, mid] + face4,
        [(16, na * LANES)] + [whole] * 9,
    )
    a, b = exchange(a, b, "stream")
    sol8, v8, acc, a, b = call(
        sixth_kernel,
        (pos, res4, u4, sol4, acc, a, b, inv4, "up8", kept, g8, "bd", "bdt"),
        [fine, fine, fine] + face8,
        [mid],
    )
    a, b = exchange(a, b, "stream")
    acc = inner(v8, acc)
    res8, sol8, u8, acc, a, b = call(
        seventh_kernel,
        (pos, kept, sol8, acc, a, b, inv8, g8, "bd", "bdt"),
        [fine, fine, fine, fine] + face8,
    )
    a, b = exchange(a, b, "stream")
    (inside,) = call(
        inner_last_kernel,
        (u8, g8, acc, res8, sol8, inv8, "bd", "bdt"),
        [(384, LANES)],
        [fine],
        scalars=0,
    )
    (out,) = call(last_kernel, (pos, res8, sol8, u8, acc, a, b, inv8, inside), [(512, LANES)])
    return out.reshape(element_load.shape)


def solution(mesh):
    placed = (P(None, "stream", "azim"), P(None, None, "stream", "azim"), P("stream", "azim"))
    return jax.shard_map(
        on_device, mesh=mesh, in_specs=placed, out_specs=P(None, "stream", "azim"), check_vma=False
    )
```

```python
import jax
import jax.numpy as jnp
import numpy as np
from jax import lax
from jax.experimental import pallas as pl
from jax.experimental.pallas import tpu as pltpu
from jax.sharding import PartitionSpec as P

ITERS = 6
LOW_EIG = 0.3
HIGH_EIG = 3.0
CENTER = 0.5 * (HIGH_EIG + LOW_EIG)
HALF_WIDTH = 0.5 * (HIGH_EIG - LOW_EIG)
FIRST_RHO = HALF_WIDTH / CENTER
SECOND_RHO = 1.0 / (2.0 * CENTER / HALF_WIDTH - FIRST_RHO)
KEEP = SECOND_RHO * FIRST_RHO
GAIN = 2.0 * SECOND_RHO / HALF_WIDTH
LANES = 128
HALF = 64
F32 = jnp.float32


def legendre_pair(degree, places):
    previous = places * 0.0 + 1.0
    current = places.copy()
    for k in range(2, degree + 1):
        following = ((2 * k - 1) * places * current - (k - 1) * previous) / k
        previous = current
        current = following
    return (current, previous)


def gll_table(points):
    degree = points - 1
    places = np.cos(np.pi * np.arange(points) / degree)
    for _ in range(60):
        top, below = legendre_pair(degree, places)
        places = places - (places * top - below) / (points * top)
    nodes = np.sort(places)
    nodes[0] = -1.0
    nodes[-1] = 1.0
    at_nodes = legendre_pair(degree, nodes)[0]
    weights = 2.0 / (degree * (degree + 1) * at_nodes**2)
    deriv = np.zeros((points, points))
    for i in range(points):
        for j in range(points):
            if i != j:
                deriv[i, j] = at_nodes[i] / (at_nodes[j] * (nodes[i] - nodes[j]))
    deriv[0, 0] = -degree * (degree + 1) / 4.0
    deriv[-1, -1] = degree * (degree + 1) / 4.0
    return (nodes, weights, deriv)


def lagrange_table(source, target):
    out = np.ones((len(target), len(source)))
    for j in range(len(source)):
        for k in range(len(source)):
            if k != j:
                out[:, j] *= (target - source[k]) / (source[j] - source[k])
    return out


N8, W8, D8 = gll_table(8)
N4, W4, D4 = gll_table(4)
N2, W2, D2 = gll_table(2)


def kron3(a, b, c):
    return np.kron(np.kron(a, b), c)


def cube(w):
    return (w[:, None, None] * w[None, :, None] * w[None, None, :]).reshape(-1)


def share(n):
    edge = np.ones(n)
    edge[0] = edge[-1] = 0.5
    return cube(edge)


def grads(d):
    i = np.eye(d.shape[0])
    return [kron3(d, i, i), kron3(i, d, i), kron3(i, i, d)]


def f32(x):
    return np.asarray(x, np.float32)


def lanes_of(column):
    return np.repeat(f32(column)[:, None], LANES, axis=1)


UP8 = lagrange_table(N4, N8)
UP4 = lagrange_table(N2, N4)
TO4 = lagrange_table(N8, N4)
TO2 = lagrange_table(N8, N2)

C_BD = f32(np.kron(np.eye(16), D8))
C_BDT = f32(np.kron(np.eye(16), D8.T))
C_BSQ = f32(np.kron(np.eye(16), (D8 * D8).T))
C_SAMPLE = f32(np.concatenate([kron3(TO4, TO4, TO4), kron3(TO2, TO2, TO2)]))
C_UP8 = f32(kron3(UP8, UP8, UP8))
C_DOWN8 = f32(kron3(UP8, UP8, UP8).T)
C_UP4 = f32(kron3(UP4, UP4, UP4))
C_DOWN4 = f32(kron3(UP4, UP4, UP4).T)
C_UP4X3 = np.zeros((192, 16), np.float32)
for layer in range(3):
    C_UP4X3[64 * layer : 64 * layer + 64, 4 * layer : 4 * layer + 8] = C_UP4
C_G4 = f32(np.concatenate(grads(D4)))
C_G4T = f32(np.concatenate(grads(D4)).T)
C_SQ4 = f32((np.concatenate(grads(D4)) ** 2).T)
C_W4 = lanes_of(cube(W4) / np.exp(kron3(TO4, TO4, TO4) @ np.log(cube(W8))))
C_W2 = lanes_of(cube(W2) / np.exp(kron3(TO2, TO2, TO2) @ np.log(cube(W8))))
C_M4 = lanes_of(share(4))
FIRST = np.r_[0:64, 64:80, 128:144]
LAST = np.r_[0:64, 112:128, 176:192]
CONSTANTS = {
    "bd": C_BD, "bdt": C_BDT, "bsq": C_BSQ, "sample": C_SAMPLE, "w4": C_W4, "w2": C_W2,
    "sq4": C_SQ4, "gm": C_G4, "gmt": C_G4T, "m4": C_M4, "down8": C_DOWN8, "down4": C_DOWN4,
    "up4": C_UP4X3, "up8": C_UP8, "gm_first": C_G4[FIRST], "gmt_first": C_G4T[:16, FIRST],
    "gm_last": C_G4[LAST], "gmt_last": C_G4T[48:, LAST],
}


def pack_constants():
    rows, places, start = [], {}, 0
    for name, value in CONSTANTS.items():
        blocks = -(-value.shape[1] // LANES)
        padded = np.zeros((value.shape[0], blocks * LANES), np.float32)
        padded[:, : value.shape[1]] = value
        rows += [padded[:, k * LANES : (k + 1) * LANES] for k in range(blocks)]
        places[name] = (start, value.shape, blocks)
        start += value.shape[0] * blocks
    return np.concatenate(rows), places


PACK, PLACES = pack_constants()


class Constant:
    def __init__(self, ref, name):
        self.ref, self.name = ref, name

    def __getitem__(self, index):
        start, (rows, columns), blocks = PLACES[self.name]
        parts = []
        for k in range(blocks):
            width = min(LANES, columns - k * LANES)
            parts.append(self.ref[start + k * rows : start + (k + 1) * rows, :width])
        value = parts[0] if blocks == 1 else jnp.concatenate(parts, axis=1)
        return value if index is Ellipsis else value[index]


def dot(a, b):
    return jnp.dot(a, b, preferred_element_type=F32, precision=lax.Precision.HIGHEST)


def iota(rows, axis):
    return lax.broadcasted_iota(jnp.int32, (rows, LANES), axis)


def wide(ref, start, size):
    return jnp.concatenate([ref[0, start : start + size], ref[1, start : start + size]], axis=1)


def put(ref, start, size, value):
    ref[0, start : start + size] = value[:, :LANES]
    ref[1, start : start + size] = value[:, LANES:]


def total(terms):
    out = terms[0]
    for t in terms[1:]:
        out = out + t
    return out


def contract(v, matrix, sign):
    n = len(v)
    h = n // 2
    even = [v[k] + v[n - 1 - k] for k in range(h)]
    odd = [v[k] - v[n - 1 - k] for k in range(h)]
    out = [None] * n
    for i in range(h):
        p = total([even[k] * float(0.5 * (matrix[i, k] + matrix[i, n - 1 - k])) for k in range(h)])
        q = total([odd[k] * float(0.5 * (matrix[i, k] - matrix[i, n - 1 - k])) for k in range(h)])
        out[i] = p + q
        out[n - 1 - i] = q - p if sign < 0 else p - q
    return out


def fine_rows(s, a):
    return s * 64 + a * 8


PLANES = [(0, 7), (1, 2), (3, 4), (5, 6)]


def pair(ref, p, base=0):
    return jnp.concatenate([wide(ref, base + 64 * s, 64) for s in p], axis=0)


def put_pair(ref, p, value):
    for k, s in enumerate(p):
        put(ref, 64 * s, 64, value[64 * k : 64 * k + 64])


def fine_stream(u, g, acc):
    for h in range(2):
        for a in range(8):
            at = [fine_rows(s, a) for s in range(8)]
            grad = contract([u[h, r : r + 8] for r in at], D8, -1)
            back = contract([grad[s] * g[h, r : r + 8] for s, r in enumerate(at)], D8.T, -1)
            for s, r in enumerate(at):
                acc[h, r : r + 8] = back[s]


def fine_cross(u, g, acc, bd, bdt, pairs):
    for p in pairs:
        flux = dot(bd[...], pair(u, p)) * pair(g, p, 1024)
        put_pair(acc, p, pair(acc, p) + dot(bdt[...], flux))
        for s in p:
            for h in range(2):
                at = [fine_rows(s, a) for a in range(8)]
                grad = contract([u[h, r : r + 8] for r in at], D8, -1)
                flux = [grad[a] * g[h, 512 + r : 520 + r] for a, r in enumerate(at)]
                back = contract(flux, D8.T, -1)
                for a, r in enumerate(at):
                    acc[h, r : r + 8] += back[a]


def fine_apply(u, g, acc, bd, bdt):
    fine_stream(u, g, acc)
    fine_cross(u, g, acc, bd, bdt, PLANES)


def fine_front(u, g, acc, bd, bdt):
    fine_stream(u, g, acc)
    fine_cross(u, g, acc, bd, bdt, PLANES[:1])
    join_fine(acc, (0, 7))


def left(x0, x1):
    near = iota(x0.shape[0], 1) < LANES - 16
    y0, y1 = pltpu.roll(x0, LANES - 16, 1), pltpu.roll(x1, LANES - 16, 1)
    return jnp.where(near, y0, y1), jnp.where(near, y1, y0)


def right(x0, x1):
    near = iota(x0.shape[0], 1) >= 16
    y0, y1 = pltpu.roll(x0, 16, 1), pltpu.roll(x1, 16, 1)
    return jnp.where(near, y0, y1), jnp.where(near, y1, y0)


def join_radial(x, points, start, rows):
    place = iota(rows, 1) % 16
    first = pl.ds(start, rows, stride=points)
    last = pl.ds(start + points - 1, rows, stride=points)
    for h in range(2):
        view = x.at[h]
        low, high = view[first, :], view[last, :]
        view[first, :] = jnp.where(place == 0, 0.0, low + pltpu.roll(high, 1, 1))
        view[last, :] = jnp.where(place == 15, 0.0, high + pltpu.roll(low, LANES - 1, 1))


def join_fine(x, planes=range(8)):
    for s in planes:
        join_radial(x, 8, 64 * s, 8)
        lo, hi = fine_rows(s, 0), fine_rows(s, 7)
        low = [x[h, lo : lo + 8] for h in range(2)]
        high = [x[h, hi : hi + 8] for h in range(2)]
        to_low, to_high = right(*high), left(*low)
        for h in range(2):
            x[h, lo : lo + 8] = low[h] + to_low[h]
            x[h, hi : hi + 8] = high[h] + to_high[h]


def join_mid(x):
    join_radial(x, 4, 0, 16)
    first = iota(8, 0) < 4
    for s in range(4):
        lo, hi = s * 16, s * 16 + 8
        low = [x[h, lo : lo + 8] for h in range(2)]
        high = [x[h, hi : hi + 8] for h in range(2)]
        to_low = right(*[pltpu.roll(t, 4, 0) for t in high])
        to_high = left(*[pltpu.roll(t, 4, 0) for t in low])
        for h in range(2):
            x[h, lo : lo + 8] = low[h] + jnp.where(first, to_low[h], 0.0)
            x[h, hi : hi + 8] = high[h] + jnp.where(first, 0.0, to_high[h])


def is_even(place, k):
    return lax.rem(place[k], 2) == 0


def full_of(x, faces, h, r, offset=0):
    even, far, near = faces
    rows = x.shape[1]
    plane = {512: 64, 64: 16}[rows]
    value = x[h, r : r + 8]
    if r < plane:
        at = offset + r
        return value + jnp.where(even, far[h, at : at + 8], near[h, at : at + 8])
    if r >= rows - plane:
        at = offset + r - (rows - plane)
        return value + jnp.where(even, near[h, at : at + 8], far[h, at : at + 8])
    return value


def send_faces(x, even, far, near, plane, offset=0):
    rows = x.shape[1]
    last = rows - plane
    one = pl.multiple_of(jnp.where(even, last, 0), 8)
    two = pl.multiple_of(jnp.where(even, 0, last), 8)
    for h in range(2):
        near[h, offset : offset + plane] = x[h, pl.ds(one, plane), :]
        far[h, offset : offset + plane] = x[h, pl.ds(two, plane), :]


def wall_mask(points):
    place, node = iota(8, 1) % 16, iota(8, 0) % points
    return ((node == 0) & (place == 0)) | ((node == points - 1) & (place == 15))


def own_part(half0, half1):
    near = iota(half0.shape[0], 1) < HALF
    return pltpu.roll(jnp.where(near, half1, half0), HALF, 1)


def tiles(rows):
    return [(h, r) for h in range(2) for r in range(0, rows, 8)]


def mid_apply(u, g4, acc, gm, gmt):
    flux = dot(gm[...], wide(u, 0, 64)) * wide(g4, 0, 192)
    put(acc, 0, 64, dot(gmt[...], flux))


def fine_diagonal(g, diag, bsq):
    square = (D8 * D8).T
    for c in range(4):
        rows = slice(128 * c, 128 * c + 128)
        diag[rows] = dot(bsq[...], g[1024 + 128 * c : 1152 + 128 * c])
    for axis in range(2):
        for fixed in range(8):
            at = [fine_rows(k, fixed) if axis == 0 else fine_rows(fixed, k) for k in range(8)]
            back = contract([g[512 * axis + r : 512 * axis + r + 8] for r in at], square, 1)
            for k, r in enumerate(at):
                diag[r : r + 8] += back[k]


def halves_up_down(a, b):
    near = iota(8, 1) < HALF
    up = jnp.where(near, a, pltpu.roll(b, HALF, 1))
    return up, jnp.where(near, pltpu.roll(a, HALF, 1), b)


def before_after(even, x, y):
    p, n = jnp.where(even, x, y), jnp.where(even, y, x)
    near = iota(8, 1) < HALF
    first = (jnp.where(near, p, 0.0), jnp.where(near, 0.0, pltpu.roll(n, HALF, 1)))
    second = (jnp.where(near, pltpu.roll(p, HALF, 1), 0.0), jnp.where(near, 0.0, n))
    return first, second


def order_kernel(pos, metric, load, order, g, rolled, far, near):
    even = is_even(pos, 1)
    slots = jnp.broadcast_to(pltpu.roll(order[...], HALF, 1), (8, LANES))
    wr = total([jnp.where(iota(8, 0) == k, float(W8[k]), 0.0) for k in range(8)])
    for r in range(0, 1536, 8):
        scale = wr * float(W8[(r % 512) // 64] * W8[(r // 8) % 8])
        g[r : r + 8] = jnp.take_along_axis(metric[r : r + 8], slots, axis=1) * scale
    for r in range(0, 512, 8):
        rolled[r : r + 8] = pltpu.roll(load[r : r + 8], HALF, 1)
    for r in range(0, 1024, 8):
        other = g[1024 + r : 1032 + r] if r < 512 else rolled[r - 512 : r - 504]
        up, down = halves_up_down(g[r : r + 8], other)
        far[r : r + 8] = jnp.where(even, down, up)
        near[r : r + 8] = jnp.where(even, up, down)


def own_kernel(g, bsq, diag):
    fine_diagonal(g, diag, bsq)


def setup_kernel(
    pos, g, rolled, diag, x, y, bsq, g8, load, diag8, face_a, face_b, ghost, ghost_diag
):
    near = iota(8, 1) < HALF
    even_a = is_even(pos, 1)

    def place(out, row, own, sides):
        out[0, row : row + 8] = jnp.where(near, sides[0], own)
        out[1, row : row + 8] = jnp.where(near, own, sides[1])

    for r in range(0, 1024, 8):
        first, second = before_after(even_a, x[r : r + 8], y[r : r + 8])
        place(g8, r, g[r : r + 8], first)
        ghost[r : r + 8] = first[0] + first[1]
        if r < 512:
            place(g8, 1024 + r, g[1024 + r : 1032 + r], second)
            ghost[1024 + r : 1032 + r] = second[0] + second[1]
        else:
            place(load, r - 512, rolled[r - 512 : r - 504], second)
    fine_diagonal(ghost, ghost_diag, bsq)
    for r in range(0, 512, 8):
        side = ghost_diag[r : r + 8]
        place(diag8, r, diag[r : r + 8], (side, side))
    for x in (load, diag8):
        join_fine(x)
    even = is_even(pos, 0)
    send_faces(load, even, face_a, face_b, 64)
    send_faces(diag8, even, face_a, face_b, 64, 64)


def coarsen_kernel(g8, w4, w2, sample, sq4, g4, diag4, edges, upper):
    low = []
    for d in range(3):
        coarse = jnp.exp(dot(sample[...], jnp.log(wide(g8, 512 * d, 512))))
        put(g4, 64 * d, 64, coarse[:64] * jnp.concatenate([w4[...], w4[...]], axis=1))
        low.append([coarse[64:72, :LANES] * w2[...], coarse[64:72, LANES:] * w2[...]])
    put(diag4, 0, 64, dot(sq4[...], wide(g4, 0, 192)))
    join_mid(diag4)

    def corner(d, i, j, k):
        row = 4 * i + 2 * j + k
        return [t[row : row + 1] for t in low[d]]

    def add(x, y):
        return [x[0] + y[0], x[1] + y[1]]

    def quarter(x):
        return [0.25 * x[0], 0.25 * x[1]]

    def outward(x):
        return [pltpu.roll(x[0], 1, 1), pltpu.roll(x[1], 1, 1)]

    es = [[quarter(add(corner(0, 0, j, k), corner(0, 1, j, k))) for k in range(2)] for j in range(2)]
    ea = [[quarter(add(corner(1, i, 0, k), corner(1, i, 1, k))) for k in range(2)] for i in range(2)]
    er = [[quarter(add(corner(2, i, j, 0), corner(2, i, j, 1))) for j in range(2)] for i in range(2)]
    col = [add(es[0][k], list(right(*es[1][k]))) for k in range(2)]
    edge_s = add(col[0], outward(col[1]))
    edge_a = [add(ea[i][0], outward(ea[i][1])) for i in range(2)]
    edge_r = [add(er[i][0], list(right(*er[i][1]))) for i in range(2)]
    off_wall = iota(1, 1) % 16 != 0
    rows = [jnp.where(off_wall, own_part(*x), 0.0) for x in (edge_s, edge_a[0], edge_a[1])]
    rows += [own_part(*x) for x in edge_r]
    none = jnp.zeros((5, LANES), F32)
    edges[...] = jnp.concatenate([rows[0], rows[1], rows[3], none], axis=0)
    upper[...] = jnp.concatenate([rows[0], rows[2], rows[4], none], axis=0)


def first_kernel(
    pos, load, diag8, a, b, g8, bd, bdt, res, inv8, u, acc, face_a, face_b
):
    even = is_even(pos, 0)
    got = (even, a, b)
    wall8 = wall_mask(8)
    for h, r in tiles(512):
        diag = full_of(diag8, got, h, r, 64)
        inv = jnp.where(wall8, 0.0, 1.0 / jnp.where(wall8, 1.0, diag))
        full = full_of(load, got, h, r)
        res[h, r : r + 8] = full
        inv8[h, r : r + 8] = inv
        u[h, r : r + 8] = inv * full * (1.0 / CENTER)
    fine_front(u, g8, acc, bd, bdt)
    send_faces(acc, even, face_a, face_b, 64)


def inner_kernel(u, g8, start, bd, bdt, acc):
    for h, r in tiles(512):
        acc[h, r : r + 8] = start[h, r : r + 8]
    fine_cross(u, g8, acc, bd, bdt, PLANES[1:])
    join_fine(acc, range(1, 7))


def second_kernel(
    pos, res, inv8, acc, a, b, diag4, upper, g8, bd, bdt, down8,
    kept, t4, face_a, face_b, u, back, part,
):
    even = is_even(pos, 0)
    got = (even, a, b)
    edge = jnp.where((iota(8, 0) == 0) | (iota(8, 0) == 7), 0.5, 1.0)
    for h, r in tiles(512):
        inv, before = inv8[h, r : r + 8], res[h, r : r + 8]
        now = before - full_of(acc, got, h, r)
        old = inv * before * (1.0 / CENTER)
        new = KEEP * old + GAIN * inv * now
        kept[h, r : r + 8] = old + new
        kept[h, 512 + r : 520 + r] = now
        kept[h, 1024 + r : 1032 + r] = new
        u[h, r : r + 8] = new
    fine_apply(u, g8, back, bd, bdt)
    for h, r in tiles(512):
        s, c = r // 64, (r // 8) % 8
        scale = (0.5 if s in (0, 7) else 1.0) * (0.5 if c in (0, 7) else 1.0)
        part[r : r + 8, h * LANES : h * LANES + LANES] = (
            kept[h, 512 + r : 520 + r] * (edge * scale) - back[h, r : r + 8]
        )
    put(t4, 0, 64, dot(down8[...], part[...]))
    join_mid(t4)
    send_faces(t4, even, face_a, face_b, 16)
    send_faces(diag4, even, face_a, face_b, 16, 16)
    for face in (face_a, face_b):
        for h in range(2):
            face[h, 32:40] = upper[...]


def third_kernel(
    pos, t4, diag4, edges, a, b, g4, gm, gmt, res, inv4, edge, acc, face_a, face_b, u
):
    even = is_even(pos, 0)
    got = (even, a, b)
    wall = wall_mask(4)
    for h, r in tiles(64):
        full = full_of(t4, got, h, r)
        diag = full_of(diag4, got, h, r, 16)
        inv = jnp.where(wall, 0.0, 1.0 / jnp.where(wall, 1.0, diag))
        res[h, r : r + 8] = full
        inv4[h, r : r + 8] = inv
        u[h, r : r + 8] = inv * full * (1.0 / CENTER)
    lower = jnp.where(even, a[0, 32:40], b[0, 32:40])
    edge[...] = edges[...] + jnp.where(iota(8, 0) == 0, 0.0, lower)
    mid_apply(u, g4, acc, gm, gmt)
    join_mid(acc)
    send_faces(acc, even, face_a, face_b, 16)


def fourth_kernel(
    pos, res, acc, inv4, edge, a, b, g4, gm, gmt, m4, down4, corners, one, two, keep, part
):
    got = (is_even(pos, 0), a, b)
    for h, r in tiles(64):
        inv, before = inv4[h, r : r + 8], res[h, r : r + 8]
        now = before - full_of(acc, got, h, r)
        old = inv * before * (1.0 / CENTER)
        new = KEEP * old + GAIN * inv * now
        keep[h, r : r + 8] = now
        keep[h, 64 + r : 72 + r] = new
        keep[h, 128 + r : 136 + r] = old + new
    even_a = is_even(pos, 1)
    one[...] = jnp.where(even_a, keep[0], keep[1])
    two[...] = jnp.where(even_a, keep[1], keep[0])
    flux = dot(gm[...], wide(keep, 64, 64)) * wide(g4, 0, 192)
    put(part, 0, 64, dot(gmt[...], flux))
    for h, r in tiles(64):
        part[h, r : r + 8] = m4[r : r + 8] * keep[h, r : r + 8] - part[h, r : r + 8]
    low = dot(down4[...], wide(part, 0, 64))
    near = iota(8, 1) < HALF
    half0 = jnp.where(near, 0.0, low[:, :LANES])
    half1 = jnp.where(near, low[:, LANES:], 0.0)

    def corner(i, j, k):
        row = 4 * i + 2 * j + k
        return [half0[row : row + 1], half1[row : row + 1]]

    lane = iota(1, 1)
    mine, extra = [], []
    for i in range(2):
        columns = []
        for k in range(2):
            shifted = right(*corner(i, 1, k))
            straight = corner(i, 0, k)
            columns.append([straight[0] + shifted[0], straight[1] + shifted[1]])
        both = [columns[0][h] + pltpu.roll(columns[1][h], 1, 1) for h in range(2)]
        both = [jnp.where(lane % 16 == 0, 0.0, t) for t in both]
        mine.append(own_part(*both))
        extra.append(both[1])
    sides = jnp.where(lane < 16, pltpu.roll(extra[0], HALF, 1), 0.0) + jnp.where(
        (lane >= 16) & (lane < 32), pltpu.roll(extra[1], HALF + 16, 1), 0.0
    )
    none = jnp.zeros((2, LANES), F32)
    corners[...] = jnp.concatenate(mine + [sides, edge[0:3], none], axis=0)


def groups(ns):
    return max(1, ns // 8)


def side_kernel(pos, to_far, to_near, one, two, g4, gm, gmt, wider, far, near_side, back):
    near = iota(8, 1) < HALF
    even, even_a = is_even(pos, 0), is_even(pos, 1)
    for r in range(0, 192, 8):
        x, y = one[r : r + 8], two[r : r + 8]
        before, after = jnp.where(even_a, x, y), jnp.where(even_a, y, x)
        x, y = to_far[r : r + 8], to_near[r : r + 8]
        lower, upper = jnp.where(even_a, x, y), jnp.where(even_a, y, x)
        halves = (jnp.where(near, before, lower), jnp.where(near, upper, after))
        for h in range(2):
            wider[h, r : r + 8] = halves[h]
    flux = dot(gm[...], wide(wider, 64, 64)) * wide(g4, 0, 192)
    put(back, 0, 64, dot(gmt[...], flux))
    one = pl.multiple_of(jnp.where(even, 48, 0), 8)
    two = pl.multiple_of(jnp.where(even, 0, 48), 8)
    for out, plane in ((near_side, one), (far, two)):
        for h in range(2):
            out[h, 0:64] = g4[h, 0:64]
            out[h, 64:80] = g4[h, pl.ds(64 + plane, 16), :]
            out[h, 80:96] = g4[h, pl.ds(128 + plane, 16), :]
            out[h, 96:112] = back[h, pl.ds(plane, 16), :]


def column_kernel(rows, first, out):
    ns = rows.shape[0] // 8
    n = ns // groups(ns)

    def field(k):
        return rows[pl.ds(k, ns, stride=8), :]

    def later(x):
        return pltpu.roll(x, 1, 0)

    sides = field(2)
    over = jnp.where(iota(ns, 1) < 16, sides + later(pltpu.roll(sides, LANES - 16, 1)), 0.0)
    out[0:ns] = field(0) + later(field(1))
    for k in range(3):
        out[(1 + k) * ns : (2 + k) * ns] = field(3 + k)
    parts = [over[k * n : k * n + n] for k in range(groups(ns))]
    out[4 * ns : 4 * ns + n] = total(
        [pltpu.roll(p, 16 * k, 1) if k else p for k, p in enumerate(parts)]
    )


def pass_kernel(rows, first, second, out):
    out[...] = rows[...]


def coarse_kernel(
    pos, columns, others, wider, far, near_side, g4, inv4, gm, gmt, up4, gm_first, gmt_first,
    gm_last, gmt_last,
    res, u, sol, acc, face_a, face_b, vals, x2, es, ea, er, es0, ea0, er0, dg, ri,
):
    ns = x2.shape[0]
    na = x2.shape[1] // LANES
    width = na * LANES

    n = ns // groups(ns)
    size = 4 * ns + n
    even_a = is_even(pos, 1)

    def rows_of(d, start, count):
        at = d // 2 * size + start
        x, y = columns[at : at + count], others[at : at + count]
        return jnp.where(even_a, x, y) if d % 2 == 0 else jnp.where(even_a, y, x)

    def field(k):
        return [rows_of(d, k * ns, ns) for d in range(na)]

    def side(d):
        packed = rows_of(d, 4 * ns, n)
        parts = [pltpu.roll(packed, LANES - 16 * k, 1) if k else packed for k in range(groups(ns))]
        return jnp.where(iota(ns, 1) < 16, jnp.concatenate(parts, axis=0), 0.0)

    def roll_l(x, k):
        return pltpu.roll(x, k % width, 1)

    lane = iota(ns, 1)
    wall, top = lane % 16 == 0, lane % 16 == 15
    at = [slice(d * LANES, d * LANES + LANES) for d in range(na)]

    def towards_next(y, d):
        return jnp.where(lane < LANES - 16, y[d], y[(d + 1) % na])

    def towards_last(y, d):
        return jnp.where(lane < 16, y[d - 1], y[d])

    ea_all, er_all = field(2), field(3)
    ea_roll = [pltpu.roll(t, 16, 1) for t in ea_all]
    for d, es_d in enumerate(field(1)):
        es0_d, ea0_d = pltpu.roll(es_d, 1, 0), towards_last(ea_roll, d)
        er0_d = pltpu.roll(er_all[d], 1, 1)
        both = es_d + es0_d + ea_all[d] + ea0_d + er_all[d] + er0_d
        es[:, at[d]], ea[:, at[d]] = es_d, ea_all[d]
        es0[:, at[d]], ea0[:, at[d]] = es0_d, ea0_d
        er[:, at[d]] = jnp.where(wall | top, 0.0, er_all[d])
        er0[:, at[d]] = jnp.where(wall | (lane % 16 == 1), 0.0, er0_d)
        dg[:, at[d]] = jnp.where(wall, 0.0, both)
        ri[:, at[d]] = jnp.where(wall, 0.0, 1.0 / jnp.where(wall, 1.0, both))

    def inner(terms):
        return jnp.sum(jnp.sum(total(terms), axis=0, keepdims=True), axis=1, keepdims=True)

    first = field(0)
    r = [first[d] + side((d - 1) % na) for d in range(na)]
    p = [ri[:, at[d]] * r[d] for d in range(na)]
    gz = inner([r[d] * p[d] for d in range(na)])
    x = [jnp.zeros_like(t) for t in r]
    for it in range(ITERS):
        ahead = [pltpu.roll(t, LANES - 16, 1) for t in p]
        behind = [pltpu.roll(t, 16, 1) for t in p]
        q, terms = [], []
        for d in range(na):
            t, k = p[d], at[d]
            out = dg[:, k] * t
            out = out - es[:, k] * pltpu.roll(t, ns - 1, 0) - es0[:, k] * pltpu.roll(t, 1, 0)
            out = out - ea[:, k] * towards_next(ahead, d) - ea0[:, k] * towards_last(behind, d)
            out = out - er[:, k] * pltpu.roll(t, LANES - 1, 1) - er0[:, k] * pltpu.roll(t, 1, 1)
            q.append(out)
            terms.append(t * out)
        alpha = gz / inner(terms)
        x = [x[d] + alpha * p[d] for d in range(na)]
        if it + 1 < ITERS:
            r = [r[d] - alpha * q[d] for d in range(na)]
            z = [ri[:, at[d]] * r[d] for d in range(na)]
            new = inner([r[d] * z[d] for d in range(na)])
            beta = new / gz
            p = [z[d] + beta * p[d] for d in range(na)]
            gz = new
    for d in range(na):
        x2[:, at[d]] = x[d]

    s, a = pos[0], pos[1]
    blocks = [lax.rem(a + na - 1, na), a, lax.rem(a + 1, na)]
    for t in range(4):
        line = x2[pl.ds(lax.rem(s + ns - 1 + t, ns), 1), :]
        for j in range(2):
            for k in range(2):
                n = 4 * t + 2 * j + k
                vals[n : n + 1, :] = roll_l(line, -(16 * j + k)) if j + k else line
    near = iota(16, 1) < HALF
    b = [
        pltpu.roll(vals[:, pl.ds(pl.multiple_of(t * LANES, LANES), LANES)], HALF, 1) for t in blocks
    ]
    ext = jnp.concatenate([jnp.where(near, b[0], b[1]), jnp.where(near, b[1], b[2])], axis=1)
    rise = dot(up4[...], ext)
    even = is_even(pos, 0)
    x, y = wide(far, 0, 112), wide(near_side, 0, 112)
    below, above = jnp.where(even, x, y), jnp.where(even, y, x)
    low = dot(gmt_last[...], dot(gm_last[...], rise[:64]) * below[:96]) + below[96:]
    high = dot(gmt_first[...], dot(gm_first[...], rise[128:]) * above[:96]) + above[96:]
    flux = dot(gm[...], rise[64:128] + wide(wider, 64, 64)) * wide(g4, 0, 192)
    back = dot(gmt[...], flux)
    put(acc, 0, 16, back[:16] + low)
    put(acc, 16, 32, back[16:48])
    put(acc, 48, 16, back[48:] + high)
    join_mid(acc)
    put(sol, 0, 64, wide(wider, 128, 64) + rise[64:128])
    for h, r in tiles(64):
        now = wider[h, r : r + 8] - acc[h, r : r + 8]
        new = inv4[h, r : r + 8] * now * (1.0 / CENTER)
        res[h, r : r + 8] = now
        u[h, r : r + 8] = new
        sol[h, r : r + 8] += new
    mid_apply(u, g4, acc, gm, gmt)
    join_mid(acc)
    send_faces(acc, even, face_a, face_b, 16)


def sixth_kernel(
    pos, res, u, sol, acc, a, b, inv4, up8, kept, g8, bd, bdt,
    out, v8, acc2, face_a, face_b, y4,
):
    even = is_even(pos, 0)
    for h, r in tiles(64):
        now = res[h, r : r + 8] - full_of(acc, (even, a, b), h, r)
        new = KEEP * u[h, r : r + 8] + GAIN * inv4[h, r : r + 8] * now
        y4[h, r : r + 8] = sol[h, r : r + 8] + new
    put(v8, 0, 512, dot(up8[...], wide(y4, 0, 64)))
    for h, r in tiles(512):
        e8 = v8[h, r : r + 8]
        out[h, r : r + 8] = kept[h, r : r + 8] + e8
        v8[h, r : r + 8] = kept[h, 1024 + r : 1032 + r] + e8
    fine_front(v8, g8, acc2, bd, bdt)
    send_faces(acc2, even, face_a, face_b, 64)


def seventh_kernel(
    pos, kept, sol, acc, a, b, inv8, g8, bd, bdt, res, out, u, acc2, face_a, face_b
):
    even = is_even(pos, 0)
    for h, r in tiles(512):
        now = kept[h, 512 + r : 520 + r] - full_of(acc, (even, a, b), h, r)
        new = inv8[h, r : r + 8] * now * (1.0 / CENTER)
        res[h, r : r + 8] = now
        u[h, r : r + 8] = new
        out[h, r : r + 8] = sol[h, r : r + 8] + new
    fine_front(u, g8, acc2, bd, bdt)
    send_faces(acc2, even, face_a, face_b, 64)


def inner_last_kernel(u, g8, acc, res, sol, inv8, bd, bdt, out, full):
    for h, r in tiles(384):
        full[h, 64 + r : 72 + r] = acc[h, 64 + r : 72 + r]
    fine_cross(u, g8, full, bd, bdt, PLANES[1:])
    join_fine(full, range(1, 7))
    for r in range(64, 448, 8):
        halves = []
        for h in range(2):
            now = res[h, r : r + 8] - full[h, r : r + 8]
            new = KEEP * u[h, r : r + 8] + GAIN * inv8[h, r : r + 8] * now
            halves.append(sol[h, r : r + 8] + new)
        out[r - 64 : r - 56] = own_part(*halves)


def last_kernel(pos, res, sol, u, acc, a, b, inv8, inner, out):
    got = (is_even(pos, 0), a, b)
    out[64:448] = inner[...]
    for r in [*range(0, 64, 8), *range(448, 512, 8)]:
        halves = []
        for h in range(2):
            now = res[h, r : r + 8] - full_of(acc, got, h, r)
            new = KEEP * u[h, r : r + 8] + GAIN * inv8[h, r : r + 8] * now
            halves.append(sol[h, r : r + 8] + new)
        out[r : r + 8] = own_part(*halves)


def call(kernel, args, outs, scratch=(), scalars=1):
    vmem = pl.BlockSpec(memory_space=pltpu.VMEM)
    smem = pl.BlockSpec(memory_space=pltpu.SMEM)
    arrays = [x for x in args if not isinstance(x, str)]
    named = len(arrays) < len(args)

    def body(*refs):
        rest = iter(refs)
        given = [next(rest) for _ in arrays[: len(arrays) - named]]
        held = next(rest) if named else None
        given = iter(given)
        full = [Constant(held, x) if isinstance(x, str) else next(given) for x in args]
        kernel(*full, *rest)

    if named:
        arrays.append(PACK)
    return pl.pallas_call(
        body,
        out_shape=[jax.ShapeDtypeStruct(s, F32) for s in outs],
        in_specs=[smem] * scalars + [vmem] * (len(arrays) - scalars),
        out_specs=[vmem] * len(outs),
        scratch_shapes=[pltpu.VMEM(s, F32) for s in scratch],
        compiler_params=pltpu.CompilerParams(vmem_limit_bytes=32 * 1024 * 1024),
        name=kernel.__name__,
    )(*arrays)


def exchange(far, near, axis):
    size = lax.axis_size(axis)
    pairs_far = [(i, (i + 1 if i % 2 else i - 1) % size) for i in range(size)]
    pairs_near = [(i, i ^ 1) for i in range(size)]
    return lax.ppermute(far, axis, pairs_far), lax.ppermute(near, axis, pairs_near)


def spread(x, axis, groups=None):
    size = len(groups[0]) if groups else lax.axis_size(axis)
    copies = jnp.broadcast_to(x[None], (size,) + x.shape)
    return lax.all_to_all(copies, axis, 0, 0, axis_index_groups=groups).reshape(-1, LANES)


def on_device(element_load, metric, element_order):
    ns, na = lax.axis_size("stream"), lax.axis_size("azim")
    fine, mid = (2, 512, LANES), (2, 64, LANES)
    face8, face4 = [(2, 64, LANES)] * 2, [(2, 16, LANES)] * 2
    pos = jnp.stack([lax.axis_index("stream"), lax.axis_index("azim")]).astype(jnp.int32)
    g, rolled, a, b = call(
        order_kernel,
        (pos, metric.reshape(1536, LANES), element_load.reshape(512, LANES), element_order),
        [(1536, LANES), (512, LANES), (1024, LANES), (1024, LANES)],
    )
    a, b = exchange(a, b, "azim")
    (diag,) = call(own_kernel, (g, "bsq"), [(512, LANES)], scalars=0)

    def inner(u, acc):
        (acc,) = call(inner_kernel, (u, g8, acc, "bd", "bdt"), [fine], (), 0)
        return acc

    g8, load, diag8, a, b = call(
        setup_kernel,
        (pos, g, rolled, diag, a, b, "bsq"),
        [(2, 1536, LANES), fine, fine] + [(2, 128, LANES)] * 2,
        [(1536, LANES), (512, LANES)],
    )
    a, b = exchange(a, b, "stream")
    res8, inv8, u8, acc, a, b = call(
        first_kernel,
        (pos, load, diag8, a, b, g8, "bd", "bdt"),
        [fine, fine, fine, fine] + face8,
    )
    a, b = exchange(a, b, "stream")
    acc = inner(u8, acc)
    g4, diag4, edges, upper = call(
        coarsen_kernel,
        (g8, "w4", "w2", "sample", "sq4"),
        [(2, 192, LANES), mid, (8, LANES), (8, LANES)],
        scalars=0,
    )
    kept, t4, a, b = call(
        second_kernel,
        (pos, res8, inv8, acc, a, b, diag4, upper, g8, "bd", "bdt", "down8"),
        [(2, 1536, LANES), mid] + [(2, 40, LANES)] * 2,
        [fine, fine, (512, 2 * LANES)],
    )
    a, b = exchange(a, b, "stream")
    res4, inv4, edges, acc, a, b = call(
        third_kernel,
        (pos, t4, diag4, edges, a, b, g4, "gm", "gmt"),
        [mid, mid, (8, LANES), mid] + face4,
        [mid],
    )
    a, b = exchange(a, b, "stream")
    corners, *kept4 = call(
        fourth_kernel,
        (pos, res4, acc, inv4, edges, a, b, g4, "gm", "gmt", "m4", "down4"),
        [(8, LANES), (192, LANES), (192, LANES)],
        [(2, 192, LANES), mid],
    )
    columns = spread(corners, "stream")
    a, b = exchange(*kept4, "azim")
    wider, a, b = call(
        side_kernel,
        (pos, *kept4, a, b, g4, "gm", "gmt"),
        [(2, 192, LANES)] + [(2, 112, LANES)] * 2,
        [mid],
    )
    sides = exchange(a, b, "stream")
    size = 4 * ns + ns // groups(ns)
    (columns,) = call(
        column_kernel, (columns, wider), [(size, LANES)], (), 0
    )
    cores = [list(range(core, na, 2)) for core in range(2)]
    columns = spread(columns, "azim", cores)
    (columns,) = call(pass_kernel, (columns, *sides), [columns.shape], (), 0)
    others = lax.ppermute(columns, "azim", [(i, i ^ 1) for i in range(na)])
    whole = (ns, na * LANES)
    res4, u4, sol4, acc, a, b = call(
        coarse_kernel,
        (
            pos,
            columns,
            others,
            wider,
            *sides,
            g4,
            inv4,
            "gm",
            "gmt",
            "up4",
            "gm_first",
            "gmt_first",
            "gm_last",
            "gmt_last",
        ),
        [mid, mid, mid, mid] + face4,
        [(16, na * LANES)] + [whole] * 9,
    )
    a, b = exchange(a, b, "stream")
    sol8, v8, acc, a, b = call(
        sixth_kernel,
        (pos, res4, u4, sol4, acc, a, b, inv4, "up8", kept, g8, "bd", "bdt"),
        [fine, fine, fine] + face8,
        [mid],
    )
    a, b = exchange(a, b, "stream")
    acc = inner(v8, acc)
    res8, sol8, u8, acc, a, b = call(
        seventh_kernel,
        (pos, kept, sol8, acc, a, b, inv8, g8, "bd", "bdt"),
        [fine, fine, fine, fine] + face8,
    )
    a, b = exchange(a, b, "stream")
    (inside,) = call(
        inner_last_kernel,
        (u8, g8, acc, res8, sol8, inv8, "bd", "bdt"),
        [(384, LANES)],
        [fine],
        scalars=0,
    )
    (out,) = call(last_kernel, (pos, res8, sol8, u8, acc, a, b, inv8, inside), [(512, LANES)])
    return out.reshape(element_load.shape)


def solution(mesh):
    placed = (P(None, "stream", "azim"), P(None, None, "stream", "azim"), P("stream", "azim"))
    return jax.shard_map(
        on_device, mesh=mesh, in_specs=placed, out_specs=P(None, "stream", "azim"), check_vma=False
    )
```

```python
import jax
import jax.numpy as jnp
import numpy as np
from jax import lax
from jax.experimental import pallas as pl
from jax.experimental.pallas import tpu as pltpu
from jax.sharding import PartitionSpec as P

ITERS = 6
LOW_EIG = 0.3
HIGH_EIG = 3.0
CENTER = 0.5 * (HIGH_EIG + LOW_EIG)
HALF_WIDTH = 0.5 * (HIGH_EIG - LOW_EIG)
FIRST_RHO = HALF_WIDTH / CENTER
SECOND_RHO = 1.0 / (2.0 * CENTER / HALF_WIDTH - FIRST_RHO)
KEEP = SECOND_RHO * FIRST_RHO
GAIN = 2.0 * SECOND_RHO / HALF_WIDTH
LANES = 128
HALF = 64
F32 = jnp.float32


def legendre_pair(degree, places):
    previous = places * 0.0 + 1.0
    current = places.copy()
    for k in range(2, degree + 1):
        following = ((2 * k - 1) * places * current - (k - 1) * previous) / k
        previous = current
        current = following
    return (current, previous)


def gll_table(points):
    degree = points - 1
    places = np.cos(np.pi * np.arange(points) / degree)
    for _ in range(60):
        top, below = legendre_pair(degree, places)
        places = places - (places * top - below) / (points * top)
    nodes = np.sort(places)
    nodes[0] = -1.0
    nodes[-1] = 1.0
    at_nodes = legendre_pair(degree, nodes)[0]
    weights = 2.0 / (degree * (degree + 1) * at_nodes**2)
    deriv = np.zeros((points, points))
    for i in range(points):
        for j in range(points):
            if i != j:
                deriv[i, j] = at_nodes[i] / (at_nodes[j] * (nodes[i] - nodes[j]))
    deriv[0, 0] = -degree * (degree + 1) / 4.0
    deriv[-1, -1] = degree * (degree + 1) / 4.0
    return (nodes, weights, deriv)


def lagrange_table(source, target):
    out = np.ones((len(target), len(source)))
    for j in range(len(source)):
        for k in range(len(source)):
            if k != j:
                out[:, j] *= (target - source[k]) / (source[j] - source[k])
    return out


N8, W8, D8 = gll_table(8)
N4, W4, D4 = gll_table(4)
N2, W2, D2 = gll_table(2)


def kron3(a, b, c):
    return np.kron(np.kron(a, b), c)


def cube(w):
    return (w[:, None, None] * w[None, :, None] * w[None, None, :]).reshape(-1)


def share(n):
    edge = np.ones(n)
    edge[0] = edge[-1] = 0.5
    return cube(edge)


def grads(d):
    i = np.eye(d.shape[0])
    return [kron3(d, i, i), kron3(i, d, i), kron3(i, i, d)]


def f32(x):
    return np.asarray(x, np.float32)


def lanes_of(column):
    return np.repeat(f32(column)[:, None], LANES, axis=1)


UP8 = lagrange_table(N4, N8)
UP4 = lagrange_table(N2, N4)
TO4 = lagrange_table(N8, N4)
TO2 = lagrange_table(N8, N2)

C_BD = f32(np.kron(np.eye(16), D8))
C_BDT = f32(np.kron(np.eye(16), D8.T))
C_BSQ = f32(np.kron(np.eye(16), (D8 * D8).T))
C_SAMPLE = f32(np.concatenate([kron3(TO4, TO4, TO4), kron3(TO2, TO2, TO2)]))
C_UP8 = f32(kron3(UP8, UP8, UP8))
C_DOWN8 = f32(kron3(UP8, UP8, UP8).T)
C_UP4 = f32(kron3(UP4, UP4, UP4))
C_DOWN4 = f32(kron3(UP4, UP4, UP4).T)
C_UP4X3 = np.zeros((192, 16), np.float32)
for layer in range(3):
    C_UP4X3[64 * layer : 64 * layer + 64, 4 * layer : 4 * layer + 8] = C_UP4
C_G4 = f32(np.concatenate(grads(D4)))
C_G4T = f32(np.concatenate(grads(D4)).T)
C_SQ4 = f32((np.concatenate(grads(D4)) ** 2).T)
C_W4 = lanes_of(cube(W4) / np.exp(kron3(TO4, TO4, TO4) @ np.log(cube(W8))))
C_W2 = lanes_of(cube(W2) / np.exp(kron3(TO2, TO2, TO2) @ np.log(cube(W8))))
C_M4 = lanes_of(share(4))
FIRST = np.r_[0:64, 64:80, 128:144]
LAST = np.r_[0:64, 112:128, 176:192]
CONSTANTS = {
    "bd": C_BD, "bdt": C_BDT, "bsq": C_BSQ, "sample": C_SAMPLE, "w4": C_W4, "w2": C_W2,
    "sq4": C_SQ4, "gm": C_G4, "gmt": C_G4T, "m4": C_M4, "down8": C_DOWN8, "down4": C_DOWN4,
    "up4": C_UP4X3, "up8": C_UP8, "gm_first": C_G4[FIRST], "gmt_first": C_G4T[:16, FIRST],
    "gm_last": C_G4[LAST], "gmt_last": C_G4T[48:, LAST],
}


def pack_constants():
    rows, places, start = [], {}, 0
    for name, value in CONSTANTS.items():
        blocks = -(-value.shape[1] // LANES)
        padded = np.zeros((value.shape[0], blocks * LANES), np.float32)
        padded[:, : value.shape[1]] = value
        rows += [padded[:, k * LANES : (k + 1) * LANES] for k in range(blocks)]
        places[name] = (start, value.shape, blocks)
        start += value.shape[0] * blocks
    return np.concatenate(rows), places


PACK, PLACES = pack_constants()


class Constant:
    def __init__(self, ref, name):
        self.ref, self.name = ref, name

    def __getitem__(self, index):
        start, (rows, columns), blocks = PLACES[self.name]
        parts = []
        for k in range(blocks):
            width = min(LANES, columns - k * LANES)
            parts.append(self.ref[start + k * rows : start + (k + 1) * rows, :width])
        value = parts[0] if blocks == 1 else jnp.concatenate(parts, axis=1)
        return value if index is Ellipsis else value[index]


def dot(a, b, precision=lax.Precision.HIGH):
    return jnp.dot(a, b, preferred_element_type=F32, precision=precision)


def iota(rows, axis):
    return lax.broadcasted_iota(jnp.int32, (rows, LANES), axis)


def wide(ref, start, size):
    return jnp.concatenate([ref[0, start : start + size], ref[1, start : start + size]], axis=1)


def put(ref, start, size, value):
    ref[0, start : start + size] = value[:, :LANES]
    ref[1, start : start + size] = value[:, LANES:]


def total(terms):
    out = terms[0]
    for t in terms[1:]:
        out = out + t
    return out


def contract(v, matrix, sign):
    n = len(v)
    h = n // 2
    even = [v[k] + v[n - 1 - k] for k in range(h)]
    odd = [v[k] - v[n - 1 - k] for k in range(h)]
    out = [None] * n
    for i in range(h):
        p = total([even[k] * float(0.5 * (matrix[i, k] + matrix[i, n - 1 - k])) for k in range(h)])
        q = total([odd[k] * float(0.5 * (matrix[i, k] - matrix[i, n - 1 - k])) for k in range(h)])
        out[i] = p + q
        out[n - 1 - i] = q - p if sign < 0 else p - q
    return out


def fine_rows(s, a):
    return s * 64 + a * 8


PLANES = [(0, 7), (1, 2), (3, 4), (5, 6)]


def pair(ref, p, base=0):
    return jnp.concatenate([wide(ref, base + 64 * s, 64) for s in p], axis=0)


def put_pair(ref, p, value):
    for k, s in enumerate(p):
        put(ref, 64 * s, 64, value[64 * k : 64 * k + 64])


def fine_stream(u, g, acc):
    for h in range(2):
        for a in range(8):
            at = [fine_rows(s, a) for s in range(8)]
            grad = contract([u[h, r : r + 8] for r in at], D8, -1)
            back = contract([grad[s] * g[h, r : r + 8] for s, r in enumerate(at)], D8.T, -1)
            for s, r in enumerate(at):
                acc[h, r : r + 8] = back[s]


def fine_cross(u, g, acc, bd, bdt, pairs):
    for p in pairs:
        flux = dot(bd[...], pair(u, p)) * pair(g, p, 1024)
        put_pair(acc, p, pair(acc, p) + dot(bdt[...], flux))
        for s in p:
            for h in range(2):
                at = [fine_rows(s, a) for a in range(8)]
                grad = contract([u[h, r : r + 8] for r in at], D8, -1)
                flux = [grad[a] * g[h, 512 + r : 520 + r] for a, r in enumerate(at)]
                back = contract(flux, D8.T, -1)
                for a, r in enumerate(at):
                    acc[h, r : r + 8] += back[a]


def fine_apply(u, g, acc, bd, bdt):
    fine_stream(u, g, acc)
    fine_cross(u, g, acc, bd, bdt, PLANES)


def fine_front(u, g, acc, bd, bdt):
    fine_stream(u, g, acc)
    fine_cross(u, g, acc, bd, bdt, PLANES[:1])
    join_fine(acc, (0, 7))


def left(x0, x1):
    near = iota(x0.shape[0], 1) < LANES - 16
    y0, y1 = pltpu.roll(x0, LANES - 16, 1), pltpu.roll(x1, LANES - 16, 1)
    return jnp.where(near, y0, y1), jnp.where(near, y1, y0)


def right(x0, x1):
    near = iota(x0.shape[0], 1) >= 16
    y0, y1 = pltpu.roll(x0, 16, 1), pltpu.roll(x1, 16, 1)
    return jnp.where(near, y0, y1), jnp.where(near, y1, y0)


def join_radial(x, points, start, rows):
    place = iota(rows, 1) % 16
    first = pl.ds(start, rows, stride=points)
    last = pl.ds(start + points - 1, rows, stride=points)
    for h in range(2):
        view = x.at[h]
        low, high = view[first, :], view[last, :]
        view[first, :] = jnp.where(place == 0, 0.0, low + pltpu.roll(high, 1, 1))
        view[last, :] = jnp.where(place == 15, 0.0, high + pltpu.roll(low, LANES - 1, 1))


def join_fine(x, planes=range(8)):
    for s in planes:
        join_radial(x, 8, 64 * s, 8)
        lo, hi = fine_rows(s, 0), fine_rows(s, 7)
        low = [x[h, lo : lo + 8] for h in range(2)]
        high = [x[h, hi : hi + 8] for h in range(2)]
        to_low, to_high = right(*high), left(*low)
        for h in range(2):
            x[h, lo : lo + 8] = low[h] + to_low[h]
            x[h, hi : hi + 8] = high[h] + to_high[h]


def join_mid(x):
    join_radial(x, 4, 0, 16)
    first = iota(8, 0) < 4
    for s in range(4):
        lo, hi = s * 16, s * 16 + 8
        low = [x[h, lo : lo + 8] for h in range(2)]
        high = [x[h, hi : hi + 8] for h in range(2)]
        to_low = right(*[pltpu.roll(t, 4, 0) for t in high])
        to_high = left(*[pltpu.roll(t, 4, 0) for t in low])
        for h in range(2):
            x[h, lo : lo + 8] = low[h] + jnp.where(first, to_low[h], 0.0)
            x[h, hi : hi + 8] = high[h] + jnp.where(first, 0.0, to_high[h])


def is_even(place, k):
    return lax.rem(place[k], 2) == 0


def full_of(x, faces, h, r, offset=0):
    even, far, near = faces
    rows = x.shape[1]
    plane = {512: 64, 64: 16}[rows]
    value = x[h, r : r + 8]
    if r < plane:
        at = offset + r
        return value + jnp.where(even, far[h, at : at + 8], near[h, at : at + 8])
    if r >= rows - plane:
        at = offset + r - (rows - plane)
        return value + jnp.where(even, near[h, at : at + 8], far[h, at : at + 8])
    return value


def send_faces(x, even, far, near, plane, offset=0):
    rows = x.shape[1]
    last = rows - plane
    one = pl.multiple_of(jnp.where(even, last, 0), 8)
    two = pl.multiple_of(jnp.where(even, 0, last), 8)
    for h in range(2):
        near[h, offset : offset + plane] = x[h, pl.ds(one, plane), :]
        far[h, offset : offset + plane] = x[h, pl.ds(two, plane), :]


def wall_mask(points):
    place, node = iota(8, 1) % 16, iota(8, 0) % points
    return ((node == 0) & (place == 0)) | ((node == points - 1) & (place == 15))


def own_part(half0, half1):
    near = iota(half0.shape[0], 1) < HALF
    return pltpu.roll(jnp.where(near, half1, half0), HALF, 1)


def tiles(rows):
    return [(h, r) for h in range(2) for r in range(0, rows, 8)]


def mid_apply(u, g4, acc, gm, gmt):
    flux = dot(gm[...], wide(u, 0, 64)) * wide(g4, 0, 192)
    put(acc, 0, 64, dot(gmt[...], flux))


def fine_diagonal(g, diag, bsq):
    square = (D8 * D8).T
    for c in range(4):
        rows = slice(128 * c, 128 * c + 128)
        diag[rows] = dot(bsq[...], g[1024 + 128 * c : 1152 + 128 * c])
    for axis in range(2):
        for fixed in range(8):
            at = [fine_rows(k, fixed) if axis == 0 else fine_rows(fixed, k) for k in range(8)]
            back = contract([g[512 * axis + r : 512 * axis + r + 8] for r in at], square, 1)
            for k, r in enumerate(at):
                diag[r : r + 8] += back[k]


def halves_up_down(a, b):
    near = iota(8, 1) < HALF
    up = jnp.where(near, a, pltpu.roll(b, HALF, 1))
    return up, jnp.where(near, pltpu.roll(a, HALF, 1), b)


def before_after(even, x, y):
    p, n = jnp.where(even, x, y), jnp.where(even, y, x)
    near = iota(8, 1) < HALF
    first = (jnp.where(near, p, 0.0), jnp.where(near, 0.0, pltpu.roll(n, HALF, 1)))
    second = (jnp.where(near, pltpu.roll(p, HALF, 1), 0.0), jnp.where(near, 0.0, n))
    return first, second


def order_kernel(pos, metric, load, order, g, rolled, far, near):
    even = is_even(pos, 1)
    slots = jnp.broadcast_to(pltpu.roll(order[...], HALF, 1), (8, LANES))
    wr = total([jnp.where(iota(8, 0) == k, float(W8[k]), 0.0) for k in range(8)])
    for r in range(0, 1536, 8):
        scale = wr * float(W8[(r % 512) // 64] * W8[(r // 8) % 8])
        g[r : r + 8] = jnp.take_along_axis(metric[r : r + 8], slots, axis=1) * scale
    for r in range(0, 512, 8):
        rolled[r : r + 8] = pltpu.roll(load[r : r + 8], HALF, 1)
    for r in range(0, 1024, 8):
        other = g[1024 + r : 1032 + r] if r < 512 else rolled[r - 512 : r - 504]
        up, down = halves_up_down(g[r : r + 8], other)
        far[r : r + 8] = jnp.where(even, down, up)
        near[r : r + 8] = jnp.where(even, up, down)


def own_kernel(g, bsq, diag):
    fine_diagonal(g, diag, bsq)


def setup_kernel(
    pos, g, rolled, diag, x, y, bsq, g8, load, diag8, face_a, face_b, ghost, ghost_diag
):
    near = iota(8, 1) < HALF
    even_a = is_even(pos, 1)

    def place(out, row, own, sides):
        out[0, row : row + 8] = jnp.where(near, sides[0], own)
        out[1, row : row + 8] = jnp.where(near, own, sides[1])

    for r in range(0, 1024, 8):
        first, second = before_after(even_a, x[r : r + 8], y[r : r + 8])
        place(g8, r, g[r : r + 8], first)
        ghost[r : r + 8] = first[0] + first[1]
        if r < 512:
            place(g8, 1024 + r, g[1024 + r : 1032 + r], second)
            ghost[1024 + r : 1032 + r] = second[0] + second[1]
        else:
            place(load, r - 512, rolled[r - 512 : r - 504], second)
    fine_diagonal(ghost, ghost_diag, bsq)
    for r in range(0, 512, 8):
        side = ghost_diag[r : r + 8]
        place(diag8, r, diag[r : r + 8], (side, side))
    for x in (load, diag8):
        join_fine(x)
    even = is_even(pos, 0)
    send_faces(load, even, face_a, face_b, 64)
    send_faces(diag8, even, face_a, face_b, 64, 64)


def coarsen_kernel(g8, w4, w2, sample, sq4, g4, diag4, edges, upper):
    low = []
    for d in range(3):
        logs = jnp.log(wide(g8, 512 * d, 512))
        coarse = jnp.exp(dot(sample[...], logs, lax.Precision.HIGHEST))
        put(g4, 64 * d, 64, coarse[:64] * jnp.concatenate([w4[...], w4[...]], axis=1))
        low.append([coarse[64:72, :LANES] * w2[...], coarse[64:72, LANES:] * w2[...]])
    put(diag4, 0, 64, dot(sq4[...], wide(g4, 0, 192)))
    join_mid(diag4)

    def corner(d, i, j, k):
        row = 4 * i + 2 * j + k
        return [t[row : row + 1] for t in low[d]]

    def add(x, y):
        return [x[0] + y[0], x[1] + y[1]]

    def quarter(x):
        return [0.25 * x[0], 0.25 * x[1]]

    def outward(x):
        return [pltpu.roll(x[0], 1, 1), pltpu.roll(x[1], 1, 1)]

    es = [[quarter(add(corner(0, 0, j, k), corner(0, 1, j, k))) for k in range(2)] for j in range(2)]
    ea = [[quarter(add(corner(1, i, 0, k), corner(1, i, 1, k))) for k in range(2)] for i in range(2)]
    er = [[quarter(add(corner(2, i, j, 0), corner(2, i, j, 1))) for j in range(2)] for i in range(2)]
    col = [add(es[0][k], list(right(*es[1][k]))) for k in range(2)]
    edge_s = add(col[0], outward(col[1]))
    edge_a = [add(ea[i][0], outward(ea[i][1])) for i in range(2)]
    edge_r = [add(er[i][0], list(right(*er[i][1]))) for i in range(2)]
    off_wall = iota(1, 1) % 16 != 0
    rows = [jnp.where(off_wall, own_part(*x), 0.0) for x in (edge_s, edge_a[0], edge_a[1])]
    rows += [own_part(*x) for x in edge_r]
    none = jnp.zeros((5, LANES), F32)
    edges[...] = jnp.concatenate([rows[0], rows[1], rows[3], none], axis=0)
    upper[...] = jnp.concatenate([rows[0], rows[2], rows[4], none], axis=0)


def first_kernel(
    pos, load, diag8, a, b, g8, bd, bdt, res, inv8, u, acc, face_a, face_b
):
    even = is_even(pos, 0)
    got = (even, a, b)
    wall8 = wall_mask(8)
    for h, r in tiles(512):
        diag = full_of(diag8, got, h, r, 64)
        inv = jnp.where(wall8, 0.0, 1.0 / jnp.where(wall8, 1.0, diag))
        full = full_of(load, got, h, r)
        res[h, r : r + 8] = full
        inv8[h, r : r + 8] = inv
        u[h, r : r + 8] = inv * full * (1.0 / CENTER)
    fine_front(u, g8, acc, bd, bdt)
    send_faces(acc, even, face_a, face_b, 64)


def inner_kernel(u, g8, start, bd, bdt, acc):
    for h, r in tiles(512):
        acc[h, r : r + 8] = start[h, r : r + 8]
    fine_cross(u, g8, acc, bd, bdt, PLANES[1:])
    join_fine(acc, range(1, 7))


def second_kernel(
    pos, res, inv8, acc, a, b, diag4, upper, g8, bd, bdt, down8,
    kept, t4, face_a, face_b, u, back, part,
):
    even = is_even(pos, 0)
    got = (even, a, b)
    edge = jnp.where((iota(8, 0) == 0) | (iota(8, 0) == 7), 0.5, 1.0)
    for h, r in tiles(512):
        inv, before = inv8[h, r : r + 8], res[h, r : r + 8]
        now = before - full_of(acc, got, h, r)
        old = inv * before * (1.0 / CENTER)
        new = KEEP * old + GAIN * inv * now
        kept[h, r : r + 8] = old + new
        kept[h, 512 + r : 520 + r] = now
        kept[h, 1024 + r : 1032 + r] = new
        u[h, r : r + 8] = new
    fine_apply(u, g8, back, bd, bdt)
    for h, r in tiles(512):
        s, c = r // 64, (r // 8) % 8
        scale = (0.5 if s in (0, 7) else 1.0) * (0.5 if c in (0, 7) else 1.0)
        part[r : r + 8, h * LANES : h * LANES + LANES] = (
            kept[h, 512 + r : 520 + r] * (edge * scale) - back[h, r : r + 8]
        )
    put(t4, 0, 64, dot(down8[...], part[...]))
    join_mid(t4)
    send_faces(t4, even, face_a, face_b, 16)
    send_faces(diag4, even, face_a, face_b, 16, 16)
    for face in (face_a, face_b):
        for h in range(2):
            face[h, 32:40] = upper[...]


def third_kernel(
    pos, t4, diag4, edges, a, b, g4, gm, gmt, res, inv4, edge, acc, face_a, face_b, u
):
    even = is_even(pos, 0)
    got = (even, a, b)
    wall = wall_mask(4)
    for h, r in tiles(64):
        full = full_of(t4, got, h, r)
        diag = full_of(diag4, got, h, r, 16)
        inv = jnp.where(wall, 0.0, 1.0 / jnp.where(wall, 1.0, diag))
        res[h, r : r + 8] = full
        inv4[h, r : r + 8] = inv
        u[h, r : r + 8] = inv * full * (1.0 / CENTER)
    lower = jnp.where(even, a[0, 32:40], b[0, 32:40])
    edge[...] = edges[...] + jnp.where(iota(8, 0) == 0, 0.0, lower)
    mid_apply(u, g4, acc, gm, gmt)
    join_mid(acc)
    send_faces(acc, even, face_a, face_b, 16)


def fourth_kernel(
    pos, res, acc, inv4, edge, a, b, g4, gm, gmt, m4, down4, corners, one, two, keep, part
):
    got = (is_even(pos, 0), a, b)
    for h, r in tiles(64):
        inv, before = inv4[h, r : r + 8], res[h, r : r + 8]
        now = before - full_of(acc, got, h, r)
        old = inv * before * (1.0 / CENTER)
        new = KEEP * old + GAIN * inv * now
        keep[h, r : r + 8] = now
        keep[h, 64 + r : 72 + r] = new
        keep[h, 128 + r : 136 + r] = old + new
    even_a = is_even(pos, 1)
    one[...] = jnp.where(even_a, keep[0], keep[1])
    two[...] = jnp.where(even_a, keep[1], keep[0])
    flux = dot(gm[...], wide(keep, 64, 64)) * wide(g4, 0, 192)
    put(part, 0, 64, dot(gmt[...], flux))
    for h, r in tiles(64):
        part[h, r : r + 8] = m4[r : r + 8] * keep[h, r : r + 8] - part[h, r : r + 8]
    low = dot(down4[...], wide(part, 0, 64))
    near = iota(8, 1) < HALF
    half0 = jnp.where(near, 0.0, low[:, :LANES])
    half1 = jnp.where(near, low[:, LANES:], 0.0)

    def corner(i, j, k):
        row = 4 * i + 2 * j + k
        return [half0[row : row + 1], half1[row : row + 1]]

    lane = iota(1, 1)
    mine, extra = [], []
    for i in range(2):
        columns = []
        for k in range(2):
            shifted = right(*corner(i, 1, k))
            straight = corner(i, 0, k)
            columns.append([straight[0] + shifted[0], straight[1] + shifted[1]])
        both = [columns[0][h] + pltpu.roll(columns[1][h], 1, 1) for h in range(2)]
        both = [jnp.where(lane % 16 == 0, 0.0, t) for t in both]
        mine.append(own_part(*both))
        extra.append(both[1])
    sides = jnp.where(lane < 16, pltpu.roll(extra[0], HALF, 1), 0.0) + jnp.where(
        (lane >= 16) & (lane < 32), pltpu.roll(extra[1], HALF + 16, 1), 0.0
    )
    none = jnp.zeros((2, LANES), F32)
    corners[...] = jnp.concatenate(mine + [sides, edge[0:3], none], axis=0)


def groups(ns):
    return max(1, ns // 8)


def side_kernel(pos, to_far, to_near, one, two, g4, gm, gmt, wider, far, near_side, back):
    near = iota(8, 1) < HALF
    even, even_a = is_even(pos, 0), is_even(pos, 1)
    for r in range(0, 192, 8):
        x, y = one[r : r + 8], two[r : r + 8]
        before, after = jnp.where(even_a, x, y), jnp.where(even_a, y, x)
        x, y = to_far[r : r + 8], to_near[r : r + 8]
        lower, upper = jnp.where(even_a, x, y), jnp.where(even_a, y, x)
        halves = (jnp.where(near, before, lower), jnp.where(near, upper, after))
        for h in range(2):
            wider[h, r : r + 8] = halves[h]
    flux = dot(gm[...], wide(wider, 64, 64)) * wide(g4, 0, 192)
    put(back, 0, 64, dot(gmt[...], flux))
    one = pl.multiple_of(jnp.where(even, 48, 0), 8)
    two = pl.multiple_of(jnp.where(even, 0, 48), 8)
    for out, plane in ((near_side, one), (far, two)):
        for h in range(2):
            out[h, 0:64] = g4[h, 0:64]
            out[h, 64:80] = g4[h, pl.ds(64 + plane, 16), :]
            out[h, 80:96] = g4[h, pl.ds(128 + plane, 16), :]
            out[h, 96:112] = back[h, pl.ds(plane, 16), :]


def column_kernel(rows, first, out):
    ns = rows.shape[0] // 8
    n = ns // groups(ns)

    def field(k):
        return rows[pl.ds(k, ns, stride=8), :]

    def later(x):
        return pltpu.roll(x, 1, 0)

    sides = field(2)
    over = jnp.where(iota(ns, 1) < 16, sides + later(pltpu.roll(sides, LANES - 16, 1)), 0.0)
    out[0:ns] = field(0) + later(field(1))
    for k in range(3):
        out[(1 + k) * ns : (2 + k) * ns] = field(3 + k)
    parts = [over[k * n : k * n + n] for k in range(groups(ns))]
    out[4 * ns : 4 * ns + n] = total(
        [pltpu.roll(p, 16 * k, 1) if k else p for k, p in enumerate(parts)]
    )


def coarse_kernel(
    pos, columns, others, wider, far, near_side, g4, inv4, gm, gmt, up4, gm_first, gmt_first,
    gm_last, gmt_last,
    res, u, sol, acc, face_a, face_b, vals, x2, es, ea, er, es0, ea0, er0, dg, ri,
):
    ns = x2.shape[0]
    na = x2.shape[1] // LANES
    width = na * LANES

    n = ns // groups(ns)
    size = 4 * ns + n
    even_a = is_even(pos, 1)

    def rows_of(d, start, count):
        at = d // 2 * size + start
        x, y = columns[at : at + count], others[at : at + count]
        return jnp.where(even_a, x, y) if d % 2 == 0 else jnp.where(even_a, y, x)

    def field(k):
        return [rows_of(d, k * ns, ns) for d in range(na)]

    def side(d):
        packed = rows_of(d, 4 * ns, n)
        parts = [pltpu.roll(packed, LANES - 16 * k, 1) if k else packed for k in range(groups(ns))]
        return jnp.where(iota(ns, 1) < 16, jnp.concatenate(parts, axis=0), 0.0)

    def roll_l(x, k):
        return pltpu.roll(x, k % width, 1)

    lane = iota(ns, 1)
    wall, top = lane % 16 == 0, lane % 16 == 15
    at = [slice(d * LANES, d * LANES + LANES) for d in range(na)]

    def towards_next(y, d):
        return jnp.where(lane < LANES - 16, y[d], y[(d + 1) % na])

    def towards_last(y, d):
        return jnp.where(lane < 16, y[d - 1], y[d])

    ea_all, er_all = field(2), field(3)
    ea_roll = [pltpu.roll(t, 16, 1) for t in ea_all]
    for d, es_d in enumerate(field(1)):
        es0_d, ea0_d = pltpu.roll(es_d, 1, 0), towards_last(ea_roll, d)
        er0_d = pltpu.roll(er_all[d], 1, 1)
        both = es_d + es0_d + ea_all[d] + ea0_d + er_all[d] + er0_d
        es[:, at[d]], ea[:, at[d]] = es_d, ea_all[d]
        es0[:, at[d]], ea0[:, at[d]] = es0_d, ea0_d
        er[:, at[d]] = jnp.where(wall | top, 0.0, er_all[d])
        er0[:, at[d]] = jnp.where(wall | (lane % 16 == 1), 0.0, er0_d)
        dg[:, at[d]] = jnp.where(wall, 0.0, both)
        ri[:, at[d]] = jnp.where(wall, 0.0, 1.0 / jnp.where(wall, 1.0, both))

    def inner(terms):
        return jnp.sum(jnp.sum(total(terms), axis=0, keepdims=True), axis=1, keepdims=True)

    first = field(0)
    r = [first[d] + side((d - 1) % na) for d in range(na)]
    p = [ri[:, at[d]] * r[d] for d in range(na)]
    gz = inner([r[d] * p[d] for d in range(na)])
    x = [jnp.zeros_like(t) for t in r]
    for it in range(ITERS):
        ahead = [pltpu.roll(t, LANES - 16, 1) for t in p]
        behind = [pltpu.roll(t, 16, 1) for t in p]
        q, terms = [], []
        for d in range(na):
            t, k = p[d], at[d]
            out = dg[:, k] * t
            out = out - es[:, k] * pltpu.roll(t, ns - 1, 0) - es0[:, k] * pltpu.roll(t, 1, 0)
            out = out - ea[:, k] * towards_next(ahead, d) - ea0[:, k] * towards_last(behind, d)
            out = out - er[:, k] * pltpu.roll(t, LANES - 1, 1) - er0[:, k] * pltpu.roll(t, 1, 1)
            q.append(out)
            terms.append(t * out)
        alpha = gz / inner(terms)
        x = [x[d] + alpha * p[d] for d in range(na)]
        if it + 1 < ITERS:
            r = [r[d] - alpha * q[d] for d in range(na)]
            z = [ri[:, at[d]] * r[d] for d in range(na)]
            new = inner([r[d] * z[d] for d in range(na)])
            beta = new / gz
            p = [z[d] + beta * p[d] for d in range(na)]
            gz = new
    for d in range(na):
        x2[:, at[d]] = x[d]

    s, a = pos[0], pos[1]
    blocks = [lax.rem(a + na - 1, na), a, lax.rem(a + 1, na)]
    for t in range(4):
        line = x2[pl.ds(lax.rem(s + ns - 1 + t, ns), 1), :]
        for j in range(2):
            for k in range(2):
                n = 4 * t + 2 * j + k
                vals[n : n + 1, :] = roll_l(line, -(16 * j + k)) if j + k else line
    near = iota(16, 1) < HALF
    b = [
        pltpu.roll(vals[:, pl.ds(pl.multiple_of(t * LANES, LANES), LANES)], HALF, 1) for t in blocks
    ]
    ext = jnp.concatenate([jnp.where(near, b[0], b[1]), jnp.where(near, b[1], b[2])], axis=1)
    rise = dot(up4[...], ext)
    even = is_even(pos, 0)
    x, y = wide(far, 0, 112), wide(near_side, 0, 112)
    below, above = jnp.where(even, x, y), jnp.where(even, y, x)
    low = dot(gmt_last[...], dot(gm_last[...], rise[:64]) * below[:96]) + below[96:]
    high = dot(gmt_first[...], dot(gm_first[...], rise[128:]) * above[:96]) + above[96:]
    flux = dot(gm[...], rise[64:128] + wide(wider, 64, 64)) * wide(g4, 0, 192)
    back = dot(gmt[...], flux)
    put(acc, 0, 16, back[:16] + low)
    put(acc, 16, 32, back[16:48])
    put(acc, 48, 16, back[48:] + high)
    join_mid(acc)
    put(sol, 0, 64, wide(wider, 128, 64) + rise[64:128])
    for h, r in tiles(64):
        now = wider[h, r : r + 8] - acc[h, r : r + 8]
        new = inv4[h, r : r + 8] * now * (1.0 / CENTER)
        res[h, r : r + 8] = now
        u[h, r : r + 8] = new
        sol[h, r : r + 8] += new
    mid_apply(u, g4, acc, gm, gmt)
    join_mid(acc)
    send_faces(acc, even, face_a, face_b, 16)


def sixth_kernel(
    pos, res, u, sol, acc, a, b, inv4, up8, kept, g8, bd, bdt,
    out, v8, acc2, face_a, face_b, y4,
):
    even = is_even(pos, 0)
    for h, r in tiles(64):
        now = res[h, r : r + 8] - full_of(acc, (even, a, b), h, r)
        new = KEEP * u[h, r : r + 8] + GAIN * inv4[h, r : r + 8] * now
        y4[h, r : r + 8] = sol[h, r : r + 8] + new
    put(v8, 0, 512, dot(up8[...], wide(y4, 0, 64)))
    for h, r in tiles(512):
        e8 = v8[h, r : r + 8]
        out[h, r : r + 8] = kept[h, r : r + 8] + e8
        v8[h, r : r + 8] = kept[h, 1024 + r : 1032 + r] + e8
    fine_front(v8, g8, acc2, bd, bdt)
    send_faces(acc2, even, face_a, face_b, 64)


def seventh_kernel(
    pos, kept, sol, acc, a, b, inv8, g8, bd, bdt, res, out, u, acc2, face_a, face_b
):
    even = is_even(pos, 0)
    for h, r in tiles(512):
        now = kept[h, 512 + r : 520 + r] - full_of(acc, (even, a, b), h, r)
        new = inv8[h, r : r + 8] * now * (1.0 / CENTER)
        res[h, r : r + 8] = now
        u[h, r : r + 8] = new
        out[h, r : r + 8] = sol[h, r : r + 8] + new
    fine_front(u, g8, acc2, bd, bdt)
    for out, plane in ((face_b, jnp.where(even, 448, 0)), (face_a, jnp.where(even, 0, 448))):
        rows = pl.ds(pl.multiple_of(plane, 8), 64)
        out[...] = own_part(acc2[0, rows, :], acc2[1, rows, :])


def inner_last_kernel(u, g8, acc, res, sol, inv8, bd, bdt, out, full):
    for h, r in tiles(384):
        full[h, 64 + r : 72 + r] = acc[h, 64 + r : 72 + r]
    fine_cross(u, g8, full, bd, bdt, PLANES[1:])
    join_fine(full, range(1, 7))
    for r in range(64, 448, 8):
        halves = []
        for h in range(2):
            now = res[h, r : r + 8] - full[h, r : r + 8]
            new = KEEP * u[h, r : r + 8] + GAIN * inv8[h, r : r + 8] * now
            halves.append(sol[h, r : r + 8] + new)
        out[r - 64 : r - 56] = own_part(*halves)


def last_kernel(pos, res, sol, u, acc, a, b, inv8, inner, out):
    even = is_even(pos, 0)
    out[64:448] = inner[...]
    for r in [*range(0, 64, 8), *range(448, 512, 8)]:
        halves = []
        for h in range(2):
            inv = inv8[h, r : r + 8]
            now = res[h, r : r + 8] - acc[h, r : r + 8]
            halves.append(sol[h, r : r + 8] + KEEP * u[h, r : r + 8] + GAIN * inv * now)
        at = r % 64
        x, y = a[at : at + 8], b[at : at + 8]
        face = jnp.where(even, x, y) if r < 64 else jnp.where(even, y, x)
        inv = own_part(inv8[0, r : r + 8], inv8[1, r : r + 8])
        out[r : r + 8] = own_part(*halves) - GAIN * inv * face


def call(kernel, args, outs, scratch=(), scalars=1):
    vmem = pl.BlockSpec(memory_space=pltpu.VMEM)
    smem = pl.BlockSpec(memory_space=pltpu.SMEM)
    arrays = [x for x in args if not isinstance(x, str)]
    named = len(arrays) < len(args)

    def body(*refs):
        rest = iter(refs)
        given = [next(rest) for _ in arrays[: len(arrays) - named]]
        held = next(rest) if named else None
        given = iter(given)
        full = [Constant(held, x) if isinstance(x, str) else next(given) for x in args]
        kernel(*full, *rest)

    if named:
        arrays.append(PACK)
    return pl.pallas_call(
        body,
        out_shape=[jax.ShapeDtypeStruct(s, F32) for s in outs],
        in_specs=[smem] * scalars + [vmem] * (len(arrays) - scalars),
        out_specs=[vmem] * len(outs),
        scratch_shapes=[pltpu.VMEM(s, F32) for s in scratch],
        compiler_params=pltpu.CompilerParams(vmem_limit_bytes=32 * 1024 * 1024),
        name=kernel.__name__,
    )(*arrays)


def exchange(far, near, axis):
    size = lax.axis_size(axis)
    pairs_far = [(i, (i + 1 if i % 2 else i - 1) % size) for i in range(size)]
    pairs_near = [(i, i ^ 1) for i in range(size)]
    return lax.ppermute(far, axis, pairs_far), lax.ppermute(near, axis, pairs_near)


def spread(x, axis, groups=None):
    size = len(groups[0]) if groups else lax.axis_size(axis)
    copies = jnp.broadcast_to(x[None], (size,) + x.shape)
    return lax.all_to_all(copies, axis, 0, 0, axis_index_groups=groups).reshape(-1, LANES)


def on_device(element_load, metric, element_order):
    ns, na = lax.axis_size("stream"), lax.axis_size("azim")
    fine, mid = (2, 512, LANES), (2, 64, LANES)
    face8, face4 = [(2, 64, LANES)] * 2, [(2, 16, LANES)] * 2
    pos = jnp.stack([lax.axis_index("stream"), lax.axis_index("azim")]).astype(jnp.int32)
    g, rolled, a, b = call(
        order_kernel,
        (pos, metric.reshape(1536, LANES), element_load.reshape(512, LANES), element_order),
        [(1536, LANES), (512, LANES), (1024, LANES), (1024, LANES)],
    )
    a, b = exchange(a, b, "azim")
    (diag,) = call(own_kernel, (g, "bsq"), [(512, LANES)], scalars=0)

    def inner(u, acc):
        (acc,) = call(inner_kernel, (u, g8, acc, "bd", "bdt"), [fine], (), 0)
        return acc

    g8, load, diag8, a, b = call(
        setup_kernel,
        (pos, g, rolled, diag, a, b, "bsq"),
        [(2, 1536, LANES), fine, fine] + [(2, 128, LANES)] * 2,
        [(1536, LANES), (512, LANES)],
    )
    a, b = exchange(a, b, "stream")
    res8, inv8, u8, acc, a, b = call(
        first_kernel,
        (pos, load, diag8, a, b, g8, "bd", "bdt"),
        [fine, fine, fine, fine] + face8,
    )
    a, b = exchange(a, b, "stream")
    acc = inner(u8, acc)
    g4, diag4, edges, upper = call(
        coarsen_kernel,
        (g8, "w4", "w2", "sample", "sq4"),
        [(2, 192, LANES), mid, (8, LANES), (8, LANES)],
        scalars=0,
    )
    kept, t4, a, b = call(
        second_kernel,
        (pos, res8, inv8, acc, a, b, diag4, upper, g8, "bd", "bdt", "down8"),
        [(2, 1536, LANES), mid] + [(2, 40, LANES)] * 2,
        [fine, fine, (512, 2 * LANES)],
    )
    a, b = exchange(a, b, "stream")
    res4, inv4, edges, acc, a, b = call(
        third_kernel,
        (pos, t4, diag4, edges, a, b, g4, "gm", "gmt"),
        [mid, mid, (8, LANES), mid] + face4,
        [mid],
    )
    a, b = exchange(a, b, "stream")
    corners, *kept4 = call(
        fourth_kernel,
        (pos, res4, acc, inv4, edges, a, b, g4, "gm", "gmt", "m4", "down4"),
        [(8, LANES), (192, LANES), (192, LANES)],
        [(2, 192, LANES), mid],
    )
    columns = spread(corners, "stream")
    a, b = exchange(*kept4, "azim")
    wider, a, b = call(
        side_kernel,
        (pos, *kept4, a, b, g4, "gm", "gmt"),
        [(2, 192, LANES)] + [(2, 112, LANES)] * 2,
        [mid],
    )
    sides = exchange(a, b, "stream")
    size = 4 * ns + ns // groups(ns)
    (columns,) = call(
        column_kernel, (columns, wider), [(size, LANES)], (), 0
    )
    cores = [list(range(core, na, 2)) for core in range(2)]
    columns = spread(columns, "azim", cores)
    others = lax.ppermute(columns, "azim", [(i, i ^ 1) for i in range(na)])
    whole = (ns, na * LANES)
    res4, u4, sol4, acc, a, b = call(
        coarse_kernel,
        (
            pos,
            columns,
            others,
            wider,
            *sides,
            g4,
            inv4,
            "gm",
            "gmt",
            "up4",
            "gm_first",
            "gmt_first",
            "gm_last",
            "gmt_last",
        ),
        [mid, mid, mid, mid] + face4,
        [(16, na * LANES)] + [whole] * 9,
    )
    a, b = exchange(a, b, "stream")
    sol8, v8, acc, a, b = call(
        sixth_kernel,
        (pos, res4, u4, sol4, acc, a, b, inv4, "up8", kept, g8, "bd", "bdt"),
        [fine, fine, fine] + face8,
        [mid],
    )
    a, b = exchange(a, b, "stream")
    acc = inner(v8, acc)
    res8, sol8, u8, acc, a, b = call(
        seventh_kernel,
        (pos, kept, sol8, acc, a, b, inv8, g8, "bd", "bdt"),
        [fine, fine, fine, fine] + [(64, LANES)] * 2,
    )
    a, b = exchange(a, b, "stream")
    (inside,) = call(
        inner_last_kernel,
        (u8, g8, acc, res8, sol8, inv8, "bd", "bdt"),
        [(384, LANES)],
        [fine],
        scalars=0,
    )
    (out,) = call(last_kernel, (pos, res8, sol8, u8, acc, a, b, inv8, inside), [(512, LANES)])
    return out.reshape(element_load.shape)


def solution(mesh):
    placed = (P(None, "stream", "azim"), P(None, None, "stream", "azim"), P("stream", "azim"))
    return jax.shard_map(
        on_device, mesh=mesh, in_specs=placed, out_specs=P(None, "stream", "azim"), check_vma=False
    )
```

```python
import jax
import jax.numpy as jnp
import numpy as np
from jax import lax
from jax.experimental import pallas as pl
from jax.experimental.pallas import tpu as pltpu
from jax.sharding import PartitionSpec as P

ITERS = 6
LOW_EIG = 0.3
HIGH_EIG = 3.0
CENTER = 0.5 * (HIGH_EIG + LOW_EIG)
HALF_WIDTH = 0.5 * (HIGH_EIG - LOW_EIG)
FIRST_RHO = HALF_WIDTH / CENTER
SECOND_RHO = 1.0 / (2.0 * CENTER / HALF_WIDTH - FIRST_RHO)
KEEP = SECOND_RHO * FIRST_RHO
GAIN = 2.0 * SECOND_RHO / HALF_WIDTH
LANES = 128
HALF = 64
F32 = jnp.float32


def legendre_pair(degree, places):
    previous = places * 0.0 + 1.0
    current = places.copy()
    for k in range(2, degree + 1):
        following = ((2 * k - 1) * places * current - (k - 1) * previous) / k
        previous = current
        current = following
    return (current, previous)


def gll_table(points):
    degree = points - 1
    places = np.cos(np.pi * np.arange(points) / degree)
    for _ in range(60):
        top, below = legendre_pair(degree, places)
        places = places - (places * top - below) / (points * top)
    nodes = np.sort(places)
    nodes[0] = -1.0
    nodes[-1] = 1.0
    at_nodes = legendre_pair(degree, nodes)[0]
    weights = 2.0 / (degree * (degree + 1) * at_nodes**2)
    deriv = np.zeros((points, points))
    for i in range(points):
        for j in range(points):
            if i != j:
                deriv[i, j] = at_nodes[i] / (at_nodes[j] * (nodes[i] - nodes[j]))
    deriv[0, 0] = -degree * (degree + 1) / 4.0
    deriv[-1, -1] = degree * (degree + 1) / 4.0
    return (nodes, weights, deriv)


def lagrange_table(source, target):
    out = np.ones((len(target), len(source)))
    for j in range(len(source)):
        for k in range(len(source)):
            if k != j:
                out[:, j] *= (target - source[k]) / (source[j] - source[k])
    return out


N8, W8, D8 = gll_table(8)
N4, W4, D4 = gll_table(4)
N2, W2, D2 = gll_table(2)


def kron3(a, b, c):
    return np.kron(np.kron(a, b), c)


def cube(w):
    return (w[:, None, None] * w[None, :, None] * w[None, None, :]).reshape(-1)


def share(n):
    edge = np.ones(n)
    edge[0] = edge[-1] = 0.5
    return cube(edge)


def grads(d):
    i = np.eye(d.shape[0])
    return [kron3(d, i, i), kron3(i, d, i), kron3(i, i, d)]


def f32(x):
    return np.asarray(x, np.float32)


def lanes_of(column):
    return np.repeat(f32(column)[:, None], LANES, axis=1)


UP8 = lagrange_table(N4, N8)
UP4 = lagrange_table(N2, N4)
TO4 = lagrange_table(N8, N4)
TO2 = lagrange_table(N8, N2)

C_BD = f32(np.kron(np.eye(16), D8))
C_BDT = f32(np.kron(np.eye(16), D8.T))
C_BSQ = f32(np.kron(np.eye(16), (D8 * D8).T))
C_SAMPLE = f32(np.concatenate([kron3(TO4, TO4, TO4), kron3(TO2, TO2, TO2)]))
C_UP8 = f32(kron3(UP8, UP8, UP8))
C_DOWN8 = f32(kron3(UP8, UP8, UP8).T)
C_UP4 = f32(kron3(UP4, UP4, UP4))
C_DOWN4 = f32(kron3(UP4, UP4, UP4).T)
C_UP4X3 = np.zeros((192, 16), np.float32)
for layer in range(3):
    C_UP4X3[64 * layer : 64 * layer + 64, 4 * layer : 4 * layer + 8] = C_UP4
C_G4 = f32(np.concatenate(grads(D4)))
C_G4T = f32(np.concatenate(grads(D4)).T)
C_SQ4 = f32((np.concatenate(grads(D4)) ** 2).T)
C_W4 = lanes_of(cube(W4) / np.exp(kron3(TO4, TO4, TO4) @ np.log(cube(W8))))
C_W2 = lanes_of(cube(W2) / np.exp(kron3(TO2, TO2, TO2) @ np.log(cube(W8))))
C_M4 = lanes_of(share(4))
FIRST = np.r_[0:16, 64:80, 128:144]
LAST = np.r_[48:64, 112:128, 176:192]


def plane_back(plane, rows):
    eye = np.eye(16, dtype=np.float32)
    return np.concatenate([eye, C_G4T[plane : plane + 16, rows[16:]]], axis=1)


CONSTANTS = {
    "bd": C_BD, "bdt": C_BDT, "bsq": C_BSQ, "sample": C_SAMPLE, "w4": C_W4, "w2": C_W2,
    "sq4": C_SQ4, "gm": C_G4, "gmt": C_G4T, "m4": C_M4, "down8": C_DOWN8, "down4": C_DOWN4,
    "up4": C_UP4X3, "up8": C_UP8, "gm_first": C_G4[FIRST], "gmt_first": plane_back(0, FIRST),
    "gm_last": C_G4[LAST], "gmt_last": plane_back(48, LAST),
}


def pack_constants():
    rows, places, start = [], {}, 0
    for name, value in CONSTANTS.items():
        blocks = -(-value.shape[1] // LANES)
        padded = np.zeros((value.shape[0], blocks * LANES), np.float32)
        padded[:, : value.shape[1]] = value
        rows += [padded[:, k * LANES : (k + 1) * LANES] for k in range(blocks)]
        places[name] = (start, value.shape, blocks)
        start += value.shape[0] * blocks
    return np.concatenate(rows), places


PACK, PLACES = pack_constants()


class Constant:
    def __init__(self, ref, name):
        self.ref, self.name = ref, name

    def __getitem__(self, index):
        start, (rows, columns), blocks = PLACES[self.name]
        parts = []
        for k in range(blocks):
            width = min(LANES, columns - k * LANES)
            parts.append(self.ref[start + k * rows : start + (k + 1) * rows, :width])
        value = parts[0] if blocks == 1 else jnp.concatenate(parts, axis=1)
        return value if index is Ellipsis else value[index]


def dot(a, b, precision=lax.Precision.HIGH):
    return jnp.dot(a, b, preferred_element_type=F32, precision=precision)


def iota(rows, axis):
    return lax.broadcasted_iota(jnp.int32, (rows, LANES), axis)


def wide(ref, start, size):
    return jnp.concatenate([ref[0, start : start + size], ref[1, start : start + size]], axis=1)


def put(ref, start, size, value):
    ref[0, start : start + size] = value[:, :LANES]
    ref[1, start : start + size] = value[:, LANES:]


def total(terms):
    out = terms[0]
    for t in terms[1:]:
        out = out + t
    return out


def contract(v, matrix, sign):
    n = len(v)
    h = n // 2
    even = [v[k] + v[n - 1 - k] for k in range(h)]
    odd = [v[k] - v[n - 1 - k] for k in range(h)]
    out = [None] * n
    for i in range(h):
        p = total([even[k] * float(0.5 * (matrix[i, k] + matrix[i, n - 1 - k])) for k in range(h)])
        q = total([odd[k] * float(0.5 * (matrix[i, k] - matrix[i, n - 1 - k])) for k in range(h)])
        out[i] = p + q
        out[n - 1 - i] = q - p if sign < 0 else p - q
    return out


def fine_rows(s, a):
    return s * 64 + a * 8


PLANES = [(0, 7), (1, 2), (3, 4), (5, 6)]


def pair(ref, p, base=0):
    return jnp.concatenate([wide(ref, base + 64 * s, 64) for s in p], axis=0)


def put_pair(ref, p, value):
    for k, s in enumerate(p):
        put(ref, 64 * s, 64, value[64 * k : 64 * k + 64])


def fine_stream(u, g, acc):
    for h in range(2):
        for a in range(8):
            at = [fine_rows(s, a) for s in range(8)]
            grad = contract([u[h, r : r + 8] for r in at], D8, -1)
            back = contract([grad[s] * g[h, r : r + 8] for s, r in enumerate(at)], D8.T, -1)
            for s, r in enumerate(at):
                acc[h, r : r + 8] = back[s]


def fine_cross(u, g, acc, bd, bdt, pairs):
    for p in pairs:
        flux = dot(bd[...], pair(u, p)) * pair(g, p, 1024)
        put_pair(acc, p, pair(acc, p) + dot(bdt[...], flux))
        for s in p:
            for h in range(2):
                at = [fine_rows(s, a) for a in range(8)]
                grad = contract([u[h, r : r + 8] for r in at], D8, -1)
                flux = [grad[a] * g[h, 512 + r : 520 + r] for a, r in enumerate(at)]
                back = contract(flux, D8.T, -1)
                for a, r in enumerate(at):
                    acc[h, r : r + 8] += back[a]


def fine_apply(u, g, acc, bd, bdt):
    fine_stream(u, g, acc)
    fine_cross(u, g, acc, bd, bdt, PLANES)


def fine_front(u, g, acc, bd, bdt):
    fine_stream(u, g, acc)
    fine_cross(u, g, acc, bd, bdt, PLANES[:1])
    join_fine(acc, (0, 7))


def left(x0, x1):
    near = iota(x0.shape[0], 1) < LANES - 16
    y0, y1 = pltpu.roll(x0, LANES - 16, 1), pltpu.roll(x1, LANES - 16, 1)
    return jnp.where(near, y0, y1), jnp.where(near, y1, y0)


def right(x0, x1):
    near = iota(x0.shape[0], 1) >= 16
    y0, y1 = pltpu.roll(x0, 16, 1), pltpu.roll(x1, 16, 1)
    return jnp.where(near, y0, y1), jnp.where(near, y1, y0)


def join_radial(x, points, start, rows):
    place = iota(rows, 1) % 16
    first = pl.ds(start, rows, stride=points)
    last = pl.ds(start + points - 1, rows, stride=points)
    for h in range(2):
        view = x.at[h]
        low, high = view[first, :], view[last, :]
        view[first, :] = jnp.where(place == 0, 0.0, low + pltpu.roll(high, 1, 1))
        view[last, :] = jnp.where(place == 15, 0.0, high + pltpu.roll(low, LANES - 1, 1))


def join_fine(x, planes=range(8)):
    for s in planes:
        join_radial(x, 8, 64 * s, 8)
        lo, hi = fine_rows(s, 0), fine_rows(s, 7)
        low = [x[h, lo : lo + 8] for h in range(2)]
        high = [x[h, hi : hi + 8] for h in range(2)]
        to_low, to_high = right(*high), left(*low)
        for h in range(2):
            x[h, lo : lo + 8] = low[h] + to_low[h]
            x[h, hi : hi + 8] = high[h] + to_high[h]


def join_mid(x):
    join_radial(x, 4, 0, 16)
    first = iota(8, 0) < 4
    for s in range(4):
        lo, hi = s * 16, s * 16 + 8
        low = [x[h, lo : lo + 8] for h in range(2)]
        high = [x[h, hi : hi + 8] for h in range(2)]
        to_low = right(*[pltpu.roll(t, 4, 0) for t in high])
        to_high = left(*[pltpu.roll(t, 4, 0) for t in low])
        for h in range(2):
            x[h, lo : lo + 8] = low[h] + jnp.where(first, to_low[h], 0.0)
            x[h, hi : hi + 8] = high[h] + jnp.where(first, 0.0, to_high[h])


def is_even(place, k):
    return lax.rem(place[k], 2) == 0


def full_of(x, faces, h, r, offset=0):
    even, far, near = faces
    rows = x.shape[1]
    plane = {512: 64, 64: 16}[rows]
    value = x[h, r : r + 8]
    if r < plane:
        at = offset + r
        return value + jnp.where(even, far[h, at : at + 8], near[h, at : at + 8])
    if r >= rows - plane:
        at = offset + r - (rows - plane)
        return value + jnp.where(even, near[h, at : at + 8], far[h, at : at + 8])
    return value


def send_faces(x, even, far, near, plane, offset=0):
    rows = x.shape[1]
    last = rows - plane
    one = pl.multiple_of(jnp.where(even, last, 0), 8)
    two = pl.multiple_of(jnp.where(even, 0, last), 8)
    for h in range(2):
        near[h, offset : offset + plane] = x[h, pl.ds(one, plane), :]
        far[h, offset : offset + plane] = x[h, pl.ds(two, plane), :]


def wall_mask(points):
    place, node = iota(8, 1) % 16, iota(8, 0) % points
    return ((node == 0) & (place == 0)) | ((node == points - 1) & (place == 15))


def own_part(half0, half1):
    near = iota(half0.shape[0], 1) < HALF
    return pltpu.roll(jnp.where(near, half1, half0), HALF, 1)


def tiles(rows):
    return [(h, r) for h in range(2) for r in range(0, rows, 8)]


def mid_apply(u, g4, acc, gm, gmt):
    flux = dot(gm[...], wide(u, 0, 64)) * wide(g4, 0, 192)
    put(acc, 0, 64, dot(gmt[...], flux))


def fine_diagonal(g, diag, bsq):
    square = (D8 * D8).T
    for c in range(4):
        rows = slice(128 * c, 128 * c + 128)
        diag[rows] = dot(bsq[...], g[1024 + 128 * c : 1152 + 128 * c])
    for axis in range(2):
        for fixed in range(8):
            at = [fine_rows(k, fixed) if axis == 0 else fine_rows(fixed, k) for k in range(8)]
            back = contract([g[512 * axis + r : 512 * axis + r + 8] for r in at], square, 1)
            for k, r in enumerate(at):
                diag[r : r + 8] += back[k]


def halves_up_down(a, b):
    near = iota(8, 1) < HALF
    up = jnp.where(near, a, pltpu.roll(b, HALF, 1))
    return up, jnp.where(near, pltpu.roll(a, HALF, 1), b)


def before_after(even, x, y):
    p, n = jnp.where(even, x, y), jnp.where(even, y, x)
    near = iota(8, 1) < HALF
    first = (jnp.where(near, p, 0.0), jnp.where(near, 0.0, pltpu.roll(n, HALF, 1)))
    second = (jnp.where(near, pltpu.roll(p, HALF, 1), 0.0), jnp.where(near, 0.0, n))
    return first, second


def order_kernel(pos, metric, load, order, g, rolled, far, near):
    even = is_even(pos, 1)
    slots = jnp.broadcast_to(pltpu.roll(order[...], HALF, 1), (8, LANES))
    wr = total([jnp.where(iota(8, 0) == k, float(W8[k]), 0.0) for k in range(8)])
    for r in range(0, 1536, 8):
        scale = wr * float(W8[(r % 512) // 64] * W8[(r // 8) % 8])
        g[r : r + 8] = jnp.take_along_axis(metric[r : r + 8], slots, axis=1) * scale
    for r in range(0, 512, 8):
        rolled[r : r + 8] = pltpu.roll(load[r : r + 8], HALF, 1)
    for r in range(0, 1024, 8):
        other = g[1024 + r : 1032 + r] if r < 512 else rolled[r - 512 : r - 504]
        up, down = halves_up_down(g[r : r + 8], other)
        far[r : r + 8] = jnp.where(even, down, up)
        near[r : r + 8] = jnp.where(even, up, down)


def own_kernel(g, bsq, diag):
    fine_diagonal(g, diag, bsq)


def setup_kernel(
    pos, g, rolled, diag, x, y, bsq, g8, load, diag8, face_a, face_b, ghost, ghost_diag
):
    near = iota(8, 1) < HALF
    even_a = is_even(pos, 1)

    def place(out, row, own, sides):
        out[0, row : row + 8] = jnp.where(near, sides[0], own)
        out[1, row : row + 8] = jnp.where(near, own, sides[1])

    for r in range(0, 1024, 8):
        first, second = before_after(even_a, x[r : r + 8], y[r : r + 8])
        place(g8, r, g[r : r + 8], first)
        ghost[r : r + 8] = first[0] + first[1]
        if r < 512:
            place(g8, 1024 + r, g[1024 + r : 1032 + r], second)
            ghost[1024 + r : 1032 + r] = second[0] + second[1]
        else:
            place(load, r - 512, rolled[r - 512 : r - 504], second)
    fine_diagonal(ghost, ghost_diag, bsq)
    for r in range(0, 512, 8):
        side = ghost_diag[r : r + 8]
        place(diag8, r, diag[r : r + 8], (side, side))
    for x in (load, diag8):
        join_fine(x)
    even = is_even(pos, 0)
    send_faces(load, even, face_a, face_b, 64)
    send_faces(diag8, even, face_a, face_b, 64, 64)


def coarsen_kernel(g8, w4, w2, sample, sq4, g4, diag4, edges, upper):
    low = []
    for d in range(3):
        logs = jnp.log(wide(g8, 512 * d, 512))
        coarse = jnp.exp(dot(sample[...], logs, lax.Precision.HIGHEST))
        put(g4, 64 * d, 64, coarse[:64] * jnp.concatenate([w4[...], w4[...]], axis=1))
        low.append([coarse[64:72, :LANES] * w2[...], coarse[64:72, LANES:] * w2[...]])
    put(diag4, 0, 64, dot(sq4[...], wide(g4, 0, 192)))
    join_mid(diag4)

    def corner(d, i, j, k):
        row = 4 * i + 2 * j + k
        return [t[row : row + 1] for t in low[d]]

    def add(x, y):
        return [x[0] + y[0], x[1] + y[1]]

    def quarter(x):
        return [0.25 * x[0], 0.25 * x[1]]

    def outward(x):
        return [pltpu.roll(x[0], 1, 1), pltpu.roll(x[1], 1, 1)]

    es = [[quarter(add(corner(0, 0, j, k), corner(0, 1, j, k))) for k in range(2)] for j in range(2)]
    ea = [[quarter(add(corner(1, i, 0, k), corner(1, i, 1, k))) for k in range(2)] for i in range(2)]
    er = [[quarter(add(corner(2, i, j, 0), corner(2, i, j, 1))) for j in range(2)] for i in range(2)]
    col = [add(es[0][k], list(right(*es[1][k]))) for k in range(2)]
    edge_s = add(col[0], outward(col[1]))
    edge_a = [add(ea[i][0], outward(ea[i][1])) for i in range(2)]
    edge_r = [add(er[i][0], list(right(*er[i][1]))) for i in range(2)]
    off_wall = iota(1, 1) % 16 != 0
    rows = [jnp.where(off_wall, own_part(*x), 0.0) for x in (edge_s, edge_a[0], edge_a[1])]
    rows += [own_part(*x) for x in edge_r]
    none = jnp.zeros((5, LANES), F32)
    edges[...] = jnp.concatenate([rows[0], rows[1], rows[3], none], axis=0)
    upper[...] = jnp.concatenate([rows[0], rows[2], rows[4], none], axis=0)


def first_kernel(
    pos, load, diag8, a, b, g8, bd, bdt, res, inv8, u, acc, face_a, face_b
):
    even = is_even(pos, 0)
    got = (even, a, b)
    wall8 = wall_mask(8)
    for h, r in tiles(512):
        diag = full_of(diag8, got, h, r, 64)
        inv = jnp.where(wall8, 0.0, 1.0 / jnp.where(wall8, 1.0, diag))
        full = full_of(load, got, h, r)
        res[h, r : r + 8] = full
        inv8[h, r : r + 8] = inv
        u[h, r : r + 8] = inv * full * (1.0 / CENTER)
    fine_front(u, g8, acc, bd, bdt)
    send_faces(acc, even, face_a, face_b, 64)


def inner_kernel(u, g8, start, bd, bdt, acc):
    for h, r in tiles(512):
        acc[h, r : r + 8] = start[h, r : r + 8]
    fine_cross(u, g8, acc, bd, bdt, PLANES[1:])
    join_fine(acc, range(1, 7))


def second_kernel(
    pos, res, inv8, acc, a, b, diag4, upper, g8, bd, bdt, down8,
    kept, t4, face_a, face_b, u, back, part,
):
    even = is_even(pos, 0)
    got = (even, a, b)
    edge = jnp.where((iota(8, 0) == 0) | (iota(8, 0) == 7), 0.5, 1.0)
    for h, r in tiles(512):
        inv, before = inv8[h, r : r + 8], res[h, r : r + 8]
        now = before - full_of(acc, got, h, r)
        old = inv * before * (1.0 / CENTER)
        new = KEEP * old + GAIN * inv * now
        kept[h, r : r + 8] = old + new
        kept[h, 512 + r : 520 + r] = now
        kept[h, 1024 + r : 1032 + r] = new
        u[h, r : r + 8] = new
    fine_apply(u, g8, back, bd, bdt)
    for h, r in tiles(512):
        s, c = r // 64, (r // 8) % 8
        scale = (0.5 if s in (0, 7) else 1.0) * (0.5 if c in (0, 7) else 1.0)
        part[r : r + 8, h * LANES : h * LANES + LANES] = (
            kept[h, 512 + r : 520 + r] * (edge * scale) - back[h, r : r + 8]
        )
    put(t4, 0, 64, dot(down8[...], part[...]))
    join_mid(t4)
    send_faces(t4, even, face_a, face_b, 16)
    send_faces(diag4, even, face_a, face_b, 16, 16)
    for face in (face_a, face_b):
        for h in range(2):
            face[h, 32:40] = upper[...]


def third_kernel(
    pos, t4, diag4, edges, a, b, g4, gm, gmt, res, inv4, edge, acc, face_a, face_b, u
):
    even = is_even(pos, 0)
    got = (even, a, b)
    wall = wall_mask(4)
    for h, r in tiles(64):
        full = full_of(t4, got, h, r)
        diag = full_of(diag4, got, h, r, 16)
        inv = jnp.where(wall, 0.0, 1.0 / jnp.where(wall, 1.0, diag))
        res[h, r : r + 8] = full
        inv4[h, r : r + 8] = inv
        u[h, r : r + 8] = inv * full * (1.0 / CENTER)
    lower = jnp.where(even, a[0, 32:40], b[0, 32:40])
    edge[...] = edges[...] + jnp.where(iota(8, 0) == 0, 0.0, lower)
    mid_apply(u, g4, acc, gm, gmt)
    join_mid(acc)
    send_faces(acc, even, face_a, face_b, 16)


def fourth_kernel(
    pos, res, acc, inv4, edge, a, b, g4, gm, gmt, m4, down4, corners, one, two, keep, part
):
    got = (is_even(pos, 0), a, b)
    for h, r in tiles(64):
        inv, before = inv4[h, r : r + 8], res[h, r : r + 8]
        now = before - full_of(acc, got, h, r)
        old = inv * before * (1.0 / CENTER)
        new = KEEP * old + GAIN * inv * now
        keep[h, r : r + 8] = now
        keep[h, 64 + r : 72 + r] = new
        keep[h, 128 + r : 136 + r] = old + new
    even_a = is_even(pos, 1)
    one[...] = jnp.where(even_a, keep[0], keep[1])
    two[...] = jnp.where(even_a, keep[1], keep[0])
    flux = dot(gm[...], wide(keep, 64, 64)) * wide(g4, 0, 192)
    put(part, 0, 64, dot(gmt[...], flux))
    for h, r in tiles(64):
        part[h, r : r + 8] = m4[r : r + 8] * keep[h, r : r + 8] - part[h, r : r + 8]
    low = dot(down4[...], wide(part, 0, 64))
    near = iota(8, 1) < HALF
    half0 = jnp.where(near, 0.0, low[:, :LANES])
    half1 = jnp.where(near, low[:, LANES:], 0.0)

    def corner(i, j, k):
        row = 4 * i + 2 * j + k
        return [half0[row : row + 1], half1[row : row + 1]]

    lane = iota(1, 1)
    mine, extra = [], []
    for i in range(2):
        columns = []
        for k in range(2):
            shifted = right(*corner(i, 1, k))
            straight = corner(i, 0, k)
            columns.append([straight[0] + shifted[0], straight[1] + shifted[1]])
        both = [columns[0][h] + pltpu.roll(columns[1][h], 1, 1) for h in range(2)]
        both = [jnp.where(lane % 16 == 0, 0.0, t) for t in both]
        mine.append(own_part(*both))
        extra.append(both[1])
    sides = jnp.where(lane < 16, pltpu.roll(extra[0], HALF, 1), 0.0) + jnp.where(
        (lane >= 16) & (lane < 32), pltpu.roll(extra[1], HALF + 16, 1), 0.0
    )
    none = jnp.zeros((2, LANES), F32)
    corners[...] = jnp.concatenate(mine + [sides, edge[0:3], none], axis=0)


def groups(ns):
    return max(1, ns // 8)


def side_kernel(pos, to_far, to_near, one, two, g4, gm, gmt, wider, far, near_side, back):
    near = iota(8, 1) < HALF
    even, even_a = is_even(pos, 0), is_even(pos, 1)
    for r in range(0, 192, 8):
        x, y = one[r : r + 8], two[r : r + 8]
        before, after = jnp.where(even_a, x, y), jnp.where(even_a, y, x)
        x, y = to_far[r : r + 8], to_near[r : r + 8]
        lower, upper = jnp.where(even_a, x, y), jnp.where(even_a, y, x)
        halves = (jnp.where(near, before, lower), jnp.where(near, upper, after))
        for h in range(2):
            wider[h, r : r + 8] = halves[h]
    flux = dot(gm[...], wide(wider, 64, 64)) * wide(g4, 0, 192)
    put(back, 0, 64, dot(gmt[...], flux))
    one = pl.multiple_of(jnp.where(even, 48, 0), 8)
    two = pl.multiple_of(jnp.where(even, 0, 48), 8)
    sums = [
        [
            total([g4[h, 16 * k : 16 * k + 16] * float(D4[k, end]) for k in range(4)])
            for end in (0, 3)
        ]
        for h in range(2)
    ]
    for out, plane, is_last in ((near_side, one, even), (far, two, jnp.logical_not(even))):
        for h in range(2):
            out[h, 0:16] = jnp.where(is_last, sums[h][1], sums[h][0])
            out[h, 16:32] = g4[h, pl.ds(64 + plane, 16), :]
            out[h, 32:48] = g4[h, pl.ds(128 + plane, 16), :]
            out[h, 48:64] = back[h, pl.ds(plane, 16), :]


def column_kernel(rows, first, out):
    ns = rows.shape[0] // 8
    n = ns // groups(ns)

    def field(k):
        return rows[pl.ds(k, ns, stride=8), :]

    def later(x):
        return pltpu.roll(x, 1, 0)

    sides = field(2)
    over = jnp.where(iota(ns, 1) < 16, sides + later(pltpu.roll(sides, LANES - 16, 1)), 0.0)
    out[0:ns] = field(0) + later(field(1))
    for k in range(3):
        out[(1 + k) * ns : (2 + k) * ns] = field(3 + k)
    parts = [over[k * n : k * n + n] for k in range(groups(ns))]
    out[4 * ns : 4 * ns + n] = total(
        [pltpu.roll(p, 16 * k, 1) if k else p for k, p in enumerate(parts)]
    )


def coarse_kernel(
    pos, columns, others, wider, far, near_side, g4, inv4, gm, gmt, up4, gm_first, gmt_first,
    gm_last, gmt_last,
    res, u, sol, acc, face_a, face_b, vals, x2, es, ea, er, es0, ea0, er0, dg, ri,
):
    ns = x2.shape[0]
    na = x2.shape[1] // LANES
    width = na * LANES

    n = ns // groups(ns)
    size = 4 * ns + n
    even_a = is_even(pos, 1)

    def rows_of(d, start, count):
        at = d // 2 * size + start
        x, y = columns[at : at + count], others[at : at + count]
        return jnp.where(even_a, x, y) if d % 2 == 0 else jnp.where(even_a, y, x)

    def field(k):
        return [rows_of(d, k * ns, ns) for d in range(na)]

    def side(d):
        packed = rows_of(d, 4 * ns, n)
        parts = [pltpu.roll(packed, LANES - 16 * k, 1) if k else packed for k in range(groups(ns))]
        return jnp.where(iota(ns, 1) < 16, jnp.concatenate(parts, axis=0), 0.0)

    def roll_l(x, k):
        return pltpu.roll(x, k % width, 1)

    lane = iota(ns, 1)
    wall, top = lane % 16 == 0, lane % 16 == 15
    at = [slice(d * LANES, d * LANES + LANES) for d in range(na)]

    def towards_next(y, d):
        return jnp.where(lane < LANES - 16, y[d], y[(d + 1) % na])

    def towards_last(y, d):
        return jnp.where(lane < 16, y[d - 1], y[d])

    ea_all, er_all = field(2), field(3)
    ea_roll = [pltpu.roll(t, 16, 1) for t in ea_all]
    for d, es_d in enumerate(field(1)):
        es0_d, ea0_d = pltpu.roll(es_d, 1, 0), towards_last(ea_roll, d)
        er0_d = pltpu.roll(er_all[d], 1, 1)
        both = es_d + es0_d + ea_all[d] + ea0_d + er_all[d] + er0_d
        es[:, at[d]], ea[:, at[d]] = es_d, ea_all[d]
        es0[:, at[d]], ea0[:, at[d]] = es0_d, ea0_d
        er[:, at[d]] = jnp.where(wall | top, 0.0, er_all[d])
        er0[:, at[d]] = jnp.where(wall | (lane % 16 == 1), 0.0, er0_d)
        dg[:, at[d]] = jnp.where(wall, 0.0, both)
        ri[:, at[d]] = jnp.where(wall, 0.0, 1.0 / jnp.where(wall, 1.0, both))

    def inner(terms):
        return jnp.sum(jnp.sum(total(terms), axis=0, keepdims=True), axis=1, keepdims=True)

    first = field(0)
    r = [first[d] + side((d - 1) % na) for d in range(na)]
    p = [ri[:, at[d]] * r[d] for d in range(na)]
    gz = inner([r[d] * p[d] for d in range(na)])
    x = [jnp.zeros_like(t) for t in r]
    for it in range(ITERS):
        ahead = [pltpu.roll(t, LANES - 16, 1) for t in p]
        behind = [pltpu.roll(t, 16, 1) for t in p]
        q, terms = [], []
        for d in range(na):
            t, k = p[d], at[d]
            out = dg[:, k] * t
            out = out - es[:, k] * pltpu.roll(t, ns - 1, 0) - es0[:, k] * pltpu.roll(t, 1, 0)
            out = out - ea[:, k] * towards_next(ahead, d) - ea0[:, k] * towards_last(behind, d)
            out = out - er[:, k] * pltpu.roll(t, LANES - 1, 1) - er0[:, k] * pltpu.roll(t, 1, 1)
            q.append(out)
            terms.append(t * out)
        alpha = gz / inner(terms)
        x = [x[d] + alpha * p[d] for d in range(na)]
        if it + 1 < ITERS:
            r = [r[d] - alpha * q[d] for d in range(na)]
            z = [ri[:, at[d]] * r[d] for d in range(na)]
            new = inner([r[d] * z[d] for d in range(na)])
            beta = new / gz
            p = [z[d] + beta * p[d] for d in range(na)]
            gz = new
    for d in range(na):
        x2[:, at[d]] = x[d]

    s, a = pos[0], pos[1]
    blocks = [lax.rem(a + na - 1, na), a, lax.rem(a + 1, na)]
    for t in range(4):
        line = x2[pl.ds(lax.rem(s + ns - 1 + t, ns), 1), :]
        for j in range(2):
            for k in range(2):
                n = 4 * t + 2 * j + k
                vals[n : n + 1, :] = roll_l(line, -(16 * j + k)) if j + k else line
    near = iota(16, 1) < HALF
    b = [
        pltpu.roll(vals[:, pl.ds(pl.multiple_of(t * LANES, LANES), LANES)], HALF, 1) for t in blocks
    ]
    ext = jnp.concatenate([jnp.where(near, b[0], b[1]), jnp.where(near, b[1], b[2])], axis=1)
    rise = dot(up4[...], ext)
    even = is_even(pos, 0)
    x, y = wide(far, 0, 64), wide(near_side, 0, 64)
    below, above = jnp.where(even, x, y), jnp.where(even, y, x)
    low = dot(gmt_last[...], dot(gm_last[...], rise[:64]) * below[:48]) + below[48:]
    high = dot(gmt_first[...], dot(gm_first[...], rise[128:]) * above[:48]) + above[48:]
    flux = dot(gm[...], rise[64:128] + wide(wider, 64, 64)) * wide(g4, 0, 192)
    back = dot(gmt[...], flux)
    put(acc, 0, 16, back[:16] + low)
    put(acc, 16, 32, back[16:48])
    put(acc, 48, 16, back[48:] + high)
    join_mid(acc)
    put(sol, 0, 64, wide(wider, 128, 64) + rise[64:128])
    for h, r in tiles(64):
        now = wider[h, r : r + 8] - acc[h, r : r + 8]
        new = inv4[h, r : r + 8] * now * (1.0 / CENTER)
        res[h, r : r + 8] = now
        u[h, r : r + 8] = new
        sol[h, r : r + 8] += new
    mid_apply(u, g4, acc, gm, gmt)
    join_mid(acc)
    send_faces(acc, even, face_a, face_b, 16)


def sixth_kernel(
    pos, res, u, sol, acc, a, b, inv4, up8, kept, g8, bd, bdt,
    out, v8, acc2, face_a, face_b, y4,
):
    even = is_even(pos, 0)
    for h, r in tiles(64):
        now = res[h, r : r + 8] - full_of(acc, (even, a, b), h, r)
        new = KEEP * u[h, r : r + 8] + GAIN * inv4[h, r : r + 8] * now
        y4[h, r : r + 8] = sol[h, r : r + 8] + new
    put(v8, 0, 512, dot(up8[...], wide(y4, 0, 64)))
    for h, r in tiles(512):
        e8 = v8[h, r : r + 8]
        out[h, r : r + 8] = kept[h, r : r + 8] + e8
        v8[h, r : r + 8] = kept[h, 1024 + r : 1032 + r] + e8
    fine_front(v8, g8, acc2, bd, bdt)
    send_faces(acc2, even, face_a, face_b, 64)


def seventh_kernel(
    pos, kept, sol, acc, a, b, inv8, g8, bd, bdt, res, out, u, acc2, face_a, face_b
):
    even = is_even(pos, 0)
    for h, r in tiles(512):
        now = kept[h, 512 + r : 520 + r] - full_of(acc, (even, a, b), h, r)
        new = inv8[h, r : r + 8] * now * (1.0 / CENTER)
        res[h, r : r + 8] = now
        u[h, r : r + 8] = new
        out[h, r : r + 8] = sol[h, r : r + 8] + new
    fine_front(u, g8, acc2, bd, bdt)
    for out, plane in ((face_b, jnp.where(even, 448, 0)), (face_a, jnp.where(even, 0, 448))):
        rows = pl.ds(pl.multiple_of(plane, 8), 64)
        out[...] = own_part(acc2[0, rows, :], acc2[1, rows, :])


def inner_last_kernel(u, g8, acc, res, sol, inv8, bd, bdt, out, full):
    for h, r in tiles(384):
        full[h, 64 + r : 72 + r] = acc[h, 64 + r : 72 + r]
    fine_cross(u, g8, full, bd, bdt, PLANES[1:])
    join_fine(full, range(1, 7))
    for r in range(64, 448, 8):
        halves = []
        for h in range(2):
            now = res[h, r : r + 8] - full[h, r : r + 8]
            new = KEEP * u[h, r : r + 8] + GAIN * inv8[h, r : r + 8] * now
            halves.append(sol[h, r : r + 8] + new)
        out[r - 64 : r - 56] = own_part(*halves)


def last_kernel(pos, res, sol, u, acc, a, b, inv8, inner, out):
    even = is_even(pos, 0)
    out[64:448] = inner[...]
    for r in [*range(0, 64, 8), *range(448, 512, 8)]:
        halves = []
        for h in range(2):
            inv = inv8[h, r : r + 8]
            now = res[h, r : r + 8] - acc[h, r : r + 8]
            halves.append(sol[h, r : r + 8] + KEEP * u[h, r : r + 8] + GAIN * inv * now)
        at = r % 64
        x, y = a[at : at + 8], b[at : at + 8]
        face = jnp.where(even, x, y) if r < 64 else jnp.where(even, y, x)
        inv = own_part(inv8[0, r : r + 8], inv8[1, r : r + 8])
        out[r : r + 8] = own_part(*halves) - GAIN * inv * face


def call(kernel, args, outs, scratch=(), scalars=1):
    vmem = pl.BlockSpec(memory_space=pltpu.VMEM)
    smem = pl.BlockSpec(memory_space=pltpu.SMEM)
    arrays = [x for x in args if not isinstance(x, str)]
    named = len(arrays) < len(args)

    def body(*refs):
        rest = iter(refs)
        given = [next(rest) for _ in arrays[: len(arrays) - named]]
        held = next(rest) if named else None
        given = iter(given)
        full = [Constant(held, x) if isinstance(x, str) else next(given) for x in args]
        kernel(*full, *rest)

    if named:
        arrays.append(PACK)
    return pl.pallas_call(
        body,
        out_shape=[jax.ShapeDtypeStruct(s, F32) for s in outs],
        in_specs=[smem] * scalars + [vmem] * (len(arrays) - scalars),
        out_specs=[vmem] * len(outs),
        scratch_shapes=[pltpu.VMEM(s, F32) for s in scratch],
        compiler_params=pltpu.CompilerParams(vmem_limit_bytes=32 * 1024 * 1024),
        name=kernel.__name__,
    )(*arrays)


def exchange(far, near, axis):
    size = lax.axis_size(axis)
    pairs_far = [(i, (i + 1 if i % 2 else i - 1) % size) for i in range(size)]
    pairs_near = [(i, i ^ 1) for i in range(size)]
    return lax.ppermute(far, axis, pairs_far), lax.ppermute(near, axis, pairs_near)


def spread(x, axis, groups=None):
    size = len(groups[0]) if groups else lax.axis_size(axis)
    copies = jnp.broadcast_to(x[None], (size,) + x.shape)
    return lax.all_to_all(copies, axis, 0, 0, axis_index_groups=groups).reshape(-1, LANES)


def on_device(element_load, metric, element_order):
    ns, na = lax.axis_size("stream"), lax.axis_size("azim")
    fine, mid = (2, 512, LANES), (2, 64, LANES)
    face8, face4 = [(2, 64, LANES)] * 2, [(2, 16, LANES)] * 2
    pos = jnp.stack([lax.axis_index("stream"), lax.axis_index("azim")]).astype(jnp.int32)
    g, rolled, a, b = call(
        order_kernel,
        (pos, metric.reshape(1536, LANES), element_load.reshape(512, LANES), element_order),
        [(1536, LANES), (512, LANES), (1024, LANES), (1024, LANES)],
    )
    a, b = exchange(a, b, "azim")
    (diag,) = call(own_kernel, (g, "bsq"), [(512, LANES)], scalars=0)

    def inner(u, acc):
        (acc,) = call(inner_kernel, (u, g8, acc, "bd", "bdt"), [fine], (), 0)
        return acc

    g8, load, diag8, a, b = call(
        setup_kernel,
        (pos, g, rolled, diag, a, b, "bsq"),
        [(2, 1536, LANES), fine, fine] + [(2, 128, LANES)] * 2,
        [(1536, LANES), (512, LANES)],
    )
    a, b = exchange(a, b, "stream")
    res8, inv8, u8, acc, a, b = call(
        first_kernel,
        (pos, load, diag8, a, b, g8, "bd", "bdt"),
        [fine, fine, fine, fine] + face8,
    )
    a, b = exchange(a, b, "stream")
    acc = inner(u8, acc)
    g4, diag4, edges, upper = call(
        coarsen_kernel,
        (g8, "w4", "w2", "sample", "sq4"),
        [(2, 192, LANES), mid, (8, LANES), (8, LANES)],
        scalars=0,
    )
    kept, t4, a, b = call(
        second_kernel,
        (pos, res8, inv8, acc, a, b, diag4, upper, g8, "bd", "bdt", "down8"),
        [(2, 1536, LANES), mid] + [(2, 40, LANES)] * 2,
        [fine, fine, (512, 2 * LANES)],
    )
    a, b = exchange(a, b, "stream")
    res4, inv4, edges, acc, a, b = call(
        third_kernel,
        (pos, t4, diag4, edges, a, b, g4, "gm", "gmt"),
        [mid, mid, (8, LANES), mid] + face4,
        [mid],
    )
    a, b = exchange(a, b, "stream")
    corners, *kept4 = call(
        fourth_kernel,
        (pos, res4, acc, inv4, edges, a, b, g4, "gm", "gmt", "m4", "down4"),
        [(8, LANES), (192, LANES), (192, LANES)],
        [(2, 192, LANES), mid],
    )
    columns = spread(corners, "stream")
    a, b = exchange(*kept4, "azim")
    wider, a, b = call(
        side_kernel,
        (pos, *kept4, a, b, g4, "gm", "gmt"),
        [(2, 192, LANES)] + face8,
        [mid],
    )
    sides = exchange(a, b, "stream")
    size = 4 * ns + ns // groups(ns)
    (columns,) = call(
        column_kernel, (columns, wider), [(size, LANES)], (), 0
    )
    cores = [list(range(core, na, 2)) for core in range(2)]
    columns = spread(columns, "azim", cores)
    others = lax.ppermute(columns, "azim", [(i, i ^ 1) for i in range(na)])
    whole = (ns, na * LANES)
    res4, u4, sol4, acc, a, b = call(
        coarse_kernel,
        (
            pos,
            columns,
            others,
            wider,
            *sides,
            g4,
            inv4,
            "gm",
            "gmt",
            "up4",
            "gm_first",
            "gmt_first",
            "gm_last",
            "gmt_last",
        ),
        [mid, mid, mid, mid] + face4,
        [(16, na * LANES)] + [whole] * 9,
    )
    a, b = exchange(a, b, "stream")
    sol8, v8, acc, a, b = call(
        sixth_kernel,
        (pos, res4, u4, sol4, acc, a, b, inv4, "up8", kept, g8, "bd", "bdt"),
        [fine, fine, fine] + face8,
        [mid],
    )
    a, b = exchange(a, b, "stream")
    acc = inner(v8, acc)
    res8, sol8, u8, acc, a, b = call(
        seventh_kernel,
        (pos, kept, sol8, acc, a, b, inv8, g8, "bd", "bdt"),
        [fine, fine, fine, fine] + [(64, LANES)] * 2,
    )
    a, b = exchange(a, b, "stream")
    (inside,) = call(
        inner_last_kernel,
        (u8, g8, acc, res8, sol8, inv8, "bd", "bdt"),
        [(384, LANES)],
        [fine],
        scalars=0,
    )
    (out,) = call(last_kernel, (pos, res8, sol8, u8, acc, a, b, inv8, inside), [(512, LANES)])
    return out.reshape(element_load.shape)


def solution(mesh):
    placed = (P(None, "stream", "azim"), P(None, None, "stream", "azim"), P("stream", "azim"))
    return jax.shard_map(
        on_device, mesh=mesh, in_specs=placed, out_specs=P(None, "stream", "azim"), check_vma=False
    )
```

```python
import jax
import jax.numpy as jnp
import numpy as np
from jax import lax
from jax.experimental import pallas as pl
from jax.experimental.pallas import tpu as pltpu
from jax.sharding import PartitionSpec as P

ITERS = 6
LOW_EIG = 0.3
HIGH_EIG = 3.0
CENTER = 0.5 * (HIGH_EIG + LOW_EIG)
HALF_WIDTH = 0.5 * (HIGH_EIG - LOW_EIG)
FIRST_RHO = HALF_WIDTH / CENTER
SECOND_RHO = 1.0 / (2.0 * CENTER / HALF_WIDTH - FIRST_RHO)
KEEP = SECOND_RHO * FIRST_RHO
GAIN = 2.0 * SECOND_RHO / HALF_WIDTH
LANES = 128
HALF = 64
F32 = jnp.float32


def legendre_pair(degree, places):
    previous = places * 0.0 + 1.0
    current = places.copy()
    for k in range(2, degree + 1):
        following = ((2 * k - 1) * places * current - (k - 1) * previous) / k
        previous = current
        current = following
    return (current, previous)


def gll_table(points):
    degree = points - 1
    places = np.cos(np.pi * np.arange(points) / degree)
    for _ in range(60):
        top, below = legendre_pair(degree, places)
        places = places - (places * top - below) / (points * top)
    nodes = np.sort(places)
    nodes[0] = -1.0
    nodes[-1] = 1.0
    at_nodes = legendre_pair(degree, nodes)[0]
    weights = 2.0 / (degree * (degree + 1) * at_nodes**2)
    deriv = np.zeros((points, points))
    for i in range(points):
        for j in range(points):
            if i != j:
                deriv[i, j] = at_nodes[i] / (at_nodes[j] * (nodes[i] - nodes[j]))
    deriv[0, 0] = -degree * (degree + 1) / 4.0
    deriv[-1, -1] = degree * (degree + 1) / 4.0
    return (nodes, weights, deriv)


def lagrange_table(source, target):
    out = np.ones((len(target), len(source)))
    for j in range(len(source)):
        for k in range(len(source)):
            if k != j:
                out[:, j] *= (target - source[k]) / (source[j] - source[k])
    return out


N8, W8, D8 = gll_table(8)
N4, W4, D4 = gll_table(4)
N2, W2, D2 = gll_table(2)


def kron3(a, b, c):
    return np.kron(np.kron(a, b), c)


def cube(w):
    return (w[:, None, None] * w[None, :, None] * w[None, None, :]).reshape(-1)


def share(n):
    edge = np.ones(n)
    edge[0] = edge[-1] = 0.5
    return cube(edge)


def grads(d):
    i = np.eye(d.shape[0])
    return [kron3(d, i, i), kron3(i, d, i), kron3(i, i, d)]


def f32(x):
    return np.asarray(x, np.float32)


def lanes_of(column):
    return np.repeat(f32(column)[:, None], LANES, axis=1)


UP8 = lagrange_table(N4, N8)
UP4 = lagrange_table(N2, N4)
TO4 = lagrange_table(N8, N4)
TO2 = lagrange_table(N8, N2)

C_BD = f32(np.kron(np.eye(16), D8))
C_BDT = f32(np.kron(np.eye(16), D8.T))
C_BSQ = f32(np.kron(np.eye(16), (D8 * D8).T))
C_SAMPLE = f32(np.concatenate([kron3(TO4, TO4, TO4), kron3(TO2, TO2, TO2)]))
C_UP8 = f32(kron3(UP8, UP8, UP8))
C_DOWN8 = f32(kron3(UP8, UP8, UP8).T)
C_UP4 = f32(kron3(UP4, UP4, UP4))
C_DOWN4 = f32(kron3(UP4, UP4, UP4).T)
C_UP4X3 = np.zeros((192, 16), np.float32)
for layer in range(3):
    C_UP4X3[64 * layer : 64 * layer + 64, 4 * layer : 4 * layer + 8] = C_UP4
C_G4 = f32(np.concatenate(grads(D4)))
C_G4T = f32(np.concatenate(grads(D4)).T)
C_SQ4 = f32((np.concatenate(grads(D4)) ** 2).T)
C_W4 = lanes_of(cube(W4) / np.exp(kron3(TO4, TO4, TO4) @ np.log(cube(W8))))
C_W2 = lanes_of(cube(W2) / np.exp(kron3(TO2, TO2, TO2) @ np.log(cube(W8))))
C_M4 = lanes_of(share(4))
FIRST = np.r_[0:16, 64:80, 128:144]
LAST = np.r_[48:64, 112:128, 176:192]


def plane_back(plane, rows):
    eye = np.eye(16, dtype=np.float32)
    return np.concatenate([eye, C_G4T[plane : plane + 16, rows[16:]]], axis=1)


CONSTANTS = {
    "bd": C_BD, "bdt": C_BDT, "bsq": C_BSQ, "sample": C_SAMPLE, "w4": C_W4, "w2": C_W2,
    "sq4": C_SQ4, "gm": C_G4, "gmt": C_G4T, "m4": C_M4, "down8": C_DOWN8, "down4": C_DOWN4,
    "up4": C_UP4X3, "up8": C_UP8, "gm_first": C_G4[FIRST], "gmt_first": plane_back(0, FIRST),
    "gm_last": C_G4[LAST], "gmt_last": plane_back(48, LAST),
}


def pack_constants():
    rows, places, start = [], {}, 0
    for name, value in CONSTANTS.items():
        blocks = -(-value.shape[1] // LANES)
        padded = np.zeros((value.shape[0], blocks * LANES), np.float32)
        padded[:, : value.shape[1]] = value
        rows += [padded[:, k * LANES : (k + 1) * LANES] for k in range(blocks)]
        places[name] = (start, value.shape, blocks)
        start += value.shape[0] * blocks
    return np.concatenate(rows), places


PACK, PLACES = pack_constants()


class Constant:
    def __init__(self, ref, name):
        self.ref, self.name = ref, name

    def __getitem__(self, index):
        start, (rows, columns), blocks = PLACES[self.name]
        parts = []
        for k in range(blocks):
            width = min(LANES, columns - k * LANES)
            parts.append(self.ref[start + k * rows : start + (k + 1) * rows, :width])
        value = parts[0] if blocks == 1 else jnp.concatenate(parts, axis=1)
        return value if index is Ellipsis else value[index]


def dot(a, b, precision=lax.Precision.HIGH):
    return jnp.dot(a, b, preferred_element_type=F32, precision=precision)


def iota(rows, axis):
    return lax.broadcasted_iota(jnp.int32, (rows, LANES), axis)


def wide(ref, start, size):
    return jnp.concatenate([ref[0, start : start + size], ref[1, start : start + size]], axis=1)


def put(ref, start, size, value):
    ref[0, start : start + size] = value[:, :LANES]
    ref[1, start : start + size] = value[:, LANES:]


def total(terms):
    out = terms[0]
    for t in terms[1:]:
        out = out + t
    return out


def contract(v, matrix, sign):
    n = len(v)
    h = n // 2
    even = [v[k] + v[n - 1 - k] for k in range(h)]
    odd = [v[k] - v[n - 1 - k] for k in range(h)]
    out = [None] * n
    for i in range(h):
        p = total([even[k] * float(0.5 * (matrix[i, k] + matrix[i, n - 1 - k])) for k in range(h)])
        q = total([odd[k] * float(0.5 * (matrix[i, k] - matrix[i, n - 1 - k])) for k in range(h)])
        out[i] = p + q
        out[n - 1 - i] = q - p if sign < 0 else p - q
    return out


def fine_rows(s, a):
    return s * 64 + a * 8


PLANES = [(0, 7), (1, 2), (3, 4), (5, 6)]


def pair(ref, p, base=0):
    return jnp.concatenate([wide(ref, base + 64 * s, 64) for s in p], axis=0)


def put_pair(ref, p, value):
    for k, s in enumerate(p):
        put(ref, 64 * s, 64, value[64 * k : 64 * k + 64])


def fine_stream(u, g, acc):
    for h in range(2):
        for a in range(8):
            at = [fine_rows(s, a) for s in range(8)]
            grad = contract([u[h, r : r + 8] for r in at], D8, -1)
            back = contract([grad[s] * g[h, r : r + 8] for s, r in enumerate(at)], D8.T, -1)
            for s, r in enumerate(at):
                acc[h, r : r + 8] = back[s]


def fine_cross(u, g, acc, bd, bdt, pairs):
    for p in pairs:
        flux = dot(bd[...], pair(u, p)) * pair(g, p, 1024)
        put_pair(acc, p, pair(acc, p) + dot(bdt[...], flux))
        for s in p:
            for h in range(2):
                at = [fine_rows(s, a) for a in range(8)]
                grad = contract([u[h, r : r + 8] for r in at], D8, -1)
                flux = [grad[a] * g[h, 512 + r : 520 + r] for a, r in enumerate(at)]
                back = contract(flux, D8.T, -1)
                for a, r in enumerate(at):
                    acc[h, r : r + 8] += back[a]


def fine_apply(u, g, acc, bd, bdt):
    fine_stream(u, g, acc)
    fine_cross(u, g, acc, bd, bdt, PLANES)


def fine_front(u, g, acc, bd, bdt):
    fine_stream(u, g, acc)
    fine_cross(u, g, acc, bd, bdt, PLANES[:1])
    join_fine(acc, (0, 7))


def left(x0, x1):
    near = iota(x0.shape[0], 1) < LANES - 16
    y0, y1 = pltpu.roll(x0, LANES - 16, 1), pltpu.roll(x1, LANES - 16, 1)
    return jnp.where(near, y0, y1), jnp.where(near, y1, y0)


def right(x0, x1):
    near = iota(x0.shape[0], 1) >= 16
    y0, y1 = pltpu.roll(x0, 16, 1), pltpu.roll(x1, 16, 1)
    return jnp.where(near, y0, y1), jnp.where(near, y1, y0)


def join_radial(x, points, start, rows):
    place = iota(rows, 1) % 16
    first = pl.ds(start, rows, stride=points)
    last = pl.ds(start + points - 1, rows, stride=points)
    for h in range(2):
        view = x.at[h]
        low, high = view[first, :], view[last, :]
        view[first, :] = jnp.where(place == 0, 0.0, low + pltpu.roll(high, 1, 1))
        view[last, :] = jnp.where(place == 15, 0.0, high + pltpu.roll(low, LANES - 1, 1))


def join_fine(x, planes=range(8)):
    for s in planes:
        join_radial(x, 8, 64 * s, 8)
        lo, hi = fine_rows(s, 0), fine_rows(s, 7)
        low = [x[h, lo : lo + 8] for h in range(2)]
        high = [x[h, hi : hi + 8] for h in range(2)]
        to_low, to_high = right(*high), left(*low)
        for h in range(2):
            x[h, lo : lo + 8] = low[h] + to_low[h]
            x[h, hi : hi + 8] = high[h] + to_high[h]


def join_mid(x):
    join_radial(x, 4, 0, 16)
    first = iota(8, 0) < 4
    for s in range(4):
        lo, hi = s * 16, s * 16 + 8
        low = [x[h, lo : lo + 8] for h in range(2)]
        high = [x[h, hi : hi + 8] for h in range(2)]
        to_low = right(*[pltpu.roll(t, 4, 0) for t in high])
        to_high = left(*[pltpu.roll(t, 4, 0) for t in low])
        for h in range(2):
            x[h, lo : lo + 8] = low[h] + jnp.where(first, to_low[h], 0.0)
            x[h, hi : hi + 8] = high[h] + jnp.where(first, 0.0, to_high[h])


def is_even(place, k):
    return lax.rem(place[k], 2) == 0


def full_of(x, faces, h, r, offset=0):
    even, far, near = faces
    rows = x.shape[1]
    plane = {512: 64, 64: 16}[rows]
    value = x[h, r : r + 8]
    if r < plane:
        at = offset + r
        return value + jnp.where(even, far[h, at : at + 8], near[h, at : at + 8])
    if r >= rows - plane:
        at = offset + r - (rows - plane)
        return value + jnp.where(even, near[h, at : at + 8], far[h, at : at + 8])
    return value


def send_faces(x, even, far, near, plane, offset=0):
    rows = x.shape[1]
    last = rows - plane
    one = pl.multiple_of(jnp.where(even, last, 0), 8)
    two = pl.multiple_of(jnp.where(even, 0, last), 8)
    for h in range(2):
        near[h, offset : offset + plane] = x[h, pl.ds(one, plane), :]
        far[h, offset : offset + plane] = x[h, pl.ds(two, plane), :]


def wall_mask(points):
    place, node = iota(8, 1) % 16, iota(8, 0) % points
    return ((node == 0) & (place == 0)) | ((node == points - 1) & (place == 15))


def own_part(half0, half1):
    near = iota(half0.shape[0], 1) < HALF
    return pltpu.roll(jnp.where(near, half1, half0), HALF, 1)


def tiles(rows):
    return [(h, r) for h in range(2) for r in range(0, rows, 8)]


def mid_apply(u, g4, acc, gm, gmt):
    flux = dot(gm[...], wide(u, 0, 64)) * wide(g4, 0, 192)
    put(acc, 0, 64, dot(gmt[...], flux))


def fine_diagonal(g, diag, bsq):
    square = (D8 * D8).T
    for c in range(4):
        rows = slice(128 * c, 128 * c + 128)
        diag[rows] = dot(bsq[...], g[1024 + 128 * c : 1152 + 128 * c])
    for axis in range(2):
        for fixed in range(8):
            at = [fine_rows(k, fixed) if axis == 0 else fine_rows(fixed, k) for k in range(8)]
            back = contract([g[512 * axis + r : 512 * axis + r + 8] for r in at], square, 1)
            for k, r in enumerate(at):
                diag[r : r + 8] += back[k]


def halves_up_down(a, b):
    near = iota(8, 1) < HALF
    up = jnp.where(near, a, pltpu.roll(b, HALF, 1))
    return up, jnp.where(near, pltpu.roll(a, HALF, 1), b)


def before_after(even, x, y):
    p, n = jnp.where(even, x, y), jnp.where(even, y, x)
    near = iota(8, 1) < HALF
    first = (jnp.where(near, p, 0.0), jnp.where(near, 0.0, pltpu.roll(n, HALF, 1)))
    second = (jnp.where(near, pltpu.roll(p, HALF, 1), 0.0), jnp.where(near, 0.0, n))
    return first, second


def order_kernel(pos, metric, load, order, g, rolled, far, near):
    even = is_even(pos, 1)
    slots = jnp.broadcast_to(pltpu.roll(order[...], HALF, 1), (8, LANES))
    wr = total([jnp.where(iota(8, 0) == k, float(W8[k]), 0.0) for k in range(8)])
    for r in range(0, 1536, 8):
        scale = wr * float(W8[(r % 512) // 64] * W8[(r // 8) % 8])
        g[r : r + 8] = jnp.take_along_axis(metric[r : r + 8], slots, axis=1) * scale
    for r in range(0, 512, 8):
        rolled[r : r + 8] = pltpu.roll(load[r : r + 8], HALF, 1)
    for r in range(0, 1024, 8):
        other = g[1024 + r : 1032 + r] if r < 512 else rolled[r - 512 : r - 504]
        up, down = halves_up_down(g[r : r + 8], other)
        far[r : r + 8] = jnp.where(even, down, up)
        near[r : r + 8] = jnp.where(even, up, down)


def own_kernel(g, bsq, diag):
    fine_diagonal(g, diag, bsq)


def setup_kernel(
    pos, g, rolled, diag, x, y, bsq, g8, load, diag8, face_a, face_b, ghost, ghost_diag
):
    near = iota(8, 1) < HALF
    even_a = is_even(pos, 1)

    def place(out, row, own, sides):
        out[0, row : row + 8] = jnp.where(near, sides[0], own)
        out[1, row : row + 8] = jnp.where(near, own, sides[1])

    for r in range(0, 1024, 8):
        first, second = before_after(even_a, x[r : r + 8], y[r : r + 8])
        place(g8, r, g[r : r + 8], first)
        ghost[r : r + 8] = first[0] + first[1]
        if r < 512:
            place(g8, 1024 + r, g[1024 + r : 1032 + r], second)
            ghost[1024 + r : 1032 + r] = second[0] + second[1]
        else:
            place(load, r - 512, rolled[r - 512 : r - 504], second)
    fine_diagonal(ghost, ghost_diag, bsq)
    for r in range(0, 512, 8):
        side = ghost_diag[r : r + 8]
        place(diag8, r, diag[r : r + 8], (side, side))
    for x in (load, diag8):
        join_fine(x)
    even = is_even(pos, 0)
    send_faces(load, even, face_a, face_b, 64)
    send_faces(diag8, even, face_a, face_b, 64, 64)


def coarsen_kernel(g8, w4, w2, sample, sq4, g4, diag4, edges, upper):
    low = []
    for d in range(3):
        logs = jnp.log(wide(g8, 512 * d, 512))
        coarse = jnp.exp(dot(sample[...], logs, lax.Precision.HIGHEST))
        put(g4, 64 * d, 64, coarse[:64] * jnp.concatenate([w4[...], w4[...]], axis=1))
        low.append([coarse[64:72, :LANES] * w2[...], coarse[64:72, LANES:] * w2[...]])
    put(diag4, 0, 64, dot(sq4[...], wide(g4, 0, 192)))
    join_mid(diag4)

    def corner(d, i, j, k):
        row = 4 * i + 2 * j + k
        return [t[row : row + 1] for t in low[d]]

    def add(x, y):
        return [x[0] + y[0], x[1] + y[1]]

    def quarter(x):
        return [0.25 * x[0], 0.25 * x[1]]

    def outward(x):
        return [pltpu.roll(x[0], 1, 1), pltpu.roll(x[1], 1, 1)]

    es = [[quarter(add(corner(0, 0, j, k), corner(0, 1, j, k))) for k in range(2)] for j in range(2)]
    ea = [[quarter(add(corner(1, i, 0, k), corner(1, i, 1, k))) for k in range(2)] for i in range(2)]
    er = [[quarter(add(corner(2, i, j, 0), corner(2, i, j, 1))) for j in range(2)] for i in range(2)]
    col = [add(es[0][k], list(right(*es[1][k]))) for k in range(2)]
    edge_s = add(col[0], outward(col[1]))
    edge_a = [add(ea[i][0], outward(ea[i][1])) for i in range(2)]
    edge_r = [add(er[i][0], list(right(*er[i][1]))) for i in range(2)]
    off_wall = iota(1, 1) % 16 != 0
    rows = [jnp.where(off_wall, own_part(*x), 0.0) for x in (edge_s, edge_a[0], edge_a[1])]
    rows += [own_part(*x) for x in edge_r]
    none = jnp.zeros((5, LANES), F32)
    edges[...] = jnp.concatenate([rows[0], rows[1], rows[3], none], axis=0)
    upper[...] = jnp.concatenate([rows[0], rows[2], rows[4], none], axis=0)


def first_kernel(
    pos, load, diag8, a, b, g8, bd, bdt, res, inv8, u, acc, face_a, face_b
):
    even = is_even(pos, 0)
    got = (even, a, b)
    wall8 = wall_mask(8)
    for h, r in tiles(512):
        diag = full_of(diag8, got, h, r, 64)
        inv = jnp.where(wall8, 0.0, 1.0 / jnp.where(wall8, 1.0, diag))
        full = full_of(load, got, h, r)
        res[h, r : r + 8] = full
        inv8[h, r : r + 8] = inv
        u[h, r : r + 8] = inv * full * (1.0 / CENTER)
    fine_front(u, g8, acc, bd, bdt)
    send_faces(acc, even, face_a, face_b, 64)


def inner_kernel(u, g8, start, bd, bdt, acc):
    for h, r in tiles(512):
        acc[h, r : r + 8] = start[h, r : r + 8]
    fine_cross(u, g8, acc, bd, bdt, PLANES[1:])
    join_fine(acc, range(1, 7))


def second_kernel(
    pos, res, inv8, acc, a, b, diag4, upper, g8, bd, bdt, down8,
    kept, t4, face_a, face_b, u, back, part,
):
    even = is_even(pos, 0)
    got = (even, a, b)
    edge = jnp.where((iota(8, 0) == 0) | (iota(8, 0) == 7), 0.5, 1.0)
    for h, r in tiles(512):
        inv, before = inv8[h, r : r + 8], res[h, r : r + 8]
        now = before - full_of(acc, got, h, r)
        old = inv * before * (1.0 / CENTER)
        new = KEEP * old + GAIN * inv * now
        kept[h, r : r + 8] = old + new
        kept[h, 512 + r : 520 + r] = now
        kept[h, 1024 + r : 1032 + r] = new
        u[h, r : r + 8] = new
    fine_apply(u, g8, back, bd, bdt)
    for h, r in tiles(512):
        s, c = r // 64, (r // 8) % 8
        scale = (0.5 if s in (0, 7) else 1.0) * (0.5 if c in (0, 7) else 1.0)
        part[r : r + 8, h * LANES : h * LANES + LANES] = (
            kept[h, 512 + r : 520 + r] * (edge * scale) - back[h, r : r + 8]
        )
    put(t4, 0, 64, dot(down8[...], part[...]))
    join_mid(t4)
    send_faces(t4, even, face_a, face_b, 16)
    send_faces(diag4, even, face_a, face_b, 16, 16)
    for face in (face_a, face_b):
        for h in range(2):
            face[h, 32:40] = upper[...]


def third_kernel(
    pos, t4, diag4, edges, a, b, g4, gm, gmt, res, inv4, edge, acc, face_a, face_b, u
):
    even = is_even(pos, 0)
    got = (even, a, b)
    wall = wall_mask(4)
    for h, r in tiles(64):
        full = full_of(t4, got, h, r)
        diag = full_of(diag4, got, h, r, 16)
        inv = jnp.where(wall, 0.0, 1.0 / jnp.where(wall, 1.0, diag))
        res[h, r : r + 8] = full
        inv4[h, r : r + 8] = inv
        u[h, r : r + 8] = inv * full * (1.0 / CENTER)
    lower = jnp.where(even, a[0, 32:40], b[0, 32:40])
    edge[...] = edges[...] + jnp.where(iota(8, 0) == 0, 0.0, lower)
    mid_apply(u, g4, acc, gm, gmt)
    join_mid(acc)
    send_faces(acc, even, face_a, face_b, 16)


def fourth_kernel(
    pos, res, acc, inv4, edge, a, b, g4, gm, gmt, m4, down4, corners, one, two, keep, part
):
    got = (is_even(pos, 0), a, b)
    for h, r in tiles(64):
        inv, before = inv4[h, r : r + 8], res[h, r : r + 8]
        now = before - full_of(acc, got, h, r)
        old = inv * before * (1.0 / CENTER)
        new = KEEP * old + GAIN * inv * now
        keep[h, r : r + 8] = now
        keep[h, 64 + r : 72 + r] = new
        keep[h, 128 + r : 136 + r] = old + new
    even_a = is_even(pos, 1)
    one[...] = jnp.where(even_a, keep[0], keep[1])
    two[...] = jnp.where(even_a, keep[1], keep[0])
    flux = dot(gm[...], wide(keep, 64, 64)) * wide(g4, 0, 192)
    put(part, 0, 64, dot(gmt[...], flux))
    for h, r in tiles(64):
        part[h, r : r + 8] = m4[r : r + 8] * keep[h, r : r + 8] - part[h, r : r + 8]
    low = dot(down4[...], wide(part, 0, 64))
    near = iota(8, 1) < HALF
    half0 = jnp.where(near, 0.0, low[:, :LANES])
    half1 = jnp.where(near, low[:, LANES:], 0.0)

    def corner(i, j, k):
        row = 4 * i + 2 * j + k
        return [half0[row : row + 1], half1[row : row + 1]]

    lane = iota(1, 1)
    mine, extra = [], []
    for i in range(2):
        columns = []
        for k in range(2):
            shifted = right(*corner(i, 1, k))
            straight = corner(i, 0, k)
            columns.append([straight[0] + shifted[0], straight[1] + shifted[1]])
        both = [columns[0][h] + pltpu.roll(columns[1][h], 1, 1) for h in range(2)]
        both = [jnp.where(lane % 16 == 0, 0.0, t) for t in both]
        mine.append(own_part(*both))
        extra.append(both[1])
    sides = jnp.where(lane < 16, pltpu.roll(extra[0], HALF, 1), 0.0) + jnp.where(
        (lane >= 16) & (lane < 32), pltpu.roll(extra[1], HALF + 16, 1), 0.0
    )
    none = jnp.zeros((2, LANES), F32)
    corners[...] = jnp.concatenate(mine + [sides, edge[0:3], none], axis=0)


def groups(ns):
    return max(1, ns // 8)


def side_kernel(pos, to_far, to_near, one, two, g4, gm, gmt, wider, far, near_side, back):
    near = iota(8, 1) < HALF
    even, even_a = is_even(pos, 0), is_even(pos, 1)
    for r in range(0, 192, 8):
        x, y = one[r : r + 8], two[r : r + 8]
        before, after = jnp.where(even_a, x, y), jnp.where(even_a, y, x)
        x, y = to_far[r : r + 8], to_near[r : r + 8]
        lower, upper = jnp.where(even_a, x, y), jnp.where(even_a, y, x)
        halves = (jnp.where(near, before, lower), jnp.where(near, upper, after))
        for h in range(2):
            wider[h, r : r + 8] = halves[h]
    flux = dot(gm[...], wide(wider, 64, 64)) * wide(g4, 0, 192)
    put(back, 0, 64, dot(gmt[...], flux))
    one = pl.multiple_of(jnp.where(even, 48, 0), 8)
    two = pl.multiple_of(jnp.where(even, 0, 48), 8)
    sums = [
        [
            total([g4[h, 16 * k : 16 * k + 16] * float(D4[k, end]) for k in range(4)])
            for end in (0, 3)
        ]
        for h in range(2)
    ]
    for out, plane, is_last in ((near_side, one, even), (far, two, jnp.logical_not(even))):
        for h in range(2):
            out[h, 0:16] = jnp.where(is_last, sums[h][1], sums[h][0])
            out[h, 16:32] = g4[h, pl.ds(64 + plane, 16), :]
            out[h, 32:48] = g4[h, pl.ds(128 + plane, 16), :]
            out[h, 48:64] = back[h, pl.ds(plane, 16), :]


def column_kernel(rows, first, out):
    ns = rows.shape[0] // 8
    n = ns // groups(ns)

    def field(k):
        return rows[pl.ds(k, ns, stride=8), :]

    def later(x):
        return pltpu.roll(x, 1, 0)

    sides = field(2)
    over = jnp.where(iota(ns, 1) < 16, sides + later(pltpu.roll(sides, LANES - 16, 1)), 0.0)
    out[0:ns] = field(0) + later(field(1))
    for k in range(3):
        out[(1 + k) * ns : (2 + k) * ns] = field(3 + k)
    parts = [over[k * n : k * n + n] for k in range(groups(ns))]
    out[4 * ns : 4 * ns + n] = total(
        [pltpu.roll(p, 16 * k, 1) if k else p for k, p in enumerate(parts)]
    )


def coarse_kernel(
    pos, columns, wider, far, near_side, g4, inv4, gm, gmt, up4, gm_first, gmt_first,
    gm_last, gmt_last,
    res, u, sol, acc, face_a, face_b, vals, x2, es, ea, er, es0, ea0, er0, dg, ri,
):
    ns = x2.shape[0]
    na = x2.shape[1] // LANES
    width = na * LANES

    n = ns // groups(ns)
    size = 4 * ns + n
    even_a = is_even(pos, 1)

    def rows_of(d, start, count):
        return columns[d * size + start : d * size + start + count]

    def field(k):
        return [rows_of(d, k * ns, ns) for d in range(na)]

    def side(d):
        packed = rows_of(d, 4 * ns, n)
        parts = [pltpu.roll(packed, LANES - 16 * k, 1) if k else packed for k in range(groups(ns))]
        return jnp.where(iota(ns, 1) < 16, jnp.concatenate(parts, axis=0), 0.0)

    def roll_l(x, k):
        return pltpu.roll(x, k % width, 1)

    lane = iota(ns, 1)
    wall, top = lane % 16 == 0, lane % 16 == 15
    at = [slice(d * LANES, d * LANES + LANES) for d in range(na)]

    def towards_next(y, d):
        return jnp.where(lane < LANES - 16, y[d], y[(d + 1) % na])

    def towards_last(y, d):
        return jnp.where(lane < 16, y[d - 1], y[d])

    ea_all, er_all = field(2), field(3)
    ea_roll = [pltpu.roll(t, 16, 1) for t in ea_all]
    for d, es_d in enumerate(field(1)):
        es0_d, ea0_d = pltpu.roll(es_d, 1, 0), towards_last(ea_roll, d)
        er0_d = pltpu.roll(er_all[d], 1, 1)
        both = es_d + es0_d + ea_all[d] + ea0_d + er_all[d] + er0_d
        es[:, at[d]], ea[:, at[d]] = es_d, ea_all[d]
        es0[:, at[d]], ea0[:, at[d]] = es0_d, ea0_d
        er[:, at[d]] = jnp.where(wall | top, 0.0, er_all[d])
        er0[:, at[d]] = jnp.where(wall | (lane % 16 == 1), 0.0, er0_d)
        dg[:, at[d]] = jnp.where(wall, 0.0, both)
        ri[:, at[d]] = jnp.where(wall, 0.0, 1.0 / jnp.where(wall, 1.0, both))

    def inner(terms):
        return jnp.sum(jnp.sum(total(terms), axis=0, keepdims=True), axis=1, keepdims=True)

    first = field(0)
    r = [first[d] + side((d - 1) % na) for d in range(na)]
    p = [ri[:, at[d]] * r[d] for d in range(na)]
    gz = inner([r[d] * p[d] for d in range(na)])
    x = [jnp.zeros_like(t) for t in r]
    for it in range(ITERS):
        ahead = [pltpu.roll(t, LANES - 16, 1) for t in p]
        behind = [pltpu.roll(t, 16, 1) for t in p]
        q, terms = [], []
        for d in range(na):
            t, k = p[d], at[d]
            out = dg[:, k] * t
            out = out - es[:, k] * pltpu.roll(t, ns - 1, 0) - es0[:, k] * pltpu.roll(t, 1, 0)
            out = out - ea[:, k] * towards_next(ahead, d) - ea0[:, k] * towards_last(behind, d)
            out = out - er[:, k] * pltpu.roll(t, LANES - 1, 1) - er0[:, k] * pltpu.roll(t, 1, 1)
            q.append(out)
            terms.append(t * out)
        alpha = gz / inner(terms)
        x = [x[d] + alpha * p[d] for d in range(na)]
        if it + 1 < ITERS:
            r = [r[d] - alpha * q[d] for d in range(na)]
            z = [ri[:, at[d]] * r[d] for d in range(na)]
            new = inner([r[d] * z[d] for d in range(na)])
            beta = new / gz
            p = [z[d] + beta * p[d] for d in range(na)]
            gz = new
    for d in range(na):
        x2[:, at[d]] = x[d]

    s, a = pos[0], pos[1]
    blocks = [lax.rem(a + na - 1, na), a, lax.rem(a + 1, na)]
    for t in range(4):
        line = x2[pl.ds(lax.rem(s + ns - 1 + t, ns), 1), :]
        for j in range(2):
            for k in range(2):
                n = 4 * t + 2 * j + k
                vals[n : n + 1, :] = roll_l(line, -(16 * j + k)) if j + k else line
    near = iota(16, 1) < HALF
    b = [
        pltpu.roll(vals[:, pl.ds(pl.multiple_of(t * LANES, LANES), LANES)], HALF, 1) for t in blocks
    ]
    ext = jnp.concatenate([jnp.where(near, b[0], b[1]), jnp.where(near, b[1], b[2])], axis=1)
    rise = dot(up4[...], ext)
    even = is_even(pos, 0)
    x, y = wide(far, 0, 64), wide(near_side, 0, 64)
    below, above = jnp.where(even, x, y), jnp.where(even, y, x)
    low = dot(gmt_last[...], dot(gm_last[...], rise[:64]) * below[:48]) + below[48:]
    high = dot(gmt_first[...], dot(gm_first[...], rise[128:]) * above[:48]) + above[48:]
    flux = dot(gm[...], rise[64:128] + wide(wider, 64, 64)) * wide(g4, 0, 192)
    back = dot(gmt[...], flux)
    put(acc, 0, 16, back[:16] + low)
    put(acc, 16, 32, back[16:48])
    put(acc, 48, 16, back[48:] + high)
    join_mid(acc)
    put(sol, 0, 64, wide(wider, 128, 64) + rise[64:128])
    for h, r in tiles(64):
        now = wider[h, r : r + 8] - acc[h, r : r + 8]
        new = inv4[h, r : r + 8] * now * (1.0 / CENTER)
        res[h, r : r + 8] = now
        u[h, r : r + 8] = new
        sol[h, r : r + 8] += new
    mid_apply(u, g4, acc, gm, gmt)
    join_mid(acc)
    send_faces(acc, even, face_a, face_b, 16)


def sixth_kernel(
    pos, res, u, sol, acc, a, b, inv4, up8, kept, g8, bd, bdt,
    out, v8, acc2, face_a, face_b, y4,
):
    even = is_even(pos, 0)
    for h, r in tiles(64):
        now = res[h, r : r + 8] - full_of(acc, (even, a, b), h, r)
        new = KEEP * u[h, r : r + 8] + GAIN * inv4[h, r : r + 8] * now
        y4[h, r : r + 8] = sol[h, r : r + 8] + new
    put(v8, 0, 512, dot(up8[...], wide(y4, 0, 64)))
    for h, r in tiles(512):
        e8 = v8[h, r : r + 8]
        out[h, r : r + 8] = kept[h, r : r + 8] + e8
        v8[h, r : r + 8] = kept[h, 1024 + r : 1032 + r] + e8
    fine_front(v8, g8, acc2, bd, bdt)
    send_faces(acc2, even, face_a, face_b, 64)


def seventh_kernel(
    pos, kept, sol, acc, a, b, inv8, g8, bd, bdt, res, out, u, acc2, face_a, face_b
):
    even = is_even(pos, 0)
    for h, r in tiles(512):
        now = kept[h, 512 + r : 520 + r] - full_of(acc, (even, a, b), h, r)
        new = inv8[h, r : r + 8] * now * (1.0 / CENTER)
        res[h, r : r + 8] = now
        u[h, r : r + 8] = new
        out[h, r : r + 8] = sol[h, r : r + 8] + new
    fine_front(u, g8, acc2, bd, bdt)
    for out, plane in ((face_b, jnp.where(even, 448, 0)), (face_a, jnp.where(even, 0, 448))):
        rows = pl.ds(pl.multiple_of(plane, 8), 64)
        out[...] = own_part(acc2[0, rows, :], acc2[1, rows, :])


def inner_last_kernel(u, g8, acc, res, sol, inv8, bd, bdt, out, full):
    for h, r in tiles(384):
        full[h, 64 + r : 72 + r] = acc[h, 64 + r : 72 + r]
    fine_cross(u, g8, full, bd, bdt, PLANES[1:])
    join_fine(full, range(1, 7))
    for r in range(64, 448, 8):
        halves = []
        for h in range(2):
            now = res[h, r : r + 8] - full[h, r : r + 8]
            new = KEEP * u[h, r : r + 8] + GAIN * inv8[h, r : r + 8] * now
            halves.append(sol[h, r : r + 8] + new)
        out[r - 64 : r - 56] = own_part(*halves)


def last_kernel(pos, res, sol, u, acc, a, b, inv8, inner, out):
    even = is_even(pos, 0)
    out[64:448] = inner[...]
    for r in [*range(0, 64, 8), *range(448, 512, 8)]:
        halves = []
        for h in range(2):
            inv = inv8[h, r : r + 8]
            now = res[h, r : r + 8] - acc[h, r : r + 8]
            halves.append(sol[h, r : r + 8] + KEEP * u[h, r : r + 8] + GAIN * inv * now)
        at = r % 64
        x, y = a[at : at + 8], b[at : at + 8]
        face = jnp.where(even, x, y) if r < 64 else jnp.where(even, y, x)
        inv = own_part(inv8[0, r : r + 8], inv8[1, r : r + 8])
        out[r : r + 8] = own_part(*halves) - GAIN * inv * face


def call(kernel, args, outs, scratch=(), scalars=1):
    vmem = pl.BlockSpec(memory_space=pltpu.VMEM)
    smem = pl.BlockSpec(memory_space=pltpu.SMEM)
    arrays = [x for x in args if not isinstance(x, str)]
    named = len(arrays) < len(args)

    def body(*refs):
        rest = iter(refs)
        given = [next(rest) for _ in arrays[: len(arrays) - named]]
        held = next(rest) if named else None
        given = iter(given)
        full = [Constant(held, x) if isinstance(x, str) else next(given) for x in args]
        kernel(*full, *rest)

    if named:
        arrays.append(PACK)
    return pl.pallas_call(
        body,
        out_shape=[jax.ShapeDtypeStruct(s, F32) for s in outs],
        in_specs=[smem] * scalars + [vmem] * (len(arrays) - scalars),
        out_specs=[vmem] * len(outs),
        scratch_shapes=[pltpu.VMEM(s, F32) for s in scratch],
        compiler_params=pltpu.CompilerParams(vmem_limit_bytes=32 * 1024 * 1024),
        name=kernel.__name__,
    )(*arrays)


def exchange(far, near, axis):
    size = lax.axis_size(axis)
    pairs_far = [(i, (i + 1 if i % 2 else i - 1) % size) for i in range(size)]
    pairs_near = [(i, i ^ 1) for i in range(size)]
    return lax.ppermute(far, axis, pairs_far), lax.ppermute(near, axis, pairs_near)


def spread(x, axis):
    size = lax.axis_size(axis)
    copies = jnp.broadcast_to(x[None], (size,) + x.shape)
    return lax.all_to_all(copies, axis, 0, 0).reshape(-1, LANES)


def on_device(element_load, metric, element_order):
    ns, na = lax.axis_size("stream"), lax.axis_size("azim")
    fine, mid = (2, 512, LANES), (2, 64, LANES)
    face8, face4 = [(2, 64, LANES)] * 2, [(2, 16, LANES)] * 2
    pos = jnp.stack([lax.axis_index("stream"), lax.axis_index("azim")]).astype(jnp.int32)
    g, rolled, a, b = call(
        order_kernel,
        (pos, metric.reshape(1536, LANES), element_load.reshape(512, LANES), element_order),
        [(1536, LANES), (512, LANES), (1024, LANES), (1024, LANES)],
    )
    a, b = exchange(a, b, "azim")
    (diag,) = call(own_kernel, (g, "bsq"), [(512, LANES)], scalars=0)

    def inner(u, acc):
        (acc,) = call(inner_kernel, (u, g8, acc, "bd", "bdt"), [fine], (), 0)
        return acc

    g8, load, diag8, a, b = call(
        setup_kernel,
        (pos, g, rolled, diag, a, b, "bsq"),
        [(2, 1536, LANES), fine, fine] + [(2, 128, LANES)] * 2,
        [(1536, LANES), (512, LANES)],
    )
    a, b = exchange(a, b, "stream")
    res8, inv8, u8, acc, a, b = call(
        first_kernel,
        (pos, load, diag8, a, b, g8, "bd", "bdt"),
        [fine, fine, fine, fine] + face8,
    )
    a, b = exchange(a, b, "stream")
    acc = inner(u8, acc)
    g4, diag4, edges, upper = call(
        coarsen_kernel,
        (g8, "w4", "w2", "sample", "sq4"),
        [(2, 192, LANES), mid, (8, LANES), (8, LANES)],
        scalars=0,
    )
    kept, t4, a, b = call(
        second_kernel,
        (pos, res8, inv8, acc, a, b, diag4, upper, g8, "bd", "bdt", "down8"),
        [(2, 1536, LANES), mid] + [(2, 40, LANES)] * 2,
        [fine, fine, (512, 2 * LANES)],
    )
    a, b = exchange(a, b, "stream")
    res4, inv4, edges, acc, a, b = call(
        third_kernel,
        (pos, t4, diag4, edges, a, b, g4, "gm", "gmt"),
        [mid, mid, (8, LANES), mid] + face4,
        [mid],
    )
    a, b = exchange(a, b, "stream")
    corners, *kept4 = call(
        fourth_kernel,
        (pos, res4, acc, inv4, edges, a, b, g4, "gm", "gmt", "m4", "down4"),
        [(8, LANES), (192, LANES), (192, LANES)],
        [(2, 192, LANES), mid],
    )
    columns = spread(corners, "stream")
    a, b = exchange(*kept4, "azim")
    wider, a, b = call(
        side_kernel,
        (pos, *kept4, a, b, g4, "gm", "gmt"),
        [(2, 192, LANES)] + face8,
        [mid],
    )
    sides = exchange(a, b, "stream")
    size = 4 * ns + ns // groups(ns)
    (columns,) = call(
        column_kernel, (columns, wider), [(size, LANES)], (), 0
    )
    columns = spread(columns, "azim")
    whole = (ns, na * LANES)
    res4, u4, sol4, acc, a, b = call(
        coarse_kernel,
        (
            pos,
            columns,
            wider,
            *sides,
            g4,
            inv4,
            "gm",
            "gmt",
            "up4",
            "gm_first",
            "gmt_first",
            "gm_last",
            "gmt_last",
        ),
        [mid, mid, mid, mid] + face4,
        [(16, na * LANES)] + [whole] * 9,
    )
    a, b = exchange(a, b, "stream")
    sol8, v8, acc, a, b = call(
        sixth_kernel,
        (pos, res4, u4, sol4, acc, a, b, inv4, "up8", kept, g8, "bd", "bdt"),
        [fine, fine, fine] + face8,
        [mid],
    )
    a, b = exchange(a, b, "stream")
    acc = inner(v8, acc)
    res8, sol8, u8, acc, a, b = call(
        seventh_kernel,
        (pos, kept, sol8, acc, a, b, inv8, g8, "bd", "bdt"),
        [fine, fine, fine, fine] + [(64, LANES)] * 2,
    )
    a, b = exchange(a, b, "stream")
    (inside,) = call(
        inner_last_kernel,
        (u8, g8, acc, res8, sol8, inv8, "bd", "bdt"),
        [(384, LANES)],
        [fine],
        scalars=0,
    )
    (out,) = call(last_kernel, (pos, res8, sol8, u8, acc, a, b, inv8, inside), [(512, LANES)])
    return out.reshape(element_load.shape)


def solution(mesh):
    placed = (P(None, "stream", "azim"), P(None, None, "stream", "azim"), P("stream", "azim"))
    return jax.shard_map(
        on_device, mesh=mesh, in_specs=placed, out_specs=P(None, "stream", "azim"), check_vma=False
    )
```

```python
import jax
import jax.numpy as jnp
import numpy as np
from jax import lax
from jax.experimental import pallas as pl
from jax.experimental.pallas import tpu as pltpu
from jax.sharding import PartitionSpec as P

ITERS = 6
LOW_EIG = 0.3
HIGH_EIG = 3.0
CENTER = 0.5 * (HIGH_EIG + LOW_EIG)
HALF_WIDTH = 0.5 * (HIGH_EIG - LOW_EIG)
FIRST_RHO = HALF_WIDTH / CENTER
SECOND_RHO = 1.0 / (2.0 * CENTER / HALF_WIDTH - FIRST_RHO)
KEEP = SECOND_RHO * FIRST_RHO
GAIN = 2.0 * SECOND_RHO / HALF_WIDTH
LANES = 128
HALF = 64
F32 = jnp.float32


def legendre_pair(degree, places):
    previous = places * 0.0 + 1.0
    current = places.copy()
    for k in range(2, degree + 1):
        following = ((2 * k - 1) * places * current - (k - 1) * previous) / k
        previous = current
        current = following
    return (current, previous)


def gll_table(points):
    degree = points - 1
    places = np.cos(np.pi * np.arange(points) / degree)
    for _ in range(60):
        top, below = legendre_pair(degree, places)
        places = places - (places * top - below) / (points * top)
    nodes = np.sort(places)
    nodes[0] = -1.0
    nodes[-1] = 1.0
    at_nodes = legendre_pair(degree, nodes)[0]
    weights = 2.0 / (degree * (degree + 1) * at_nodes**2)
    deriv = np.zeros((points, points))
    for i in range(points):
        for j in range(points):
            if i != j:
                deriv[i, j] = at_nodes[i] / (at_nodes[j] * (nodes[i] - nodes[j]))
    deriv[0, 0] = -degree * (degree + 1) / 4.0
    deriv[-1, -1] = degree * (degree + 1) / 4.0
    return (nodes, weights, deriv)


def lagrange_table(source, target):
    out = np.ones((len(target), len(source)))
    for j in range(len(source)):
        for k in range(len(source)):
            if k != j:
                out[:, j] *= (target - source[k]) / (source[j] - source[k])
    return out


N8, W8, D8 = gll_table(8)
N4, W4, D4 = gll_table(4)
N2, W2, D2 = gll_table(2)


def kron3(a, b, c):
    return np.kron(np.kron(a, b), c)


def cube(w):
    return (w[:, None, None] * w[None, :, None] * w[None, None, :]).reshape(-1)


def share(n):
    edge = np.ones(n)
    edge[0] = edge[-1] = 0.5
    return cube(edge)


def grads(d):
    i = np.eye(d.shape[0])
    return [kron3(d, i, i), kron3(i, d, i), kron3(i, i, d)]


def f32(x):
    return np.asarray(x, np.float32)


def lanes_of(column):
    return np.repeat(f32(column)[:, None], LANES, axis=1)


UP8 = lagrange_table(N4, N8)
UP4 = lagrange_table(N2, N4)
TO4 = lagrange_table(N8, N4)
TO2 = lagrange_table(N8, N2)

C_BD = f32(np.kron(np.eye(16), D8))
C_BDT = f32(np.kron(np.eye(16), D8.T))
C_BSQ = f32(np.kron(np.eye(16), (D8 * D8).T))
C_SAMPLE = f32(np.concatenate([kron3(TO4, TO4, TO4), kron3(TO2, TO2, TO2)]))
C_UP8 = f32(kron3(UP8, UP8, UP8))
C_DOWN8 = f32(kron3(UP8, UP8, UP8).T)
C_UP4 = f32(kron3(UP4, UP4, UP4))
C_DOWN4 = f32(kron3(UP4, UP4, UP4).T)
C_UP4X3 = np.zeros((192, 16), np.float32)
for layer in range(3):
    C_UP4X3[64 * layer : 64 * layer + 64, 4 * layer : 4 * layer + 8] = C_UP4
C_G4 = f32(np.concatenate(grads(D4)))
C_G4T = f32(np.concatenate(grads(D4)).T)
C_SQ4 = f32((np.concatenate(grads(D4)) ** 2).T)
C_W4 = lanes_of(cube(W4) / np.exp(kron3(TO4, TO4, TO4) @ np.log(cube(W8))))
C_W2 = lanes_of(cube(W2) / np.exp(kron3(TO2, TO2, TO2) @ np.log(cube(W8))))
C_M4 = lanes_of(share(4))
FIRST = np.r_[0:16, 64:80, 128:144]
LAST = np.r_[48:64, 112:128, 176:192]


def plane_back(plane, rows):
    eye = np.eye(16, dtype=np.float32)
    return np.concatenate([eye, C_G4T[plane : plane + 16, rows[16:]]], axis=1)


CONSTANTS = {
    "bd": C_BD, "bdt": C_BDT, "bsq": C_BSQ, "sample": C_SAMPLE, "w4": C_W4, "w2": C_W2,
    "sq4": C_SQ4, "gm": C_G4, "gmt": C_G4T, "m4": C_M4, "down8": C_DOWN8, "down4": C_DOWN4,
    "up4": C_UP4X3, "up8": C_UP8, "gm_first": C_G4[FIRST], "gmt_first": plane_back(0, FIRST),
    "gm_last": C_G4[LAST], "gmt_last": plane_back(48, LAST),
}


def pack_constants():
    rows, places, start = [], {}, 0
    for name, value in CONSTANTS.items():
        blocks = -(-value.shape[1] // LANES)
        padded = np.zeros((value.shape[0], blocks * LANES), np.float32)
        padded[:, : value.shape[1]] = value
        rows += [padded[:, k * LANES : (k + 1) * LANES] for k in range(blocks)]
        places[name] = (start, value.shape, blocks)
        start += value.shape[0] * blocks
    return np.concatenate(rows), places


PACK, PLACES = pack_constants()


class Constant:
    def __init__(self, ref, name):
        self.ref, self.name = ref, name

    def __getitem__(self, index):
        start, (rows, columns), blocks = PLACES[self.name]
        parts = []
        for k in range(blocks):
            width = min(LANES, columns - k * LANES)
            parts.append(self.ref[start + k * rows : start + (k + 1) * rows, :width])
        value = parts[0] if blocks == 1 else jnp.concatenate(parts, axis=1)
        return value if index is Ellipsis else value[index]


def dot(a, b, precision=lax.Precision.HIGH):
    return jnp.dot(a, b, preferred_element_type=F32, precision=precision)


def iota(rows, axis):
    return lax.broadcasted_iota(jnp.int32, (rows, LANES), axis)


def wide(ref, start, size):
    return jnp.concatenate([ref[0, start : start + size], ref[1, start : start + size]], axis=1)


def put(ref, start, size, value):
    ref[0, start : start + size] = value[:, :LANES]
    ref[1, start : start + size] = value[:, LANES:]


def total(terms):
    out = terms[0]
    for t in terms[1:]:
        out = out + t
    return out


def contract(v, matrix, sign):
    n = len(v)
    h = n // 2
    even = [v[k] + v[n - 1 - k] for k in range(h)]
    odd = [v[k] - v[n - 1 - k] for k in range(h)]
    out = [None] * n
    for i in range(h):
        p = total([even[k] * float(0.5 * (matrix[i, k] + matrix[i, n - 1 - k])) for k in range(h)])
        q = total([odd[k] * float(0.5 * (matrix[i, k] - matrix[i, n - 1 - k])) for k in range(h)])
        out[i] = p + q
        out[n - 1 - i] = q - p if sign < 0 else p - q
    return out


def fine_rows(s, a):
    return s * 64 + a * 8


PLANES = [(0, 7), (1, 2), (3, 4), (5, 6)]


def pair(ref, p, base=0):
    return jnp.concatenate([wide(ref, base + 64 * s, 64) for s in p], axis=0)


def put_pair(ref, p, value):
    for k, s in enumerate(p):
        put(ref, 64 * s, 64, value[64 * k : 64 * k + 64])


def fine_stream(u, g, acc):
    for h in range(2):
        for a in range(8):
            at = [fine_rows(s, a) for s in range(8)]
            grad = contract([u[h, r : r + 8] for r in at], D8, -1)
            back = contract([grad[s] * g[h, r : r + 8] for s, r in enumerate(at)], D8.T, -1)
            for s, r in enumerate(at):
                acc[h, r : r + 8] = back[s]


def fine_cross(u, g, acc, bd, bdt, pairs):
    for p in pairs:
        flux = dot(bd[...], pair(u, p)) * pair(g, p, 1024)
        put_pair(acc, p, pair(acc, p) + dot(bdt[...], flux))
        for s in p:
            for h in range(2):
                at = [fine_rows(s, a) for a in range(8)]
                grad = contract([u[h, r : r + 8] for r in at], D8, -1)
                flux = [grad[a] * g[h, 512 + r : 520 + r] for a, r in enumerate(at)]
                back = contract(flux, D8.T, -1)
                for a, r in enumerate(at):
                    acc[h, r : r + 8] += back[a]


def fine_apply(u, g, acc, bd, bdt):
    fine_stream(u, g, acc)
    fine_cross(u, g, acc, bd, bdt, PLANES)


def fine_front(u, g, acc, bd, bdt):
    fine_stream(u, g, acc)
    fine_cross(u, g, acc, bd, bdt, PLANES[:1])
    join_fine(acc, (0, 7))


def left(x0, x1):
    near = iota(x0.shape[0], 1) < LANES - 16
    y0, y1 = pltpu.roll(x0, LANES - 16, 1), pltpu.roll(x1, LANES - 16, 1)
    return jnp.where(near, y0, y1), jnp.where(near, y1, y0)


def right(x0, x1):
    near = iota(x0.shape[0], 1) >= 16
    y0, y1 = pltpu.roll(x0, 16, 1), pltpu.roll(x1, 16, 1)
    return jnp.where(near, y0, y1), jnp.where(near, y1, y0)


def join_radial(x, points, start, rows):
    place = iota(rows, 1) % 16
    first = pl.ds(start, rows, stride=points)
    last = pl.ds(start + points - 1, rows, stride=points)
    for h in range(2):
        view = x.at[h]
        low, high = view[first, :], view[last, :]
        view[first, :] = jnp.where(place == 0, 0.0, low + pltpu.roll(high, 1, 1))
        view[last, :] = jnp.where(place == 15, 0.0, high + pltpu.roll(low, LANES - 1, 1))


def join_fine(x, planes=range(8)):
    for s in planes:
        join_radial(x, 8, 64 * s, 8)
        lo, hi = fine_rows(s, 0), fine_rows(s, 7)
        low = [x[h, lo : lo + 8] for h in range(2)]
        high = [x[h, hi : hi + 8] for h in range(2)]
        to_low, to_high = right(*high), left(*low)
        for h in range(2):
            x[h, lo : lo + 8] = low[h] + to_low[h]
            x[h, hi : hi + 8] = high[h] + to_high[h]


def join_mid(x):
    join_radial(x, 4, 0, 16)
    first = iota(8, 0) < 4
    for s in range(4):
        lo, hi = s * 16, s * 16 + 8
        low = [x[h, lo : lo + 8] for h in range(2)]
        high = [x[h, hi : hi + 8] for h in range(2)]
        to_low = right(*[pltpu.roll(t, 4, 0) for t in high])
        to_high = left(*[pltpu.roll(t, 4, 0) for t in low])
        for h in range(2):
            x[h, lo : lo + 8] = low[h] + jnp.where(first, to_low[h], 0.0)
            x[h, hi : hi + 8] = high[h] + jnp.where(first, 0.0, to_high[h])


def is_even(place, k):
    return lax.rem(place[k], 2) == 0


def full_of(x, faces, h, r, offset=0):
    even, far, near = faces
    rows = x.shape[1]
    plane = {512: 64, 64: 16}[rows]
    value = x[h, r : r + 8]
    if r < plane:
        at = offset + r
        return value + jnp.where(even, far[h, at : at + 8], near[h, at : at + 8])
    if r >= rows - plane:
        at = offset + r - (rows - plane)
        return value + jnp.where(even, near[h, at : at + 8], far[h, at : at + 8])
    return value


def send_faces(x, even, far, near, plane, offset=0):
    rows = x.shape[1]
    last = rows - plane
    one = pl.multiple_of(jnp.where(even, last, 0), 8)
    two = pl.multiple_of(jnp.where(even, 0, last), 8)
    for h in range(2):
        near[h, offset : offset + plane] = x[h, pl.ds(one, plane), :]
        far[h, offset : offset + plane] = x[h, pl.ds(two, plane), :]


def wall_mask(points):
    place, node = iota(8, 1) % 16, iota(8, 0) % points
    return ((node == 0) & (place == 0)) | ((node == points - 1) & (place == 15))


def own_part(half0, half1):
    near = iota(half0.shape[0], 1) < HALF
    return pltpu.roll(jnp.where(near, half1, half0), HALF, 1)


def tiles(rows):
    return [(h, r) for h in range(2) for r in range(0, rows, 8)]


def mid_apply(u, g4, acc, gm, gmt):
    flux = dot(gm[...], wide(u, 0, 64)) * wide(g4, 0, 192)
    put(acc, 0, 64, dot(gmt[...], flux))


def fine_diagonal(g, diag, bsq):
    square = (D8 * D8).T
    for c in range(4):
        rows = slice(128 * c, 128 * c + 128)
        diag[rows] = dot(bsq[...], g[1024 + 128 * c : 1152 + 128 * c])
    for axis in range(2):
        for fixed in range(8):
            at = [fine_rows(k, fixed) if axis == 0 else fine_rows(fixed, k) for k in range(8)]
            back = contract([g[512 * axis + r : 512 * axis + r + 8] for r in at], square, 1)
            for k, r in enumerate(at):
                diag[r : r + 8] += back[k]


def halves_up_down(a, b):
    near = iota(8, 1) < HALF
    up = jnp.where(near, a, pltpu.roll(b, HALF, 1))
    return up, jnp.where(near, pltpu.roll(a, HALF, 1), b)


def before_after(even, x, y):
    p, n = jnp.where(even, x, y), jnp.where(even, y, x)
    near = iota(8, 1) < HALF
    first = (jnp.where(near, p, 0.0), jnp.where(near, 0.0, pltpu.roll(n, HALF, 1)))
    second = (jnp.where(near, pltpu.roll(p, HALF, 1), 0.0), jnp.where(near, 0.0, n))
    return first, second


def order_kernel(pos, metric, load, order, g, rolled, far, near):
    even = is_even(pos, 1)
    slots = jnp.broadcast_to(pltpu.roll(order[...], HALF, 1), (8, LANES))
    wr = total([jnp.where(iota(8, 0) == k, float(W8[k]), 0.0) for k in range(8)])
    for r in range(0, 1536, 8):
        scale = wr * float(W8[(r % 512) // 64] * W8[(r // 8) % 8])
        g[r : r + 8] = jnp.take_along_axis(metric[r : r + 8], slots, axis=1) * scale
    for r in range(0, 512, 8):
        rolled[r : r + 8] = pltpu.roll(load[r : r + 8], HALF, 1)
    for r in range(0, 1024, 8):
        other = g[1024 + r : 1032 + r] if r < 512 else rolled[r - 512 : r - 504]
        up, down = halves_up_down(g[r : r + 8], other)
        far[r : r + 8] = jnp.where(even, down, up)
        near[r : r + 8] = jnp.where(even, up, down)


def own_kernel(g, bsq, diag):
    fine_diagonal(g, diag, bsq)


def setup_kernel(
    pos, g, rolled, diag, x, y, bsq, g8, load, diag8, face_a, face_b, ghost, ghost_diag
):
    near = iota(8, 1) < HALF
    even_a = is_even(pos, 1)

    def place(out, row, own, sides):
        out[0, row : row + 8] = jnp.where(near, sides[0], own)
        out[1, row : row + 8] = jnp.where(near, own, sides[1])

    for r in range(0, 1024, 8):
        first, second = before_after(even_a, x[r : r + 8], y[r : r + 8])
        place(g8, r, g[r : r + 8], first)
        ghost[r : r + 8] = first[0] + first[1]
        if r < 512:
            place(g8, 1024 + r, g[1024 + r : 1032 + r], second)
            ghost[1024 + r : 1032 + r] = second[0] + second[1]
        else:
            place(load, r - 512, rolled[r - 512 : r - 504], second)
    fine_diagonal(ghost, ghost_diag, bsq)
    for r in range(0, 512, 8):
        side = ghost_diag[r : r + 8]
        place(diag8, r, diag[r : r + 8], (side, side))
    for x in (load, diag8):
        join_fine(x)
    even = is_even(pos, 0)
    send_faces(load, even, face_a, face_b, 64)
    send_faces(diag8, even, face_a, face_b, 64, 64)


def coarsen_kernel(g8, w4, w2, sample, sq4, g4, diag4, edges, upper):
    low = []
    for d in range(3):
        logs = jnp.log(wide(g8, 512 * d, 512))
        coarse = jnp.exp(dot(sample[...], logs, lax.Precision.HIGHEST))
        put(g4, 64 * d, 64, coarse[:64] * jnp.concatenate([w4[...], w4[...]], axis=1))
        low.append([coarse[64:72, :LANES] * w2[...], coarse[64:72, LANES:] * w2[...]])
    put(diag4, 0, 64, dot(sq4[...], wide(g4, 0, 192)))
    join_mid(diag4)

    def corner(d, i, j, k):
        row = 4 * i + 2 * j + k
        return [t[row : row + 1] for t in low[d]]

    def add(x, y):
        return [x[0] + y[0], x[1] + y[1]]

    def quarter(x):
        return [0.25 * x[0], 0.25 * x[1]]

    def outward(x):
        return [pltpu.roll(x[0], 1, 1), pltpu.roll(x[1], 1, 1)]

    es = [[quarter(add(corner(0, 0, j, k), corner(0, 1, j, k))) for k in range(2)] for j in range(2)]
    ea = [[quarter(add(corner(1, i, 0, k), corner(1, i, 1, k))) for k in range(2)] for i in range(2)]
    er = [[quarter(add(corner(2, i, j, 0), corner(2, i, j, 1))) for j in range(2)] for i in range(2)]
    col = [add(es[0][k], list(right(*es[1][k]))) for k in range(2)]
    edge_s = add(col[0], outward(col[1]))
    edge_a = [add(ea[i][0], outward(ea[i][1])) for i in range(2)]
    edge_r = [add(er[i][0], list(right(*er[i][1]))) for i in range(2)]
    off_wall = iota(1, 1) % 16 != 0
    rows = [jnp.where(off_wall, own_part(*x), 0.0) for x in (edge_s, edge_a[0], edge_a[1])]
    rows += [own_part(*x) for x in edge_r]
    none = jnp.zeros((5, LANES), F32)
    edges[...] = jnp.concatenate([rows[0], rows[1], rows[3], none], axis=0)
    upper[...] = jnp.concatenate([rows[0], rows[2], rows[4], none], axis=0)


def first_kernel(
    pos, load, diag8, a, b, g8, bd, bdt, res, inv8, u, acc, face_a, face_b
):
    even = is_even(pos, 0)
    got = (even, a, b)
    wall8 = wall_mask(8)
    for h, r in tiles(512):
        diag = full_of(diag8, got, h, r, 64)
        inv = jnp.where(wall8, 0.0, 1.0 / jnp.where(wall8, 1.0, diag))
        full = full_of(load, got, h, r)
        res[h, r : r + 8] = full
        inv8[h, r : r + 8] = inv
        u[h, r : r + 8] = inv * full * (1.0 / CENTER)
    fine_front(u, g8, acc, bd, bdt)
    send_faces(acc, even, face_a, face_b, 64)


def inner_kernel(u, g8, start, bd, bdt, acc):
    for h, r in tiles(512):
        acc[h, r : r + 8] = start[h, r : r + 8]
    fine_cross(u, g8, acc, bd, bdt, PLANES[1:])
    join_fine(acc, range(1, 7))


def second_kernel(
    pos, res, inv8, acc, a, b, diag4, upper, g8, bd, bdt, down8,
    kept, t4, face_a, face_b, u, back, part,
):
    even = is_even(pos, 0)
    got = (even, a, b)
    edge = jnp.where((iota(8, 0) == 0) | (iota(8, 0) == 7), 0.5, 1.0)
    for h, r in tiles(512):
        inv, before = inv8[h, r : r + 8], res[h, r : r + 8]
        now = before - full_of(acc, got, h, r)
        old = inv * before * (1.0 / CENTER)
        new = KEEP * old + GAIN * inv * now
        kept[h, r : r + 8] = old + new
        kept[h, 512 + r : 520 + r] = now
        kept[h, 1024 + r : 1032 + r] = new
        u[h, r : r + 8] = new
    fine_apply(u, g8, back, bd, bdt)
    for h, r in tiles(512):
        s, c = r // 64, (r // 8) % 8
        scale = (0.5 if s in (0, 7) else 1.0) * (0.5 if c in (0, 7) else 1.0)
        part[r : r + 8, h * LANES : h * LANES + LANES] = (
            kept[h, 512 + r : 520 + r] * (edge * scale) - back[h, r : r + 8]
        )
    put(t4, 0, 64, dot(down8[...], part[...]))
    join_mid(t4)
    send_faces(t4, even, face_a, face_b, 16)
    send_faces(diag4, even, face_a, face_b, 16, 16)
    for face in (face_a, face_b):
        for h in range(2):
            face[h, 32:40] = upper[...]


def third_kernel(
    pos, t4, diag4, edges, a, b, g4, gm, gmt, res, inv4, edge, acc, face_a, face_b, u
):
    even = is_even(pos, 0)
    got = (even, a, b)
    wall = wall_mask(4)
    for h, r in tiles(64):
        full = full_of(t4, got, h, r)
        diag = full_of(diag4, got, h, r, 16)
        inv = jnp.where(wall, 0.0, 1.0 / jnp.where(wall, 1.0, diag))
        res[h, r : r + 8] = full
        inv4[h, r : r + 8] = inv
        u[h, r : r + 8] = inv * full * (1.0 / CENTER)
    lower = jnp.where(even, a[0, 32:40], b[0, 32:40])
    edge[...] = edges[...] + jnp.where(iota(8, 0) == 0, 0.0, lower)
    mid_apply(u, g4, acc, gm, gmt)
    join_mid(acc)
    send_faces(acc, even, face_a, face_b, 16)


def fourth_kernel(
    pos, res, acc, inv4, edge, a, b, g4, gm, gmt, m4, down4, corners, one, two, keep, part
):
    got = (is_even(pos, 0), a, b)
    for h, r in tiles(64):
        inv, before = inv4[h, r : r + 8], res[h, r : r + 8]
        now = before - full_of(acc, got, h, r)
        old = inv * before * (1.0 / CENTER)
        new = KEEP * old + GAIN * inv * now
        keep[h, r : r + 8] = now
        keep[h, 64 + r : 72 + r] = new
        keep[h, 128 + r : 136 + r] = old + new
    even_a = is_even(pos, 1)
    one[...] = jnp.where(even_a, keep[0], keep[1])
    two[...] = jnp.where(even_a, keep[1], keep[0])
    flux = dot(gm[...], wide(keep, 64, 64)) * wide(g4, 0, 192)
    put(part, 0, 64, dot(gmt[...], flux))
    for h, r in tiles(64):
        part[h, r : r + 8] = m4[r : r + 8] * keep[h, r : r + 8] - part[h, r : r + 8]
    low = dot(down4[...], wide(part, 0, 64))
    near = iota(8, 1) < HALF
    half0 = jnp.where(near, 0.0, low[:, :LANES])
    half1 = jnp.where(near, low[:, LANES:], 0.0)

    def corner(i, j, k):
        row = 4 * i + 2 * j + k
        return [half0[row : row + 1], half1[row : row + 1]]

    lane = iota(1, 1)
    mine, extra = [], []
    for i in range(2):
        columns = []
        for k in range(2):
            shifted = right(*corner(i, 1, k))
            straight = corner(i, 0, k)
            columns.append([straight[0] + shifted[0], straight[1] + shifted[1]])
        both = [columns[0][h] + pltpu.roll(columns[1][h], 1, 1) for h in range(2)]
        both = [jnp.where(lane % 16 == 0, 0.0, t) for t in both]
        mine.append(own_part(*both))
        extra.append(both[1])
    sides = jnp.where(lane < 16, pltpu.roll(extra[0], HALF, 1), 0.0) + jnp.where(
        (lane >= 16) & (lane < 32), pltpu.roll(extra[1], HALF + 16, 1), 0.0
    )
    none = jnp.zeros((2, LANES), F32)
    corners[...] = jnp.concatenate(mine + [sides, edge[0:3], none], axis=0)


def groups(ns):
    return max(1, ns // 8)


def side_kernel(pos, to_far, to_near, one, two, g4, gm, gmt, wider, far, near_side, back):
    near = iota(8, 1) < HALF
    even, even_a = is_even(pos, 0), is_even(pos, 1)
    for r in range(0, 192, 8):
        x, y = one[r : r + 8], two[r : r + 8]
        before, after = jnp.where(even_a, x, y), jnp.where(even_a, y, x)
        x, y = to_far[r : r + 8], to_near[r : r + 8]
        lower, upper = jnp.where(even_a, x, y), jnp.where(even_a, y, x)
        halves = (jnp.where(near, before, lower), jnp.where(near, upper, after))
        for h in range(2):
            wider[h, r : r + 8] = halves[h]
    flux = dot(gm[...], wide(wider, 64, 64)) * wide(g4, 0, 192)
    put(back, 0, 64, dot(gmt[...], flux))
    one = pl.multiple_of(jnp.where(even, 48, 0), 8)
    two = pl.multiple_of(jnp.where(even, 0, 48), 8)
    sums = [
        [
            total([g4[h, 16 * k : 16 * k + 16] * float(D4[k, end]) for k in range(4)])
            for end in (0, 3)
        ]
        for h in range(2)
    ]
    for out, plane, is_last in ((near_side, one, even), (far, two, jnp.logical_not(even))):
        for h in range(2):
            out[h, 0:16] = jnp.where(is_last, sums[h][1], sums[h][0])
            out[h, 16:32] = g4[h, pl.ds(64 + plane, 16), :]
            out[h, 32:48] = g4[h, pl.ds(128 + plane, 16), :]
            out[h, 48:64] = back[h, pl.ds(plane, 16), :]


def column_kernel(rows, out):
    ns = rows.shape[0] // 8
    n = ns // groups(ns)

    def field(k):
        return rows[pl.ds(k, ns, stride=8), :]

    def later(x):
        return pltpu.roll(x, 1, 0)

    sides = field(2)
    over = jnp.where(iota(ns, 1) < 16, sides + later(pltpu.roll(sides, LANES - 16, 1)), 0.0)
    out[0:ns] = field(0) + later(field(1))
    for k in range(3):
        out[(1 + k) * ns : (2 + k) * ns] = field(3 + k)
    parts = [over[k * n : k * n + n] for k in range(groups(ns))]
    out[4 * ns : 4 * ns + n] = total(
        [pltpu.roll(p, 16 * k, 1) if k else p for k, p in enumerate(parts)]
    )


def coarse_kernel(
    pos, columns, others, wider, far, near_side, g4, inv4, gm, gmt, up4, gm_first, gmt_first,
    gm_last, gmt_last,
    res, u, sol, acc, face_a, face_b, vals, x2, es, ea, er, es0, ea0, er0, dg, ri,
):
    ns = x2.shape[0]
    na = x2.shape[1] // LANES
    width = na * LANES

    n = ns // groups(ns)
    size = 4 * ns + n
    even_a = is_even(pos, 1)

    def rows_of(d, start, count):
        at = d // 2 * size + start
        x, y = columns[at : at + count], others[at : at + count]
        return jnp.where(even_a, x, y) if d % 2 == 0 else jnp.where(even_a, y, x)

    def field(k):
        return [rows_of(d, k * ns, ns) for d in range(na)]

    def side(d):
        packed = rows_of(d, 4 * ns, n)
        parts = [pltpu.roll(packed, LANES - 16 * k, 1) if k else packed for k in range(groups(ns))]
        return jnp.where(iota(ns, 1) < 16, jnp.concatenate(parts, axis=0), 0.0)

    def roll_l(x, k):
        return pltpu.roll(x, k % width, 1)

    lane = iota(ns, 1)
    wall, top = lane % 16 == 0, lane % 16 == 15
    at = [slice(d * LANES, d * LANES + LANES) for d in range(na)]

    def towards_next(y, d):
        return jnp.where(lane < LANES - 16, y[d], y[(d + 1) % na])

    def towards_last(y, d):
        return jnp.where(lane < 16, y[d - 1], y[d])

    ea_all, er_all = field(2), field(3)
    ea_roll = [pltpu.roll(t, 16, 1) for t in ea_all]
    for d, es_d in enumerate(field(1)):
        es0_d, ea0_d = pltpu.roll(es_d, 1, 0), towards_last(ea_roll, d)
        er0_d = pltpu.roll(er_all[d], 1, 1)
        both = es_d + es0_d + ea_all[d] + ea0_d + er_all[d] + er0_d
        es[:, at[d]], ea[:, at[d]] = es_d, ea_all[d]
        es0[:, at[d]], ea0[:, at[d]] = es0_d, ea0_d
        er[:, at[d]] = jnp.where(wall | top, 0.0, er_all[d])
        er0[:, at[d]] = jnp.where(wall | (lane % 16 == 1), 0.0, er0_d)
        dg[:, at[d]] = jnp.where(wall, 0.0, both)
        ri[:, at[d]] = jnp.where(wall, 0.0, 1.0 / jnp.where(wall, 1.0, both))

    def inner(terms):
        return jnp.sum(jnp.sum(total(terms), axis=0, keepdims=True), axis=1, keepdims=True)

    first = field(0)
    r = [first[d] + side((d - 1) % na) for d in range(na)]
    p = [ri[:, at[d]] * r[d] for d in range(na)]
    gz = inner([r[d] * p[d] for d in range(na)])
    x = [jnp.zeros_like(t) for t in r]
    for it in range(ITERS):
        ahead = [pltpu.roll(t, LANES - 16, 1) for t in p]
        behind = [pltpu.roll(t, 16, 1) for t in p]
        q, terms = [], []
        for d in range(na):
            t, k = p[d], at[d]
            out = dg[:, k] * t
            out = out - es[:, k] * pltpu.roll(t, ns - 1, 0) - es0[:, k] * pltpu.roll(t, 1, 0)
            out = out - ea[:, k] * towards_next(ahead, d) - ea0[:, k] * towards_last(behind, d)
            out = out - er[:, k] * pltpu.roll(t, LANES - 1, 1) - er0[:, k] * pltpu.roll(t, 1, 1)
            q.append(out)
            terms.append(t * out)
        alpha = gz / inner(terms)
        x = [x[d] + alpha * p[d] for d in range(na)]
        if it + 1 < ITERS:
            r = [r[d] - alpha * q[d] for d in range(na)]
            z = [ri[:, at[d]] * r[d] for d in range(na)]
            new = inner([r[d] * z[d] for d in range(na)])
            beta = new / gz
            p = [z[d] + beta * p[d] for d in range(na)]
            gz = new
    for d in range(na):
        x2[:, at[d]] = x[d]

    s, a = pos[0], pos[1]
    blocks = [lax.rem(a + na - 1, na), a, lax.rem(a + 1, na)]
    for t in range(4):
        line = x2[pl.ds(lax.rem(s + ns - 1 + t, ns), 1), :]
        for j in range(2):
            for k in range(2):
                n = 4 * t + 2 * j + k
                vals[n : n + 1, :] = roll_l(line, -(16 * j + k)) if j + k else line
    near = iota(16, 1) < HALF
    b = [
        pltpu.roll(vals[:, pl.ds(pl.multiple_of(t * LANES, LANES), LANES)], HALF, 1) for t in blocks
    ]
    ext = jnp.concatenate([jnp.where(near, b[0], b[1]), jnp.where(near, b[1], b[2])], axis=1)
    rise = dot(up4[...], ext)
    even = is_even(pos, 0)
    x, y = wide(far, 0, 64), wide(near_side, 0, 64)
    below, above = jnp.where(even, x, y), jnp.where(even, y, x)
    low = dot(gmt_last[...], dot(gm_last[...], rise[:64]) * below[:48]) + below[48:]
    high = dot(gmt_first[...], dot(gm_first[...], rise[128:]) * above[:48]) + above[48:]
    flux = dot(gm[...], rise[64:128] + wide(wider, 64, 64)) * wide(g4, 0, 192)
    back = dot(gmt[...], flux)
    put(acc, 0, 16, back[:16] + low)
    put(acc, 16, 32, back[16:48])
    put(acc, 48, 16, back[48:] + high)
    join_mid(acc)
    put(sol, 0, 64, wide(wider, 128, 64) + rise[64:128])
    for h, r in tiles(64):
        now = wider[h, r : r + 8] - acc[h, r : r + 8]
        new = inv4[h, r : r + 8] * now * (1.0 / CENTER)
        res[h, r : r + 8] = now
        u[h, r : r + 8] = new
        sol[h, r : r + 8] += new
    mid_apply(u, g4, acc, gm, gmt)
    join_mid(acc)
    send_faces(acc, even, face_a, face_b, 16)


def sixth_kernel(
    pos, res, u, sol, acc, a, b, inv4, up8, kept, g8, bd, bdt,
    out, v8, acc2, face_a, face_b, y4,
):
    even = is_even(pos, 0)
    for h, r in tiles(64):
        now = res[h, r : r + 8] - full_of(acc, (even, a, b), h, r)
        new = KEEP * u[h, r : r + 8] + GAIN * inv4[h, r : r + 8] * now
        y4[h, r : r + 8] = sol[h, r : r + 8] + new
    put(v8, 0, 512, dot(up8[...], wide(y4, 0, 64)))
    for h, r in tiles(512):
        e8 = v8[h, r : r + 8]
        out[h, r : r + 8] = kept[h, r : r + 8] + e8
        v8[h, r : r + 8] = kept[h, 1024 + r : 1032 + r] + e8
    fine_front(v8, g8, acc2, bd, bdt)
    send_faces(acc2, even, face_a, face_b, 64)


def seventh_kernel(
    pos, kept, sol, acc, a, b, inv8, g8, bd, bdt, res, out, u, acc2, face_a, face_b
):
    even = is_even(pos, 0)
    for h, r in tiles(512):
        now = kept[h, 512 + r : 520 + r] - full_of(acc, (even, a, b), h, r)
        new = inv8[h, r : r + 8] * now * (1.0 / CENTER)
        res[h, r : r + 8] = now
        u[h, r : r + 8] = new
        out[h, r : r + 8] = sol[h, r : r + 8] + new
    fine_front(u, g8, acc2, bd, bdt)
    for out, plane in ((face_b, jnp.where(even, 448, 0)), (face_a, jnp.where(even, 0, 448))):
        rows = pl.ds(pl.multiple_of(plane, 8), 64)
        out[...] = own_part(acc2[0, rows, :], acc2[1, rows, :])


def inner_last_kernel(u, g8, acc, res, sol, inv8, bd, bdt, out, full):
    for h, r in tiles(384):
        full[h, 64 + r : 72 + r] = acc[h, 64 + r : 72 + r]
    fine_cross(u, g8, full, bd, bdt, PLANES[1:])
    join_fine(full, range(1, 7))
    for r in range(64, 448, 8):
        halves = []
        for h in range(2):
            now = res[h, r : r + 8] - full[h, r : r + 8]
            new = KEEP * u[h, r : r + 8] + GAIN * inv8[h, r : r + 8] * now
            halves.append(sol[h, r : r + 8] + new)
        out[r - 64 : r - 56] = own_part(*halves)


def last_kernel(pos, res, sol, u, acc, a, b, inv8, inner, out):
    even = is_even(pos, 0)
    out[64:448] = inner[...]
    for r in [*range(0, 64, 8), *range(448, 512, 8)]:
        halves = []
        for h in range(2):
            inv = inv8[h, r : r + 8]
            now = res[h, r : r + 8] - acc[h, r : r + 8]
            halves.append(sol[h, r : r + 8] + KEEP * u[h, r : r + 8] + GAIN * inv * now)
        at = r % 64
        x, y = a[at : at + 8], b[at : at + 8]
        face = jnp.where(even, x, y) if r < 64 else jnp.where(even, y, x)
        inv = own_part(inv8[0, r : r + 8], inv8[1, r : r + 8])
        out[r : r + 8] = own_part(*halves) - GAIN * inv * face


def call(kernel, args, outs, scratch=(), scalars=1):
    vmem = pl.BlockSpec(memory_space=pltpu.VMEM)
    smem = pl.BlockSpec(memory_space=pltpu.SMEM)
    arrays = [x for x in args if not isinstance(x, str)]
    named = len(arrays) < len(args)

    def body(*refs):
        rest = iter(refs)
        given = [next(rest) for _ in arrays[: len(arrays) - named]]
        held = next(rest) if named else None
        given = iter(given)
        full = [Constant(held, x) if isinstance(x, str) else next(given) for x in args]
        kernel(*full, *rest)

    if named:
        arrays.append(PACK)
    return pl.pallas_call(
        body,
        out_shape=[jax.ShapeDtypeStruct(s, F32) for s in outs],
        in_specs=[smem] * scalars + [vmem] * (len(arrays) - scalars),
        out_specs=[vmem] * len(outs),
        scratch_shapes=[pltpu.VMEM(s, F32) for s in scratch],
        compiler_params=pltpu.CompilerParams(vmem_limit_bytes=32 * 1024 * 1024),
        name=kernel.__name__,
    )(*arrays)


def exchange(far, near, axis):
    size = lax.axis_size(axis)
    pairs_far = [(i, (i + 1 if i % 2 else i - 1) % size) for i in range(size)]
    pairs_near = [(i, i ^ 1) for i in range(size)]
    return lax.ppermute(far, axis, pairs_far), lax.ppermute(near, axis, pairs_near)


def spread(x, axis, groups=None):
    size = len(groups[0]) if groups else lax.axis_size(axis)
    copies = jnp.broadcast_to(x[None], (size,) + x.shape)
    return lax.all_to_all(copies, axis, 0, 0, axis_index_groups=groups).reshape(-1, LANES)


def on_device(element_load, metric, element_order):
    ns, na = lax.axis_size("stream"), lax.axis_size("azim")
    fine, mid = (2, 512, LANES), (2, 64, LANES)
    face8, face4 = [(2, 64, LANES)] * 2, [(2, 16, LANES)] * 2
    pos = jnp.stack([lax.axis_index("stream"), lax.axis_index("azim")]).astype(jnp.int32)
    g, rolled, a, b = call(
        order_kernel,
        (pos, metric.reshape(1536, LANES), element_load.reshape(512, LANES), element_order),
        [(1536, LANES), (512, LANES), (1024, LANES), (1024, LANES)],
    )
    a, b = exchange(a, b, "azim")
    (diag,) = call(own_kernel, (g, "bsq"), [(512, LANES)], scalars=0)

    def inner(u, acc):
        (acc,) = call(inner_kernel, (u, g8, acc, "bd", "bdt"), [fine], (), 0)
        return acc

    g8, load, diag8, a, b = call(
        setup_kernel,
        (pos, g, rolled, diag, a, b, "bsq"),
        [(2, 1536, LANES), fine, fine] + [(2, 128, LANES)] * 2,
        [(1536, LANES), (512, LANES)],
    )
    a, b = exchange(a, b, "stream")
    res8, inv8, u8, acc, a, b = call(
        first_kernel,
        (pos, load, diag8, a, b, g8, "bd", "bdt"),
        [fine, fine, fine, fine] + face8,
    )
    a, b = exchange(a, b, "stream")
    acc = inner(u8, acc)
    g4, diag4, edges, upper = call(
        coarsen_kernel,
        (g8, "w4", "w2", "sample", "sq4"),
        [(2, 192, LANES), mid, (8, LANES), (8, LANES)],
        scalars=0,
    )
    kept, t4, a, b = call(
        second_kernel,
        (pos, res8, inv8, acc, a, b, diag4, upper, g8, "bd", "bdt", "down8"),
        [(2, 1536, LANES), mid] + [(2, 40, LANES)] * 2,
        [fine, fine, (512, 2 * LANES)],
    )
    a, b = exchange(a, b, "stream")
    res4, inv4, edges, acc, a, b = call(
        third_kernel,
        (pos, t4, diag4, edges, a, b, g4, "gm", "gmt"),
        [mid, mid, (8, LANES), mid] + face4,
        [mid],
    )
    a, b = exchange(a, b, "stream")
    corners, *kept4 = call(
        fourth_kernel,
        (pos, res4, acc, inv4, edges, a, b, g4, "gm", "gmt", "m4", "down4"),
        [(8, LANES), (192, LANES), (192, LANES)],
        [(2, 192, LANES), mid],
    )
    columns = spread(corners, "stream")
    a, b = exchange(*kept4, "azim")
    wider, a, b = call(
        side_kernel,
        (pos, *kept4, a, b, g4, "gm", "gmt"),
        [(2, 192, LANES)] + face8,
        [mid],
    )
    sides = exchange(a, b, "stream")
    size = 4 * ns + ns // groups(ns)
    (columns,) = call(
        column_kernel, (columns,), [(size, LANES)], (), 0
    )
    cores = [list(range(core, na, 2)) for core in range(2)]
    columns = spread(columns, "azim", cores)
    others = lax.ppermute(columns, "azim", [(i, i ^ 1) for i in range(na)])
    whole = (ns, na * LANES)
    res4, u4, sol4, acc, a, b = call(
        coarse_kernel,
        (
            pos,
            columns,
            others,
            wider,
            *sides,
            g4,
            inv4,
            "gm",
            "gmt",
            "up4",
            "gm_first",
            "gmt_first",
            "gm_last",
            "gmt_last",
        ),
        [mid, mid, mid, mid] + face4,
        [(16, na * LANES)] + [whole] * 9,
    )
    a, b = exchange(a, b, "stream")
    sol8, v8, acc, a, b = call(
        sixth_kernel,
        (pos, res4, u4, sol4, acc, a, b, inv4, "up8", kept, g8, "bd", "bdt"),
        [fine, fine, fine] + face8,
        [mid],
    )
    a, b = exchange(a, b, "stream")
    acc = inner(v8, acc)
    res8, sol8, u8, acc, a, b = call(
        seventh_kernel,
        (pos, kept, sol8, acc, a, b, inv8, g8, "bd", "bdt"),
        [fine, fine, fine, fine] + [(64, LANES)] * 2,
    )
    a, b = exchange(a, b, "stream")
    (inside,) = call(
        inner_last_kernel,
        (u8, g8, acc, res8, sol8, inv8, "bd", "bdt"),
        [(384, LANES)],
        [fine],
        scalars=0,
    )
    (out,) = call(last_kernel, (pos, res8, sol8, u8, acc, a, b, inv8, inside), [(512, LANES)])
    return out.reshape(element_load.shape)


def solution(mesh):
    placed = (P(None, "stream", "azim"), P(None, None, "stream", "azim"), P("stream", "azim"))
    return jax.shard_map(
        on_device, mesh=mesh, in_specs=placed, out_specs=P(None, "stream", "azim"), check_vma=False
    )
```
